32 devices in a mesh: seq: 4 (over x, core), dp: 8 (over z, y).
Axes of the slice: x: 2, y: 2, z: 4, core: 2. Of those that a mesh axis runs over, the one named last changes fastest.
Arguments:
- long_tokens: bfloat16 [16, 512, 1024], P('dp', 'seq'), may hold values from -6 to 6
- short_tokens: bfloat16 [64, 128, 1024], P(('seq', 'dp')), may hold values from -6 to 6
- long_grad_out: bfloat16 [16, 512, 1024], P('dp', 'seq'), may hold values from -6 to 6
- short_grad_out: bfloat16 [64, 128, 1024], P(('seq', 'dp')), may hold values from -6 to 6
- query_weight: bfloat16 [1024, 1024], P(('seq', 'dp')), may hold values from -0.25 to 0.25
- key_weight: bfloat16 [1024, 1024], P(('seq', 'dp')), may hold values from -0.25 to 0.25
- value_weight: bfloat16 [1024, 1024], P(('seq', 'dp')), may hold values from -0.1875 to 0.1875
- output_weight: bfloat16 [1024, 1024], P(('seq', 'dp')), may hold values from -1 to 1
- attn_gain: bfloat16 [1024], P(('seq', 'dp')), may hold values from 0.25 to 1.75
- ffn_gain: bfloat16 [1024], P(('seq', 'dp')), may hold values from 0.25 to 1.75
- rel_table: bfloat16 [512], P(('seq', 'dp')), may hold values from -4 to 4
- router_weight: bfloat16 [1024, 8], P(('seq', 'dp')), may hold values from -0.375 to 0.375
- gate_weight: bfloat16 [8, 1024, 2816], P('dp', 'seq'), may hold values from -0.1875 to 0.1875
- up_weight: bfloat16 [8, 1024, 2816], P('dp', 'seq'), may hold values from -0.1875 to 0.1875
- down_weight: bfloat16 [8, 1024, 2816], P('dp', 'seq'), may hold values from -0.21875 to 0.21875
- long_positions: int32 [16, 512], P('dp'), may hold values from 0 to 1022, as said below
- short_positions: int32 [64, 128], P(('seq', 'dp')), may hold values from 0 to 254, as said below
- long_lengths: int32 [16], P('dp'), may hold values from 64 to 512, as said below
- short_lengths: int32 [64], P(('seq', 'dp')), may hold values from 16 to 128, as said below
- long_routes: int32 [16, 512, 2], P('dp', 'seq'), may hold values from 0 to 7, all different within a row
- short_routes: int32 [64, 128, 2], P(('seq', 'dp')), may hold values from 0 to 7, all different within a row
Outputs:
- long_out: bfloat16 [16, 512, 1024], P('dp', 'seq')
- short_out: bfloat16 [64, 128, 1024], P(('seq', 'dp'))
- long_grad_in: float32 [16, 512, 1024], P('dp', 'seq')
- short_grad_in: float32 [64, 128, 1024], P(('seq', 'dp'))
- query_grad: float32 [1024, 1024], P(('seq', 'dp'))
- key_grad: float32 [1024, 1024], P(('seq', 'dp'))
- value_grad: float32 [1024, 1024], P(('seq', 'dp'))
- output_grad: float32 [1024, 1024], P(('seq', 'dp'))
- attn_gain_grad: float32 [1024], P(('seq', 'dp'))
- ffn_gain_grad: float32 [1024], P(('seq', 'dp'))
- table_grad: float32 [512], P(('seq', 'dp'))
- router_grad: float32 [1024, 8], P(('seq', 'dp'))
- gate_grad: float32 [8, 1024, 2816], P('dp', 'seq')
- up_grad: float32 [8, 1024, 2816], P('dp', 'seq')
- down_grad: float32 [8, 1024, 2816], P('dp', 'seq')
The draws below stay inside these ranges and needn't reach their ends.
Inputs may be any that keep to these rules, and one draw needn't show every extreme that they name: `long_positions`: in each item the positions start at 0 and rise by 1 or 2 from one token to the next. `short_positions`: in each item the positions start at 0 and rise by 1 or 2 from one token to the next. `long_lengths`: of the 2 long items of each index of dp, one has length 512. `short_lengths`: of the 16 short items of each index of seq, one has length 128.
All inputs are finite; a program needn't handle non-finite values.
Results may differ from the reference program's by a relative error of at most 0.017.
The reference program's roundings to bfloat16 on the way count: a program that leaves them out, or rounds other values in their place, can miss the bound.
Values may be sent and summed in bfloat16 or wider, within the bound.
A program may use at most 256 MiB of HBM per device.

```python
import math
import jax
import jax.numpy as jnp
from jax import lax

D = 1024
HEADS = 16
HEAD = 64
FF = 2816
BUCKETS = 32
LONG_LEN = 512
SHORT_LEN = 128
LONG_DP = 2
SHORT_DEV = 2
EXPERTS = 8
QUARTER = 128
LONG_ITEMS = 16
SHORT_ITEMS = 64
TOK_DEV = 512
CAP = 160
N_SEQ = 4
N_DP = 8
DEVICES = 32


def rising(key, number, length):
    stride_key, widest_key = jax.random.split(key)
    strides = jax.random.randint(stride_key, (number, length), 1, 3, dtype=jnp.int32)
    widest = jax.random.randint(widest_key, (1, 1), 0, number, dtype=jnp.int32)
    strides = jnp.where(jnp.arange(number, dtype=jnp.int32)[:, None] == widest, 2, strides).astype(jnp.int32)
    return jnp.cumsum(strides, axis=1, dtype=jnp.int32) - strides[:, :1]


def ragged(key, number, grouping, longest):
    size_key, pick_key = jax.random.split(key)
    lengths = jax.random.randint(size_key, (number // grouping, grouping), longest // 8, longest + 1, dtype=jnp.int32)
    chosen = jax.random.randint(pick_key, (number // grouping, 1), 0, grouping, dtype=jnp.int32)
    filled = jnp.where(jnp.arange(grouping, dtype=jnp.int32)[None, :] == chosen, longest, lengths)
    return filled.reshape(number)


def draw_long_positions(key, part):
    key = jax.random.fold_in(key, 11)
    return rising(key, LONG_ITEMS, LONG_LEN)


def draw_short_positions(key, part):
    key = jax.random.fold_in(key, 12)
    return rising(key, SHORT_ITEMS, SHORT_LEN)


def draw_long_lengths(key, part):
    key = jax.random.fold_in(key, 13)
    return ragged(key, LONG_ITEMS, LONG_DP, LONG_LEN)


def draw_short_lengths(key, part):
    key = jax.random.fold_in(key, 14)
    return ragged(key, SHORT_ITEMS, SHORT_ITEMS // N_SEQ, SHORT_LEN)


def levels(stream_key, dims, shards, low, top_value):
    level = 1.0
    for axis_at, blocks in shards:
        heights = jax.random.uniform(jax.random.fold_in(jax.random.fold_in(stream_key, 6), axis_at), (blocks,), jnp.float32, low / len(shards), top_value / len(shards))
        level = level * jnp.repeat(jnp.exp(heights), dims[axis_at] // blocks).reshape((-1,) + (1,) * (len(dims) - 1 - axis_at))
    return level


def picks_of(own_key, rows, number_of, top, lift):
    ranking = jax.random.permutation(jax.random.fold_in(own_key, 1), number_of)
    favour = ranking
    for power in range(3):
        favour = favour * favour // number_of
    favour = favour * lift // number_of
    lots = jax.random.randint(jax.random.fold_in(own_key, 2), (rows, number_of), 0, 4096) + favour
    fixed_rows = jax.random.permutation(jax.random.fold_in(own_key, 3), rows)[jnp.arange(number_of) % rows]
    lots = jnp.where(jnp.arange(rows)[:, None] == fixed_rows[None, :], 1 << 14, lots)
    priority = lots * number_of + jnp.arange(number_of)
    return lax.top_k(priority.astype(jnp.int32), top)[1].astype(jnp.int32)


def gaussian(stream_key, shape, deviation, bound, cuts=(), kind=jnp.bfloat16):
    entries = deviation * jax.random.normal(stream_key, shape, jnp.float32)
    if cuts:
        entries = entries * levels(stream_key, shape, cuts, -0.22, 0.18)
    return jnp.clip(entries, -bound, bound).astype(kind)


def setup_inputs(seed: int = 0) -> dict:
    arg_keys = jax.random.split(jax.random.key(seed), 22)
    return {
        "long_tokens": gaussian(arg_keys[0], (LONG_ITEMS, LONG_LEN, D), 1.0, 6.0, ((0, 8), (1, 4))),
        "short_tokens": gaussian(arg_keys[1], (SHORT_ITEMS, SHORT_LEN, D), 1.0, 6.0, ((0, 32),)),
        "long_grad_out": gaussian(arg_keys[2], (LONG_ITEMS, LONG_LEN, D), 1.0, 6.0, ((0, 8), (1, 4))),
        "short_grad_out": gaussian(arg_keys[3], (SHORT_ITEMS, SHORT_LEN, D), 1.0, 6.0, ((0, 32),)),
        "query_weight": gaussian(arg_keys[4], (D, D), (0.5 * D ** -0.5), 0.25, ((0, 32),)),
        "key_weight": gaussian(arg_keys[5], (D, D), (0.5 * D ** -0.5), 0.25, ((0, 32),)),
        "value_weight": gaussian(arg_keys[6], (D, D), D ** -0.5, 0.1875, ((0, 32),)),
        "output_weight": gaussian(arg_keys[7], (D, D), (D // 32) ** -0.5, 1.0, ((0, 32),)),
        "attn_gain": jnp.clip(1.0 + 0.15 * jax.random.normal(arg_keys[8], (D,), jnp.float32), 0.25, 1.75).astype(jnp.bfloat16),
        "ffn_gain": jnp.clip(1.0 + 0.15 * jax.random.normal(arg_keys[9], (D,), jnp.float32), 0.25, 1.75).astype(jnp.bfloat16),
        "rel_table": gaussian(arg_keys[10], (HEADS * BUCKETS,), 1.0, 4.0, ((0, 32),)),
        "router_weight": gaussian(arg_keys[11], (D, EXPERTS), (0.75 * D ** -0.5), 0.375, ((0, 32),)),
        "gate_weight": gaussian(arg_keys[12], (EXPERTS, D, FF), D ** -0.5, 0.1875, ((0, 8), (1, 4))),
        "up_weight": gaussian(arg_keys[13], (EXPERTS, D, FF), D ** -0.5, 0.1875, ((0, 8), (1, 4))),
        "down_weight": gaussian(arg_keys[14], (EXPERTS, D, FF), (FF // 4) ** -0.5, 0.21875, ((0, 8), (1, 4))),
        "long_positions": draw_long_positions(jax.random.fold_in(arg_keys[21], 71), 0),
        "short_positions": draw_short_positions(jax.random.fold_in(arg_keys[21], 71), 0),
        "long_lengths": draw_long_lengths(jax.random.fold_in(arg_keys[21], 71), 0),
        "short_lengths": draw_short_lengths(jax.random.fold_in(arg_keys[21], 71), 0),
        "long_routes": picks_of(arg_keys[19], LONG_ITEMS * LONG_LEN, EXPERTS, 2, 2048).reshape((LONG_ITEMS, LONG_LEN, 2)),
        "short_routes": picks_of(arg_keys[20], SHORT_ITEMS * SHORT_LEN, EXPERTS, 2, 2048).reshape((SHORT_ITEMS, SHORT_LEN, 2)),
    }


@jax.custom_vjp
def low(v):
    return lax.optimization_barrier(v.astype(jnp.bfloat16)).astype(jnp.float32)

@jax.custom_vjp
def low_back(v):
    return v

def low_keep(v):
    return (low(v), None)

def low_pass(kept, grad):
    return (grad,)

def back_keep(v):
    return (v, None)

def back_low(kept, grad):
    return (low(grad),)
low.defvjp(low_keep, low_pass)
low_back.defvjp(back_keep, back_low)
far_edges = (12, 16, 23, 32, 46, 64, 91)
epsilon = 1e-06
masked = -1e+30
highest = lax.Precision.HIGHEST

def low_both(tensor):
    return low_back(low(tensor))

def bucket_of(query_pos, key_pos):
    offset = key_pos[..., None, :] - query_pos[..., :, None]
    distance = jnp.abs(offset)
    beyond = jnp.zeros_like(distance)
    for border in far_edges:
        beyond = beyond + (distance >= border).astype(jnp.int32)
    inner = jnp.where(distance < 8, distance, 8 + beyond)
    return (inner + jnp.where(offset > 0, BUCKETS // 2, 0)).astype(jnp.int32)

def rms_norm(hidden, gain):
    scale = lax.rsqrt(lax.optimization_barrier(jnp.mean(hidden * hidden, axis=-1, keepdims=True)) + epsilon)
    return hidden * scale * gain

def gelu_mul(gate_pre, up_pre):
    return jax.nn.gelu(gate_pre, approximate=True) * up_pre

def gate_values(logits, choose):
    probs = jax.nn.softmax(logits, axis=-1)
    chosen = lax.optimization_barrier(jnp.sum(choose * probs[:, None, :], axis=-1))
    return chosen / lax.optimization_barrier(jnp.sum(chosen, axis=-1, keepdims=True))

def attend(normed, positions, lengths, projections, bias_table):
    item_count, seq_len = (normed.shape[0], normed.shape[1])
    heads_shape = (item_count, seq_len, HEADS, HEAD)
    queries = low_both(jnp.einsum('bld,de->ble', normed, projections[0], precision=highest)).reshape(heads_shape)
    key_rows = low_both(jnp.einsum('bld,de->ble', normed, projections[1], precision=highest)).reshape(heads_shape)
    value_rows = low_both(jnp.einsum('bld,de->ble', normed, projections[2], precision=highest)).reshape(heads_shape)
    scores = jnp.einsum('bqhd,bkhd->bhqk', queries, key_rows, precision=highest)
    rel_bias = jnp.moveaxis(jnp.take(bias_table, bucket_of(positions, positions), axis=1), 0, 1)
    scores = low_back(scores + rel_bias)
    key_ok = jnp.arange(seq_len, dtype=jnp.int32)[None, :] < lengths[:, None]
    scores = jnp.where(key_ok[:, None, None, :], scores, masked)
    probs = low(jax.nn.softmax(scores, axis=-1))
    mixed = jnp.einsum('bhqk,bkhd->bqhd', probs, value_rows, precision=highest)
    return low_both(mixed).reshape(item_count, seq_len, HEADS * HEAD)

def by_groups(normed, positions, lengths, projections, bias_table):
    group_size = math.gcd(normed.shape[0], max(1, 4096 // normed.shape[1]))
    blocks = normed.shape[0] // group_size
    packed = (normed.reshape(blocks, group_size, normed.shape[1], normed.shape[2]), positions.reshape(blocks, group_size, positions.shape[1]), lengths.reshape(blocks, group_size))

    def advance(pack):
        return attend(pack[0], pack[1], pack[2], projections, bias_table)
    result = lax.map(jax.checkpoint(advance), packed)
    return result.reshape(normed.shape)

def expert_apply(pack):
    inputs, gate_matrix, up_matrix, down_matrix = pack
    gate_pre = low_back(jnp.dot(inputs, gate_matrix, precision=highest))
    up_pre = low_back(jnp.dot(inputs, up_matrix, precision=highest))
    hidden = low(gelu_mul(gate_pre, up_pre))
    return low_both(jnp.einsum('rf,df->rd', hidden, down_matrix, precision=highest))

def to_devices(long_rows, short_rows):
    lead = long_rows.reshape(N_DP, LONG_DP, N_SEQ, QUARTER, -1)
    lead = jnp.transpose(lead, (2, 0, 1, 3, 4)).reshape(N_SEQ, N_DP, LONG_DP * QUARTER, -1)
    trail = short_rows.reshape(N_SEQ, N_DP, SHORT_DEV * SHORT_LEN, -1)
    return jnp.concatenate([lead, trail], axis=2).reshape(N_SEQ * N_DP * TOK_DEV, -1)

def from_devices(rows):
    last_dim = rows.shape[-1]
    stacked = rows.reshape(N_SEQ, N_DP, TOK_DEV, last_dim)
    lead = stacked[:, :, :LONG_DP * QUARTER].reshape(N_SEQ, N_DP, LONG_DP, QUARTER, last_dim)
    lead = jnp.transpose(lead, (1, 2, 0, 3, 4)).reshape(LONG_ITEMS, LONG_LEN, last_dim)
    trail = stacked[:, :, LONG_DP * QUARTER:].reshape(SHORT_ITEMS, SHORT_LEN, last_dim)
    return (lead, trail)

def reference(long_tokens, short_tokens, long_grad_out, short_grad_out, query_weight, key_weight, value_weight, output_weight, attn_gain, ffn_gain, rel_table, router_weight, gate_weight, up_weight, down_weight, long_positions, short_positions, long_lengths, short_lengths, long_routes, short_routes):
    routes = to_devices(long_routes, short_routes).reshape(DEVICES, TOK_DEV * 2)
    member = (routes[..., None] == jnp.arange(EXPERTS, dtype=jnp.int32)).astype(jnp.int32)
    queue_pos = lax.optimization_barrier(jnp.sum(jnp.cumsum(member, axis=1) * member, axis=2)) - 1
    route_kept = queue_pos < CAP
    device_ids = jnp.arange(DEVICES, dtype=jnp.int32)[:, None]
    total_slots = EXPERTS * DEVICES * CAP
    slot_index = jnp.where(route_kept, routes * (DEVICES * CAP) + device_ids * CAP + queue_pos, total_slots).reshape(-1).astype(jnp.int32)
    pair_ids = (device_ids * (TOK_DEV * 2) + jnp.arange(TOK_DEV * 2, dtype=jnp.int32)[None, :]).reshape(-1).astype(jnp.int32)
    slot_pair = jnp.zeros(total_slots + 1, jnp.int32).at[slot_index].set(pair_ids)[:-1]
    slot_used = jnp.zeros(total_slots + 1, jnp.float32).at[slot_index].set(1.0)[:-1]
    pair_slot = jnp.where(route_kept.reshape(-1), slot_index, 0).astype(jnp.int32)
    kept_two = route_kept.reshape(-1, 2).astype(jnp.float32)
    choose = (routes.reshape(-1, 2)[..., None] == jnp.arange(EXPERTS, dtype=jnp.int32)).astype(jnp.float32)

    def forward(long_in, short_in, q_matrix, k_matrix, v_matrix, o_matrix, gain_one, gain_two, table_flat, router, gate_all, up_all, down_all):
        bias_table = table_flat.reshape(HEADS, BUCKETS)
        projections = (q_matrix, k_matrix, v_matrix)
        long_norm = low(rms_norm(long_in, gain_one))
        short_norm = low(rms_norm(short_in, gain_one))
        long_mix = by_groups(long_norm, long_positions, long_lengths, projections, bias_table)
        short_mix = by_groups(short_norm, short_positions, short_lengths, projections, bias_table)
        long_mid = long_in + low_back(jnp.einsum('bld,de->ble', long_mix, o_matrix, precision=highest))
        short_mid = short_in + low_back(jnp.einsum('bld,de->ble', short_mix, o_matrix, precision=highest))
        middle = to_devices(long_mid, short_mid)
        normed_two = low(rms_norm(middle, gain_two))
        logits = low_back(jnp.dot(normed_two, router, precision=highest))
        gate_share = gate_values(logits, choose) * kept_two
        inputs = low_back(jnp.take(normed_two, slot_pair // 2, axis=0) * slot_used[:, None])
        expert_rows = lax.map(jax.checkpoint(expert_apply), (inputs.reshape(EXPERTS, DEVICES * CAP, D), gate_all, up_all, down_all))
        pair_out = jnp.take(expert_rows.reshape(total_slots, D), pair_slot, axis=0).reshape(-1, 2, D)
        final = middle + gate_share[:, 0:1] * pair_out[:, 0] + gate_share[:, 1:2] * pair_out[:, 1]
        return from_devices(final)
    floats = [source.astype(jnp.float32) for source in (long_tokens, short_tokens, query_weight, key_weight, value_weight, output_weight, attn_gain, ffn_gain, rel_table, router_weight, gate_weight, up_weight, down_weight)]
    results, pullback = jax.vjp(forward, *floats)
    gradients = pullback((long_grad_out.astype(jnp.float32), short_grad_out.astype(jnp.float32)))
    return (results[0].astype(jnp.bfloat16), results[1].astype(jnp.bfloat16), gradients[0], gradients[1], gradients[2], gradients[3], gradients[4], gradients[5], gradients[6], gradients[7], gradients[8], gradients[9], gradients[10], gradients[11], gradients[12])
```

```python
import functools

import jax
import jax.numpy as jnp
from jax import lax
from jax.experimental import pallas as pl
from jax.experimental.pallas import tpu as pltpu
from jax.sharding import PartitionSpec as P

MESH = pl.DeviceIdType.MESH

HEADS = 16
HEAD = 64
BUCKETS = 32


far_edges = (12, 16, 23, 32, 46, 64, 91)
epsilon = 1e-06
masked = -1e30


def bucket_of(query_pos, key_pos):
    offset = key_pos[..., None, :] - query_pos[..., :, None]
    distance = jnp.abs(offset)
    beyond = jnp.zeros_like(distance)
    for border in far_edges:
        beyond = beyond + (distance >= border).astype(jnp.int32)
    inner = jnp.where(distance < 8, distance, 8 + beyond)
    return inner + jnp.where(offset > 0, BUCKETS // 2, 0)


def rms_norm(hidden, gain):
    scale = lax.rsqrt(jnp.mean(hidden * hidden, axis=-1, keepdims=True) + epsilon)
    return hidden * scale * gain


def gelu_mul(gate_pre, up_pre):
    return jax.nn.gelu(gate_pre, approximate=True) * up_pre


def gate_values(logits, choose):
    probs = jax.nn.softmax(logits, axis=-1)
    chosen = jnp.sum(choose * probs[:, None, :], axis=-1)
    return chosen / jnp.sum(chosen, axis=-1, keepdims=True)


def score_block(queries, key_rows, query_pos, key_pos, key_ok, bias_table):
    batch_size, rows, model_width = queries.shape
    columns = key_rows.shape[1]
    scores = jnp.einsum(
        "bqhd,bkhd->bhqk",
        queries.reshape(batch_size, rows, HEADS, HEAD),
        key_rows.reshape(batch_size, columns, HEADS, HEAD),
        preferred_element_type=jnp.float32,
    )
    onehot = (
        bucket_of(query_pos, key_pos)[..., None] == jnp.arange(BUCKETS, dtype=jnp.int32)
    ).astype(jnp.bfloat16)
    rel_bias = jnp.einsum("bqkn,hn->bhqk", onehot, bias_table, preferred_element_type=jnp.float32)
    return (jnp.where(key_ok[:, None, None, :], scores + rel_bias, masked), onehot)


def attention_forward(queries, key_rows, value_rows, query_pos, key_pos, key_ok, bias_table):
    scores, onehot = score_block(queries, key_rows, query_pos, key_pos, key_ok, bias_table)
    batch_size, rows, model_width = queries.shape
    columns = key_rows.shape[1]
    row_peak = jnp.max(scores, axis=-1, keepdims=True)
    lifted = jnp.exp(scores - row_peak)
    row_total = jnp.sum(lifted, axis=-1, keepdims=True)
    probs = lifted / row_total
    mixed = jnp.einsum(
        "bhqk,bkhd->bqhd",
        probs.astype(jnp.bfloat16),
        value_rows.reshape(batch_size, columns, HEADS, HEAD),
        preferred_element_type=jnp.float32,
    )
    return (
        mixed.astype(jnp.bfloat16).reshape(batch_size, rows, model_width),
        (row_peak + jnp.log(row_total))[..., 0],
    )


def attention_backward(
    queries, key_rows, value_rows, mixed_grad, log_total, query_pos, key_pos, key_ok, bias_table
):
    scores, onehot = score_block(queries, key_rows, query_pos, key_pos, key_ok, bias_table)
    batch_size, rows, model_width = queries.shape
    columns = key_rows.shape[1]
    probs = jnp.exp(scores - log_total[..., None])
    grad_four = mixed_grad.reshape(batch_size, rows, HEADS, HEAD)
    value_four = value_rows.reshape(batch_size, columns, HEADS, HEAD)
    query_four = queries.reshape(batch_size, rows, HEADS, HEAD)
    key_four = key_rows.reshape(batch_size, columns, HEADS, HEAD)
    prob_grad = jnp.einsum(
        "bqhd,bkhd->bhqk", grad_four, value_four, preferred_element_type=jnp.float32
    )
    score_grad = (probs * (prob_grad - jnp.sum(probs * prob_grad, axis=-1, keepdims=True))).astype(
        jnp.bfloat16
    )
    query_part = jnp.einsum(
        "bhqk,bkhd->bqhd", score_grad, key_four, preferred_element_type=jnp.float32
    ).reshape(batch_size, rows, model_width)
    key_part = jnp.einsum(
        "bhqk,bqhd->bkhd", score_grad, query_four, preferred_element_type=jnp.float32
    ).reshape(batch_size, columns, model_width)
    value_part = jnp.einsum(
        "bhqk,bqhd->bkhd", probs.astype(jnp.bfloat16), grad_four, preferred_element_type=jnp.float32
    ).reshape(batch_size, columns, model_width)
    table_part = jnp.einsum("bhqk,bqkn->hn", score_grad, onehot, preferred_element_type=jnp.float32)
    return (query_part, key_part, value_part, table_part)


def gather_kernel(dims, pieces, na, *refs):
    X, C, Z, Y = dims
    n = len(pieces)
    lsem, zs, zr, hs, hr, cs, cr = refs[2*na:]
    routes = [p[3] for p in pieces]
    ins = [refs[m].at[pl.ds(r0, nr)] for m, r0, nr, _ in pieces]
    class V:
        def __init__(self, ref, r0, nr): self.ref, self.r0, self.nr = ref, r0, nr
        @property
        def at(self): return self
        def __getitem__(self, k):
            k = k + (slice(None),) * (4 - len(k)) + (pl.ds(self.r0, self.nr),)
            return self.ref.at[k]
    outs = [V(refs[na + m], r0, nr) for m, r0, nr, _ in pieces]
    s = lax.axis_index("seq"); g = lax.axis_index("dp")
    x, c = s // C, lax.rem(s, C)
    z, y = g // Y, lax.rem(g, Y)
    def zdev(k): return (s, lax.rem(z + k, Z) * Y + y)
    ydev = (s, z * Y + (1 - y)); xdev = ((1 - x) * C + c, g); cdev = (x * C + 1 - c, g)
    bar = pltpu.get_barrier_semaphore()
    for d in [zdev(k) for k in range(1, Z)] + [ydev, xdev, cdev]:
        pl.semaphore_signal(bar, inc=1, device_id=d, device_id_type=MESH)
    pl.semaphore_wait(bar, Z + 2)
    def rc(src, dst, ss, rs, dev):
        cp = pltpu.make_async_remote_copy(src_ref=src, dst_ref=dst, send_sem=ss, recv_sem=rs, device_id=dev, device_id_type=MESH)
        cp.start(); return cp
    sends = []
    local = []; zc = []
    for m in range(n):
        lc = pltpu.make_async_copy(ins[m], outs[m].at[x, c, z, y], lsem.at[m]); lc.start(); local.append(lc)
        zc.append([rc(ins[m], outs[m].at[x, c, z, y], zs.at[m, k], zr.at[m, k], zdev(k)) for k in range(1, Z)])
    h = [[None, None] for _ in range(n)]
    cc = [[None]*3 for _ in range(n)]
    for t in range(n + 2):
        for stage in range(3):
            m = t - stage
            if not 0 <= m < n: continue
            o = outs[m]; route = routes[m]
            if stage == 0:
                local[m].wait()
                for q in zc[m]: q.wait_recv()
                mine = o.at[x, c, :, y]
                h[m][0] = rc(mine, mine, hs.at[m,0], hr.at[m,0], xdev if route == 0 else ydev)
                cc[m][0] = rc(mine, mine, cs.at[m,0], cr.at[m,0], cdev)
            elif stage == 1:
                h[m][0].wait_recv()
                if route == 0:
                    both = o.at[:, c, :, y]; got = o.at[1 - x, c, :, y]
                else:
                    both = o.at[x, c]; got = o.at[x, c, :, 1 - y]
                h[m][1] = rc(both, both, hs.at[m,1], hr.at[m,1], ydev if route == 0 else xdev)
                cc[m][1] = rc(got, got, cs.at[m,1], cr.at[m,1], cdev)
            else:
                h[m][1].wait_recv()
                got = o.at[:, c, :, 1 - y] if route == 0 else o.at[1 - x, c]
                cc[m][2] = rc(got, got, cs.at[m,2], cr.at[m,2], cdev)
    for m in range(n):
        for q in zc[m]: q.wait_send()
        for q in h[m]: q.wait_send()
        for q in cc[m]: q.wait()
def gather_all(arrays, pieces, dims, cid):
    X, C, Z, Y = dims; na = len(arrays); n = len(pieces)
    sem = pltpu.SemaphoreType.DMA
    return pl.pallas_call(functools.partial(gather_kernel, dims, pieces, na),
        out_shape=[jax.ShapeDtypeStruct((X, C, Z, Y) + a.shape, a.dtype) for a in arrays],
        in_specs=[pl.BlockSpec(memory_space=pl.ANY)] * na, out_specs=[pl.BlockSpec(memory_space=pl.ANY)] * na,
        scratch_shapes=[sem((n,)), sem((n, Z)), sem((n, Z)), sem((n, 2)), sem((n, 2)), sem((n, 3)), sem((n, 3))],
        compiler_params=pltpu.CompilerParams(collective_id=cid, has_side_effects=True))(*arrays)


def scatter_kernel(dims, pieces, n, *refs):
    X, C, Z, Y = dims
    ins, outs = refs[:n], refs[n:2*n]
    np_ = len(pieces)
    bufs = refs[2*n:2*n+7*np_]
    sems = refs[2*n+7*np_:]
    cs, cr, hs, hr, zs, zr = sems
    s = lax.axis_index("seq"); g = lax.axis_index("dp")
    x, c = s // C, lax.rem(s, C)
    z, y = g // Y, lax.rem(g, Y)
    def zdev(k): return (s, lax.rem(z + k, Z) * Y + y)
    ydev = (s, z * Y + (1 - y)); xdev = ((1 - x) * C + c, g); cdev = (x * C + 1 - c, g)
    bar = pltpu.get_barrier_semaphore()
    for d in [zdev(k) for k in range(1, Z)] + [ydev, xdev, cdev]:
        pl.semaphore_signal(bar, inc=1, device_id=d, device_id_type=MESH)
    pl.semaphore_wait(bar, Z + 2)
    def rc(src, dst, ss, rs, dev):
        cp = pltpu.make_async_remote_copy(src_ref=src, dst_ref=dst, send_sem=ss, recv_sem=rs, device_id=dev, device_id_type=MESH)
        cp.start(); return cp
    def add(dst, a, b):
        dst[...] = (a.astype(jnp.float32) + b.astype(jnp.float32)).astype(dst.dtype)
    first = []
    for i, (m, r0, nr, route) in enumerate(pieces):
        cb = bufs[7*i]
        src = ins[m].at[:, 1 - c, :, :, pl.ds(r0, nr)]
        first.append(rc(src, cb, cs.at[i], cr.at[i], cdev))
    hh = [[None, None] for _ in pieces]; zz = [None] * np_
    for t in range(np_ + 3):
        for stage in range(4):
            i = t - stage
            if not 0 <= i < np_: continue
            m, r0, nr, route = pieces[i]
            cb, a1, b1, a2, b2, a3, b3 = bufs[7*i:7*i+7]
            if stage == 0:
                first[i].wait_recv()
                add(a1, ins[m][:, c, :, :, pl.ds(r0, nr)], cb[...])
                src = a1.at[:, :, 1 - y] if route == 0 else a1.at[1 - x]
                hh[i][0] = rc(src, b1, hs.at[i, 0], hr.at[i, 0], ydev if route == 0 else xdev)
            elif stage == 1:
                hh[i][0].wait_recv()
                add(a2, a1[:, :, y] if route == 0 else a1[x], b1[...])
                src = a2.at[1 - x] if route == 0 else a2.at[:, 1 - y]
                hh[i][1] = rc(src, b2, hs.at[i, 1], hr.at[i, 1], xdev if route == 0 else ydev)
            elif stage == 2:
                hh[i][1].wait_recv()
                add(a3, a2[x] if route == 0 else a2[:, y], b2[...])
                zz[i] = [rc(a3.at[lax.rem(z + k, Z)], b3.at[k - 1], zs.at[i, k], zr.at[i, k], zdev(k)) for k in range(1, Z)]
            else:
                tot = a3[z].astype(jnp.float32)
                for k in range(1, Z):
                    zz[i][k-1].wait_recv()
                    tot += b3[k - 1].astype(jnp.float32)
                outs[m][pl.ds(r0, nr), :] = tot
    for i in range(np_):
        first[i].wait_send()
        for q in hh[i]: q.wait_send()
        for q in zz[i]: q.wait_send()
def scatter_all(arrays, pieces, dims, cid):
    X, C, Z, Y = dims; n = len(arrays); q = len(pieces)
    sem = pltpu.SemaphoreType.DMA
    scr = []
    for m, r0, nr, route in pieces:
        w = arrays[m].shape[-1]; dt = arrays[m].dtype
        h1 = (X, Z) if route == 0 else (Z, Y)
        for lead in ((X, Z, Y), (X, Z, Y), h1, h1, (Z,), (Z,), (Z - 1,)):
            scr.append(pltpu.VMEM(lead + (nr, w), dt))
    return pl.pallas_call(functools.partial(scatter_kernel, dims, pieces, n),
        out_shape=[jax.ShapeDtypeStruct(a.shape[-2:], jnp.float32) for a in arrays],
        in_specs=[pl.BlockSpec(memory_space=pltpu.VMEM)] * n, out_specs=[pl.BlockSpec(memory_space=pltpu.VMEM)] * n,
        scratch_shapes=scr + [sem((q,)), sem((q,)), sem((q, 2)), sem((q, 2)), sem((q, Z)), sem((q, Z))],
        compiler_params=pltpu.CompilerParams(collective_id=cid, has_side_effects=True, vmem_limit_bytes=48*2**20))(*arrays)


def on_device(
    long_tokens,
    short_tokens,
    long_grad_out,
    short_grad_out,
    query_weight,
    key_weight,
    value_weight,
    output_weight,
    attn_gain,
    ffn_gain,
    rel_table,
    router_weight,
    gate_weight,
    up_weight,
    down_weight,
    long_positions,
    short_positions,
    long_lengths,
    short_lengths,
    long_routes,
    short_routes,
):
    long_items, quarter, model_width = long_tokens.shape
    short_items, short_len = (short_tokens.shape[0], short_tokens.shape[1])
    long_rows = long_items * quarter
    tokens = long_rows + short_items * short_len
    local_experts = gate_weight.shape[0]
    dp_size = lax.axis_size("dp")
    experts = local_experts * dp_size
    capacity = (5 * tokens + 2 * experts - 1) // (2 * experts)
    seq_index = lax.axis_index("seq")
    seq_size = lax.axis_size("seq")
    dims = (seq_size // 2, 2, dp_size // 2, 2)
    devices = seq_size * dp_size
    table_part, router_part = rel_table.shape[0], router_weight.size
    gain_part = attn_gain.shape[0]
    small_size = 2 * gain_part + table_part + router_part
    small = jnp.concatenate([attn_gain, ffn_gain, rel_table, router_weight.reshape(-1)])
    small = jnp.pad(small, (0, -small_size % 2048)).reshape(-1, 128)
    rows_part = query_weight.shape[0]
    cuts = 2 if rows_part % 32 == 0 else 1
    cut = rows_part // cuts
    pieces = tuple((m, h * cut, cut, (m + h) % 2) for m in range(4) for h in range(cuts))
    gathered = gather_all(
        (query_weight, key_weight, value_weight, output_weight, small),
        pieces[: 3 * cuts] + ((4, 0, small.shape[0], 0),) + pieces[3 * cuts :],
        dims,
        0,
    )
    small_all = gathered[4].reshape(devices, -1)
    attn_set = tuple(block.reshape(devices * rows_part, model_width) for block in gathered[:4]) + (
        small_all[:, :gain_part].reshape(-1),
        small_all[:, gain_part : 2 * gain_part].reshape(-1),
        small_all[:, 2 * gain_part : 2 * gain_part + table_part].reshape(-1),
        small_all[:, 2 * gain_part + table_part : small_size].reshape(model_width, experts),
    )
    expert_set = (
        lax.all_gather(gate_weight, "seq", axis=1, tiled=True),
        lax.all_gather(up_weight, "seq", axis=1, tiled=True),
        lax.all_gather(down_weight, "seq", axis=1, tiled=True),
    )
    resid_in = jnp.concatenate(
        [long_tokens.reshape(long_rows, model_width), short_tokens.reshape(-1, model_width)], 0
    ).astype(jnp.float32)
    gain_first = attn_set[4].astype(jnp.float32)
    normed = rms_norm(resid_in, gain_first).astype(jnp.bfloat16)
    projected = [
        jnp.dot(normed, matrix, preferred_element_type=jnp.float32).astype(jnp.bfloat16)
        for matrix in attn_set[:3]
    ]
    long_q, long_k, long_v = [
        block[:long_rows].reshape(long_items, quarter, model_width) for block in projected
    ]
    short_q, short_k, short_v = [
        block[long_rows:].reshape(short_items, short_len, model_width) for block in projected
    ]
    bias_table = attn_set[6].reshape(HEADS, BUCKETS)
    long_keys, long_values = (
        lax.all_gather(long_k, "seq", axis=1, tiled=True),
        lax.all_gather(long_v, "seq", axis=1, tiled=True),
    )
    key_span = long_keys.shape[1]
    query_pos = lax.dynamic_slice_in_dim(long_positions, seq_index * quarter, quarter, 1)
    long_ok = jnp.arange(key_span, dtype=jnp.int32)[None, :] < long_lengths[:, None]
    short_ok = jnp.arange(short_len, dtype=jnp.int32)[None, :] < short_lengths[:, None]
    long_mix, long_lse = attention_forward(
        long_q, long_keys, long_values, query_pos, long_positions, long_ok, bias_table
    )
    short_mix, short_lse = attention_forward(
        short_q, short_k, short_v, short_positions, short_positions, short_ok, bias_table
    )
    mixed_all = jnp.concatenate(
        [long_mix.reshape(long_rows, model_width), short_mix.reshape(-1, model_width)], 0
    )
    resid_mid = resid_in + jnp.dot(mixed_all, attn_set[3], preferred_element_type=jnp.float32)
    gain_second = attn_set[5].astype(jnp.float32)
    normed_two = rms_norm(resid_mid, gain_second).astype(jnp.bfloat16)
    logits = jnp.dot(normed_two, attn_set[7], preferred_element_type=jnp.float32)
    routes = jnp.concatenate([long_routes.reshape(-1, 2), short_routes.reshape(-1, 2)], 0)
    choose = (routes[..., None] == jnp.arange(experts, dtype=jnp.int32)).astype(jnp.float32)
    gate_share, gate_pull = jax.vjp(lambda logit_in: gate_values(logit_in, choose), logits)
    flat_routes = routes.reshape(-1)
    member = (flat_routes[:, None] == jnp.arange(experts, dtype=jnp.int32)).astype(jnp.int32)
    queue_pos = jnp.sum(jnp.cumsum(member, axis=0) * member, axis=1) - 1
    route_kept = queue_pos < capacity
    slot_index = jnp.where(route_kept, flat_routes * capacity + queue_pos, experts * capacity)
    slot_pair = (
        jnp.zeros(experts * capacity + 1, jnp.int32)
        .at[slot_index]
        .set(jnp.arange(2 * tokens, dtype=jnp.int32))[:-1]
    )
    slot_used = jnp.zeros(experts * capacity + 1, jnp.bool_).at[slot_index].set(True)[:-1]
    pair_slot = jnp.where(route_kept, slot_index, 0)
    outgoing = jnp.where(
        slot_used[:, None], jnp.take(normed_two, slot_pair // 2, axis=0), 0
    ).reshape(experts, capacity, model_width)
    gate_full, up_full, down_full = expert_set
    arrived = lax.all_to_all(outgoing, "dp", split_axis=0, concat_axis=0, tiled=True)
    slot_count = arrived.shape[1]
    inputs = arrived.reshape(dp_size, local_experts, slot_count, model_width)
    gate_pre = jnp.einsum("slcd,ldf->slcf", inputs, gate_full, preferred_element_type=jnp.float32)
    up_pre = jnp.einsum("slcd,ldf->slcf", inputs, up_full, preferred_element_type=jnp.float32)
    hidden = gelu_mul(gate_pre, up_pre).astype(jnp.bfloat16)
    result = jnp.einsum(
        "slcf,ldf->slcd", hidden, down_full, preferred_element_type=jnp.float32
    ).astype(jnp.bfloat16)
    returned = lax.all_to_all(
        result.reshape(experts, slot_count, model_width),
        "dp",
        split_axis=0,
        concat_axis=0,
        tiled=True,
    )
    ffn_width = hidden.shape[-1]
    back_rows, expert_in, gate_pre, up_pre, hidden = (
        returned,
        arrived,
        gate_pre.reshape(experts, slot_count, ffn_width),
        up_pre.reshape(experts, slot_count, ffn_width),
        hidden.reshape(experts, slot_count, ffn_width),
    )
    pair_out = (
        jnp.where(
            route_kept[:, None],
            jnp.take(back_rows.reshape(experts * capacity, model_width), pair_slot, axis=0),
            0,
        )
        .reshape(tokens, 2, model_width)
        .astype(jnp.float32)
    )
    kept_two = route_kept.reshape(tokens, 2).astype(jnp.float32)
    weighting = gate_share * kept_two
    final = resid_mid + weighting[:, 0:1] * pair_out[:, 0] + weighting[:, 1:2] * pair_out[:, 1]
    final_low = final.astype(jnp.bfloat16)
    long_out = final_low[:long_rows].reshape(long_items, quarter, model_width)
    short_out = final_low[long_rows:].reshape(short_items, short_len, model_width)
    grad_out = jnp.concatenate(
        [long_grad_out.reshape(long_rows, model_width), short_grad_out.reshape(-1, model_width)], 0
    ).astype(jnp.float32)
    pair_grad = (
        (weighting[:, :, None] * grad_out[:, None, :])
        .astype(jnp.bfloat16)
        .reshape(2 * tokens, model_width)
    )
    share_grad = kept_two * jnp.sum(grad_out[:, None, :] * pair_out, axis=-1)
    logit_grad = gate_pull(share_grad)[0].astype(jnp.bfloat16)
    out_slots = jnp.where(slot_used[:, None], jnp.take(pair_grad, slot_pair, axis=0), 0).reshape(
        experts, capacity, model_width
    )
    attn_back, expert_back = attn_set, expert_set
    gate_back, up_back, down_back = expert_back
    arrived_grad = lax.all_to_all(out_slots, "dp", split_axis=0, concat_axis=0, tiled=True)
    shape_four = (dp_size, local_experts, capacity, -1)
    grad_four = arrived_grad.reshape(dp_size, local_experts, capacity, model_width)
    hidden_grad = jnp.einsum(
        "slcd,ldf->slcf", grad_four, down_back, preferred_element_type=jnp.float32
    )
    unused_geglu, geglu_pull = jax.vjp(
        gelu_mul, gate_pre.reshape(shape_four), up_pre.reshape(shape_four)
    )
    gate_pre_grad, up_pre_grad = geglu_pull(hidden_grad)
    gate_pre_grad = gate_pre_grad.astype(jnp.bfloat16)
    up_pre_grad = up_pre_grad.astype(jnp.bfloat16)
    input_grad = (
        jnp.einsum("slcf,ldf->slcd", gate_pre_grad, gate_back, preferred_element_type=jnp.float32)
        + jnp.einsum("slcf,ldf->slcd", up_pre_grad, up_back, preferred_element_type=jnp.float32)
    ).astype(jnp.bfloat16)
    returned_grad = lax.all_to_all(
        input_grad.reshape(experts, capacity, model_width),
        "dp",
        split_axis=0,
        concat_axis=0,
        tiled=True,
    )
    inputs_four = expert_in.reshape(dp_size, local_experts, capacity, model_width)
    hidden_four = hidden.reshape(shape_four)
    gate_local = jnp.einsum(
        "slcd,slcf->ldf", inputs_four, gate_pre_grad, preferred_element_type=jnp.float32
    )
    up_local = jnp.einsum(
        "slcd,slcf->ldf", inputs_four, up_pre_grad, preferred_element_type=jnp.float32
    )
    down_local = jnp.einsum(
        "slcd,slcf->ldf", grad_four, hidden_four, preferred_element_type=jnp.float32
    )
    gate_grad, up_grad, down_grad = (
        lax.psum_scatter(
            gate_local.astype(jnp.bfloat16), "seq", scatter_dimension=1, tiled=True
        ).astype(jnp.float32),
        lax.psum_scatter(
            up_local.astype(jnp.bfloat16), "seq", scatter_dimension=1, tiled=True
        ).astype(jnp.float32),
        lax.psum_scatter(
            down_local.astype(jnp.bfloat16), "seq", scatter_dimension=1, tiled=True
        ).astype(jnp.float32),
    )
    route_grad = (
        jnp.where(
            route_kept[:, None],
            jnp.take(returned_grad.reshape(experts * capacity, model_width), pair_slot, axis=0),
            0,
        )
        .reshape(tokens, 2, model_width)
        .astype(jnp.float32)
    )
    normed_two_grad = (
        route_grad[:, 0]
        + route_grad[:, 1]
        + jnp.einsum("te,de->td", logit_grad, attn_back[7], preferred_element_type=jnp.float32)
    )
    router_local = jnp.einsum(
        "td,te->de", normed_two, logit_grad, preferred_element_type=jnp.float32
    )
    unused_mid, norm_two_pull = jax.vjp(rms_norm, resid_mid, attn_back[5].astype(jnp.float32))
    mid_norm_grad, ffn_gain_local = norm_two_pull(normed_two_grad)
    middle_grad = grad_out + mid_norm_grad
    branch_grad = middle_grad.astype(jnp.bfloat16)
    output_local = jnp.einsum(
        "td,te->de", mixed_all, branch_grad, preferred_element_type=jnp.float32
    )
    mix_grad = jnp.einsum(
        "te,de->td", branch_grad, attn_back[3], preferred_element_type=jnp.float32
    ).astype(jnp.bfloat16)
    long_mix_grad = mix_grad[:long_rows].reshape(long_items, quarter, model_width)
    short_mix_grad = mix_grad[long_rows:].reshape(short_items, short_len, model_width)
    table_back = attn_back[6].reshape(HEADS, BUCKETS)

    def long_item(pack):
        single = [member_item[None] for member_item in pack]
        parts = attention_backward(
            single[0],
            single[1],
            single[2],
            single[3],
            single[4],
            single[5],
            single[6],
            single[7],
            table_back,
        )
        return (parts[0][0], parts[1][0], parts[2][0], parts[3])

    long_parts = lax.map(
        long_item,
        (
            long_q,
            long_keys,
            long_values,
            long_mix_grad,
            long_lse,
            query_pos,
            long_positions,
            long_ok,
        ),
    )
    long_key_grad, long_value_grad = (
        lax.psum_scatter(
            long_parts[1].astype(jnp.bfloat16), "seq", scatter_dimension=1, tiled=True
        ).astype(jnp.float32),
        lax.psum_scatter(
            long_parts[2].astype(jnp.bfloat16), "seq", scatter_dimension=1, tiled=True
        ).astype(jnp.float32),
    )
    short_parts = attention_backward(
        short_q,
        short_k,
        short_v,
        short_mix_grad,
        short_lse,
        short_positions,
        short_positions,
        short_ok,
        table_back,
    )
    query_act = jnp.concatenate(
        [long_parts[0].reshape(long_rows, model_width), short_parts[0].reshape(-1, model_width)], 0
    ).astype(jnp.bfloat16)
    key_act = jnp.concatenate(
        [long_key_grad.reshape(long_rows, model_width), short_parts[1].reshape(-1, model_width)], 0
    ).astype(jnp.bfloat16)
    value_act = jnp.concatenate(
        [long_value_grad.reshape(long_rows, model_width), short_parts[2].reshape(-1, model_width)],
        0,
    ).astype(jnp.bfloat16)
    table_local = (jnp.sum(long_parts[3], axis=0) + short_parts[3]).reshape(-1)
    normed_grad = (
        jnp.einsum("te,de->td", query_act, attn_back[0], preferred_element_type=jnp.float32)
        + jnp.einsum("te,de->td", key_act, attn_back[1], preferred_element_type=jnp.float32)
        + jnp.einsum("te,de->td", value_act, attn_back[2], preferred_element_type=jnp.float32)
    )
    query_local = jnp.einsum("td,te->de", normed, query_act, preferred_element_type=jnp.float32)
    key_local = jnp.einsum("td,te->de", normed, key_act, preferred_element_type=jnp.float32)
    value_local = jnp.einsum("td,te->de", normed, value_act, preferred_element_type=jnp.float32)
    unused_in, norm_one_pull = jax.vjp(rms_norm, resid_in, attn_back[4].astype(jnp.float32))
    in_norm_grad, attn_gain_local = norm_one_pull(normed_grad)
    input_grad_all = middle_grad + in_norm_grad
    long_grad_in = input_grad_all[:long_rows].reshape(long_items, quarter, model_width)
    short_grad_in = input_grad_all[long_rows:].reshape(short_items, short_len, model_width)
    shares = (gain_part, gain_part, table_part, router_part)
    small_local = jnp.concatenate(
        [
            part.reshape(devices, -1)
            for part in (attn_gain_local, ffn_gain_local, table_local, router_local)
        ],
        1,
    )
    small_local = jnp.pad(small_local, ((0, 0), (0, -small_size % 1024)))
    small_rows = small_local.shape[1] // 128
    mats = tuple(
        part.astype(jnp.bfloat16).reshape(dims + (rows_part, model_width))
        for part in (output_local, query_local, key_local, value_local)
    )
    scattered = scatter_all(
        mats + (small_local.reshape(dims + (small_rows, 128)),),
        pieces[:cuts] + ((4, 0, small_rows, 0),) + pieces[cuts:],
        dims,
        1,
    )
    small_sum = scattered[4].reshape(-1)
    edges = [sum(shares[:k]) for k in range(5)]
    summed = (scattered[1], scattered[2], scattered[3], scattered[0]) + tuple(
        small_sum[edges[k] : edges[k + 1]] for k in range(3)
    ) + (small_sum[edges[3] : edges[4]].reshape(rows_part, experts),)
    return (
        long_out,
        short_out,
        long_grad_in,
        short_grad_in,
        summed[0],
        summed[1],
        summed[2],
        summed[3],
        summed[4],
        summed[5],
        summed[6],
        summed[7],
        gate_grad,
        up_grad,
        down_grad,
    )


def solution(mesh):
    placed = (
        P("dp", "seq", None),
        P(("seq", "dp"), None, None),
        P("dp", "seq", None),
        P(("seq", "dp"), None, None),
        P(("seq", "dp"), None),
        P(("seq", "dp"), None),
        P(("seq", "dp"), None),
        P(("seq", "dp"), None),
        P(("seq", "dp")),
        P(("seq", "dp")),
        P(("seq", "dp")),
        P(("seq", "dp"), None),
        P("dp", "seq", None),
        P("dp", "seq", None),
        P("dp", "seq", None),
        P("dp", None),
        P(("seq", "dp"), None),
        P("dp"),
        P(("seq", "dp")),
        P("dp", "seq", None),
        P(("seq", "dp"), None, None),
    )
    return jax.shard_map(
        on_device,
        mesh=mesh,
        in_specs=placed,
        out_specs=(
            P("dp", "seq", None),
            P(("seq", "dp"), None, None),
            P("dp", "seq", None),
            P(("seq", "dp"), None, None),
            P(("seq", "dp"), None),
            P(("seq", "dp"), None),
            P(("seq", "dp"), None),
            P(("seq", "dp"), None),
            P(("seq", "dp")),
            P(("seq", "dp")),
            P(("seq", "dp")),
            P(("seq", "dp"), None),
            P("dp", "seq", None),
            P("dp", "seq", None),
            P("dp", "seq", None),
        ),
        check_vma=False,
    )
```

```python
import functools

import jax
import jax.numpy as jnp
from jax import lax
from jax.experimental import pallas as pl
from jax.experimental.pallas import tpu as pltpu
from jax.sharding import PartitionSpec as P

MESH = pl.DeviceIdType.MESH

HEADS = 16
HEAD = 64
BUCKETS = 32


epsilon = 1e-06
masked = -1e30


def rms_norm(hidden, gain):
    scale = lax.rsqrt(jnp.mean(hidden * hidden, axis=-1, keepdims=True) + epsilon)
    return hidden * scale * gain


def gelu_mul(gate_pre, up_pre):
    return jax.nn.gelu(gate_pre, approximate=True) * up_pre


def gate_values(logits, choose):
    probs = jax.nn.softmax(logits, axis=-1)
    chosen = jnp.sum(choose * probs[:, None, :], axis=-1)
    return chosen / jnp.sum(chosen, axis=-1, keepdims=True)


def gather_kernel(dims, pieces, na, *refs):
    X, C, Z, Y = dims
    n = len(pieces)
    lsem, zs, zr, hs, hr, cs, cr = refs[2*na:]
    routes = [p[3] for p in pieces]
    ins = [refs[m].at[pl.ds(r0, nr)] for m, r0, nr, _ in pieces]
    class V:
        def __init__(self, ref, r0, nr): self.ref, self.r0, self.nr = ref, r0, nr
        @property
        def at(self): return self
        def __getitem__(self, k):
            k = k + (slice(None),) * (4 - len(k)) + (pl.ds(self.r0, self.nr),)
            return self.ref.at[k]
    outs = [V(refs[na + m], r0, nr) for m, r0, nr, _ in pieces]
    s = lax.axis_index("seq"); g = lax.axis_index("dp")
    x, c = s // C, lax.rem(s, C)
    z, y = g // Y, lax.rem(g, Y)
    def zdev(k): return (s, lax.rem(z + k, Z) * Y + y)
    ydev = (s, z * Y + (1 - y)); xdev = ((1 - x) * C + c, g); cdev = (x * C + 1 - c, g)
    bar = pltpu.get_barrier_semaphore()
    for d in [zdev(k) for k in range(1, Z)] + [ydev, xdev, cdev]:
        pl.semaphore_signal(bar, inc=1, device_id=d, device_id_type=MESH)
    pl.semaphore_wait(bar, Z + 2)
    def rc(src, dst, ss, rs, dev):
        cp = pltpu.make_async_remote_copy(src_ref=src, dst_ref=dst, send_sem=ss, recv_sem=rs, device_id=dev, device_id_type=MESH)
        cp.start(); return cp
    sends = []
    local = []; zc = []
    for m in range(n):
        lc = pltpu.make_async_copy(ins[m], outs[m].at[x, c, z, y], lsem.at[m]); lc.start(); local.append(lc)
        zc.append([rc(ins[m], outs[m].at[x, c, z, y], zs.at[m, k], zr.at[m, k], zdev(k)) for k in range(1, Z)])
    h = [[None, None] for _ in range(n)]
    cc = [[None]*3 for _ in range(n)]
    for t in range(n + 2):
        for stage in range(3):
            m = t - stage
            if not 0 <= m < n: continue
            o = outs[m]; route = routes[m]
            if stage == 0:
                local[m].wait()
                for q in zc[m]: q.wait_recv()
                mine = o.at[x, c, :, y]
                h[m][0] = rc(mine, mine, hs.at[m,0], hr.at[m,0], xdev if route == 0 else ydev)
                cc[m][0] = rc(mine, mine, cs.at[m,0], cr.at[m,0], cdev)
            elif stage == 1:
                h[m][0].wait_recv()
                if route == 0:
                    both = o.at[:, c, :, y]; got = o.at[1 - x, c, :, y]
                else:
                    both = o.at[x, c]; got = o.at[x, c, :, 1 - y]
                h[m][1] = rc(both, both, hs.at[m,1], hr.at[m,1], ydev if route == 0 else xdev)
                cc[m][1] = rc(got, got, cs.at[m,1], cr.at[m,1], cdev)
            else:
                h[m][1].wait_recv()
                got = o.at[:, c, :, 1 - y] if route == 0 else o.at[1 - x, c]
                cc[m][2] = rc(got, got, cs.at[m,2], cr.at[m,2], cdev)
    for m in range(n):
        for q in zc[m]: q.wait_send()
        for q in h[m]: q.wait_send()
        for q in cc[m]: q.wait()
def gather_all(arrays, pieces, dims, cid):
    X, C, Z, Y = dims; na = len(arrays); n = len(pieces)
    sem = pltpu.SemaphoreType.DMA
    return pl.pallas_call(functools.partial(gather_kernel, dims, pieces, na),
        out_shape=[jax.ShapeDtypeStruct((X, C, Z, Y) + a.shape, a.dtype) for a in arrays],
        in_specs=[pl.BlockSpec(memory_space=pl.ANY)] * na, out_specs=[pl.BlockSpec(memory_space=pl.ANY)] * na,
        scratch_shapes=[sem((n,)), sem((n, Z)), sem((n, Z)), sem((n, 2)), sem((n, 2)), sem((n, 3)), sem((n, 3))],
        compiler_params=pltpu.CompilerParams(collective_id=cid, has_side_effects=True))(*arrays)


def scatter_kernel(dims, pieces, n, *refs):
    X, C, Z, Y = dims
    ins, outs = refs[:n], refs[n:2*n]
    np_ = len(pieces)
    bufs = refs[2*n:2*n+7*np_]
    sems = refs[2*n+7*np_:]
    cs, cr, hs, hr, zs, zr = sems
    s = lax.axis_index("seq"); g = lax.axis_index("dp")
    x, c = s // C, lax.rem(s, C)
    z, y = g // Y, lax.rem(g, Y)
    def zdev(k): return (s, lax.rem(z + k, Z) * Y + y)
    ydev = (s, z * Y + (1 - y)); xdev = ((1 - x) * C + c, g); cdev = (x * C + 1 - c, g)
    bar = pltpu.get_barrier_semaphore()
    for d in [zdev(k) for k in range(1, Z)] + [ydev, xdev, cdev]:
        pl.semaphore_signal(bar, inc=1, device_id=d, device_id_type=MESH)
    pl.semaphore_wait(bar, Z + 2)
    def rc(src, dst, ss, rs, dev):
        cp = pltpu.make_async_remote_copy(src_ref=src, dst_ref=dst, send_sem=ss, recv_sem=rs, device_id=dev, device_id_type=MESH)
        cp.start(); return cp
    def add(dst, a, b):
        dst[...] = (a.astype(jnp.float32) + b.astype(jnp.float32)).astype(dst.dtype)
    first = []
    for i, (m, r0, nr, route) in enumerate(pieces):
        cb = bufs[7*i]
        src = ins[m].at[:, 1 - c, :, :, pl.ds(r0, nr)]
        first.append(rc(src, cb, cs.at[i], cr.at[i], cdev))
    hh = [[None, None] for _ in pieces]; zz = [None] * np_
    for t in range(np_ + 3):
        for stage in range(4):
            i = t - stage
            if not 0 <= i < np_: continue
            m, r0, nr, route = pieces[i]
            cb, a1, b1, a2, b2, a3, b3 = bufs[7*i:7*i+7]
            if stage == 0:
                first[i].wait_recv()
                add(a1, ins[m][:, c, :, :, pl.ds(r0, nr)], cb[...])
                src = a1.at[:, :, 1 - y] if route == 0 else a1.at[1 - x]
                hh[i][0] = rc(src, b1, hs.at[i, 0], hr.at[i, 0], ydev if route == 0 else xdev)
            elif stage == 1:
                hh[i][0].wait_recv()
                add(a2, a1[:, :, y] if route == 0 else a1[x], b1[...])
                src = a2.at[1 - x] if route == 0 else a2.at[:, 1 - y]
                hh[i][1] = rc(src, b2, hs.at[i, 1], hr.at[i, 1], xdev if route == 0 else ydev)
            elif stage == 2:
                hh[i][1].wait_recv()
                add(a3, a2[x] if route == 0 else a2[:, y], b2[...])
                zz[i] = [rc(a3.at[lax.rem(z + k, Z)], b3.at[k - 1], zs.at[i, k], zr.at[i, k], zdev(k)) for k in range(1, Z)]
            else:
                tot = a3[z].astype(jnp.float32)
                for k in range(1, Z):
                    zz[i][k-1].wait_recv()
                    tot += b3[k - 1].astype(jnp.float32)
                outs[m][pl.ds(r0, nr), :] = tot
    for i in range(np_):
        first[i].wait_send()
        for q in hh[i]: q.wait_send()
        for q in zz[i]: q.wait_send()
def scatter_all(arrays, pieces, dims, cid):
    X, C, Z, Y = dims; n = len(arrays); q = len(pieces)
    sem = pltpu.SemaphoreType.DMA
    scr = []
    for m, r0, nr, route in pieces:
        w = arrays[m].shape[-1]; dt = arrays[m].dtype
        h1 = (X, Z) if route == 0 else (Z, Y)
        for lead in ((X, Z, Y), (X, Z, Y), h1, h1, (Z,), (Z,), (Z - 1,)):
            scr.append(pltpu.VMEM(lead + (nr, w), dt))
    return pl.pallas_call(functools.partial(scatter_kernel, dims, pieces, n),
        out_shape=[jax.ShapeDtypeStruct(a.shape[-2:], jnp.float32) for a in arrays],
        in_specs=[pl.BlockSpec(memory_space=pltpu.VMEM)] * n, out_specs=[pl.BlockSpec(memory_space=pltpu.VMEM)] * n,
        scratch_shapes=scr + [sem((q,)), sem((q,)), sem((q, 2)), sem((q, 2)), sem((q, Z)), sem((q, Z))],
        compiler_params=pltpu.CompilerParams(collective_id=cid, has_side_effects=True, vmem_limit_bytes=48*2**20))(*arrays)


EDGES = (-90, -63, -45, -31, -22, -15, -11, -7, -6, -5, -4, -3, -2, -1, 0, 1, 2, 3, 4, 5, 6, 7, 8, 12, 16, 23, 32, 46, 64, 91)
ORDER = (15, 14, 13, 12, 11, 10, 9, 8, 7, 6, 5, 4, 3, 2, 1, 0, 17, 18, 19, 20, 21, 22, 23, 24, 25, 26, 27, 28, 29, 30, 31)
FAR = (12, 16, 23, 32, 46, 64, 91)
def fill_buckets(out, q_col, k_row, length, base):
    r = k_row - q_col
    n = jnp.abs(r)
    far = jnp.full(r.shape, 8, jnp.int32)
    for e in FAR:
        far += (n >= e).astype(jnp.int32)
    b = jnp.where(n < 8, n, far) + jnp.where(r > 0, 16, 0)
    j = lax.broadcasted_iota(jnp.int32, r.shape, 1) + base
    out[...] = jnp.where(j < length, b, 32)
def dot(a, b, ca, cb):
    return lax.dot_general(a, b, (((ca,), (cb,)), ((), ())), preferred_element_type=jnp.float32)
def probs_of(qs, kk, tabs, bucket_ref, blocks):
    s = dot(qs, kk, 1, 1)
    t = [jnp.broadcast_to(tab, (128, 128)) for tab in tabs]
    bias = [jnp.concatenate([jnp.take_along_axis(x, bucket_ref[c], axis=1) for x in t], axis=0) for c in range(blocks)]
    s = s + (jnp.concatenate(bias, axis=1) if blocks > 1 else bias[0])
    p = jnp.exp(s - jnp.max(s, axis=1, keepdims=True))
    return p * (1.0 / jnp.sum(p, axis=1, keepdims=True))
def stack_heads(rows, first):
    return jnp.concatenate([jnp.where(first, rows, 0), jnp.where(first, 0, rows)], axis=0)
def attn_setup(nl, ns, blocks, ll, sl, lcol, lrow, scol, srow, lb, sb):
    me = lax.axis_index("seq")
    for b in range(nl):
        for c in range(blocks):
            fill_buckets(lb.at[b, c], lcol[b, me], lrow[b, c], ll[b], c * 128)
    for b in range(ns):
        fill_buckets(sb.at[b, 0], scol[b, 0], srow[b, 0], sl[b], 0)
def attn_fwd_kernel(nl, ns, blocks, ll, sl, q, k, v, kl, vl, tab, lcol, lrow, scol, srow, mixed, lb, sb):
    attn_setup(nl, ns, blocks, ll, sl, lcol, lrow, scol, srow, lb, sb)
    first = lax.broadcasted_iota(jnp.int32, (128, 128), 1) < 64
    @pl.loop(0, 8)
    def _(hp):
        cols = pl.ds(pl.multiple_of(hp * 128, 128), 128)
        for b in range(nl + ns):
            rows = pl.ds(b * 128, 128)
            n = blocks if b < nl else 1
            if b < nl:
                kk = kl[:, b, :, cols].reshape(n * 128, 128); vv = vl[:, b, :, cols].reshape(n * 128, 128)
            else:
                kk = k[rows, cols]; vv = v[rows, cols]
            qq = q[rows, cols]
            p = probs_of(stack_heads(qq, first), kk, (tab[2 * hp], tab[2 * hp + 1]), lb.at[b] if b < nl else sb.at[b - nl], n)
            out = dot(p.astype(jnp.bfloat16), vv, 1, 0)
            mixed[rows, cols] = jnp.where(first, out[:128], out[128:]).astype(jnp.bfloat16)
def attn_bwd_kernel(nl, ns, blocks, ll, sl, q, k, v, kl, vl, mg, tab, lcol, lrow, scol, srow, dq, dk, dv, dkl, dvl, seg, lb, sb, li, si):
    attn_setup(nl, ns, blocks, ll, sl, lcol, lrow, scol, srow, lb, sb)
    me = lax.axis_index("seq")
    lane = lax.broadcasted_iota(jnp.int32, (128, 128), 1)
    edge = jnp.full((128, 128), 4096, jnp.int32)
    for i, e in enumerate(EDGES):
        edge = jnp.where(lane == i, e, edge)
    edge = jnp.where(lane > len(EDGES), -4096, edge)
    def places(out, q_col, k_col, k_first):
        t = lax.broadcasted_iota(jnp.int32, (128, 256), 1) + k_first
        below = jnp.sum((k_col < t).astype(jnp.int32), axis=0, keepdims=True)
        at = jnp.clip(q_col + edge - k_first, 0, 255)
        lo = jnp.take_along_axis(jnp.broadcast_to(below[:, :128], (128, 128)), at & 127, axis=1)
        hi = jnp.take_along_axis(jnp.broadcast_to(below[:, 128:], (128, 128)), at & 127, axis=1)
        out[...] = jnp.where(at < 128, lo, hi) - 1
    for b in range(nl):
        for c in range(blocks):
            places(li.at[b, c], lcol[b, me], lcol[b, c], lrow[b, c, 0, 0])
    for b in range(ns):
        places(si.at[b, 0], scol[b, 0], scol[b, 0], srow[b, 0, 0, 0])
    seg[...] = jnp.zeros_like(seg)
    first = lane < 64
    row = lax.broadcasted_iota(jnp.int32, (128, 128), 0)
    tri = jnp.where(row <= lane, 1.0, 0.0).astype(jnp.bfloat16)
    @pl.loop(0, 8)
    def _(hp):
        cols = pl.ds(pl.multiple_of(hp * 128, 128), 128)
        for b in range(nl + ns):
            rows = pl.ds(b * 128, 128)
            n = blocks if b < nl else 1
            if b < nl:
                kk = kl[:, b, :, cols].reshape(n * 128, 128); vv = vl[:, b, :, cols].reshape(n * 128, 128)
            else:
                kk = k[rows, cols]; vv = v[rows, cols]
            qq = q[rows, cols]; gg = mg[rows, cols]
            idx = li.at[b] if b < nl else si.at[b - nl]
            qs = stack_heads(qq, first); gs = stack_heads(gg, first)
            p = probs_of(qs, kk, (tab[2 * hp], tab[2 * hp + 1]), lb.at[b] if b < nl else sb.at[b - nl], n)
            dp = dot(gs, vv, 1, 1)
            ds = (p * (dp - jnp.sum(p * dp, axis=1, keepdims=True))).astype(jnp.bfloat16)
            dqs = dot(ds, kk, 1, 0)
            dkt = dot(qs, ds, 0, 0)
            dvt = dot(gs, p.astype(jnp.bfloat16), 0, 0)
            sums = [0, 0]
            for c in range(n):
                pre = dot(ds[:, c * 128:(c + 1) * 128], tri, 1, 0)
                at = idx[c]
                for e in range(2):
                    sums[e] += jnp.where(at >= 0, jnp.take_along_axis(pre[e * 128:(e + 1) * 128], jnp.maximum(at, 0), axis=1), 0.0)
            for e in range(2):
                seg[2 * hp + e] += jnp.sum(sums[e], axis=0, keepdims=True)
            dq[rows, cols] = jnp.where(first, dqs[:128], dqs[128:]).astype(jnp.bfloat16)
            dkt = dkt.T.astype(jnp.bfloat16); dvt = dvt.T.astype(jnp.bfloat16)
            if b < nl:
                dkl[:, b, :, cols] = dkt.reshape(n, 128, 128); dvl[:, b, :, cols] = dvt.reshape(n, 128, 128)
            else:
                dk[pl.ds((b - nl) * 128, 128), cols] = dkt; dv[pl.ds((b - nl) * 128, 128), cols] = dvt
def attention(backward, nl, ns, blocks, arrays, tokens, width):
    sm, vm = pl.BlockSpec(memory_space=pltpu.SMEM), pl.BlockSpec(memory_space=pltpu.VMEM)
    bf = jnp.bfloat16
    rows = jax.ShapeDtypeStruct((tokens, width), bf)
    buckets = [pltpu.VMEM((nl, blocks, 128, 128), jnp.int32), pltpu.VMEM((ns, 1, 128, 128), jnp.int32)]
    if backward:
        short = jax.ShapeDtypeStruct((ns * 128, width), bf)
        long = jax.ShapeDtypeStruct((blocks, nl, 128, width), bf)
        outs = [rows, short, short, long, long, jax.ShapeDtypeStruct((16, 1, 128), jnp.float32)]
        body = functools.partial(attn_bwd_kernel, nl, ns, blocks); scr = buckets * 2
    else:
        outs = [rows]; body = functools.partial(attn_fwd_kernel, nl, ns, blocks); scr = buckets
    return pl.pallas_call(body, out_shape=outs, in_specs=[sm, sm] + [vm] * (len(arrays) - 2), out_specs=[vm] * len(outs),
        scratch_shapes=scr, compiler_params=pltpu.CompilerParams(vmem_limit_bytes=56 * 2**20))(*arrays)


def seq_places(C):
    s = lax.axis_index("seq"); g = lax.axis_index("dp")
    x, c = s // C, lax.rem(s, C)
    return s, x, c, ((1 - x) * C + c, g), (x * C + 1 - c, g)
def greet(devs):
    bar = pltpu.get_barrier_semaphore()
    for d in devs:
        pl.semaphore_signal(bar, inc=1, device_id=d, device_id_type=MESH)
    pl.semaphore_wait(bar, len(devs))
def remote(src, dst, ss, rs, dev):
    cp = pltpu.make_async_remote_copy(src_ref=src, dst_ref=dst, send_sem=ss, recv_sem=rs, device_id=dev, device_id_type=MESH)
    cp.start()
    return cp
def seq_gather_kernel(n, items, rows, *refs):
    ins, outs = refs[:n], refs[n:2 * n]
    lsem, ss, rs = refs[2 * n:]
    s, x, c, xdev, cdev = seq_places(2)
    far = (1 - x) * 2 + c
    greet([xdev, cdev])
    local, a, b = [], [], []
    pieces = [(m, i) for m in range(n) for i in range(items)]
    for k, (m, i) in enumerate(pieces):
        src = ins[m].at[pl.ds(i * rows, rows)]
        a.append(remote(src, outs[m].at[s, i], ss.at[k, 0], rs.at[k, 0], xdev))
        b.append(remote(src, outs[m].at[s, i], ss.at[k, 1], rs.at[k, 1], cdev))
        cp = pltpu.make_async_copy(src, outs[m].at[s, i], lsem.at[k]); cp.start(); local.append(cp)
    f = []
    for k, (m, i) in enumerate(pieces):
        a[k].wait_recv()
        f.append(remote(outs[m].at[far, i], outs[m].at[far, i], ss.at[k, 2], rs.at[k, 2], cdev))
    for k in range(len(pieces)):
        local[k].wait(); a[k].wait_send(); b[k].wait(); f[k].wait()
def seq_gather(arrays, items, rows, seq, cid):
    n = len(arrays); q = n * items
    sem = pltpu.SemaphoreType.DMA
    any_ = pl.BlockSpec(memory_space=pltpu.VMEM)
    return pl.pallas_call(functools.partial(seq_gather_kernel, n, items, rows),
        out_shape=[jax.ShapeDtypeStruct((seq, items, rows, a.shape[-1]), a.dtype) for a in arrays],
        in_specs=[any_] * n, out_specs=[any_] * n,
        scratch_shapes=[sem((q,)), sem((q, 3)), sem((q, 3))],
        compiler_params=pltpu.CompilerParams(collective_id=cid, has_side_effects=True, vmem_limit_bytes=48*2**20))(*arrays)
def seq_sum_kernel(n, items, *refs):
    ins, outs = refs[:n], refs[n:2 * n]
    cb, a1, b1, ss, rs = refs[2 * n:]
    s, x, c, xdev, cdev = seq_places(2)
    greet([xdev, cdev])
    pieces = [(m, i) for m in range(n) for i in range(items)]
    first = [[None, None] for _ in pieces]
    second = []
    f32 = jnp.float32
    for far in range(2):
        xx = 1 - x if far == 0 else x
        for k, (m, i) in enumerate(pieces):
            first[k][far] = remote(ins[m].at[xx * 2 + 1 - c, i], cb.at[k, far], ss.at[k, far], rs.at[k, far], cdev)
    for k, (m, i) in enumerate(pieces):
        first[k][0].wait_recv()
        a1[k] = (ins[m][(1 - x) * 2 + c, i].astype(f32) + cb[k, 0].astype(f32)).astype(a1.dtype)
        second.append(remote(a1.at[k], b1.at[k], ss.at[k, 2], rs.at[k, 2], xdev))
    for k, (m, i) in enumerate(pieces):
        first[k][1].wait_recv()
        second[k].wait_recv()
        outs[m][i] = (ins[m][s, i].astype(f32) + cb[k, 1].astype(f32) + b1[k].astype(f32)).astype(outs[m].dtype)
    for k in range(len(pieces)):
        first[k][0].wait_send(); first[k][1].wait_send(); second[k].wait_send()
def seq_sum(arrays, cid):
    n = len(arrays); seq, items, rows, w = arrays[0].shape; q = n * items
    sem = pltpu.SemaphoreType.DMA; dt = arrays[0].dtype
    vm = pl.BlockSpec(memory_space=pltpu.VMEM)
    return pl.pallas_call(functools.partial(seq_sum_kernel, n, items),
        out_shape=[jax.ShapeDtypeStruct((items, rows, w), dt) for a in arrays],
        in_specs=[vm] * n, out_specs=[vm] * n,
        scratch_shapes=[pltpu.VMEM((q, 2, rows, w), dt), pltpu.VMEM((q, rows, w), dt), pltpu.VMEM((q, rows, w), dt), sem((q, 3)), sem((q, 3))],
        compiler_params=pltpu.CompilerParams(collective_id=cid, has_side_effects=True, vmem_limit_bytes=48 * 2**20))(*arrays)


def on_device(
    long_tokens,
    short_tokens,
    long_grad_out,
    short_grad_out,
    query_weight,
    key_weight,
    value_weight,
    output_weight,
    attn_gain,
    ffn_gain,
    rel_table,
    router_weight,
    gate_weight,
    up_weight,
    down_weight,
    long_positions,
    short_positions,
    long_lengths,
    short_lengths,
    long_routes,
    short_routes,
):
    long_items, quarter, model_width = long_tokens.shape
    short_items, short_len = (short_tokens.shape[0], short_tokens.shape[1])
    long_rows = long_items * quarter
    tokens = long_rows + short_items * short_len
    local_experts = gate_weight.shape[0]
    dp_size = lax.axis_size("dp")
    experts = local_experts * dp_size
    capacity = (5 * tokens + 2 * experts - 1) // (2 * experts)
    seq_index = lax.axis_index("seq")
    seq_size = lax.axis_size("seq")
    dims = (seq_size // 2, 2, dp_size // 2, 2)
    devices = seq_size * dp_size
    table_part, router_part = rel_table.shape[0], router_weight.size
    gain_part = attn_gain.shape[0]
    small_size = 2 * gain_part + table_part + router_part
    small = jnp.concatenate([attn_gain, ffn_gain, rel_table, router_weight.reshape(-1)])
    small = jnp.pad(small, (0, -small_size % 2048)).reshape(-1, 128)
    rows_part = query_weight.shape[0]
    cuts = 2 if rows_part % 32 == 0 else 1
    cut = rows_part // cuts
    pieces = tuple((m, h * cut, cut, (m + h) % 2) for m in range(4) for h in range(cuts))
    gathered = gather_all(
        (query_weight, key_weight, value_weight, output_weight, small),
        pieces[: 3 * cuts] + ((4, 0, small.shape[0], 0),) + pieces[3 * cuts :],
        dims,
        0,
    )
    small_all = gathered[4].reshape(devices, -1)
    attn_set = tuple(block.reshape(devices * rows_part, model_width) for block in gathered[:4]) + (
        small_all[:, :gain_part].reshape(-1),
        small_all[:, gain_part : 2 * gain_part].reshape(-1),
        small_all[:, 2 * gain_part : 2 * gain_part + table_part].reshape(-1),
        small_all[:, 2 * gain_part + table_part : small_size].reshape(model_width, experts),
    )
    expert_set = (
        lax.all_gather(gate_weight, "seq", axis=1, tiled=True),
        lax.all_gather(up_weight, "seq", axis=1, tiled=True),
        lax.all_gather(down_weight, "seq", axis=1, tiled=True),
    )
    resid_in = jnp.concatenate(
        [long_tokens.reshape(long_rows, model_width), short_tokens.reshape(-1, model_width)], 0
    ).astype(jnp.float32)
    gain_first = attn_set[4].astype(jnp.float32)
    normed = rms_norm(resid_in, gain_first).astype(jnp.bfloat16)
    projected = [
        jnp.dot(normed, matrix, preferred_element_type=jnp.float32).astype(jnp.bfloat16)
        for matrix in attn_set[:3]
    ]
    queries, keys, values = projected
    long_keys, long_values = seq_gather((keys, values), long_items, quarter, seq_size, 2)
    table = attn_set[6].reshape(HEADS, 1, BUCKETS).astype(jnp.float32)
    table = jnp.pad(table, ((0, 0), (0, 0), (0, 128 - BUCKETS)), constant_values=masked)
    attn_args = (
        table,
        long_positions.reshape(long_items, seq_size, quarter, 1),
        long_positions.reshape(long_items, seq_size, 1, quarter),
        short_positions.reshape(short_items, 1, short_len, 1),
        short_positions.reshape(short_items, 1, 1, short_len),
    )
    lead_args = (long_lengths, short_lengths, queries, keys, values, long_keys, long_values)
    (mixed_all,) = attention(
        False, long_items, short_items, seq_size, lead_args + attn_args, tokens, model_width
    )
    resid_mid = resid_in + jnp.dot(mixed_all, attn_set[3], preferred_element_type=jnp.float32)
    gain_second = attn_set[5].astype(jnp.float32)
    normed_two = rms_norm(resid_mid, gain_second).astype(jnp.bfloat16)
    logits = jnp.dot(normed_two, attn_set[7], preferred_element_type=jnp.float32)
    routes = jnp.concatenate([long_routes.reshape(-1, 2), short_routes.reshape(-1, 2)], 0)
    choose = (routes[..., None] == jnp.arange(experts, dtype=jnp.int32)).astype(jnp.float32)
    gate_share, gate_pull = jax.vjp(lambda logit_in: gate_values(logit_in, choose), logits)
    flat_routes = routes.reshape(-1)
    member = (flat_routes[:, None] == jnp.arange(experts, dtype=jnp.int32)).astype(jnp.int32)
    queue_pos = jnp.sum(jnp.cumsum(member, axis=0) * member, axis=1) - 1
    route_kept = queue_pos < capacity
    slot_index = jnp.where(route_kept, flat_routes * capacity + queue_pos, experts * capacity)
    slot_pair = (
        jnp.zeros(experts * capacity + 1, jnp.int32)
        .at[slot_index]
        .set(jnp.arange(2 * tokens, dtype=jnp.int32))[:-1]
    )
    slot_used = jnp.zeros(experts * capacity + 1, jnp.bool_).at[slot_index].set(True)[:-1]
    pair_slot = jnp.where(route_kept, slot_index, 0)
    outgoing = jnp.where(
        slot_used[:, None], jnp.take(normed_two, slot_pair // 2, axis=0), 0
    ).reshape(experts, capacity, model_width)
    gate_full, up_full, down_full = expert_set
    arrived = lax.all_to_all(outgoing, "dp", split_axis=0, concat_axis=0, tiled=True)
    slot_count = arrived.shape[1]
    inputs = arrived.reshape(dp_size, local_experts, slot_count, model_width)
    gate_pre = jnp.einsum("slcd,ldf->slcf", inputs, gate_full, preferred_element_type=jnp.float32)
    up_pre = jnp.einsum("slcd,ldf->slcf", inputs, up_full, preferred_element_type=jnp.float32)
    hidden = gelu_mul(gate_pre, up_pre).astype(jnp.bfloat16)
    result = jnp.einsum(
        "slcf,ldf->slcd", hidden, down_full, preferred_element_type=jnp.float32
    ).astype(jnp.bfloat16)
    returned = lax.all_to_all(
        result.reshape(experts, slot_count, model_width),
        "dp",
        split_axis=0,
        concat_axis=0,
        tiled=True,
    )
    ffn_width = hidden.shape[-1]
    back_rows, expert_in, gate_pre, up_pre, hidden = (
        returned,
        arrived,
        gate_pre.reshape(experts, slot_count, ffn_width),
        up_pre.reshape(experts, slot_count, ffn_width),
        hidden.reshape(experts, slot_count, ffn_width),
    )
    pair_out = (
        jnp.where(
            route_kept[:, None],
            jnp.take(back_rows.reshape(experts * capacity, model_width), pair_slot, axis=0),
            0,
        )
        .reshape(tokens, 2, model_width)
        .astype(jnp.float32)
    )
    kept_two = route_kept.reshape(tokens, 2).astype(jnp.float32)
    weighting = gate_share * kept_two
    final = resid_mid + weighting[:, 0:1] * pair_out[:, 0] + weighting[:, 1:2] * pair_out[:, 1]
    final_low = final.astype(jnp.bfloat16)
    long_out = final_low[:long_rows].reshape(long_items, quarter, model_width)
    short_out = final_low[long_rows:].reshape(short_items, short_len, model_width)
    grad_out = jnp.concatenate(
        [long_grad_out.reshape(long_rows, model_width), short_grad_out.reshape(-1, model_width)], 0
    ).astype(jnp.float32)
    pair_grad = (
        (weighting[:, :, None] * grad_out[:, None, :])
        .astype(jnp.bfloat16)
        .reshape(2 * tokens, model_width)
    )
    share_grad = kept_two * jnp.sum(grad_out[:, None, :] * pair_out, axis=-1)
    logit_grad = gate_pull(share_grad)[0].astype(jnp.bfloat16)
    out_slots = jnp.where(slot_used[:, None], jnp.take(pair_grad, slot_pair, axis=0), 0).reshape(
        experts, capacity, model_width
    )
    attn_back, expert_back = attn_set, expert_set
    gate_back, up_back, down_back = expert_back
    arrived_grad = lax.all_to_all(out_slots, "dp", split_axis=0, concat_axis=0, tiled=True)
    shape_four = (dp_size, local_experts, capacity, -1)
    grad_four = arrived_grad.reshape(dp_size, local_experts, capacity, model_width)
    hidden_grad = jnp.einsum(
        "slcd,ldf->slcf", grad_four, down_back, preferred_element_type=jnp.float32
    )
    unused_geglu, geglu_pull = jax.vjp(
        gelu_mul, gate_pre.reshape(shape_four), up_pre.reshape(shape_four)
    )
    gate_pre_grad, up_pre_grad = geglu_pull(hidden_grad)
    gate_pre_grad = gate_pre_grad.astype(jnp.bfloat16)
    up_pre_grad = up_pre_grad.astype(jnp.bfloat16)
    input_grad = (
        jnp.einsum("slcf,ldf->slcd", gate_pre_grad, gate_back, preferred_element_type=jnp.float32)
        + jnp.einsum("slcf,ldf->slcd", up_pre_grad, up_back, preferred_element_type=jnp.float32)
    ).astype(jnp.bfloat16)
    returned_grad = lax.all_to_all(
        input_grad.reshape(experts, capacity, model_width),
        "dp",
        split_axis=0,
        concat_axis=0,
        tiled=True,
    )
    inputs_four = expert_in.reshape(dp_size, local_experts, capacity, model_width)
    hidden_four = hidden.reshape(shape_four)
    gate_local = jnp.einsum(
        "slcd,slcf->ldf", inputs_four, gate_pre_grad, preferred_element_type=jnp.float32
    )
    up_local = jnp.einsum(
        "slcd,slcf->ldf", inputs_four, up_pre_grad, preferred_element_type=jnp.float32
    )
    down_local = jnp.einsum(
        "slcd,slcf->ldf", grad_four, hidden_four, preferred_element_type=jnp.float32
    )
    gate_grad, up_grad, down_grad = (
        lax.psum_scatter(
            gate_local.astype(jnp.bfloat16), "seq", scatter_dimension=1, tiled=True
        ).astype(jnp.float32),
        lax.psum_scatter(
            up_local.astype(jnp.bfloat16), "seq", scatter_dimension=1, tiled=True
        ).astype(jnp.float32),
        lax.psum_scatter(
            down_local.astype(jnp.bfloat16), "seq", scatter_dimension=1, tiled=True
        ).astype(jnp.float32),
    )
    route_grad = (
        jnp.where(
            route_kept[:, None],
            jnp.take(returned_grad.reshape(experts * capacity, model_width), pair_slot, axis=0),
            0,
        )
        .reshape(tokens, 2, model_width)
        .astype(jnp.float32)
    )
    normed_two_grad = (
        route_grad[:, 0]
        + route_grad[:, 1]
        + jnp.einsum("te,de->td", logit_grad, attn_back[7], preferred_element_type=jnp.float32)
    )
    router_local = jnp.einsum(
        "td,te->de", normed_two, logit_grad, preferred_element_type=jnp.float32
    )
    unused_mid, norm_two_pull = jax.vjp(rms_norm, resid_mid, attn_back[5].astype(jnp.float32))
    mid_norm_grad, ffn_gain_local = norm_two_pull(normed_two_grad)
    middle_grad = grad_out + mid_norm_grad
    branch_grad = middle_grad.astype(jnp.bfloat16)
    output_local = jnp.einsum(
        "td,te->de", mixed_all, branch_grad, preferred_element_type=jnp.float32
    )
    mix_grad = jnp.einsum(
        "te,de->td", branch_grad, attn_back[3], preferred_element_type=jnp.float32
    ).astype(jnp.bfloat16)
    query_act, short_key, short_value, long_key, long_value, table_sums = attention(
        True,
        long_items,
        short_items,
        seq_size,
        lead_args + (mix_grad,) + attn_args,
        tokens,
        model_width,
    )
    long_key, long_value = seq_sum((long_key, long_value), 3)
    key_act = jnp.concatenate([long_key.reshape(long_rows, model_width), short_key], 0)
    value_act = jnp.concatenate([long_value.reshape(long_rows, model_width), short_value], 0)
    upto = table_sums.reshape(HEADS, 128)[:, : len(ORDER)]
    within = upto - jnp.pad(upto[:, :-1], ((0, 0), (1, 0)))
    table_local = jnp.stack(
        [
            within[:, ORDER.index(n)] if n in ORDER else jnp.zeros(HEADS, jnp.float32)
            for n in range(BUCKETS)
        ],
        1,
    ).reshape(-1)
    normed_grad = (
        jnp.einsum("te,de->td", query_act, attn_back[0], preferred_element_type=jnp.float32)
        + jnp.einsum("te,de->td", key_act, attn_back[1], preferred_element_type=jnp.float32)
        + jnp.einsum("te,de->td", value_act, attn_back[2], preferred_element_type=jnp.float32)
    )
    query_local = jnp.einsum("td,te->de", normed, query_act, preferred_element_type=jnp.float32)
    key_local = jnp.einsum("td,te->de", normed, key_act, preferred_element_type=jnp.float32)
    value_local = jnp.einsum("td,te->de", normed, value_act, preferred_element_type=jnp.float32)
    unused_in, norm_one_pull = jax.vjp(rms_norm, resid_in, attn_back[4].astype(jnp.float32))
    in_norm_grad, attn_gain_local = norm_one_pull(normed_grad)
    input_grad_all = middle_grad + in_norm_grad
    long_grad_in = input_grad_all[:long_rows].reshape(long_items, quarter, model_width)
    short_grad_in = input_grad_all[long_rows:].reshape(short_items, short_len, model_width)
    shares = (gain_part, gain_part, table_part, router_part)
    small_local = jnp.concatenate(
        [
            part.reshape(devices, -1)
            for part in (attn_gain_local, ffn_gain_local, table_local, router_local)
        ],
        1,
    )
    small_local = jnp.pad(small_local, ((0, 0), (0, -small_size % 1024)))
    small_rows = small_local.shape[1] // 128
    mats = tuple(
        part.astype(jnp.bfloat16).reshape(dims + (rows_part, model_width))
        for part in (output_local, query_local, key_local, value_local)
    )
    scattered = scatter_all(
        mats + (small_local.reshape(dims + (small_rows, 128)),),
        pieces[:cuts] + ((4, 0, small_rows, 0),) + pieces[cuts:],
        dims,
        1,
    )
    small_sum = scattered[4].reshape(-1)
    edges = [sum(shares[:k]) for k in range(5)]
    summed = (scattered[1], scattered[2], scattered[3], scattered[0]) + tuple(
        small_sum[edges[k] : edges[k + 1]] for k in range(3)
    ) + (small_sum[edges[3] : edges[4]].reshape(rows_part, experts),)
    return (
        long_out,
        short_out,
        long_grad_in,
        short_grad_in,
        summed[0],
        summed[1],
        summed[2],
        summed[3],
        summed[4],
        summed[5],
        summed[6],
        summed[7],
        gate_grad,
        up_grad,
        down_grad,
    )


def solution(mesh):
    placed = (
        P("dp", "seq", None),
        P(("seq", "dp"), None, None),
        P("dp", "seq", None),
        P(("seq", "dp"), None, None),
        P(("seq", "dp"), None),
        P(("seq", "dp"), None),
        P(("seq", "dp"), None),
        P(("seq", "dp"), None),
        P(("seq", "dp")),
        P(("seq", "dp")),
        P(("seq", "dp")),
        P(("seq", "dp"), None),
        P("dp", "seq", None),
        P("dp", "seq", None),
        P("dp", "seq", None),
        P("dp", None),
        P(("seq", "dp"), None),
        P("dp"),
        P(("seq", "dp")),
        P("dp", "seq", None),
        P(("seq", "dp"), None, None),
    )
    return jax.shard_map(
        on_device,
        mesh=mesh,
        in_specs=placed,
        out_specs=(
            P("dp", "seq", None),
            P(("seq", "dp"), None, None),
            P("dp", "seq", None),
            P(("seq", "dp"), None, None),
            P(("seq", "dp"), None),
            P(("seq", "dp"), None),
            P(("seq", "dp"), None),
            P(("seq", "dp"), None),
            P(("seq", "dp")),
            P(("seq", "dp")),
            P(("seq", "dp")),
            P(("seq", "dp"), None),
            P("dp", "seq", None),
            P("dp", "seq", None),
            P("dp", "seq", None),
        ),
        check_vma=False,
    )
```

```python
import functools

import jax
import jax.numpy as jnp
from jax import lax
from jax.experimental import pallas as pl
from jax.experimental.pallas import tpu as pltpu
from jax.sharding import PartitionSpec as P

MESH = pl.DeviceIdType.MESH

HEADS = 16
HEAD = 64
BUCKETS = 32


epsilon = 1e-06
masked = -1e30


def rms_norm(hidden, gain):
    scale = lax.rsqrt(jnp.mean(hidden * hidden, axis=-1, keepdims=True) + epsilon)
    return hidden * scale * gain


def gate_values(logits, choose):
    probs = jax.nn.softmax(logits, axis=-1)
    chosen = jnp.sum(choose * probs[:, None, :], axis=-1)
    return chosen / jnp.sum(chosen, axis=-1, keepdims=True)


def gather_kernel(dims, pieces, na, *refs):
    X, C, Z, Y = dims
    n = len(pieces)
    lsem, zs, zr, hs, hr, cs, cr = refs[2*na:]
    routes = [p[3] for p in pieces]
    ins = [refs[m].at[pl.ds(r0, nr)] for m, r0, nr, _ in pieces]
    class V:
        def __init__(self, ref, r0, nr): self.ref, self.r0, self.nr = ref, r0, nr
        @property
        def at(self): return self
        def __getitem__(self, k):
            k = k + (slice(None),) * (4 - len(k)) + (pl.ds(self.r0, self.nr),)
            return self.ref.at[k]
    outs = [V(refs[na + m], r0, nr) for m, r0, nr, _ in pieces]
    s = lax.axis_index("seq"); g = lax.axis_index("dp")
    x, c = s // C, lax.rem(s, C)
    z, y = g // Y, lax.rem(g, Y)
    def zdev(k): return (s, lax.rem(z + k, Z) * Y + y)
    ydev = (s, z * Y + (1 - y)); xdev = ((1 - x) * C + c, g); cdev = (x * C + 1 - c, g)
    bar = pltpu.get_barrier_semaphore()
    for d in [zdev(k) for k in range(1, Z)] + [ydev, xdev, cdev]:
        pl.semaphore_signal(bar, inc=1, device_id=d, device_id_type=MESH)
    pl.semaphore_wait(bar, Z + 2)
    def rc(src, dst, ss, rs, dev):
        cp = pltpu.make_async_remote_copy(src_ref=src, dst_ref=dst, send_sem=ss, recv_sem=rs, device_id=dev, device_id_type=MESH)
        cp.start(); return cp
    sends = []
    local = []; zc = []
    for m in range(n):
        lc = pltpu.make_async_copy(ins[m], outs[m].at[x, c, z, y], lsem.at[m]); lc.start(); local.append(lc)
        zc.append([rc(ins[m], outs[m].at[x, c, z, y], zs.at[m, k], zr.at[m, k], zdev(k)) for k in range(1, Z)])
    h = [[None, None] for _ in range(n)]
    cc = [[None]*3 for _ in range(n)]
    for t in range(n + 2):
        for stage in range(3):
            m = t - stage
            if not 0 <= m < n: continue
            o = outs[m]; route = routes[m]
            if stage == 0:
                local[m].wait()
                for q in zc[m]: q.wait_recv()
                mine = o.at[x, c, :, y]
                h[m][0] = rc(mine, mine, hs.at[m,0], hr.at[m,0], xdev if route == 0 else ydev)
                cc[m][0] = rc(mine, mine, cs.at[m,0], cr.at[m,0], cdev)
            elif stage == 1:
                h[m][0].wait_recv()
                if route == 0:
                    both = o.at[:, c, :, y]; got = o.at[1 - x, c, :, y]
                else:
                    both = o.at[x, c]; got = o.at[x, c, :, 1 - y]
                h[m][1] = rc(both, both, hs.at[m,1], hr.at[m,1], ydev if route == 0 else xdev)
                cc[m][1] = rc(got, got, cs.at[m,1], cr.at[m,1], cdev)
            else:
                h[m][1].wait_recv()
                got = o.at[:, c, :, 1 - y] if route == 0 else o.at[1 - x, c]
                cc[m][2] = rc(got, got, cs.at[m,2], cr.at[m,2], cdev)
    for m in range(n):
        for q in zc[m]: q.wait_send()
        for q in h[m]: q.wait_send()
        for q in cc[m]: q.wait()
def gather_all(arrays, pieces, dims, cid):
    X, C, Z, Y = dims; na = len(arrays); n = len(pieces)
    sem = pltpu.SemaphoreType.DMA
    return pl.pallas_call(functools.partial(gather_kernel, dims, pieces, na),
        out_shape=[jax.ShapeDtypeStruct((X, C, Z, Y) + a.shape, a.dtype) for a in arrays],
        in_specs=[pl.BlockSpec(memory_space=pl.ANY)] * na, out_specs=[pl.BlockSpec(memory_space=pl.ANY)] * na,
        scratch_shapes=[sem((n,)), sem((n, Z)), sem((n, Z)), sem((n, 2)), sem((n, 2)), sem((n, 3)), sem((n, 3))],
        compiler_params=pltpu.CompilerParams(collective_id=cid, has_side_effects=True))(*arrays)


def scatter_kernel(dims, pieces, n, *refs):
    X, C, Z, Y = dims
    ins, outs = refs[:n], refs[n:2*n]
    np_ = len(pieces)
    bufs = refs[2*n:2*n+7*np_]
    sems = refs[2*n+7*np_:]
    cs, cr, hs, hr, zs, zr = sems
    s = lax.axis_index("seq"); g = lax.axis_index("dp")
    x, c = s // C, lax.rem(s, C)
    z, y = g // Y, lax.rem(g, Y)
    def zdev(k): return (s, lax.rem(z + k, Z) * Y + y)
    ydev = (s, z * Y + (1 - y)); xdev = ((1 - x) * C + c, g); cdev = (x * C + 1 - c, g)
    bar = pltpu.get_barrier_semaphore()
    for d in [zdev(k) for k in range(1, Z)] + [ydev, xdev, cdev]:
        pl.semaphore_signal(bar, inc=1, device_id=d, device_id_type=MESH)
    pl.semaphore_wait(bar, Z + 2)
    def rc(src, dst, ss, rs, dev):
        cp = pltpu.make_async_remote_copy(src_ref=src, dst_ref=dst, send_sem=ss, recv_sem=rs, device_id=dev, device_id_type=MESH)
        cp.start(); return cp
    def add(dst, a, b):
        dst[...] = (a.astype(jnp.float32) + b.astype(jnp.float32)).astype(dst.dtype)
    first = []
    for i, (m, r0, nr, route) in enumerate(pieces):
        cb = bufs[7*i]
        src = ins[m].at[:, 1 - c, :, :, pl.ds(r0, nr)]
        first.append(rc(src, cb, cs.at[i], cr.at[i], cdev))
    hh = [[None, None] for _ in pieces]; zz = [None] * np_
    for t in range(np_ + 3):
        for stage in range(4):
            i = t - stage
            if not 0 <= i < np_: continue
            m, r0, nr, route = pieces[i]
            cb, a1, b1, a2, b2, a3, b3 = bufs[7*i:7*i+7]
            if stage == 0:
                first[i].wait_recv()
                add(a1, ins[m][:, c, :, :, pl.ds(r0, nr)], cb[...])
                src = a1.at[:, :, 1 - y] if route == 0 else a1.at[1 - x]
                hh[i][0] = rc(src, b1, hs.at[i, 0], hr.at[i, 0], ydev if route == 0 else xdev)
            elif stage == 1:
                hh[i][0].wait_recv()
                add(a2, a1[:, :, y] if route == 0 else a1[x], b1[...])
                src = a2.at[1 - x] if route == 0 else a2.at[:, 1 - y]
                hh[i][1] = rc(src, b2, hs.at[i, 1], hr.at[i, 1], xdev if route == 0 else ydev)
            elif stage == 2:
                hh[i][1].wait_recv()
                add(a3, a2[x] if route == 0 else a2[:, y], b2[...])
                zz[i] = [rc(a3.at[lax.rem(z + k, Z)], b3.at[k - 1], zs.at[i, k], zr.at[i, k], zdev(k)) for k in range(1, Z)]
            else:
                tot = a3[z].astype(jnp.float32)
                for k in range(1, Z):
                    zz[i][k-1].wait_recv()
                    tot += b3[k - 1].astype(jnp.float32)
                outs[m][pl.ds(r0, nr), :] = tot
    for i in range(np_):
        first[i].wait_send()
        for q in hh[i]: q.wait_send()
        for q in zz[i]: q.wait_send()
def scatter_all(arrays, pieces, dims, cid):
    X, C, Z, Y = dims; n = len(arrays); q = len(pieces)
    sem = pltpu.SemaphoreType.DMA
    scr = []
    for m, r0, nr, route in pieces:
        w = arrays[m].shape[-1]; dt = arrays[m].dtype
        h1 = (X, Z) if route == 0 else (Z, Y)
        for lead in ((X, Z, Y), (X, Z, Y), h1, h1, (Z,), (Z,), (Z - 1,)):
            scr.append(pltpu.VMEM(lead + (nr, w), dt))
    return pl.pallas_call(functools.partial(scatter_kernel, dims, pieces, n),
        out_shape=[jax.ShapeDtypeStruct(a.shape[-2:], jnp.float32) for a in arrays],
        in_specs=[pl.BlockSpec(memory_space=pltpu.VMEM)] * n, out_specs=[pl.BlockSpec(memory_space=pltpu.VMEM)] * n,
        scratch_shapes=scr + [sem((q,)), sem((q,)), sem((q, 2)), sem((q, 2)), sem((q, Z)), sem((q, Z))],
        compiler_params=pltpu.CompilerParams(collective_id=cid, has_side_effects=True, vmem_limit_bytes=48*2**20))(*arrays)


EDGES = (-90, -63, -45, -31, -22, -15, -11, -7, -6, -5, -4, -3, -2, -1, 0, 1, 2, 3, 4, 5, 6, 7, 8, 12, 16, 23, 32, 46, 64, 91)
ORDER = (15, 14, 13, 12, 11, 10, 9, 8, 7, 6, 5, 4, 3, 2, 1, 0, 17, 18, 19, 20, 21, 22, 23, 24, 25, 26, 27, 28, 29, 30, 31)
FAR = (12, 16, 23, 32, 46, 64, 91)
def fill_buckets(out, q_col, k_row, length, base):
    r = k_row - q_col
    n = jnp.abs(r)
    far = jnp.full(r.shape, 8, jnp.int32)
    for e in FAR:
        far += (n >= e).astype(jnp.int32)
    b = jnp.where(n < 8, n, far) + jnp.where(r > 0, 16, 0)
    j = lax.broadcasted_iota(jnp.int32, r.shape, 1) + base
    out[...] = jnp.where(j < length, b, 32)
def dot(a, b, ca, cb):
    return lax.dot_general(a, b, (((ca,), (cb,)), ((), ())), preferred_element_type=jnp.float32)
def probs_of(qs, kk, tabs, bucket_ref, blocks):
    s = dot(qs, kk, 1, 1)
    t = [jnp.broadcast_to(tab, (128, 128)) for tab in tabs]
    bias = [jnp.concatenate([jnp.take_along_axis(x, bucket_ref[c], axis=1) for x in t], axis=0) for c in range(blocks)]
    s = s + (jnp.concatenate(bias, axis=1) if blocks > 1 else bias[0])
    p = jnp.exp(s - jnp.max(s, axis=1, keepdims=True))
    return p * (1.0 / jnp.sum(p, axis=1, keepdims=True))
def stack_heads(rows, first):
    return jnp.concatenate([jnp.where(first, rows, 0), jnp.where(first, 0, rows)], axis=0)
def attn_setup(nl, ns, blocks, ll, sl, lcol, lrow, scol, srow, lb, sb):
    me = lax.axis_index("seq")
    for b in range(nl):
        for c in range(blocks):
            fill_buckets(lb.at[b, c], lcol[b, me], lrow[b, c], ll[b], c * 128)
    for b in range(ns):
        fill_buckets(sb.at[b, 0], scol[b, 0], srow[b, 0], sl[b], 0)
def attn_fwd_kernel(nl, ns, blocks, ll, sl, q, k, v, kl, vl, tab, lcol, lrow, scol, srow, mixed, lb, sb):
    attn_setup(nl, ns, blocks, ll, sl, lcol, lrow, scol, srow, lb, sb)
    first = lax.broadcasted_iota(jnp.int32, (128, 128), 1) < 64
    @pl.loop(0, 8)
    def _(hp):
        cols = pl.ds(pl.multiple_of(hp * 128, 128), 128)
        for b in range(nl + ns):
            rows = pl.ds(b * 128, 128)
            n = blocks if b < nl else 1
            if b < nl:
                kk = kl[:, b, :, cols].reshape(n * 128, 128); vv = vl[:, b, :, cols].reshape(n * 128, 128)
            else:
                kk = k[rows, cols]; vv = v[rows, cols]
            qq = q[rows, cols]
            p = probs_of(stack_heads(qq, first), kk, (tab[2 * hp], tab[2 * hp + 1]), lb.at[b] if b < nl else sb.at[b - nl], n)
            out = dot(p.astype(jnp.bfloat16), vv, 1, 0)
            mixed[rows, cols] = jnp.where(first, out[:128], out[128:]).astype(jnp.bfloat16)
def attn_bwd_kernel(nl, ns, blocks, ll, sl, q, k, v, kl, vl, mg, tab, lcol, lrow, scol, srow, dq, dk, dv, dkl, dvl, seg, lb, sb, li, si):
    attn_setup(nl, ns, blocks, ll, sl, lcol, lrow, scol, srow, lb, sb)
    me = lax.axis_index("seq")
    lane = lax.broadcasted_iota(jnp.int32, (128, 128), 1)
    edge = jnp.full((128, 128), 4096, jnp.int32)
    for i, e in enumerate(EDGES):
        edge = jnp.where(lane == i, e, edge)
    edge = jnp.where(lane > len(EDGES), -4096, edge)
    def places(out, q_col, k_col, k_first):
        t = lax.broadcasted_iota(jnp.int32, (128, 256), 1) + k_first
        below = jnp.sum((k_col < t).astype(jnp.int32), axis=0, keepdims=True)
        at = jnp.clip(q_col + edge - k_first, 0, 255)
        lo = jnp.take_along_axis(jnp.broadcast_to(below[:, :128], (128, 128)), at & 127, axis=1)
        hi = jnp.take_along_axis(jnp.broadcast_to(below[:, 128:], (128, 128)), at & 127, axis=1)
        out[...] = jnp.where(at < 128, lo, hi) - 1
    for b in range(nl):
        for c in range(blocks):
            places(li.at[b, c], lcol[b, me], lcol[b, c], lrow[b, c, 0, 0])
    for b in range(ns):
        places(si.at[b, 0], scol[b, 0], scol[b, 0], srow[b, 0, 0, 0])
    seg[...] = jnp.zeros_like(seg)
    first = lane < 64
    row = lax.broadcasted_iota(jnp.int32, (128, 128), 0)
    tri = jnp.where(row <= lane, 1.0, 0.0).astype(jnp.bfloat16)
    @pl.loop(0, 8)
    def _(hp):
        cols = pl.ds(pl.multiple_of(hp * 128, 128), 128)
        for b in range(nl + ns):
            rows = pl.ds(b * 128, 128)
            n = blocks if b < nl else 1
            if b < nl:
                kk = kl[:, b, :, cols].reshape(n * 128, 128); vv = vl[:, b, :, cols].reshape(n * 128, 128)
            else:
                kk = k[rows, cols]; vv = v[rows, cols]
            qq = q[rows, cols]; gg = mg[rows, cols]
            idx = li.at[b] if b < nl else si.at[b - nl]
            qs = stack_heads(qq, first); gs = stack_heads(gg, first)
            p = probs_of(qs, kk, (tab[2 * hp], tab[2 * hp + 1]), lb.at[b] if b < nl else sb.at[b - nl], n)
            dp = dot(gs, vv, 1, 1)
            ds = (p * (dp - jnp.sum(p * dp, axis=1, keepdims=True))).astype(jnp.bfloat16)
            dqs = dot(ds, kk, 1, 0)
            dkt = dot(qs, ds, 0, 0)
            dvt = dot(gs, p.astype(jnp.bfloat16), 0, 0)
            sums = [0, 0]
            for c in range(n):
                pre = dot(ds[:, c * 128:(c + 1) * 128], tri, 1, 0)
                at = idx[c]
                for e in range(2):
                    sums[e] += jnp.where(at >= 0, jnp.take_along_axis(pre[e * 128:(e + 1) * 128], jnp.maximum(at, 0), axis=1), 0.0)
            for e in range(2):
                seg[2 * hp + e] += jnp.sum(sums[e], axis=0, keepdims=True)
            dq[rows, cols] = jnp.where(first, dqs[:128], dqs[128:]).astype(jnp.bfloat16)
            dkt = dkt.T.astype(jnp.bfloat16); dvt = dvt.T.astype(jnp.bfloat16)
            if b < nl:
                dkl[:, b, :, cols] = dkt.reshape(n, 128, 128); dvl[:, b, :, cols] = dvt.reshape(n, 128, 128)
            else:
                dk[pl.ds((b - nl) * 128, 128), cols] = dkt; dv[pl.ds((b - nl) * 128, 128), cols] = dvt
def attention(backward, nl, ns, blocks, arrays, tokens, width):
    sm, vm = pl.BlockSpec(memory_space=pltpu.SMEM), pl.BlockSpec(memory_space=pltpu.VMEM)
    bf = jnp.bfloat16
    rows = jax.ShapeDtypeStruct((tokens, width), bf)
    buckets = [pltpu.VMEM((nl, blocks, 128, 128), jnp.int32), pltpu.VMEM((ns, 1, 128, 128), jnp.int32)]
    if backward:
        short = jax.ShapeDtypeStruct((ns * 128, width), bf)
        long = jax.ShapeDtypeStruct((blocks, nl, 128, width), bf)
        outs = [rows, short, short, long, long, jax.ShapeDtypeStruct((16, 1, 128), jnp.float32)]
        body = functools.partial(attn_bwd_kernel, nl, ns, blocks); scr = buckets * 2
    else:
        outs = [rows]; body = functools.partial(attn_fwd_kernel, nl, ns, blocks); scr = buckets
    return pl.pallas_call(body, out_shape=outs, in_specs=[sm, sm] + [vm] * (len(arrays) - 2), out_specs=[vm] * len(outs),
        scratch_shapes=scr, compiler_params=pltpu.CompilerParams(vmem_limit_bytes=56 * 2**20))(*arrays)


def seq_places(C):
    s = lax.axis_index("seq"); g = lax.axis_index("dp")
    x, c = s // C, lax.rem(s, C)
    return s, x, c, ((1 - x) * C + c, g), (x * C + 1 - c, g)
def greet(devs):
    bar = pltpu.get_barrier_semaphore()
    for d in devs:
        pl.semaphore_signal(bar, inc=1, device_id=d, device_id_type=MESH)
    pl.semaphore_wait(bar, len(devs))
def remote(src, dst, ss, rs, dev):
    cp = pltpu.make_async_remote_copy(src_ref=src, dst_ref=dst, send_sem=ss, recv_sem=rs, device_id=dev, device_id_type=MESH)
    cp.start()
    return cp
def seq_gather_kernel(n, items, rows, *refs):
    ins, outs = refs[:n], refs[n:2 * n]
    lsem, ss, rs = refs[2 * n:]
    s, x, c, xdev, cdev = seq_places(2)
    far = (1 - x) * 2 + c
    greet([xdev, cdev])
    local, a, b = [], [], []
    pieces = [(m, i) for m in range(n) for i in range(items)]
    for k, (m, i) in enumerate(pieces):
        src = ins[m].at[pl.ds(i * rows, rows)]
        a.append(remote(src, outs[m].at[s, i], ss.at[k, 0], rs.at[k, 0], xdev))
        b.append(remote(src, outs[m].at[s, i], ss.at[k, 1], rs.at[k, 1], cdev))
        cp = pltpu.make_async_copy(src, outs[m].at[s, i], lsem.at[k]); cp.start(); local.append(cp)
    f = []
    for k, (m, i) in enumerate(pieces):
        a[k].wait_recv()
        f.append(remote(outs[m].at[far, i], outs[m].at[far, i], ss.at[k, 2], rs.at[k, 2], cdev))
    for k in range(len(pieces)):
        local[k].wait(); a[k].wait_send(); b[k].wait(); f[k].wait()
def seq_gather(arrays, items, rows, seq, cid):
    n = len(arrays); q = n * items
    sem = pltpu.SemaphoreType.DMA
    any_ = pl.BlockSpec(memory_space=pltpu.VMEM)
    return pl.pallas_call(functools.partial(seq_gather_kernel, n, items, rows),
        out_shape=[jax.ShapeDtypeStruct((seq, items, rows, a.shape[-1]), a.dtype) for a in arrays],
        in_specs=[any_] * n, out_specs=[any_] * n,
        scratch_shapes=[sem((q,)), sem((q, 3)), sem((q, 3))],
        compiler_params=pltpu.CompilerParams(collective_id=cid, has_side_effects=True, vmem_limit_bytes=48*2**20))(*arrays)
def seq_sum_kernel(n, items, *refs):
    ins, outs = refs[:n], refs[n:2 * n]
    cb, a1, b1, ss, rs = refs[2 * n:]
    s, x, c, xdev, cdev = seq_places(2)
    greet([xdev, cdev])
    pieces = [(m, i) for m in range(n) for i in range(items)]
    first = [[None, None] for _ in pieces]
    second = []
    f32 = jnp.float32
    for far in range(2):
        xx = 1 - x if far == 0 else x
        for k, (m, i) in enumerate(pieces):
            first[k][far] = remote(ins[m].at[xx * 2 + 1 - c, i], cb.at[k, far], ss.at[k, far], rs.at[k, far], cdev)
    for k, (m, i) in enumerate(pieces):
        first[k][0].wait_recv()
        a1[k] = (ins[m][(1 - x) * 2 + c, i].astype(f32) + cb[k, 0].astype(f32)).astype(a1.dtype)
        second.append(remote(a1.at[k], b1.at[k], ss.at[k, 2], rs.at[k, 2], xdev))
    for k, (m, i) in enumerate(pieces):
        first[k][1].wait_recv()
        second[k].wait_recv()
        outs[m][i] = (ins[m][s, i].astype(f32) + cb[k, 1].astype(f32) + b1[k].astype(f32)).astype(outs[m].dtype)
    for k in range(len(pieces)):
        first[k][0].wait_send(); first[k][1].wait_send(); second[k].wait_send()
def seq_sum(arrays, cid):
    n = len(arrays); seq, items, rows, w = arrays[0].shape; q = n * items
    sem = pltpu.SemaphoreType.DMA; dt = arrays[0].dtype
    vm = pl.BlockSpec(memory_space=pltpu.VMEM)
    return pl.pallas_call(functools.partial(seq_sum_kernel, n, items),
        out_shape=[jax.ShapeDtypeStruct((items, rows, w), dt) for a in arrays],
        in_specs=[vm] * n, out_specs=[vm] * n,
        scratch_shapes=[pltpu.VMEM((q, 2, rows, w), dt), pltpu.VMEM((q, rows, w), dt), pltpu.VMEM((q, rows, w), dt), sem((q, 3)), sem((q, 3))],
        compiler_params=pltpu.CompilerParams(collective_id=cid, has_side_effects=True, vmem_limit_bytes=48 * 2**20))(*arrays)


def gelu_parts(v):
    c, a = 0.7978845608, 0.044715
    v2 = v * v
    t = jnp.tanh(c * v * (1.0 + a * v2))
    half = 0.5 * (1.0 + t)
    return v * half, half + 0.5 * v * (1.0 - t * t) * (c * (1.0 + 3.0 * a * v2))
def expert_kernel(cap, per, order, wcut, tile, xs, gs, wgi, wui, wdi, eo_out, ri_out, dg_out, du_out, dd_out,
                  wg, wu, wd, xr, gr, hid, gg, ug, eo, ri, xt, gt, stage,
                  lsem, xss, xrs, gss, grs, ess, ers, rss, rrs, wss, wrs, wls, osem, ssem):
    dp = lax.axis_size("dp")
    f32, bf = jnp.float32, jnp.bfloat16
    s, x, c, xdev, cdev = seq_places(2)
    g = lax.axis_index("dp")
    def peer(k): return (s, g ^ k)
    greet([xdev, cdev] + [peer(k) for k in range(1, dp)])
    rows_w = wgi.shape[0]; ff = wgi.shape[1]; width = xs.shape[2]
    piece = rows_w // wcut
    own, far = s * rows_w, ((1 - x) * 2 + c) * rows_w
    mats = ((wgi, wg), (wui, wu), (wdi, wd))
    wx, wc, wl = [], [], []
    for h in range(wcut):
        for m, (src, dst) in enumerate(mats):
            n = len(wx)
            a = src.at[pl.ds(h * piece, piece)]
            b = dst.at[pl.ds(own + h * piece, piece)]
            wx.append(remote(a, b, wss.at[n, 0], wrs.at[n, 0], xdev))
            wc.append(remote(a, b, wss.at[n, 1], wrs.at[n, 1], cdev))
            cp = pltpu.make_async_copy(a, b, wls.at[n]); cp.start(); wl.append(cp)
    sx, sg = {}, {}
    for k in [k for p in order for k in range(p * per, (p + 1) * per)]:
        at = pl.ds(k * cap, cap)
        if k == 0:
            sx[0] = pltpu.make_async_copy(xs.at[g], xr.at[at], lsem.at[0]); sx[0].start()
            sg[0] = pltpu.make_async_copy(gs.at[g], gr.at[at], lsem.at[1]); sg[0].start()
        else:
            sx[k] = remote(xs.at[g ^ k], xr.at[at], xss.at[k], xrs.at[k], peer(k))
            sg[k] = remote(gs.at[g ^ k], gr.at[at], gss.at[k], grs.at[k], peer(k))
    wf = []
    for h in range(wcut):
        for m, (src, dst) in enumerate(mats):
            n = len(wf)
            wx[n].wait_recv()
            b = dst.at[pl.ds(far + h * piece, piece)]
            wf.append(remote(b, b, wss.at[n, 2], wrs.at[n, 2], cdev))
    for n in range(len(wf)):
        wl[n].wait(); wc[n].wait_recv(); wf[n].wait_recv()
    ntile = ff // tile
    re, rr = {}, {}
    for p in order:
        ks = list(range(p * per, (p + 1) * per))
        for k in ks:
            if k == 0: sx[0].wait(); sg[0].wait()
            else: sx[k].wait_recv(); sg[k].wait_recv()
        rows = pl.ds(p * per * cap, per * cap)
        @pl.loop(0, ntile)
        def _(t):
            cols = pl.ds(pl.multiple_of(t * tile, 128), tile)
            gp = jnp.dot(xr[rows, :], wg[:, cols], preferred_element_type=f32)
            up = jnp.dot(xr[rows, :], wu[:, cols], preferred_element_type=f32)
            hg = jnp.dot(gr[rows, :], wd[:, cols], preferred_element_type=f32)
            act, der = gelu_parts(gp)
            hid[rows, cols] = (act * up).astype(bf)
            gg[rows, cols] = (hg * up * der).astype(bf)
            ug[rows, cols] = (hg * act).astype(bf)
        @pl.loop(0, width // 256)
        def _(t):
            part = pl.ds(pl.multiple_of(t * 256, 256), 256)
            eo[rows, part] = dot(hid[rows, :], wd[part, :], 1, 1).astype(bf)
            ri[rows, part] = (dot(gg[rows, :], wg[part, :], 1, 1) + dot(ug[rows, :], wu[part, :], 1, 1)).astype(bf)
        for k in ks:
            at = pl.ds(k * cap, cap)
            if k == 0:
                re[0] = pltpu.make_async_copy(eo.at[at], eo_out.at[g], lsem.at[2]); re[0].start()
                rr[0] = pltpu.make_async_copy(ri.at[at], ri_out.at[g], lsem.at[3]); rr[0].start()
            else:
                re[k] = remote(eo.at[at], eo_out.at[g], ess.at[k], ers.at[k], peer(k))
                rr[k] = remote(ri.at[at], ri_out.at[g], rss.at[k], rrs.at[k], peer(k))
    total = dp * cap
    @pl.loop(0, total // 256)
    def _(t):
        at = pl.ds(pl.multiple_of(t * 256, 256), 256)
        xt[:, at] = xr[at, :].T
        gt[:, at] = gr[at, :].T
    for m, (lhs, rhs, out) in enumerate(((gt, hid, dd_out), (xt, gg, dg_out), (xt, ug, du_out))):
        @pl.loop(0, ntile)
        def _(t):
            cols = pl.ds(pl.multiple_of(t * tile, 128), tile)
            res = jnp.dot(lhs[...], rhs[:, cols], preferred_element_type=f32).astype(bf)
            stage[...] = res
            cp = pltpu.make_async_copy(stage, out.at[:, cols], osem.at[0])
            cp.start(); cp.wait()
    for n in range(len(wf)):
        wx[n].wait_send(); wc[n].wait_send(); wf[n].wait_send()
    for k in range(dp):
        if k == 0:
            re[0].wait(); rr[0].wait()
        else:
            sx[k].wait_send(); sg[k].wait_send(); re[k].wait(); rr[k].wait()
def expert_all(xs, gs, wg, wu, wd, seq, cid):
    dp, cap, width = xs.shape
    ff = wg.shape[1]; total = dp * cap
    group = 320
    per = group // cap
    ng = dp // per
    order = [p for p in range(ng // 2, ng)] + [p for p in range(ng // 2 - 1, -1, -1)]
    sem = pltpu.SemaphoreType.DMA
    bf = jnp.bfloat16
    any_ = pl.BlockSpec(memory_space=pl.ANY)
    V = pltpu.VMEM
    tile = 256
    wcut = 2
    full = (seq * wg.shape[0], ff)
    back = jax.ShapeDtypeStruct((dp, cap, width), bf)
    loc = jax.ShapeDtypeStruct(full, bf)
    return pl.pallas_call(functools.partial(expert_kernel, cap, per, order, wcut, tile),
        out_shape=[back, back, loc, loc, loc],
        in_specs=[any_] * 5, out_specs=[any_] * 5,
        scratch_shapes=[V(full, bf)] * 3 + [V((total, width), bf)] * 2 + [V((total, ff), bf)] * 3 + [V((total, width), bf)] * 2
        + [V((width, total), bf)] * 2 + [V((width, tile), bf)]
        + [sem((4,))] + [sem((dp,))] * 8 + [sem((3 * wcut, 3))] * 2 + [sem((3 * wcut,)), sem((1,)), sem((1,))],
        compiler_params=pltpu.CompilerParams(collective_id=cid, has_side_effects=True, vmem_limit_bytes=63 * 2**20))(xs, gs, wg, wu, wd)


def on_device(
    long_tokens,
    short_tokens,
    long_grad_out,
    short_grad_out,
    query_weight,
    key_weight,
    value_weight,
    output_weight,
    attn_gain,
    ffn_gain,
    rel_table,
    router_weight,
    gate_weight,
    up_weight,
    down_weight,
    long_positions,
    short_positions,
    long_lengths,
    short_lengths,
    long_routes,
    short_routes,
):
    long_items, quarter, model_width = long_tokens.shape
    short_items, short_len = (short_tokens.shape[0], short_tokens.shape[1])
    long_rows = long_items * quarter
    tokens = long_rows + short_items * short_len
    local_experts = gate_weight.shape[0]
    dp_size = lax.axis_size("dp")
    experts = local_experts * dp_size
    capacity = (5 * tokens + 2 * experts - 1) // (2 * experts)
    seq_index = lax.axis_index("seq")
    seq_size = lax.axis_size("seq")
    dims = (seq_size // 2, 2, dp_size // 2, 2)
    devices = seq_size * dp_size
    table_part, router_part = rel_table.shape[0], router_weight.size
    gain_part = attn_gain.shape[0]
    small_size = 2 * gain_part + table_part + router_part
    small = jnp.concatenate([attn_gain, ffn_gain, rel_table, router_weight.reshape(-1)])
    small = jnp.pad(small, (0, -small_size % 2048)).reshape(-1, 128)
    rows_part = query_weight.shape[0]
    cuts = 2 if rows_part % 32 == 0 else 1
    cut = rows_part // cuts
    pieces = tuple((m, h * cut, cut, (m + h) % 2) for m in range(4) for h in range(cuts))
    gathered = gather_all(
        (query_weight, key_weight, value_weight, output_weight, small),
        pieces[: 3 * cuts] + ((4, 0, small.shape[0], 0),) + pieces[3 * cuts :],
        dims,
        0,
    )
    small_all = gathered[4].reshape(devices, -1)
    attn_set = tuple(block.reshape(devices * rows_part, model_width) for block in gathered[:4]) + (
        small_all[:, :gain_part].reshape(-1),
        small_all[:, gain_part : 2 * gain_part].reshape(-1),
        small_all[:, 2 * gain_part : 2 * gain_part + table_part].reshape(-1),
        small_all[:, 2 * gain_part + table_part : small_size].reshape(model_width, experts),
    )
    resid_in = jnp.concatenate(
        [long_tokens.reshape(long_rows, model_width), short_tokens.reshape(-1, model_width)], 0
    ).astype(jnp.float32)
    gain_first = attn_set[4].astype(jnp.float32)
    normed = rms_norm(resid_in, gain_first).astype(jnp.bfloat16)
    projected = [
        jnp.dot(normed, matrix, preferred_element_type=jnp.float32).astype(jnp.bfloat16)
        for matrix in attn_set[:3]
    ]
    queries, keys, values = projected
    long_keys, long_values = seq_gather((keys, values), long_items, quarter, seq_size, 2)
    table = attn_set[6].reshape(HEADS, 1, BUCKETS).astype(jnp.float32)
    table = jnp.pad(table, ((0, 0), (0, 0), (0, 128 - BUCKETS)), constant_values=masked)
    attn_args = (
        table,
        long_positions.reshape(long_items, seq_size, quarter, 1),
        long_positions.reshape(long_items, seq_size, 1, quarter),
        short_positions.reshape(short_items, 1, short_len, 1),
        short_positions.reshape(short_items, 1, 1, short_len),
    )
    lead_args = (long_lengths, short_lengths, queries, keys, values, long_keys, long_values)
    (mixed_all,) = attention(
        False, long_items, short_items, seq_size, lead_args + attn_args, tokens, model_width
    )
    resid_mid = resid_in + jnp.dot(mixed_all, attn_set[3], preferred_element_type=jnp.float32)
    gain_second = attn_set[5].astype(jnp.float32)
    normed_two = rms_norm(resid_mid, gain_second).astype(jnp.bfloat16)
    logits = jnp.dot(normed_two, attn_set[7], preferred_element_type=jnp.float32)
    routes = jnp.concatenate([long_routes.reshape(-1, 2), short_routes.reshape(-1, 2)], 0)
    choose = (routes[..., None] == jnp.arange(experts, dtype=jnp.int32)).astype(jnp.float32)
    gate_share, gate_pull = jax.vjp(lambda logit_in: gate_values(logit_in, choose), logits)
    flat_routes = routes.reshape(-1)
    member = (flat_routes[:, None] == jnp.arange(experts, dtype=jnp.int32)).astype(jnp.int32)
    queue_pos = jnp.sum(jnp.cumsum(member, axis=0) * member, axis=1) - 1
    route_kept = queue_pos < capacity
    slot_index = jnp.where(route_kept, flat_routes * capacity + queue_pos, experts * capacity)
    slot_pair = (
        jnp.zeros(experts * capacity + 1, jnp.int32)
        .at[slot_index]
        .set(jnp.arange(2 * tokens, dtype=jnp.int32))[:-1]
    )
    slot_used = jnp.zeros(experts * capacity + 1, jnp.bool_).at[slot_index].set(True)[:-1]
    pair_slot = jnp.where(route_kept, slot_index, 0)
    outgoing = jnp.where(
        slot_used[:, None], jnp.take(normed_two, slot_pair // 2, axis=0), 0
    ).reshape(experts, capacity, model_width)
    kept_two = route_kept.reshape(tokens, 2).astype(jnp.float32)
    weighting = gate_share * kept_two
    grad_out = jnp.concatenate(
        [long_grad_out.reshape(long_rows, model_width), short_grad_out.reshape(-1, model_width)], 0
    ).astype(jnp.float32)
    pair_grad = (
        (weighting[:, :, None] * grad_out[:, None, :])
        .astype(jnp.bfloat16)
        .reshape(2 * tokens, model_width)
    )
    out_slots = jnp.where(slot_used[:, None], jnp.take(pair_grad, slot_pair, axis=0), 0).reshape(
        experts, capacity, model_width
    )
    back_rows, returned_grad, gate_local, up_local, down_local = expert_all(
        outgoing, out_slots, gate_weight[0], up_weight[0], down_weight[0], seq_size, 4
    )
    pair_out = (
        jnp.where(
            route_kept[:, None],
            jnp.take(back_rows.reshape(experts * capacity, model_width), pair_slot, axis=0),
            0,
        )
        .reshape(tokens, 2, model_width)
        .astype(jnp.float32)
    )
    final = resid_mid + weighting[:, 0:1] * pair_out[:, 0] + weighting[:, 1:2] * pair_out[:, 1]
    final_low = final.astype(jnp.bfloat16)
    long_out = final_low[:long_rows].reshape(long_items, quarter, model_width)
    short_out = final_low[long_rows:].reshape(short_items, short_len, model_width)
    share_grad = kept_two * jnp.sum(grad_out[:, None, :] * pair_out, axis=-1)
    logit_grad = gate_pull(share_grad)[0].astype(jnp.bfloat16)
    attn_back = attn_set
    gate_grad, up_grad, down_grad = (
        lax.psum_scatter(part[None], "seq", scatter_dimension=1, tiled=True).astype(jnp.float32)
        for part in (gate_local, up_local, down_local)
    )
    route_grad = (
        jnp.where(
            route_kept[:, None],
            jnp.take(returned_grad.reshape(experts * capacity, model_width), pair_slot, axis=0),
            0,
        )
        .reshape(tokens, 2, model_width)
        .astype(jnp.float32)
    )
    normed_two_grad = (
        route_grad[:, 0]
        + route_grad[:, 1]
        + jnp.einsum("te,de->td", logit_grad, attn_back[7], preferred_element_type=jnp.float32)
    )
    router_local = jnp.einsum(
        "td,te->de", normed_two, logit_grad, preferred_element_type=jnp.float32
    )
    unused_mid, norm_two_pull = jax.vjp(rms_norm, resid_mid, attn_back[5].astype(jnp.float32))
    mid_norm_grad, ffn_gain_local = norm_two_pull(normed_two_grad)
    middle_grad = grad_out + mid_norm_grad
    branch_grad = middle_grad.astype(jnp.bfloat16)
    output_local = jnp.einsum(
        "td,te->de", mixed_all, branch_grad, preferred_element_type=jnp.float32
    )
    mix_grad = jnp.einsum(
        "te,de->td", branch_grad, attn_back[3], preferred_element_type=jnp.float32
    ).astype(jnp.bfloat16)
    query_act, short_key, short_value, long_key, long_value, table_sums = attention(
        True,
        long_items,
        short_items,
        seq_size,
        lead_args + (mix_grad,) + attn_args,
        tokens,
        model_width,
    )
    long_key, long_value = seq_sum((long_key, long_value), 3)
    key_act = jnp.concatenate([long_key.reshape(long_rows, model_width), short_key], 0)
    value_act = jnp.concatenate([long_value.reshape(long_rows, model_width), short_value], 0)
    upto = table_sums.reshape(HEADS, 128)[:, : len(ORDER)]
    within = upto - jnp.pad(upto[:, :-1], ((0, 0), (1, 0)))
    table_local = jnp.stack(
        [
            within[:, ORDER.index(n)] if n in ORDER else jnp.zeros(HEADS, jnp.float32)
            for n in range(BUCKETS)
        ],
        1,
    ).reshape(-1)
    normed_grad = (
        jnp.einsum("te,de->td", query_act, attn_back[0], preferred_element_type=jnp.float32)
        + jnp.einsum("te,de->td", key_act, attn_back[1], preferred_element_type=jnp.float32)
        + jnp.einsum("te,de->td", value_act, attn_back[2], preferred_element_type=jnp.float32)
    )
    query_local = jnp.einsum("td,te->de", normed, query_act, preferred_element_type=jnp.float32)
    key_local = jnp.einsum("td,te->de", normed, key_act, preferred_element_type=jnp.float32)
    value_local = jnp.einsum("td,te->de", normed, value_act, preferred_element_type=jnp.float32)
    unused_in, norm_one_pull = jax.vjp(rms_norm, resid_in, attn_back[4].astype(jnp.float32))
    in_norm_grad, attn_gain_local = norm_one_pull(normed_grad)
    input_grad_all = middle_grad + in_norm_grad
    long_grad_in = input_grad_all[:long_rows].reshape(long_items, quarter, model_width)
    short_grad_in = input_grad_all[long_rows:].reshape(short_items, short_len, model_width)
    shares = (gain_part, gain_part, table_part, router_part)
    small_local = jnp.concatenate(
        [
            part.reshape(devices, -1)
            for part in (attn_gain_local, ffn_gain_local, table_local, router_local)
        ],
        1,
    )
    small_local = jnp.pad(small_local, ((0, 0), (0, -small_size % 1024)))
    small_rows = small_local.shape[1] // 128
    mats = tuple(
        part.astype(jnp.bfloat16).reshape(dims + (rows_part, model_width))
        for part in (output_local, query_local, key_local, value_local)
    )
    scattered = scatter_all(
        mats + (small_local.reshape(dims + (small_rows, 128)),),
        pieces[:cuts] + ((4, 0, small_rows, 0),) + pieces[cuts:],
        dims,
        1,
    )
    small_sum = scattered[4].reshape(-1)
    edges = [sum(shares[:k]) for k in range(5)]
    summed = (scattered[1], scattered[2], scattered[3], scattered[0]) + tuple(
        small_sum[edges[k] : edges[k + 1]] for k in range(3)
    ) + (small_sum[edges[3] : edges[4]].reshape(rows_part, experts),)
    return (
        long_out,
        short_out,
        long_grad_in,
        short_grad_in,
        summed[0],
        summed[1],
        summed[2],
        summed[3],
        summed[4],
        summed[5],
        summed[6],
        summed[7],
        gate_grad,
        up_grad,
        down_grad,
    )


def solution(mesh):
    placed = (
        P("dp", "seq", None),
        P(("seq", "dp"), None, None),
        P("dp", "seq", None),
        P(("seq", "dp"), None, None),
        P(("seq", "dp"), None),
        P(("seq", "dp"), None),
        P(("seq", "dp"), None),
        P(("seq", "dp"), None),
        P(("seq", "dp")),
        P(("seq", "dp")),
        P(("seq", "dp")),
        P(("seq", "dp"), None),
        P("dp", "seq", None),
        P("dp", "seq", None),
        P("dp", "seq", None),
        P("dp", None),
        P(("seq", "dp"), None),
        P("dp"),
        P(("seq", "dp")),
        P("dp", "seq", None),
        P(("seq", "dp"), None, None),
    )
    return jax.shard_map(
        on_device,
        mesh=mesh,
        in_specs=placed,
        out_specs=(
            P("dp", "seq", None),
            P(("seq", "dp"), None, None),
            P("dp", "seq", None),
            P(("seq", "dp"), None, None),
            P(("seq", "dp"), None),
            P(("seq", "dp"), None),
            P(("seq", "dp"), None),
            P(("seq", "dp"), None),
            P(("seq", "dp")),
            P(("seq", "dp")),
            P(("seq", "dp")),
            P(("seq", "dp"), None),
            P("dp", "seq", None),
            P("dp", "seq", None),
            P("dp", "seq", None),
        ),
        check_vma=False,
    )
```

```python
import functools

import jax
import jax.numpy as jnp
from jax import lax
from jax.experimental import pallas as pl
from jax.experimental.pallas import tpu as pltpu
from jax.sharding import PartitionSpec as P

MESH = pl.DeviceIdType.MESH

HEADS = 16
HEAD = 64
BUCKETS = 32


epsilon = 1e-06
masked = -1e30


def rms_norm(hidden, gain):
    scale = lax.rsqrt(jnp.mean(hidden * hidden, axis=-1, keepdims=True) + epsilon)
    return hidden * scale * gain


def gate_values(logits, choose):
    probs = jax.nn.softmax(logits, axis=-1)
    chosen = jnp.sum(choose * probs[:, None, :], axis=-1)
    return chosen / jnp.sum(chosen, axis=-1, keepdims=True)


def gather_kernel(dims, pieces, na, *refs):
    X, C, Z, Y = dims
    n = len(pieces)
    lsem, zs, zr, hs, hr, cs, cr = refs[2*na:]
    routes = [p[3] for p in pieces]
    ins = [refs[m].at[pl.ds(r0, nr)] for m, r0, nr, _ in pieces]
    class V:
        def __init__(self, ref, r0, nr): self.ref, self.r0, self.nr = ref, r0, nr
        @property
        def at(self): return self
        def __getitem__(self, k):
            k = k + (slice(None),) * (4 - len(k)) + (pl.ds(self.r0, self.nr),)
            return self.ref.at[k]
    outs = [V(refs[na + m], r0, nr) for m, r0, nr, _ in pieces]
    s = lax.axis_index("seq"); g = lax.axis_index("dp")
    x, c = s // C, lax.rem(s, C)
    z, y = g // Y, lax.rem(g, Y)
    def zdev(k): return (s, lax.rem(z + k, Z) * Y + y)
    ydev = (s, z * Y + (1 - y)); xdev = ((1 - x) * C + c, g); cdev = (x * C + 1 - c, g)
    bar = pltpu.get_barrier_semaphore()
    for d in [zdev(k) for k in range(1, Z)] + [ydev, xdev, cdev]:
        pl.semaphore_signal(bar, inc=1, device_id=d, device_id_type=MESH)
    pl.semaphore_wait(bar, Z + 2)
    def rc(src, dst, ss, rs, dev):
        cp = pltpu.make_async_remote_copy(src_ref=src, dst_ref=dst, send_sem=ss, recv_sem=rs, device_id=dev, device_id_type=MESH)
        cp.start(); return cp
    sends = []
    local = []; zc = []
    for m in range(n):
        lc = pltpu.make_async_copy(ins[m], outs[m].at[x, c, z, y], lsem.at[m]); lc.start(); local.append(lc)
        zc.append([rc(ins[m], outs[m].at[x, c, z, y], zs.at[m, k], zr.at[m, k], zdev(k)) for k in range(1, Z)])
    h = [[None, None] for _ in range(n)]
    cc = [[None]*3 for _ in range(n)]
    for t in range(n + 2):
        for stage in range(3):
            m = t - stage
            if not 0 <= m < n: continue
            o = outs[m]; route = routes[m]
            if stage == 0:
                local[m].wait()
                for q in zc[m]: q.wait_recv()
                mine = o.at[x, c, :, y]
                h[m][0] = rc(mine, mine, hs.at[m,0], hr.at[m,0], xdev if route == 0 else ydev)
                cc[m][0] = rc(mine, mine, cs.at[m,0], cr.at[m,0], cdev)
            elif stage == 1:
                h[m][0].wait_recv()
                if route == 0:
                    both = o.at[:, c, :, y]; got = o.at[1 - x, c, :, y]
                else:
                    both = o.at[x, c]; got = o.at[x, c, :, 1 - y]
                h[m][1] = rc(both, both, hs.at[m,1], hr.at[m,1], ydev if route == 0 else xdev)
                cc[m][1] = rc(got, got, cs.at[m,1], cr.at[m,1], cdev)
            else:
                h[m][1].wait_recv()
                got = o.at[:, c, :, 1 - y] if route == 0 else o.at[1 - x, c]
                cc[m][2] = rc(got, got, cs.at[m,2], cr.at[m,2], cdev)
    for m in range(n):
        for q in zc[m]: q.wait_send()
        for q in h[m]: q.wait_send()
        for q in cc[m]: q.wait()
def gather_all(arrays, pieces, dims, cid):
    X, C, Z, Y = dims; na = len(arrays); n = len(pieces)
    sem = pltpu.SemaphoreType.DMA
    return pl.pallas_call(functools.partial(gather_kernel, dims, pieces, na),
        out_shape=[jax.ShapeDtypeStruct((X, C, Z, Y) + a.shape, a.dtype) for a in arrays],
        in_specs=[pl.BlockSpec(memory_space=pl.ANY)] * na, out_specs=[pl.BlockSpec(memory_space=pl.ANY)] * na,
        scratch_shapes=[sem((n,)), sem((n, Z)), sem((n, Z)), sem((n, 2)), sem((n, 2)), sem((n, 3)), sem((n, 3))],
        compiler_params=pltpu.CompilerParams(collective_id=cid, has_side_effects=True))(*arrays)


def scatter_kernel(dims, pieces, n, *refs):
    X, C, Z, Y = dims
    ins, outs = refs[:n], refs[n:2*n]
    np_ = len(pieces)
    bufs = refs[2*n:2*n+7*np_]
    sems = refs[2*n+7*np_:]
    cs, cr, hs, hr, zs, zr = sems
    s = lax.axis_index("seq"); g = lax.axis_index("dp")
    x, c = s // C, lax.rem(s, C)
    z, y = g // Y, lax.rem(g, Y)
    def zdev(k): return (s, lax.rem(z + k, Z) * Y + y)
    ydev = (s, z * Y + (1 - y)); xdev = ((1 - x) * C + c, g); cdev = (x * C + 1 - c, g)
    bar = pltpu.get_barrier_semaphore()
    for d in [zdev(k) for k in range(1, Z)] + [ydev, xdev, cdev]:
        pl.semaphore_signal(bar, inc=1, device_id=d, device_id_type=MESH)
    pl.semaphore_wait(bar, Z + 2)
    def rc(src, dst, ss, rs, dev):
        cp = pltpu.make_async_remote_copy(src_ref=src, dst_ref=dst, send_sem=ss, recv_sem=rs, device_id=dev, device_id_type=MESH)
        cp.start(); return cp
    def add(dst, a, b):
        dst[...] = (a.astype(jnp.float32) + b.astype(jnp.float32)).astype(dst.dtype)
    first = []
    for i, (m, r0, nr, route) in enumerate(pieces):
        cb = bufs[7*i]
        src = ins[m].at[:, 1 - c, :, :, pl.ds(r0, nr)]
        first.append(rc(src, cb, cs.at[i], cr.at[i], cdev))
    hh = [[None, None] for _ in pieces]; zz = [None] * np_
    for t in range(np_ + 3):
        for stage in range(4):
            i = t - stage
            if not 0 <= i < np_: continue
            m, r0, nr, route = pieces[i]
            cb, a1, b1, a2, b2, a3, b3 = bufs[7*i:7*i+7]
            if stage == 0:
                first[i].wait_recv()
                add(a1, ins[m][:, c, :, :, pl.ds(r0, nr)], cb[...])
                src = a1.at[:, :, 1 - y] if route == 0 else a1.at[1 - x]
                hh[i][0] = rc(src, b1, hs.at[i, 0], hr.at[i, 0], ydev if route == 0 else xdev)
            elif stage == 1:
                hh[i][0].wait_recv()
                add(a2, a1[:, :, y] if route == 0 else a1[x], b1[...])
                src = a2.at[1 - x] if route == 0 else a2.at[:, 1 - y]
                hh[i][1] = rc(src, b2, hs.at[i, 1], hr.at[i, 1], xdev if route == 0 else ydev)
            elif stage == 2:
                hh[i][1].wait_recv()
                add(a3, a2[x] if route == 0 else a2[:, y], b2[...])
                zz[i] = [rc(a3.at[lax.rem(z + k, Z)], b3.at[k - 1], zs.at[i, k], zr.at[i, k], zdev(k)) for k in range(1, Z)]
            else:
                tot = a3[z].astype(jnp.float32)
                for k in range(1, Z):
                    zz[i][k-1].wait_recv()
                    tot += b3[k - 1].astype(jnp.float32)
                outs[m][pl.ds(r0, nr), :] = tot
    for i in range(np_):
        first[i].wait_send()
        for q in hh[i]: q.wait_send()
        for q in zz[i]: q.wait_send()
def scatter_all(arrays, pieces, dims, cid):
    X, C, Z, Y = dims; n = len(arrays); q = len(pieces)
    sem = pltpu.SemaphoreType.DMA
    scr = []
    for m, r0, nr, route in pieces:
        w = arrays[m].shape[-1]; dt = arrays[m].dtype
        h1 = (X, Z) if route == 0 else (Z, Y)
        for lead in ((X, Z, Y), (X, Z, Y), h1, h1, (Z,), (Z,), (Z - 1,)):
            scr.append(pltpu.VMEM(lead + (nr, w), dt))
    return pl.pallas_call(functools.partial(scatter_kernel, dims, pieces, n),
        out_shape=[jax.ShapeDtypeStruct(a.shape[-2:], jnp.float32) for a in arrays],
        in_specs=[pl.BlockSpec(memory_space=pltpu.VMEM)] * n, out_specs=[pl.BlockSpec(memory_space=pltpu.VMEM)] * n,
        scratch_shapes=scr + [sem((q,)), sem((q,)), sem((q, 2)), sem((q, 2)), sem((q, Z)), sem((q, Z))],
        compiler_params=pltpu.CompilerParams(collective_id=cid, has_side_effects=True, vmem_limit_bytes=48*2**20))(*arrays)


EDGES = (-90, -63, -45, -31, -22, -15, -11, -7, -6, -5, -4, -3, -2, -1, 0, 1, 2, 3, 4, 5, 6, 7, 8, 12, 16, 23, 32, 46, 64, 91)
ORDER = (15, 14, 13, 12, 11, 10, 9, 8, 7, 6, 5, 4, 3, 2, 1, 0, 17, 18, 19, 20, 21, 22, 23, 24, 25, 26, 27, 28, 29, 30, 31)
FAR = (12, 16, 23, 32, 46, 64, 91)
def fill_buckets(out, q_col, k_row, length, base):
    r = k_row - q_col
    n = jnp.abs(r)
    far = jnp.full(r.shape, 8, jnp.int32)
    for e in FAR:
        far += (n >= e).astype(jnp.int32)
    b = jnp.where(n < 8, n, far) + jnp.where(r > 0, 16, 0)
    j = lax.broadcasted_iota(jnp.int32, r.shape, 1) + base
    out[...] = jnp.where(j < length, b, 32)
def dot(a, b, ca, cb):
    return lax.dot_general(a, b, (((ca,), (cb,)), ((), ())), preferred_element_type=jnp.float32)
def probs_of(qs, kk, tabs, bucket_ref, blocks):
    s = dot(qs, kk, 1, 1)
    t = [jnp.broadcast_to(tab, (128, 128)) for tab in tabs]
    bias = [jnp.concatenate([jnp.take_along_axis(x, bucket_ref[c], axis=1) for x in t], axis=0) for c in range(blocks)]
    s = s + (jnp.concatenate(bias, axis=1) if blocks > 1 else bias[0])
    p = jnp.exp(s - jnp.max(s, axis=1, keepdims=True))
    return p * (1.0 / jnp.sum(p, axis=1, keepdims=True))
def stack_heads(rows, first):
    return jnp.concatenate([jnp.where(first, rows, 0), jnp.where(first, 0, rows)], axis=0)
def attn_setup(nl, ns, blocks, ll, sl, lcol, lrow, scol, srow, lb, sb):
    me = lax.axis_index("seq")
    for b in range(nl):
        for c in range(blocks):
            fill_buckets(lb.at[b, c], lcol[b, me], lrow[b, c], ll[b], c * 128)
    for b in range(ns):
        fill_buckets(sb.at[b, 0], scol[b, 0], srow[b, 0], sl[b], 0)
def attn_fwd_kernel(nl, ns, blocks, ll, sl, q, k, v, kl, vl, tab, lcol, lrow, scol, srow, mixed, lb, sb):
    attn_setup(nl, ns, blocks, ll, sl, lcol, lrow, scol, srow, lb, sb)
    first = lax.broadcasted_iota(jnp.int32, (128, 128), 1) < 64
    @pl.loop(0, 8)
    def _(hp):
        cols = pl.ds(pl.multiple_of(hp * 128, 128), 128)
        for b in range(nl + ns):
            rows = pl.ds(b * 128, 128)
            n = blocks if b < nl else 1
            if b < nl:
                kk = kl[:, b, :, cols].reshape(n * 128, 128); vv = vl[:, b, :, cols].reshape(n * 128, 128)
            else:
                kk = k[rows, cols]; vv = v[rows, cols]
            qq = q[rows, cols]
            p = probs_of(stack_heads(qq, first), kk, (tab[2 * hp], tab[2 * hp + 1]), lb.at[b] if b < nl else sb.at[b - nl], n)
            out = dot(p.astype(jnp.bfloat16), vv, 1, 0)
            mixed[rows, cols] = jnp.where(first, out[:128], out[128:]).astype(jnp.bfloat16)
def attn_bwd_kernel(nl, ns, blocks, ll, sl, q, k, v, kl, vl, mg, tab, lcol, lrow, scol, srow, dq, dk, dv, dkl, dvl, seg, lb, sb, li, si):
    attn_setup(nl, ns, blocks, ll, sl, lcol, lrow, scol, srow, lb, sb)
    me = lax.axis_index("seq")
    lane = lax.broadcasted_iota(jnp.int32, (128, 128), 1)
    edge = jnp.full((128, 128), 4096, jnp.int32)
    for i, e in enumerate(EDGES):
        edge = jnp.where(lane == i, e, edge)
    edge = jnp.where(lane > len(EDGES), -4096, edge)
    def places(out, q_col, k_col, k_first):
        t = lax.broadcasted_iota(jnp.int32, (128, 256), 1) + k_first
        below = jnp.sum((k_col < t).astype(jnp.int32), axis=0, keepdims=True)
        at = jnp.clip(q_col + edge - k_first, 0, 255)
        lo = jnp.take_along_axis(jnp.broadcast_to(below[:, :128], (128, 128)), at & 127, axis=1)
        hi = jnp.take_along_axis(jnp.broadcast_to(below[:, 128:], (128, 128)), at & 127, axis=1)
        out[...] = jnp.where(at < 128, lo, hi) - 1
    for b in range(nl):
        for c in range(blocks):
            places(li.at[b, c], lcol[b, me], lcol[b, c], lrow[b, c, 0, 0])
    for b in range(ns):
        places(si.at[b, 0], scol[b, 0], scol[b, 0], srow[b, 0, 0, 0])
    seg[...] = jnp.zeros_like(seg)
    first = lane < 64
    row = lax.broadcasted_iota(jnp.int32, (128, 128), 0)
    tri = jnp.where(row <= lane, 1.0, 0.0).astype(jnp.bfloat16)
    @pl.loop(0, 8)
    def _(hp):
        cols = pl.ds(pl.multiple_of(hp * 128, 128), 128)
        for b in range(nl + ns):
            rows = pl.ds(b * 128, 128)
            n = blocks if b < nl else 1
            if b < nl:
                kk = kl[:, b, :, cols].reshape(n * 128, 128); vv = vl[:, b, :, cols].reshape(n * 128, 128)
            else:
                kk = k[rows, cols]; vv = v[rows, cols]
            qq = q[rows, cols]; gg = mg[rows, cols]
            idx = li.at[b] if b < nl else si.at[b - nl]
            qs = stack_heads(qq, first); gs = stack_heads(gg, first)
            p = probs_of(qs, kk, (tab[2 * hp], tab[2 * hp + 1]), lb.at[b] if b < nl else sb.at[b - nl], n)
            dp = dot(gs, vv, 1, 1)
            ds = (p * (dp - jnp.sum(p * dp, axis=1, keepdims=True))).astype(jnp.bfloat16)
            dqs = dot(ds, kk, 1, 0)
            dkt = dot(qs, ds, 0, 0)
            dvt = dot(gs, p.astype(jnp.bfloat16), 0, 0)
            sums = [0, 0]
            for c in range(n):
                pre = dot(ds[:, c * 128:(c + 1) * 128], tri, 1, 0)
                at = idx[c]
                for e in range(2):
                    sums[e] += jnp.where(at >= 0, jnp.take_along_axis(pre[e * 128:(e + 1) * 128], jnp.maximum(at, 0), axis=1), 0.0)
            for e in range(2):
                seg[2 * hp + e] += jnp.sum(sums[e], axis=0, keepdims=True)
            dq[rows, cols] = jnp.where(first, dqs[:128], dqs[128:]).astype(jnp.bfloat16)
            dkt = dkt.T.astype(jnp.bfloat16); dvt = dvt.T.astype(jnp.bfloat16)
            if b < nl:
                dkl[:, b, :, cols] = dkt.reshape(n, 128, 128); dvl[:, b, :, cols] = dvt.reshape(n, 128, 128)
            else:
                dk[pl.ds((b - nl) * 128, 128), cols] = dkt; dv[pl.ds((b - nl) * 128, 128), cols] = dvt
def attention(backward, nl, ns, blocks, arrays, tokens, width):
    sm, vm = pl.BlockSpec(memory_space=pltpu.SMEM), pl.BlockSpec(memory_space=pltpu.VMEM)
    bf = jnp.bfloat16
    rows = jax.ShapeDtypeStruct((tokens, width), bf)
    buckets = [pltpu.VMEM((nl, blocks, 128, 128), jnp.int32), pltpu.VMEM((ns, 1, 128, 128), jnp.int32)]
    if backward:
        short = jax.ShapeDtypeStruct((ns * 128, width), bf)
        long = jax.ShapeDtypeStruct((blocks, nl, 128, width), bf)
        outs = [rows, short, short, long, long, jax.ShapeDtypeStruct((16, 1, 128), jnp.float32)]
        body = functools.partial(attn_bwd_kernel, nl, ns, blocks); scr = buckets * 2
    else:
        outs = [rows]; body = functools.partial(attn_fwd_kernel, nl, ns, blocks); scr = buckets
    return pl.pallas_call(body, out_shape=outs, in_specs=[sm, sm] + [vm] * (len(arrays) - 2), out_specs=[vm] * len(outs),
        scratch_shapes=scr, compiler_params=pltpu.CompilerParams(vmem_limit_bytes=56 * 2**20))(*arrays)


def seq_places(C):
    s = lax.axis_index("seq"); g = lax.axis_index("dp")
    x, c = s // C, lax.rem(s, C)
    return s, x, c, ((1 - x) * C + c, g), (x * C + 1 - c, g)
def greet(devs):
    bar = pltpu.get_barrier_semaphore()
    for d in devs:
        pl.semaphore_signal(bar, inc=1, device_id=d, device_id_type=MESH)
    pl.semaphore_wait(bar, len(devs))
def remote(src, dst, ss, rs, dev):
    cp = pltpu.make_async_remote_copy(src_ref=src, dst_ref=dst, send_sem=ss, recv_sem=rs, device_id=dev, device_id_type=MESH)
    cp.start()
    return cp
def seq_gather_kernel(n, items, rows, *refs):
    ins, outs = refs[:n], refs[n:2 * n]
    lsem, ss, rs = refs[2 * n:]
    s, x, c, xdev, cdev = seq_places(2)
    far = (1 - x) * 2 + c
    greet([xdev, cdev])
    local, a, b = [], [], []
    pieces = [(m, i) for m in range(n) for i in range(items)]
    for k, (m, i) in enumerate(pieces):
        src = ins[m].at[pl.ds(i * rows, rows)]
        a.append(remote(src, outs[m].at[s, i], ss.at[k, 0], rs.at[k, 0], xdev))
        b.append(remote(src, outs[m].at[s, i], ss.at[k, 1], rs.at[k, 1], cdev))
        cp = pltpu.make_async_copy(src, outs[m].at[s, i], lsem.at[k]); cp.start(); local.append(cp)
    f = []
    for k, (m, i) in enumerate(pieces):
        a[k].wait_recv()
        f.append(remote(outs[m].at[far, i], outs[m].at[far, i], ss.at[k, 2], rs.at[k, 2], cdev))
    for k in range(len(pieces)):
        local[k].wait(); a[k].wait_send(); b[k].wait(); f[k].wait()
def seq_gather(arrays, items, rows, seq, cid):
    n = len(arrays); q = n * items
    sem = pltpu.SemaphoreType.DMA
    any_ = pl.BlockSpec(memory_space=pltpu.VMEM)
    return pl.pallas_call(functools.partial(seq_gather_kernel, n, items, rows),
        out_shape=[jax.ShapeDtypeStruct((seq, items, rows, a.shape[-1]), a.dtype) for a in arrays],
        in_specs=[any_] * n, out_specs=[any_] * n,
        scratch_shapes=[sem((q,)), sem((q, 3)), sem((q, 3))],
        compiler_params=pltpu.CompilerParams(collective_id=cid, has_side_effects=True, vmem_limit_bytes=48*2**20))(*arrays)
def seq_sum_kernel(n, items, *refs):
    ins, outs = refs[:n], refs[n:2 * n]
    cb, a1, b1, ss, rs = refs[2 * n:]
    s, x, c, xdev, cdev = seq_places(2)
    greet([xdev, cdev])
    pieces = [(m, i) for m in range(n) for i in range(items)]
    first = [[None, None] for _ in pieces]
    second = []
    f32 = jnp.float32
    for far in range(2):
        xx = 1 - x if far == 0 else x
        for k, (m, i) in enumerate(pieces):
            first[k][far] = remote(ins[m].at[xx * 2 + 1 - c, i], cb.at[k, far], ss.at[k, far], rs.at[k, far], cdev)
    for k, (m, i) in enumerate(pieces):
        first[k][0].wait_recv()
        a1[k] = (ins[m][(1 - x) * 2 + c, i].astype(f32) + cb[k, 0].astype(f32)).astype(a1.dtype)
        second.append(remote(a1.at[k], b1.at[k], ss.at[k, 2], rs.at[k, 2], xdev))
    for k, (m, i) in enumerate(pieces):
        first[k][1].wait_recv()
        second[k].wait_recv()
        outs[m][i] = (ins[m][s, i].astype(f32) + cb[k, 1].astype(f32) + b1[k].astype(f32)).astype(outs[m].dtype)
    for k in range(len(pieces)):
        first[k][0].wait_send(); first[k][1].wait_send(); second[k].wait_send()
def seq_sum(arrays, cid):
    n = len(arrays); seq, items, rows, w = arrays[0].shape; q = n * items
    sem = pltpu.SemaphoreType.DMA; dt = arrays[0].dtype
    vm = pl.BlockSpec(memory_space=pltpu.VMEM)
    return pl.pallas_call(functools.partial(seq_sum_kernel, n, items),
        out_shape=[jax.ShapeDtypeStruct((items, rows, w), dt) for a in arrays],
        in_specs=[vm] * n, out_specs=[vm] * n,
        scratch_shapes=[pltpu.VMEM((q, 2, rows, w), dt), pltpu.VMEM((q, rows, w), dt), pltpu.VMEM((q, rows, w), dt), sem((q, 3)), sem((q, 3))],
        compiler_params=pltpu.CompilerParams(collective_id=cid, has_side_effects=True, vmem_limit_bytes=48 * 2**20))(*arrays)


def gelu_parts(v):
    c, a = 0.7978845608, 0.044715
    v2 = v * v
    t = jnp.tanh(c * v * (1.0 + a * v2))
    half = 0.5 * (1.0 + t)
    return v * half, half + 0.5 * v * (1.0 - t * t) * (c * (1.0 + 3.0 * a * v2))
RING, LAG = 6, 4
def expert_kernel(cap, per, order, todo, wcut, tile, whole_down, xs, gs, wgi, wui, wdi, eo_out, ri_out, grads, eo_h, ri_h,
                  wall, xr, gr, hall, lall, eo, ri, cb, ab, xb, ob,
                  lsem, xss, xrs, gss, grs, ess, ers, rss, rrs, wss, wrs, wls, css, crs, ass, ars, osem, free):
    dp = lax.axis_size("dp")
    f32, bf = jnp.float32, jnp.bfloat16
    s, x, c, xdev, cdev = seq_places(2)
    g = lax.axis_index("dp")
    def peer(k): return (s, g ^ k)
    greet([xdev, cdev] + [peer(k) for k in range(1, dp)])
    rows_w, ff = wgi.shape; width = xs.shape[2]
    piece = rows_w // wcut
    wx, wc, wl = [], [], []
    shared = ((wgi, 1), (wui, 2)) if whole_down else ((wgi, 1), (wui, 2), (wdi, 0))
    parts = [(src, m, h * piece) for h in range(wcut) for src, m in shared]
    for n, (src, m, r0) in enumerate(parts):
        a = src.at[pl.ds(r0, piece)]
        b = wall.at[m, x, c, pl.ds(r0, piece)]
        wx.append(remote(a, b, wss.at[n, 0], wrs.at[n, 0], xdev))
        wc.append(remote(a, b, wss.at[n, 1], wrs.at[n, 1], cdev))
        cp = pltpu.make_async_copy(a, b, wls.at[n]); cp.start(); wl.append(cp)
    if whole_down:
        cp = pltpu.make_async_copy(wdi, wall.at[0], wls.at[len(parts)]); cp.start(); wl.append(cp)
    sx, sg = {}, {}
    for k in [k for p in order for k in range(p * per, (p + 1) * per)]:
        at = pl.ds(k * cap, cap)
        if k == 0:
            sx[0] = pltpu.make_async_copy(xs.at[g], xr.at[at], lsem.at[0]); sx[0].start()
            sg[0] = pltpu.make_async_copy(gs.at[g], gr.at[at], lsem.at[1]); sg[0].start()
        else:
            sx[k] = remote(xs.at[g ^ k], xr.at[at], xss.at[k], xrs.at[k], peer(k))
            sg[k] = remote(gs.at[g ^ k], gr.at[at], gss.at[k], grs.at[k], peer(k))
    wf = []
    for n, (src, m, r0) in enumerate(parts):
        wx[n].wait_recv()
        b = wall.at[m, 1 - x, c, pl.ds(r0, piece)]
        wf.append(remote(b, b, wss.at[n, 2], wrs.at[n, 2], cdev))
    for cp in wl: cp.wait()
    for n in range(len(parts)):
        wc[n].wait_recv(); wf[n].wait_recv()
    ntile = ff // tile
    re, rr = {}, {}
    wide = 4 * rows_w
    for p in todo:
        ks = list(range(p * per, (p + 1) * per))
        for k in ks:
            if k == 0: sx[0].wait(); sg[0].wait()
            else: sx[k].wait_recv(); sg[k].wait_recv()
        rows = pl.ds(p * per * cap, per * cap)
        @pl.loop(0, ntile)
        def _(t):
            cols = pl.ds(pl.multiple_of(t * tile, 128), tile)
            w = lambda m: wall[m, :, :, :, cols].reshape(wide, tile)
            gp = jnp.dot(xr[rows, :], w(1), preferred_element_type=f32)
            up = jnp.dot(xr[rows, :], w(2), preferred_element_type=f32)
            hg = jnp.dot(gr[rows, :], w(0), preferred_element_type=f32)
            act, der = gelu_parts(gp)
            hall[0, rows, cols] = (act * up).astype(bf)
            hall[1, rows, cols] = (hg * up * der).astype(bf)
            hall[2, rows, cols] = (hg * act).astype(bf)
        @pl.loop(0, 4)
        def _(t):
            part = pl.ds(pl.multiple_of(t * rows_w, 128), rows_w)
            tx, tc = t // 2, lax.rem(t, 2)
            eo[:, part] = dot(hall[0, rows, :], wall[0, tx, tc], 1, 1).astype(bf)
            ri[:, part] = (dot(hall[1, rows, :], wall[1, tx, tc], 1, 1) + dot(hall[2, rows, :], wall[2, tx, tc], 1, 1)).astype(bf)
        keep = [pltpu.make_async_copy(eo, eo_h.at[rows], lsem.at[4]), pltpu.make_async_copy(ri, ri_h.at[rows], lsem.at[5])]
        for cp in keep: cp.start()
        for cp in keep: cp.wait()
        for k in ks:
            at = pl.ds(k * cap, cap)
            if k == 0:
                re[0] = pltpu.make_async_copy(eo_h.at[at], eo_out.at[g], lsem.at[2]); re[0].start()
                rr[0] = pltpu.make_async_copy(ri_h.at[at], ri_out.at[g], lsem.at[3]); rr[0].start()
            else:
                re[k] = remote(eo_h.at[at], eo_out.at[g], ess.at[k], ers.at[k], peer(k))
                rr[k] = remote(ri_h.at[at], ri_out.at[g], rss.at[k], rrs.at[k], peer(k))
    for n in range(len(parts)):
        wx[n].wait_send(); wc[n].wait_send(); wf[n].wait_send()
    total = dp * cap
    @pl.loop(0, total // 256)
    def _(t):
        at = pl.ds(pl.multiple_of(t * 256, 256), 256)
        lall[1, :, at] = xr[at, :].T
        lall[0, :, at] = gr[at, :].T
    nt = 3 * ntile
    def place(n):
        m = n // ntile
        return m, pl.ds(pl.multiple_of((n - m * ntile) * tile, 128), tile)
    def to_core(n):
        m, cols = place(n); r = lax.rem(n, RING)
        return pltpu.make_async_remote_copy(src_ref=wall.at[m, :, 1 - c, :, cols], dst_ref=cb.at[r], send_sem=css.at[r],
            recv_sem=crs.at[r], device_id=cdev, device_id_type=MESH)
    def to_chip(n):
        r = lax.rem(n, RING)
        return pltpu.make_async_remote_copy(src_ref=ab.at[r], dst_ref=xb.at[r], send_sem=ass.at[r],
            recv_sem=ars.at[r], device_id=xdev, device_id_type=MESH)
    def to_out(n):
        m, cols = place(n); r = lax.rem(n, 2)
        return pltpu.make_async_copy(ob.at[r], grads.at[m, :, cols], osem.at[r])
    @pl.loop(0, nt + LAG)
    def _(n):
        @pl.when(n < nt)
        def _():
            m, cols = place(n)
            res = jnp.dot(lall[jnp.minimum(m, 1)], hall[m, :, cols], preferred_element_type=f32)
            wall[m, :, :, :, cols] = res.astype(bf).reshape(2, 2, rows_w, tile)
            @pl.when(n >= RING)
            def _(): pl.semaphore_wait(free.at[0], 1)
            to_core(n).start()
        @pl.when((n >= 1) & (n <= nt))
        def _():
            i = n - 1
            m, cols = place(i); r = lax.rem(i, RING)
            to_core(i).wait_recv()
            @pl.when(i >= RING)
            def _():
                to_chip(i).wait_send()
                pl.semaphore_wait(free.at[1], 1)
            ab[r] = (wall[m, 1 - x, c, :, cols].astype(f32) + cb[r, 1 - x].astype(f32)).astype(bf)
            to_chip(i).start()
        @pl.when(n >= LAG)
        def _():
            j = n - LAG
            m, cols = place(j); r = lax.rem(j, RING)
            to_chip(j).wait_recv()
            to_core(j).wait_send()
            @pl.when(j >= 2)
            def _(): to_out(j).wait()
            ob[lax.rem(j, 2)] = wall[m, x, c, :, cols].astype(f32) + cb[r, x].astype(f32) + xb[r].astype(f32)
            to_out(j).start()
            @pl.when(j < nt - RING)
            def _():
                pl.semaphore_signal(free.at[0], inc=1, device_id=cdev, device_id_type=MESH)
                pl.semaphore_signal(free.at[1], inc=1, device_id=xdev, device_id_type=MESH)
    for j in range(nt - 2, nt): to_out(j).wait()
    for i in range(nt - RING, nt): to_chip(i).wait_send()
    for k in range(dp):
        if k == 0:
            re[0].wait(); rr[0].wait()
        else:
            sx[k].wait_send(); sg[k].wait_send(); re[k].wait(); rr[k].wait()
def expert_all(xs, gs, wg, wu, wd, seq, cid):
    dp, cap, width = xs.shape
    rows_w, ff = wg.shape; total = dp * cap
    whole_down = wd.shape[0] != rows_w
    if whole_down: wd = wd.reshape(seq // 2, 2, rows_w, ff)
    group = 320
    per = group // cap
    ng = dp // per
    order = [p for p in range(ng // 2, ng)] + [p for p in range(ng // 2 - 1, -1, -1)]
    todo = list(range(ng))
    sem = pltpu.SemaphoreType.DMA
    bf = jnp.bfloat16
    any_ = pl.BlockSpec(memory_space=pl.ANY)
    V = pltpu.VMEM
    tile = 256
    wcut = 2
    back = jax.ShapeDtypeStruct((dp, cap, width), bf)
    flat = jax.ShapeDtypeStruct((total, width), bf)
    return pl.pallas_call(functools.partial(expert_kernel, cap, per, order, todo, wcut, tile, whole_down),
        out_shape=[back, back, jax.ShapeDtypeStruct((3, rows_w, ff), jnp.float32), flat, flat],
        in_specs=[any_] * 5, out_specs=[any_] * 5,
        scratch_shapes=[V((3, seq // 2, 2, rows_w, ff), bf), V((total, width), bf), V((total, width), bf), V((3, total, ff), bf),
        V((2, width, total), bf), V((group, width), bf), V((group, width), bf),
        V((RING, seq // 2, rows_w, tile), bf), V((RING, rows_w, tile), bf), V((RING, rows_w, tile), bf), V((2, rows_w, tile), jnp.float32)]
        + [sem((6,))] + [sem((dp,))] * 8 + [sem((3 * wcut, 3))] * 2 + [sem((3 * wcut + 1,))] + [sem((RING,))] * 4 + [sem((2,)), pltpu.SemaphoreType.REGULAR((2,))],
        compiler_params=pltpu.CompilerParams(collective_id=cid, has_side_effects=True, vmem_limit_bytes=63 * 2**20))(xs, gs, wg, wu, wd)[:3]


def on_device(
    long_tokens,
    short_tokens,
    long_grad_out,
    short_grad_out,
    query_weight,
    key_weight,
    value_weight,
    output_weight,
    attn_gain,
    ffn_gain,
    rel_table,
    router_weight,
    gate_weight,
    up_weight,
    down_weight,
    long_positions,
    short_positions,
    long_lengths,
    short_lengths,
    long_routes,
    short_routes,
):
    long_items, quarter, model_width = long_tokens.shape
    short_items, short_len = (short_tokens.shape[0], short_tokens.shape[1])
    long_rows = long_items * quarter
    tokens = long_rows + short_items * short_len
    local_experts = gate_weight.shape[0]
    dp_size = lax.axis_size("dp")
    experts = local_experts * dp_size
    capacity = (5 * tokens + 2 * experts - 1) // (2 * experts)
    seq_index = lax.axis_index("seq")
    seq_size = lax.axis_size("seq")
    dims = (seq_size // 2, 2, dp_size // 2, 2)
    devices = seq_size * dp_size
    table_part, router_part = rel_table.shape[0], router_weight.size
    gain_part = attn_gain.shape[0]
    small_size = 2 * gain_part + table_part + router_part
    small = jnp.concatenate([attn_gain, ffn_gain, rel_table, router_weight.reshape(-1)])
    small = jnp.pad(small, (0, -small_size % 2048)).reshape(-1, 128)
    rows_part = query_weight.shape[0]
    cuts = 2 if rows_part % 32 == 0 else 1
    cut = rows_part // cuts
    pieces = tuple((m, h * cut, cut, (m + h) % 2) for m in range(4) for h in range(cuts))
    gathered = gather_all(
        (query_weight, key_weight, value_weight, output_weight, small),
        pieces[: 3 * cuts] + ((4, 0, small.shape[0], 0),) + pieces[3 * cuts :],
        dims,
        0,
    )
    small_all = gathered[4].reshape(devices, -1)
    attn_set = tuple(block.reshape(devices * rows_part, model_width) for block in gathered[:4]) + (
        small_all[:, :gain_part].reshape(-1),
        small_all[:, gain_part : 2 * gain_part].reshape(-1),
        small_all[:, 2 * gain_part : 2 * gain_part + table_part].reshape(-1),
        small_all[:, 2 * gain_part + table_part : small_size].reshape(model_width, experts),
    )
    resid_in = jnp.concatenate(
        [long_tokens.reshape(long_rows, model_width), short_tokens.reshape(-1, model_width)], 0
    ).astype(jnp.float32)
    gain_first = attn_set[4].astype(jnp.float32)
    normed = rms_norm(resid_in, gain_first).astype(jnp.bfloat16)
    projected = [
        jnp.dot(normed, matrix, preferred_element_type=jnp.float32).astype(jnp.bfloat16)
        for matrix in attn_set[:3]
    ]
    queries, keys, values = projected
    long_keys, long_values = seq_gather((keys, values), long_items, quarter, seq_size, 2)
    table = attn_set[6].reshape(HEADS, 1, BUCKETS).astype(jnp.float32)
    table = jnp.pad(table, ((0, 0), (0, 0), (0, 128 - BUCKETS)), constant_values=masked)
    attn_args = (
        table,
        long_positions.reshape(long_items, seq_size, quarter, 1),
        long_positions.reshape(long_items, seq_size, 1, quarter),
        short_positions.reshape(short_items, 1, short_len, 1),
        short_positions.reshape(short_items, 1, 1, short_len),
    )
    lead_args = (long_lengths, short_lengths, queries, keys, values, long_keys, long_values)
    (mixed_all,) = attention(
        False, long_items, short_items, seq_size, lead_args + attn_args, tokens, model_width
    )
    resid_mid = resid_in + jnp.dot(mixed_all, attn_set[3], preferred_element_type=jnp.float32)
    gain_second = attn_set[5].astype(jnp.float32)
    normed_two = rms_norm(resid_mid, gain_second).astype(jnp.bfloat16)
    logits = jnp.dot(normed_two, attn_set[7], preferred_element_type=jnp.float32)
    routes = jnp.concatenate([long_routes.reshape(-1, 2), short_routes.reshape(-1, 2)], 0)
    choose = (routes[..., None] == jnp.arange(experts, dtype=jnp.int32)).astype(jnp.float32)
    gate_share, gate_pull = jax.vjp(lambda logit_in: gate_values(logit_in, choose), logits)
    flat_routes = routes.reshape(-1)
    member = (flat_routes[:, None] == jnp.arange(experts, dtype=jnp.int32)).astype(jnp.int32)
    queue_pos = jnp.sum(jnp.cumsum(member, axis=0) * member, axis=1) - 1
    route_kept = queue_pos < capacity
    slot_index = jnp.where(route_kept, flat_routes * capacity + queue_pos, experts * capacity)
    slot_pair = (
        jnp.zeros(experts * capacity + 1, jnp.int32)
        .at[slot_index]
        .set(jnp.arange(2 * tokens, dtype=jnp.int32))[:-1]
    )
    slot_used = jnp.zeros(experts * capacity + 1, jnp.bool_).at[slot_index].set(True)[:-1]
    pair_slot = jnp.where(route_kept, slot_index, 0)
    outgoing = jnp.where(
        slot_used[:, None], jnp.take(normed_two, slot_pair // 2, axis=0), 0
    ).reshape(experts, capacity, model_width)
    kept_two = route_kept.reshape(tokens, 2).astype(jnp.float32)
    weighting = gate_share * kept_two
    grad_out = jnp.concatenate(
        [long_grad_out.reshape(long_rows, model_width), short_grad_out.reshape(-1, model_width)], 0
    ).astype(jnp.float32)
    pair_grad = (
        (weighting[:, :, None] * grad_out[:, None, :])
        .astype(jnp.bfloat16)
        .reshape(2 * tokens, model_width)
    )
    out_slots = jnp.where(slot_used[:, None], jnp.take(pair_grad, slot_pair, axis=0), 0).reshape(
        experts, capacity, model_width
    )
    later_down, unused_keys = lax.optimization_barrier((down_weight[0], long_keys))
    down_full = lax.all_gather(later_down, "seq", axis=0, tiled=True)
    back_rows, returned_grad, expert_grads = expert_all(
        outgoing, out_slots, gate_weight[0], up_weight[0], down_full, seq_size, 4
    )
    pair_out = (
        jnp.where(
            route_kept[:, None],
            jnp.take(back_rows.reshape(experts * capacity, model_width), pair_slot, axis=0),
            0,
        )
        .reshape(tokens, 2, model_width)
        .astype(jnp.float32)
    )
    final = resid_mid + weighting[:, 0:1] * pair_out[:, 0] + weighting[:, 1:2] * pair_out[:, 1]
    final_low = final.astype(jnp.bfloat16)
    long_out = final_low[:long_rows].reshape(long_items, quarter, model_width)
    short_out = final_low[long_rows:].reshape(short_items, short_len, model_width)
    share_grad = kept_two * jnp.sum(grad_out[:, None, :] * pair_out, axis=-1)
    logit_grad = gate_pull(share_grad)[0].astype(jnp.bfloat16)
    attn_back = attn_set
    down_grad, gate_grad, up_grad = (expert_grads[m : m + 1] for m in range(3))
    route_grad = (
        jnp.where(
            route_kept[:, None],
            jnp.take(returned_grad.reshape(experts * capacity, model_width), pair_slot, axis=0),
            0,
        )
        .reshape(tokens, 2, model_width)
        .astype(jnp.float32)
    )
    normed_two_grad = (
        route_grad[:, 0]
        + route_grad[:, 1]
        + jnp.einsum("te,de->td", logit_grad, attn_back[7], preferred_element_type=jnp.float32)
    )
    router_local = jnp.einsum(
        "td,te->de", normed_two, logit_grad, preferred_element_type=jnp.float32
    )
    unused_mid, norm_two_pull = jax.vjp(rms_norm, resid_mid, attn_back[5].astype(jnp.float32))
    mid_norm_grad, ffn_gain_local = norm_two_pull(normed_two_grad)
    middle_grad = grad_out + mid_norm_grad
    branch_grad = middle_grad.astype(jnp.bfloat16)
    output_local = jnp.einsum(
        "td,te->de", mixed_all, branch_grad, preferred_element_type=jnp.float32
    )
    mix_grad = jnp.einsum(
        "te,de->td", branch_grad, attn_back[3], preferred_element_type=jnp.float32
    ).astype(jnp.bfloat16)
    query_act, short_key, short_value, long_key, long_value, table_sums = attention(
        True,
        long_items,
        short_items,
        seq_size,
        lead_args + (mix_grad,) + attn_args,
        tokens,
        model_width,
    )
    long_key, long_value = seq_sum((long_key, long_value), 3)
    key_act = jnp.concatenate([long_key.reshape(long_rows, model_width), short_key], 0)
    value_act = jnp.concatenate([long_value.reshape(long_rows, model_width), short_value], 0)
    upto = table_sums.reshape(HEADS, 128)[:, : len(ORDER)]
    within = upto - jnp.pad(upto[:, :-1], ((0, 0), (1, 0)))
    table_local = jnp.stack(
        [
            within[:, ORDER.index(n)] if n in ORDER else jnp.zeros(HEADS, jnp.float32)
            for n in range(BUCKETS)
        ],
        1,
    ).reshape(-1)
    normed_grad = (
        jnp.einsum("te,de->td", query_act, attn_back[0], preferred_element_type=jnp.float32)
        + jnp.einsum("te,de->td", key_act, attn_back[1], preferred_element_type=jnp.float32)
        + jnp.einsum("te,de->td", value_act, attn_back[2], preferred_element_type=jnp.float32)
    )
    query_local = jnp.einsum("td,te->de", normed, query_act, preferred_element_type=jnp.float32)
    key_local = jnp.einsum("td,te->de", normed, key_act, preferred_element_type=jnp.float32)
    value_local = jnp.einsum("td,te->de", normed, value_act, preferred_element_type=jnp.float32)
    unused_in, norm_one_pull = jax.vjp(rms_norm, resid_in, attn_back[4].astype(jnp.float32))
    in_norm_grad, attn_gain_local = norm_one_pull(normed_grad)
    input_grad_all = middle_grad + in_norm_grad
    long_grad_in = input_grad_all[:long_rows].reshape(long_items, quarter, model_width)
    short_grad_in = input_grad_all[long_rows:].reshape(short_items, short_len, model_width)
    shares = (gain_part, gain_part, table_part, router_part)
    small_local = jnp.concatenate(
        [
            part.reshape(devices, -1)
            for part in (attn_gain_local, ffn_gain_local, table_local, router_local)
        ],
        1,
    )
    small_local = jnp.pad(small_local, ((0, 0), (0, -small_size % 1024)))
    small_rows = small_local.shape[1] // 128
    mats = tuple(
        part.astype(jnp.bfloat16).reshape(dims + (rows_part, model_width))
        for part in (output_local, query_local, key_local, value_local)
    )
    scattered = scatter_all(
        mats + (small_local.reshape(dims + (small_rows, 128)),),
        pieces[:cuts] + ((4, 0, small_rows, 0),) + pieces[cuts:],
        dims,
        1,
    )
    small_sum = scattered[4].reshape(-1)
    edges = [sum(shares[:k]) for k in range(5)]
    summed = (scattered[1], scattered[2], scattered[3], scattered[0]) + tuple(
        small_sum[edges[k] : edges[k + 1]] for k in range(3)
    ) + (small_sum[edges[3] : edges[4]].reshape(rows_part, experts),)
    return (
        long_out,
        short_out,
        long_grad_in,
        short_grad_in,
        summed[0],
        summed[1],
        summed[2],
        summed[3],
        summed[4],
        summed[5],
        summed[6],
        summed[7],
        gate_grad,
        up_grad,
        down_grad,
    )


def solution(mesh):
    placed = (
        P("dp", "seq", None),
        P(("seq", "dp"), None, None),
        P("dp", "seq", None),
        P(("seq", "dp"), None, None),
        P(("seq", "dp"), None),
        P(("seq", "dp"), None),
        P(("seq", "dp"), None),
        P(("seq", "dp"), None),
        P(("seq", "dp")),
        P(("seq", "dp")),
        P(("seq", "dp")),
        P(("seq", "dp"), None),
        P("dp", "seq", None),
        P("dp", "seq", None),
        P("dp", "seq", None),
        P("dp", None),
        P(("seq", "dp"), None),
        P("dp"),
        P(("seq", "dp")),
        P("dp", "seq", None),
        P(("seq", "dp"), None, None),
    )
    return jax.shard_map(
        on_device,
        mesh=mesh,
        in_specs=placed,
        out_specs=(
            P("dp", "seq", None),
            P(("seq", "dp"), None, None),
            P("dp", "seq", None),
            P(("seq", "dp"), None, None),
            P(("seq", "dp"), None),
            P(("seq", "dp"), None),
            P(("seq", "dp"), None),
            P(("seq", "dp"), None),
            P(("seq", "dp")),
            P(("seq", "dp")),
            P(("seq", "dp")),
            P(("seq", "dp"), None),
            P("dp", "seq", None),
            P("dp", "seq", None),
            P("dp", "seq", None),
        ),
        check_vma=False,
    )
```

```python
import functools

import jax
import jax.numpy as jnp
from jax import lax
from jax.experimental import pallas as pl
from jax.experimental.pallas import tpu as pltpu
from jax.sharding import PartitionSpec as P

MESH = pl.DeviceIdType.MESH

HEADS = 16
HEAD = 64
BUCKETS = 32


epsilon = 1e-06
masked = -1e30


def rms_norm(hidden, gain):
    scale = lax.rsqrt(jnp.mean(hidden * hidden, axis=-1, keepdims=True) + epsilon)
    return hidden * scale * gain


def gather_kernel(dims, pieces, na, *refs):
    X, C, Z, Y = dims
    n = len(pieces)
    lsem, zs, zr, hs, hr, cs, cr = refs[2*na:]
    routes = [p[3] for p in pieces]
    ins = [refs[m].at[pl.ds(r0, nr)] for m, r0, nr, _ in pieces]
    class V:
        def __init__(self, ref, r0, nr): self.ref, self.r0, self.nr = ref, r0, nr
        @property
        def at(self): return self
        def __getitem__(self, k):
            k = k + (slice(None),) * (4 - len(k)) + (pl.ds(self.r0, self.nr),)
            return self.ref.at[k]
    outs = [V(refs[na + m], r0, nr) for m, r0, nr, _ in pieces]
    s = lax.axis_index("seq"); g = lax.axis_index("dp")
    x, c = s // C, lax.rem(s, C)
    z, y = g // Y, lax.rem(g, Y)
    def zdev(k): return (s, lax.rem(z + k, Z) * Y + y)
    ydev = (s, z * Y + (1 - y)); xdev = ((1 - x) * C + c, g); cdev = (x * C + 1 - c, g)
    bar = pltpu.get_barrier_semaphore()
    for d in [zdev(k) for k in range(1, Z)] + [ydev, xdev, cdev]:
        pl.semaphore_signal(bar, inc=1, device_id=d, device_id_type=MESH)
    pl.semaphore_wait(bar, Z + 2)
    def rc(src, dst, ss, rs, dev):
        cp = pltpu.make_async_remote_copy(src_ref=src, dst_ref=dst, send_sem=ss, recv_sem=rs, device_id=dev, device_id_type=MESH)
        cp.start(); return cp
    sends = []
    local = []; zc = []
    for m in range(n):
        lc = pltpu.make_async_copy(ins[m], outs[m].at[x, c, z, y], lsem.at[m]); lc.start(); local.append(lc)
        zc.append([rc(ins[m], outs[m].at[x, c, z, y], zs.at[m, k], zr.at[m, k], zdev(k)) for k in range(1, Z)])
    h = [[None, None] for _ in range(n)]
    cc = [[None]*3 for _ in range(n)]
    for t in range(n + 2):
        for stage in range(3):
            m = t - stage
            if not 0 <= m < n: continue
            o = outs[m]; route = routes[m]
            if stage == 0:
                local[m].wait()
                for q in zc[m]: q.wait_recv()
                mine = o.at[x, c, :, y]
                h[m][0] = rc(mine, mine, hs.at[m,0], hr.at[m,0], xdev if route == 0 else ydev)
                cc[m][0] = rc(mine, mine, cs.at[m,0], cr.at[m,0], cdev)
            elif stage == 1:
                h[m][0].wait_recv()
                if route == 0:
                    both = o.at[:, c, :, y]; got = o.at[1 - x, c, :, y]
                else:
                    both = o.at[x, c]; got = o.at[x, c, :, 1 - y]
                h[m][1] = rc(both, both, hs.at[m,1], hr.at[m,1], ydev if route == 0 else xdev)
                cc[m][1] = rc(got, got, cs.at[m,1], cr.at[m,1], cdev)
            else:
                h[m][1].wait_recv()
                got = o.at[:, c, :, 1 - y] if route == 0 else o.at[1 - x, c]
                cc[m][2] = rc(got, got, cs.at[m,2], cr.at[m,2], cdev)
    for m in range(n):
        for q in zc[m]: q.wait_send()
        for q in h[m]: q.wait_send()
        for q in cc[m]: q.wait()
def gather_all(arrays, pieces, dims, cid):
    X, C, Z, Y = dims; na = len(arrays); n = len(pieces)
    sem = pltpu.SemaphoreType.DMA
    return pl.pallas_call(functools.partial(gather_kernel, dims, pieces, na),
        out_shape=[jax.ShapeDtypeStruct((X, C, Z, Y) + a.shape, a.dtype) for a in arrays],
        in_specs=[pl.BlockSpec(memory_space=pl.ANY)] * na, out_specs=[pl.BlockSpec(memory_space=pl.ANY)] * na,
        scratch_shapes=[sem((n,)), sem((n, Z)), sem((n, Z)), sem((n, 2)), sem((n, 2)), sem((n, 3)), sem((n, 3))],
        compiler_params=pltpu.CompilerParams(collective_id=cid, has_side_effects=True))(*arrays)


def scatter_kernel(dims, pieces, n, *refs):
    X, C, Z, Y = dims
    ins, outs = refs[:n], refs[n:2*n]
    np_ = len(pieces)
    bufs = refs[2*n:2*n+7*np_]
    sems = refs[2*n+7*np_:]
    cs, cr, hs, hr, zs, zr = sems
    s = lax.axis_index("seq"); g = lax.axis_index("dp")
    x, c = s // C, lax.rem(s, C)
    z, y = g // Y, lax.rem(g, Y)
    def zdev(k): return (s, lax.rem(z + k, Z) * Y + y)
    ydev = (s, z * Y + (1 - y)); xdev = ((1 - x) * C + c, g); cdev = (x * C + 1 - c, g)
    bar = pltpu.get_barrier_semaphore()
    for d in [zdev(k) for k in range(1, Z)] + [ydev, xdev, cdev]:
        pl.semaphore_signal(bar, inc=1, device_id=d, device_id_type=MESH)
    pl.semaphore_wait(bar, Z + 2)
    def rc(src, dst, ss, rs, dev):
        cp = pltpu.make_async_remote_copy(src_ref=src, dst_ref=dst, send_sem=ss, recv_sem=rs, device_id=dev, device_id_type=MESH)
        cp.start(); return cp
    def add(dst, a, b):
        dst[...] = (a.astype(jnp.float32) + b.astype(jnp.float32)).astype(dst.dtype)
    first = []
    for i, (m, r0, nr, route) in enumerate(pieces):
        cb = bufs[7*i]
        src = ins[m].at[:, 1 - c, :, :, pl.ds(r0, nr)]
        first.append(rc(src, cb, cs.at[i], cr.at[i], cdev))
    hh = [[None, None] for _ in pieces]; zz = [None] * np_
    for t in range(np_ + 3):
        for stage in range(4):
            i = t - stage
            if not 0 <= i < np_: continue
            m, r0, nr, route = pieces[i]
            cb, a1, b1, a2, b2, a3, b3 = bufs[7*i:7*i+7]
            if stage == 0:
                first[i].wait_recv()
                add(a1, ins[m][:, c, :, :, pl.ds(r0, nr)], cb[...])
                src = a1.at[:, :, 1 - y] if route == 0 else a1.at[1 - x]
                hh[i][0] = rc(src, b1, hs.at[i, 0], hr.at[i, 0], ydev if route == 0 else xdev)
            elif stage == 1:
                hh[i][0].wait_recv()
                add(a2, a1[:, :, y] if route == 0 else a1[x], b1[...])
                src = a2.at[1 - x] if route == 0 else a2.at[:, 1 - y]
                hh[i][1] = rc(src, b2, hs.at[i, 1], hr.at[i, 1], xdev if route == 0 else ydev)
            elif stage == 2:
                hh[i][1].wait_recv()
                add(a3, a2[x] if route == 0 else a2[:, y], b2[...])
                zz[i] = [rc(a3.at[lax.rem(z + k, Z)], b3.at[k - 1], zs.at[i, k], zr.at[i, k], zdev(k)) for k in range(1, Z)]
            else:
                tot = a3[z].astype(jnp.float32)
                for k in range(1, Z):
                    zz[i][k-1].wait_recv()
                    tot += b3[k - 1].astype(jnp.float32)
                outs[m][pl.ds(r0, nr), :] = tot
    for i in range(np_):
        first[i].wait_send()
        for q in hh[i]: q.wait_send()
        for q in zz[i]: q.wait_send()
def scatter_all(arrays, pieces, dims, cid):
    X, C, Z, Y = dims; n = len(arrays); q = len(pieces)
    sem = pltpu.SemaphoreType.DMA
    scr = []
    for m, r0, nr, route in pieces:
        w = arrays[m].shape[-1]; dt = arrays[m].dtype
        h1 = (X, Z) if route == 0 else (Z, Y)
        for lead in ((X, Z, Y), (X, Z, Y), h1, h1, (Z,), (Z,), (Z - 1,)):
            scr.append(pltpu.VMEM(lead + (nr, w), dt))
    return pl.pallas_call(functools.partial(scatter_kernel, dims, pieces, n),
        out_shape=[jax.ShapeDtypeStruct(a.shape[-2:], jnp.float32) for a in arrays],
        in_specs=[pl.BlockSpec(memory_space=pltpu.VMEM)] * n, out_specs=[pl.BlockSpec(memory_space=pltpu.VMEM)] * n,
        scratch_shapes=scr + [sem((q,)), sem((q,)), sem((q, 2)), sem((q, 2)), sem((q, Z)), sem((q, Z))],
        compiler_params=pltpu.CompilerParams(collective_id=cid, has_side_effects=True, vmem_limit_bytes=48*2**20))(*arrays)


EDGES = (-90, -63, -45, -31, -22, -15, -11, -7, -6, -5, -4, -3, -2, -1, 0, 1, 2, 3, 4, 5, 6, 7, 8, 12, 16, 23, 32, 46, 64, 91)
ORDER = (15, 14, 13, 12, 11, 10, 9, 8, 7, 6, 5, 4, 3, 2, 1, 0, 17, 18, 19, 20, 21, 22, 23, 24, 25, 26, 27, 28, 29, 30, 31)
FAR = (12, 16, 23, 32, 46, 64, 91)
def fill_buckets(out, q_col, k_row, length, base):
    r = k_row - q_col
    n = jnp.abs(r)
    far = jnp.full(r.shape, 8, jnp.int32)
    for e in FAR:
        far += (n >= e).astype(jnp.int32)
    b = jnp.where(n < 8, n, far) + jnp.where(r > 0, 16, 0)
    j = lax.broadcasted_iota(jnp.int32, r.shape, 1) + base
    out[...] = jnp.where(j < length, b, 32)
def dot(a, b, ca, cb):
    return lax.dot_general(a, b, (((ca,), (cb,)), ((), ())), preferred_element_type=jnp.float32)
def probs_of(qs, kk, tabs, bucket_ref, blocks):
    s = dot(qs, kk, 1, 1)
    t = [jnp.broadcast_to(tab, (128, 128)) for tab in tabs]
    bias = [jnp.concatenate([jnp.take_along_axis(x, bucket_ref[c], axis=1) for x in t], axis=0) for c in range(blocks)]
    s = s + (jnp.concatenate(bias, axis=1) if blocks > 1 else bias[0])
    p = jnp.exp(s - jnp.max(s, axis=1, keepdims=True))
    return p * (1.0 / jnp.sum(p, axis=1, keepdims=True))
def stack_heads(rows, first):
    return jnp.concatenate([jnp.where(first, rows, 0), jnp.where(first, 0, rows)], axis=0)
def attn_setup(nl, ns, blocks, ll, sl, lcol, lrow, scol, srow, lb, sb):
    me = lax.axis_index("seq")
    for b in range(nl):
        for c in range(blocks):
            fill_buckets(lb.at[b, c], lcol[b, me], lrow[b, c], ll[b], c * 128)
    for b in range(ns):
        fill_buckets(sb.at[b, 0], scol[b, 0], srow[b, 0], sl[b], 0)
def rows_of(long_ref, short_ref, t, nl, ns):
    if t == 0:
        return long_ref[...].reshape(nl * 128, -1)
    return short_ref[...].reshape(ns * 128, -1)
def rms_scale(mid):
    return lax.rsqrt(jnp.mean(mid * mid, axis=-1, keepdims=True) + epsilon)
def attn_fwd_kernel(nl, ns, blocks, experts, cap, ll, sl, q, k, v, kl, vl, tab, lcol, lrow, scol, srow,
                    xl, xsh, gl, gsh, wo, gain, rt, rrow, mixed, mid, xs, gs, logits, lb, sb, n2, gb):
    attn_setup(nl, ns, blocks, ll, sl, lcol, lrow, scol, srow, lb, sb)
    first = lax.broadcasted_iota(jnp.int32, (128, 128), 1) < 64
    @pl.loop(0, 8)
    def _(hp):
        cols = pl.ds(pl.multiple_of(hp * 128, 128), 128)
        for b in range(nl + ns):
            rows = pl.ds(b * 128, 128)
            n = blocks if b < nl else 1
            if b < nl:
                kk = kl[:, b, :, cols].reshape(n * 128, 128); vv = vl[:, b, :, cols].reshape(n * 128, 128)
            else:
                kk = k[rows, cols]; vv = v[rows, cols]
            p = probs_of(stack_heads(q[rows, cols], first), kk, (tab[2 * hp], tab[2 * hp + 1]), lb.at[b] if b < nl else sb.at[b - nl], n)
            out = dot(p.astype(jnp.bfloat16), vv, 1, 0)
            mixed[rows, cols] = jnp.where(first, out[:128], out[128:]).astype(jnp.bfloat16)
    f32, bf = jnp.float32, jnp.bfloat16
    tokens = q.shape[0]
    for t in range(2):
        rows = pl.ds(t * 256, 256)
        m = rows_of(xl, xsh, t, nl, ns).astype(f32) + jnp.dot(mixed[rows, :], wo[...], preferred_element_type=f32)
        mid[rows, :] = m
        n2[rows, :] = (m * rms_scale(m) * gain[...]).astype(bf)
        gb[rows, :] = rows_of(gl, gsh, t, nl, ns)
    logits[...] = dot(n2[...], rt[...], 1, 1)
    logit_t = dot(rt[...], n2[...], 1, 1)[:experts]
    e_iota = lax.broadcasted_iota(jnp.int32, (experts, tokens), 0)
    member = ((e_iota == rrow[0:1, :]) | (e_iota == rrow[1:2, :])).astype(f32)
    e = jnp.exp(logit_t - jnp.max(logit_t, axis=0, keepdims=True))
    p = e / jnp.sum(e, axis=0, keepdims=True)
    chosen = member * p
    before = (lax.broadcasted_iota(jnp.int32, (tokens, tokens), 0) < lax.broadcasted_iota(jnp.int32, (tokens, tokens), 1)).astype(f32).astype(bf)
    place = jnp.dot(member.astype(bf), before, preferred_element_type=f32)
    kept = (member > 0.5) & (place < cap)
    weight = jnp.where(kept, chosen / jnp.sum(chosen, axis=0, keepdims=True), 0.0)
    slot = jnp.where(kept, place.astype(jnp.int32), -1)
    s_iota = lax.broadcasted_iota(jnp.int32, (cap, tokens), 0)
    for i in range(experts):
        pick = (s_iota == slot[i:i + 1, :]).astype(f32)
        scale = jnp.sum(pick * weight[i:i + 1, :], axis=1, keepdims=True)
        pick = pick.astype(bf)
        xs[i] = jnp.dot(pick, n2[...], preferred_element_type=f32).astype(bf)
        gs[i] = (jnp.dot(pick, gb[...], preferred_element_type=f32) * scale).astype(bf)
def attn_bwd_kernel(nl, ns, blocks, experts, cap, ll, sl, q, k, v, kl, vl, tab, lcol, lrow, scol, srow,
                    eo, ri, mid, mixed, logits, rcol, gl, gsh, wo, gain, rt,
                    dq, dk, dv, dkl, dvl, seg, final, midg, wog, fgg, rtg, lb, sb, li, si, mg, bg, n2, lg, fin, bk, sh):
    f32, bf = jnp.float32, jnp.bfloat16
    tokens = q.shape[0]
    lane = lax.broadcasted_iota(jnp.int32, (tokens, 128), 1)
    member = ((lane == rcol[:, 0:1]) | (lane == rcol[:, 1:2])).astype(f32)
    after = (lax.broadcasted_iota(jnp.int32, (tokens, tokens), 1) < lax.broadcasted_iota(jnp.int32, (tokens, tokens), 0)).astype(f32).astype(bf)
    place = jnp.dot(after, member.astype(bf), preferred_element_type=f32)
    kept = (member > 0.5) & (place < cap)
    slot = jnp.where(kept, place.astype(jnp.int32), -1)
    lgt = jnp.where(lane < experts, logits[...], -1e30)
    ex = jnp.exp(lgt - jnp.max(lgt, axis=1, keepdims=True))
    p = ex / jnp.sum(ex, axis=1, keepdims=True)
    chosen = member * p
    both = jnp.sum(chosen, axis=1, keepdims=True)
    gate = chosen / both
    fg = jnp.zeros((1, q.shape[1]), f32)
    for t in range(2):
        at = slice(t * 256, t * 256 + 256)
        rows = pl.ds(t * 256, 256)
        g = rows_of(gl, gsh, t, nl, ns).astype(f32)
        m = mid[rows, :]
        fin[...] = m
        bk[...] = jnp.zeros_like(m)
        sh[...] = jnp.zeros_like(sh)
        s_iota = lax.broadcasted_iota(jnp.int32, (256, cap), 1)
        slot_t, weight_t, lane_t = slot[at], jnp.where(kept[at], gate[at], 0.0), lane[:256]
        @pl.loop(0, experts)
        def _(i):
            this = lane_t == i
            mine = jnp.sum(jnp.where(this, slot_t, 0), axis=1, keepdims=True)
            weight = jnp.sum(jnp.where(this, weight_t, 0.0), axis=1, keepdims=True)
            pick = (s_iota == mine).astype(f32).astype(bf)
            pair = jnp.dot(pick, eo[i], preferred_element_type=f32)
            fin[...] += weight * pair
            sh[...] = jnp.where(this, jnp.sum(rows_of(gl, gsh, t, nl, ns).astype(f32) * pair, axis=1, keepdims=True), sh[...])
            bk[...] += jnp.dot(pick, ri[i], preferred_element_type=f32)
        final[rows, :] = fin[...].astype(bf)
        share, back = sh[...], bk[...]
        mean = jnp.sum(share * gate[at], axis=1, keepdims=True)
        pg = member[at] * (share - mean) / both[at]
        lgrad = (p[at] * (pg - jnp.sum(p[at] * pg, axis=1, keepdims=True))).astype(bf)
        lg[rows, :] = lgrad
        r2 = rms_scale(m)
        u = m * r2
        n2[rows, :] = (u * gain[...]).astype(bf)
        back += jnp.dot(lgrad, rt[...], preferred_element_type=f32)
        fg += jnp.sum(back * u, axis=0, keepdims=True)
        w = back * gain[...]
        out = g + r2 * (w - u * jnp.mean(w * u, axis=-1, keepdims=True))
        midg[rows, :] = out
        bg[rows, :] = out.astype(bf)
        mg[rows, :] = dot(out.astype(bf), wo[...], 1, 1).astype(bf)
    fgg[...] = fg
    rtg[...] = dot(lg[...], n2[...], 0, 0)[:experts]
    wog[...] = dot(mixed[...], bg[...], 0, 0).astype(bf)
    attn_setup(nl, ns, blocks, ll, sl, lcol, lrow, scol, srow, lb, sb)
    me = lax.axis_index("seq")
    lane = lax.broadcasted_iota(jnp.int32, (128, 128), 1)
    edge = jnp.full((128, 128), 4096, jnp.int32)
    for i, e in enumerate(EDGES):
        edge = jnp.where(lane == i, e, edge)
    edge = jnp.where(lane > len(EDGES), -4096, edge)
    def places(out, q_col, k_col, k_first):
        t = lax.broadcasted_iota(jnp.int32, (128, 256), 1) + k_first
        below = jnp.sum((k_col < t).astype(jnp.int32), axis=0, keepdims=True)
        at = jnp.clip(q_col + edge - k_first, 0, 255)
        lo = jnp.take_along_axis(jnp.broadcast_to(below[:, :128], (128, 128)), at & 127, axis=1)
        hi = jnp.take_along_axis(jnp.broadcast_to(below[:, 128:], (128, 128)), at & 127, axis=1)
        out[...] = jnp.where(at < 128, lo, hi) - 1
    for b in range(nl):
        for c in range(blocks):
            places(li.at[b, c], lcol[b, me], lcol[b, c], lrow[b, c, 0, 0])
    for b in range(ns):
        places(si.at[b, 0], scol[b, 0], scol[b, 0], srow[b, 0, 0, 0])
    seg[...] = jnp.zeros_like(seg)
    first = lane < 64
    row = lax.broadcasted_iota(jnp.int32, (128, 128), 0)
    tri = jnp.where(row <= lane, 1.0, 0.0).astype(jnp.bfloat16)
    @pl.loop(0, 8)
    def _(hp):
        cols = pl.ds(pl.multiple_of(hp * 128, 128), 128)
        for b in range(nl + ns):
            rows = pl.ds(b * 128, 128)
            n = blocks if b < nl else 1
            if b < nl:
                kk = kl[:, b, :, cols].reshape(n * 128, 128); vv = vl[:, b, :, cols].reshape(n * 128, 128)
            else:
                kk = k[rows, cols]; vv = v[rows, cols]
            idx = li.at[b] if b < nl else si.at[b - nl]
            qs = stack_heads(q[rows, cols], first); gs = stack_heads(mg[rows, cols], first)
            p = probs_of(qs, kk, (tab[2 * hp], tab[2 * hp + 1]), lb.at[b] if b < nl else sb.at[b - nl], n)
            dp = dot(gs, vv, 1, 1)
            ds = (p * (dp - jnp.sum(p * dp, axis=1, keepdims=True))).astype(jnp.bfloat16)
            dqs = dot(ds, kk, 1, 0)
            dkt = dot(qs, ds, 0, 0)
            dvt = dot(gs, p.astype(jnp.bfloat16), 0, 0)
            sums = [0, 0]
            for c in range(n):
                pre = dot(ds[:, c * 128:(c + 1) * 128], tri, 1, 0)
                at = idx[c]
                for e in range(2):
                    sums[e] += jnp.where(at >= 0, jnp.take_along_axis(pre[e * 128:(e + 1) * 128], jnp.maximum(at, 0), axis=1), 0.0)
            for e in range(2):
                seg[2 * hp + e] += jnp.sum(sums[e], axis=0, keepdims=True)
            dq[rows, cols] = jnp.where(first, dqs[:128], dqs[128:]).astype(jnp.bfloat16)
            dkt = dkt.T.astype(jnp.bfloat16); dvt = dvt.T.astype(jnp.bfloat16)
            if b < nl:
                dkl[:, b, :, cols] = dkt.reshape(n, 128, 128); dvl[:, b, :, cols] = dvt.reshape(n, 128, 128)
            else:
                dk[pl.ds((b - nl) * 128, 128), cols] = dkt; dv[pl.ds((b - nl) * 128, 128), cols] = dvt
def attention(backward, nl, ns, blocks, experts, cap, arrays, tokens, width):
    sm, vm = pl.BlockSpec(memory_space=pltpu.SMEM), pl.BlockSpec(memory_space=pltpu.VMEM)
    bf, f32 = jnp.bfloat16, jnp.float32
    S = jax.ShapeDtypeStruct
    rows = S((tokens, width), bf)
    buckets = [pltpu.VMEM((nl, blocks, 128, 128), jnp.int32), pltpu.VMEM((ns, 1, 128, 128), jnp.int32)]
    row_buf = pltpu.VMEM((tokens, width), bf)
    if backward:
        short = S((ns * 128, width), bf)
        long = S((blocks, nl, 128, width), bf)
        outs = [rows, short, short, long, long, S((16, 1, 128), f32), rows, S((tokens, width), f32), S((width, width), bf),
                S((1, width), f32), S((experts, width), f32)]
        body = functools.partial(attn_bwd_kernel, nl, ns, blocks, experts, cap)
        scr = buckets * 2 + [row_buf] * 3 + [pltpu.VMEM((tokens, 128), bf)] + [pltpu.VMEM((256, width), f32)] * 2 + [pltpu.VMEM((256, 128), f32)]
    else:
        slots = S((experts, cap, width), bf)
        outs = [rows, S((tokens, width), f32), slots, slots, S((tokens, 128), f32)]
        body = functools.partial(attn_fwd_kernel, nl, ns, blocks, experts, cap); scr = buckets + [row_buf] * 2
    return pl.pallas_call(body, out_shape=outs, in_specs=[sm, sm] + [vm] * (len(arrays) - 2), out_specs=[vm] * len(outs),
        scratch_shapes=scr, compiler_params=pltpu.CompilerParams(vmem_limit_bytes=60 * 2**20))(*arrays)

def seq_places(C):
    s = lax.axis_index("seq"); g = lax.axis_index("dp")
    x, c = s // C, lax.rem(s, C)
    return s, x, c, ((1 - x) * C + c, g), (x * C + 1 - c, g)
def greet(devs):
    bar = pltpu.get_barrier_semaphore()
    for d in devs:
        pl.semaphore_signal(bar, inc=1, device_id=d, device_id_type=MESH)
    pl.semaphore_wait(bar, len(devs))
def remote(src, dst, ss, rs, dev):
    cp = pltpu.make_async_remote_copy(src_ref=src, dst_ref=dst, send_sem=ss, recv_sem=rs, device_id=dev, device_id_type=MESH)
    cp.start()
    return cp
def seq_gather_kernel(n, items, rows, *refs):
    ins, outs = refs[:n], refs[n:2 * n]
    lsem, ss, rs = refs[2 * n:]
    s, x, c, xdev, cdev = seq_places(2)
    far = (1 - x) * 2 + c
    greet([xdev, cdev])
    local, a, b = [], [], []
    pieces = [(m, i) for m in range(n) for i in range(items)]
    for k, (m, i) in enumerate(pieces):
        src = ins[m].at[pl.ds(i * rows, rows)]
        a.append(remote(src, outs[m].at[s, i], ss.at[k, 0], rs.at[k, 0], xdev))
        b.append(remote(src, outs[m].at[s, i], ss.at[k, 1], rs.at[k, 1], cdev))
        cp = pltpu.make_async_copy(src, outs[m].at[s, i], lsem.at[k]); cp.start(); local.append(cp)
    f = []
    for k, (m, i) in enumerate(pieces):
        a[k].wait_recv()
        f.append(remote(outs[m].at[far, i], outs[m].at[far, i], ss.at[k, 2], rs.at[k, 2], cdev))
    for k in range(len(pieces)):
        local[k].wait(); a[k].wait_send(); b[k].wait(); f[k].wait()
def seq_gather(arrays, items, rows, seq, cid):
    n = len(arrays); q = n * items
    sem = pltpu.SemaphoreType.DMA
    any_ = pl.BlockSpec(memory_space=pltpu.VMEM)
    return pl.pallas_call(functools.partial(seq_gather_kernel, n, items, rows),
        out_shape=[jax.ShapeDtypeStruct((seq, items, rows, a.shape[-1]), a.dtype) for a in arrays],
        in_specs=[any_] * n, out_specs=[any_] * n,
        scratch_shapes=[sem((q,)), sem((q, 3)), sem((q, 3))],
        compiler_params=pltpu.CompilerParams(collective_id=cid, has_side_effects=True, vmem_limit_bytes=48*2**20))(*arrays)
def seq_sum_kernel(n, items, *refs):
    ins, outs = refs[:n], refs[n:2 * n]
    cb, a1, b1, ss, rs = refs[2 * n:]
    s, x, c, xdev, cdev = seq_places(2)
    greet([xdev, cdev])
    pieces = [(m, i) for m in range(n) for i in range(items)]
    first = [[None, None] for _ in pieces]
    second = []
    f32 = jnp.float32
    for far in range(2):
        xx = 1 - x if far == 0 else x
        for k, (m, i) in enumerate(pieces):
            first[k][far] = remote(ins[m].at[xx * 2 + 1 - c, i], cb.at[k, far], ss.at[k, far], rs.at[k, far], cdev)
    for k, (m, i) in enumerate(pieces):
        first[k][0].wait_recv()
        a1[k] = (ins[m][(1 - x) * 2 + c, i].astype(f32) + cb[k, 0].astype(f32)).astype(a1.dtype)
        second.append(remote(a1.at[k], b1.at[k], ss.at[k, 2], rs.at[k, 2], xdev))
    for k, (m, i) in enumerate(pieces):
        first[k][1].wait_recv()
        second[k].wait_recv()
        outs[m][i] = (ins[m][s, i].astype(f32) + cb[k, 1].astype(f32) + b1[k].astype(f32)).astype(outs[m].dtype)
    for k in range(len(pieces)):
        first[k][0].wait_send(); first[k][1].wait_send(); second[k].wait_send()
def seq_sum(arrays, cid):
    n = len(arrays); seq, items, rows, w = arrays[0].shape; q = n * items
    sem = pltpu.SemaphoreType.DMA; dt = arrays[0].dtype
    vm = pl.BlockSpec(memory_space=pltpu.VMEM)
    return pl.pallas_call(functools.partial(seq_sum_kernel, n, items),
        out_shape=[jax.ShapeDtypeStruct((items, rows, w), dt) for a in arrays],
        in_specs=[vm] * n, out_specs=[vm] * n,
        scratch_shapes=[pltpu.VMEM((q, 2, rows, w), dt), pltpu.VMEM((q, rows, w), dt), pltpu.VMEM((q, rows, w), dt), sem((q, 3)), sem((q, 3))],
        compiler_params=pltpu.CompilerParams(collective_id=cid, has_side_effects=True, vmem_limit_bytes=48 * 2**20))(*arrays)


def gelu_parts(v):
    c, a = 0.7978845608, 0.044715
    v2 = v * v
    t = jnp.tanh(c * v * (1.0 + a * v2))
    half = 0.5 * (1.0 + t)
    return v * half, half + 0.5 * v * (1.0 - t * t) * (c * (1.0 + 3.0 * a * v2))
RING, LAG = 6, 4
def expert_kernel(cap, per, order, todo, wcut, tile, whole_down, xs, gs, wgi, wui, wdi, eo_out, ri_out, grads, eo_h, ri_h,
                  wall, xr, gr, hall, lall, eo, ri, cb, ab, xb, ob,
                  lsem, xss, xrs, gss, grs, ess, ers, rss, rrs, wss, wrs, wls, css, crs, ass, ars, osem, free):
    dp = lax.axis_size("dp")
    f32, bf = jnp.float32, jnp.bfloat16
    s, x, c, xdev, cdev = seq_places(2)
    g = lax.axis_index("dp")
    def peer(k): return (s, g ^ k)
    greet([xdev, cdev] + [peer(k) for k in range(1, dp)])
    rows_w, ff = wgi.shape; width = xs.shape[2]
    piece = rows_w // wcut
    wx, wc, wl = [], [], []
    shared = ((wgi, 1), (wui, 2)) if whole_down else ((wgi, 1), (wui, 2), (wdi, 0))
    parts = [(src, m, h * piece) for h in range(wcut) for src, m in shared]
    for n, (src, m, r0) in enumerate(parts):
        a = src.at[pl.ds(r0, piece)]
        b = wall.at[m, x, c, pl.ds(r0, piece)]
        wx.append(remote(a, b, wss.at[n, 0], wrs.at[n, 0], xdev))
        wc.append(remote(a, b, wss.at[n, 1], wrs.at[n, 1], cdev))
        cp = pltpu.make_async_copy(a, b, wls.at[n]); cp.start(); wl.append(cp)
    if whole_down:
        cp = pltpu.make_async_copy(wdi, wall.at[0], wls.at[len(parts)]); cp.start(); wl.append(cp)
    sx, sg = {}, {}
    for k in [k for p in order for k in range(p * per, (p + 1) * per)]:
        at = pl.ds(k * cap, cap)
        if k == 0:
            sx[0] = pltpu.make_async_copy(xs.at[g], xr.at[at], lsem.at[0]); sx[0].start()
            sg[0] = pltpu.make_async_copy(gs.at[g], gr.at[at], lsem.at[1]); sg[0].start()
        else:
            sx[k] = remote(xs.at[g ^ k], xr.at[at], xss.at[k], xrs.at[k], peer(k))
            sg[k] = remote(gs.at[g ^ k], gr.at[at], gss.at[k], grs.at[k], peer(k))
    wf = []
    for n, (src, m, r0) in enumerate(parts):
        wx[n].wait_recv()
        b = wall.at[m, 1 - x, c, pl.ds(r0, piece)]
        wf.append(remote(b, b, wss.at[n, 2], wrs.at[n, 2], cdev))
    for cp in wl: cp.wait()
    for n in range(len(parts)):
        wc[n].wait_recv(); wf[n].wait_recv()
    ntile = ff // tile
    re, rr = {}, {}
    wide = 4 * rows_w
    for p in todo:
        ks = list(range(p * per, (p + 1) * per))
        for k in ks:
            if k == 0: sx[0].wait(); sg[0].wait()
            else: sx[k].wait_recv(); sg[k].wait_recv()
        rows = pl.ds(p * per * cap, per * cap)
        @pl.loop(0, ntile)
        def _(t):
            cols = pl.ds(pl.multiple_of(t * tile, 128), tile)
            w = lambda m: wall[m, :, :, :, cols].reshape(wide, tile)
            gp = jnp.dot(xr[rows, :], w(1), preferred_element_type=f32)
            up = jnp.dot(xr[rows, :], w(2), preferred_element_type=f32)
            hg = jnp.dot(gr[rows, :], w(0), preferred_element_type=f32)
            act, der = gelu_parts(gp)
            hall[0, rows, cols] = (act * up).astype(bf)
            hall[1, rows, cols] = (hg * up * der).astype(bf)
            hall[2, rows, cols] = (hg * act).astype(bf)
        @pl.loop(0, 4)
        def _(t):
            part = pl.ds(pl.multiple_of(t * rows_w, 128), rows_w)
            tx, tc = t // 2, lax.rem(t, 2)
            eo[:, part] = dot(hall[0, rows, :], wall[0, tx, tc], 1, 1).astype(bf)
            ri[:, part] = (dot(hall[1, rows, :], wall[1, tx, tc], 1, 1) + dot(hall[2, rows, :], wall[2, tx, tc], 1, 1)).astype(bf)
        keep = [pltpu.make_async_copy(eo, eo_h.at[rows], lsem.at[4]), pltpu.make_async_copy(ri, ri_h.at[rows], lsem.at[5])]
        for cp in keep: cp.start()
        for cp in keep: cp.wait()
        for k in ks:
            at = pl.ds(k * cap, cap)
            if k == 0:
                re[0] = pltpu.make_async_copy(eo_h.at[at], eo_out.at[g], lsem.at[2]); re[0].start()
                rr[0] = pltpu.make_async_copy(ri_h.at[at], ri_out.at[g], lsem.at[3]); rr[0].start()
            else:
                re[k] = remote(eo_h.at[at], eo_out.at[g], ess.at[k], ers.at[k], peer(k))
                rr[k] = remote(ri_h.at[at], ri_out.at[g], rss.at[k], rrs.at[k], peer(k))
    for n in range(len(parts)):
        wx[n].wait_send(); wc[n].wait_send(); wf[n].wait_send()
    total = dp * cap
    @pl.loop(0, total // 256)
    def _(t):
        at = pl.ds(pl.multiple_of(t * 256, 256), 256)
        lall[1, :, at] = xr[at, :].T
        lall[0, :, at] = gr[at, :].T
    nt = 3 * ntile
    def place(n):
        m = n // ntile
        return m, pl.ds(pl.multiple_of((n - m * ntile) * tile, 128), tile)
    def to_core(n):
        m, cols = place(n); r = lax.rem(n, RING)
        return pltpu.make_async_remote_copy(src_ref=wall.at[m, :, 1 - c, :, cols], dst_ref=cb.at[r], send_sem=css.at[r],
            recv_sem=crs.at[r], device_id=cdev, device_id_type=MESH)
    def to_chip(n):
        r = lax.rem(n, RING)
        return pltpu.make_async_remote_copy(src_ref=ab.at[r], dst_ref=xb.at[r], send_sem=ass.at[r],
            recv_sem=ars.at[r], device_id=xdev, device_id_type=MESH)
    def to_out(n):
        m, cols = place(n); r = lax.rem(n, 2)
        return pltpu.make_async_copy(ob.at[r], grads.at[m, :, cols], osem.at[r])
    @pl.loop(0, nt + LAG)
    def _(n):
        @pl.when(n < nt)
        def _():
            m, cols = place(n)
            res = jnp.dot(lall[jnp.minimum(m, 1)], hall[m, :, cols], preferred_element_type=f32)
            wall[m, :, :, :, cols] = res.astype(bf).reshape(2, 2, rows_w, tile)
            @pl.when(n >= RING)
            def _(): pl.semaphore_wait(free.at[0], 1)
            to_core(n).start()
        @pl.when((n >= 1) & (n <= nt))
        def _():
            i = n - 1
            m, cols = place(i); r = lax.rem(i, RING)
            to_core(i).wait_recv()
            @pl.when(i >= RING)
            def _():
                to_chip(i).wait_send()
                pl.semaphore_wait(free.at[1], 1)
            ab[r] = (wall[m, 1 - x, c, :, cols].astype(f32) + cb[r, 1 - x].astype(f32)).astype(bf)
            to_chip(i).start()
        @pl.when(n >= LAG)
        def _():
            j = n - LAG
            m, cols = place(j); r = lax.rem(j, RING)
            to_chip(j).wait_recv()
            to_core(j).wait_send()
            @pl.when(j >= 2)
            def _(): to_out(j).wait()
            ob[lax.rem(j, 2)] = wall[m, x, c, :, cols].astype(f32) + cb[r, x].astype(f32) + xb[r].astype(f32)
            to_out(j).start()
            @pl.when(j < nt - RING)
            def _():
                pl.semaphore_signal(free.at[0], inc=1, device_id=cdev, device_id_type=MESH)
                pl.semaphore_signal(free.at[1], inc=1, device_id=xdev, device_id_type=MESH)
    for j in range(nt - 2, nt): to_out(j).wait()
    for i in range(nt - RING, nt): to_chip(i).wait_send()
    for k in range(dp):
        if k == 0:
            re[0].wait(); rr[0].wait()
        else:
            sx[k].wait_send(); sg[k].wait_send(); re[k].wait(); rr[k].wait()
def expert_all(xs, gs, wg, wu, wd, seq, cid):
    dp, cap, width = xs.shape
    rows_w, ff = wg.shape; total = dp * cap
    whole_down = wd.shape[0] != rows_w
    if whole_down: wd = wd.reshape(seq // 2, 2, rows_w, ff)
    group = 320
    per = group // cap
    ng = dp // per
    order = [p for p in range(ng // 2, ng)] + [p for p in range(ng // 2 - 1, -1, -1)]
    todo = list(range(ng))
    sem = pltpu.SemaphoreType.DMA
    bf = jnp.bfloat16
    any_ = pl.BlockSpec(memory_space=pl.ANY)
    V = pltpu.VMEM
    tile = 256
    wcut = 2
    back = jax.ShapeDtypeStruct((dp, cap, width), bf)
    flat = jax.ShapeDtypeStruct((total, width), bf)
    return pl.pallas_call(functools.partial(expert_kernel, cap, per, order, todo, wcut, tile, whole_down),
        out_shape=[back, back, jax.ShapeDtypeStruct((3, rows_w, ff), jnp.float32), flat, flat],
        in_specs=[any_] * 5, out_specs=[any_] * 5,
        scratch_shapes=[V((3, seq // 2, 2, rows_w, ff), bf), V((total, width), bf), V((total, width), bf), V((3, total, ff), bf),
        V((2, width, total), bf), V((group, width), bf), V((group, width), bf),
        V((RING, seq // 2, rows_w, tile), bf), V((RING, rows_w, tile), bf), V((RING, rows_w, tile), bf), V((2, rows_w, tile), jnp.float32)]
        + [sem((6,))] + [sem((dp,))] * 8 + [sem((3 * wcut, 3))] * 2 + [sem((3 * wcut + 1,))] + [sem((RING,))] * 4 + [sem((2,)), pltpu.SemaphoreType.REGULAR((2,))],
        compiler_params=pltpu.CompilerParams(collective_id=cid, has_side_effects=True, vmem_limit_bytes=63 * 2**20))(xs, gs, wg, wu, wd)[:3]


def on_device(
    long_tokens,
    short_tokens,
    long_grad_out,
    short_grad_out,
    query_weight,
    key_weight,
    value_weight,
    output_weight,
    attn_gain,
    ffn_gain,
    rel_table,
    router_weight,
    gate_weight,
    up_weight,
    down_weight,
    long_positions,
    short_positions,
    long_lengths,
    short_lengths,
    long_routes,
    short_routes,
):
    long_items, quarter, model_width = long_tokens.shape
    short_items, short_len = (short_tokens.shape[0], short_tokens.shape[1])
    long_rows = long_items * quarter
    tokens = long_rows + short_items * short_len
    local_experts = gate_weight.shape[0]
    dp_size = lax.axis_size("dp")
    experts = local_experts * dp_size
    capacity = (5 * tokens + 2 * experts - 1) // (2 * experts)
    seq_size = lax.axis_size("seq")
    dims = (seq_size // 2, 2, dp_size // 2, 2)
    devices = seq_size * dp_size
    table_part, router_part = rel_table.shape[0], router_weight.size
    gain_part = attn_gain.shape[0]
    small_size = 2 * gain_part + table_part + router_part
    small = jnp.concatenate([attn_gain, ffn_gain, rel_table, router_weight.reshape(-1)])
    small = jnp.pad(small, (0, -small_size % 2048)).reshape(-1, 128)
    rows_part = query_weight.shape[0]
    cuts = 2 if rows_part % 32 == 0 else 1
    cut = rows_part // cuts
    pieces = tuple((m, h * cut, cut, (m + h) % 2) for m in range(4) for h in range(cuts))
    gathered = gather_all(
        (query_weight, key_weight, value_weight, output_weight, small),
        pieces[: 3 * cuts] + ((4, 0, small.shape[0], 0),) + pieces[3 * cuts :],
        dims,
        0,
    )
    small_all = gathered[4].reshape(devices, -1)
    attn_set = tuple(block.reshape(devices * rows_part, model_width) for block in gathered[:4]) + (
        small_all[:, :gain_part].reshape(-1),
        small_all[:, gain_part : 2 * gain_part].reshape(-1),
        small_all[:, 2 * gain_part : 2 * gain_part + table_part].reshape(-1),
        small_all[:, 2 * gain_part + table_part : small_size].reshape(model_width, experts),
    )
    resid_in = jnp.concatenate(
        [long_tokens.reshape(long_rows, model_width), short_tokens.reshape(-1, model_width)], 0
    ).astype(jnp.float32)
    gain_first = attn_set[4].astype(jnp.float32)
    normed = rms_norm(resid_in, gain_first).astype(jnp.bfloat16)
    projected = [
        jnp.dot(normed, matrix, preferred_element_type=jnp.float32).astype(jnp.bfloat16)
        for matrix in attn_set[:3]
    ]
    queries, keys, values = projected
    long_keys, long_values = seq_gather((keys, values), long_items, quarter, seq_size, 2)
    table = attn_set[6].reshape(HEADS, 1, BUCKETS).astype(jnp.float32)
    table = jnp.pad(table, ((0, 0), (0, 0), (0, 128 - BUCKETS)), constant_values=masked)
    routes = jnp.concatenate([long_routes.reshape(-1, 2), short_routes.reshape(-1, 2)], 0)
    router_t = jnp.pad(attn_set[7].T, ((0, 128 - experts), (0, 0)))
    gain_second = attn_set[5].astype(jnp.float32).reshape(1, model_width)
    sizes = (long_items, short_items, seq_size, experts, capacity)
    attn_args = (
        long_lengths,
        short_lengths,
        queries,
        keys,
        values,
        long_keys,
        long_values,
        table,
        long_positions.reshape(long_items, seq_size, quarter, 1),
        long_positions.reshape(long_items, seq_size, 1, quarter),
        short_positions.reshape(short_items, 1, short_len, 1),
        short_positions.reshape(short_items, 1, 1, short_len),
    )
    tail_args = (long_grad_out, short_grad_out, attn_set[3], gain_second, router_t)
    mixed_all, resid_mid, outgoing, out_slots, logits = attention(
        False,
        *sizes,
        attn_args + (long_tokens, short_tokens) + tail_args + (routes.T,),
        tokens,
        model_width,
    )
    later_down, unused_keys = lax.optimization_barrier((down_weight[0], long_keys))
    down_full = lax.all_gather(later_down, "seq", axis=0, tiled=True)
    back_rows, returned_grad, expert_grads = expert_all(
        outgoing, out_slots, gate_weight[0], up_weight[0], down_full, seq_size, 4
    )
    (
        query_act,
        short_key,
        short_value,
        long_key,
        long_value,
        table_sums,
        final_low,
        middle_grad,
        output_local,
        ffn_gain_local,
        router_local,
    ) = attention(
        True,
        *sizes,
        attn_args
        + (back_rows, returned_grad, resid_mid, mixed_all, logits, routes)
        + tail_args,
        tokens,
        model_width,
    )
    long_out = final_low[:long_rows].reshape(long_items, quarter, model_width)
    short_out = final_low[long_rows:].reshape(short_items, short_len, model_width)
    down_grad, gate_grad, up_grad = (expert_grads[m : m + 1] for m in range(3))
    attn_back = attn_set
    long_key, long_value = seq_sum((long_key, long_value), 3)
    key_act = jnp.concatenate([long_key.reshape(long_rows, model_width), short_key], 0)
    value_act = jnp.concatenate([long_value.reshape(long_rows, model_width), short_value], 0)
    upto = table_sums.reshape(HEADS, 128)[:, : len(ORDER)]
    within = upto - jnp.pad(upto[:, :-1], ((0, 0), (1, 0)))
    table_local = jnp.stack(
        [
            within[:, ORDER.index(n)] if n in ORDER else jnp.zeros(HEADS, jnp.float32)
            for n in range(BUCKETS)
        ],
        1,
    ).reshape(-1)
    normed_grad = (
        jnp.einsum("te,de->td", query_act, attn_back[0], preferred_element_type=jnp.float32)
        + jnp.einsum("te,de->td", key_act, attn_back[1], preferred_element_type=jnp.float32)
        + jnp.einsum("te,de->td", value_act, attn_back[2], preferred_element_type=jnp.float32)
    )
    query_local = jnp.einsum("td,te->de", normed, query_act, preferred_element_type=jnp.float32)
    key_local = jnp.einsum("td,te->de", normed, key_act, preferred_element_type=jnp.float32)
    value_local = jnp.einsum("td,te->de", normed, value_act, preferred_element_type=jnp.float32)
    unused_in, norm_one_pull = jax.vjp(rms_norm, resid_in, attn_back[4].astype(jnp.float32))
    in_norm_grad, attn_gain_local = norm_one_pull(normed_grad)
    input_grad_all = middle_grad + in_norm_grad
    long_grad_in = input_grad_all[:long_rows].reshape(long_items, quarter, model_width)
    short_grad_in = input_grad_all[long_rows:].reshape(short_items, short_len, model_width)
    shares = (gain_part, gain_part, table_part, router_part)
    small_local = jnp.concatenate(
        [
            part.reshape(devices, -1)
            for part in (attn_gain_local, ffn_gain_local, table_local, router_local.T)
        ],
        1,
    )
    small_local = jnp.pad(small_local, ((0, 0), (0, -small_size % 1024)))
    small_rows = small_local.shape[1] // 128
    mats = tuple(
        part.astype(jnp.bfloat16).reshape(dims + (rows_part, model_width))
        for part in (output_local, query_local, key_local, value_local)
    )
    scattered = scatter_all(
        mats + (small_local.reshape(dims + (small_rows, 128)),),
        pieces[:cuts] + ((4, 0, small_rows, 0),) + pieces[cuts:],
        dims,
        1,
    )
    small_sum = scattered[4].reshape(-1)
    edges = [sum(shares[:k]) for k in range(5)]
    summed = (scattered[1], scattered[2], scattered[3], scattered[0]) + tuple(
        small_sum[edges[k] : edges[k + 1]] for k in range(3)
    ) + (small_sum[edges[3] : edges[4]].reshape(rows_part, experts),)
    return (
        long_out,
        short_out,
        long_grad_in,
        short_grad_in,
        summed[0],
        summed[1],
        summed[2],
        summed[3],
        summed[4],
        summed[5],
        summed[6],
        summed[7],
        gate_grad,
        up_grad,
        down_grad,
    )


def solution(mesh):
    placed = (
        P("dp", "seq", None),
        P(("seq", "dp"), None, None),
        P("dp", "seq", None),
        P(("seq", "dp"), None, None),
        P(("seq", "dp"), None),
        P(("seq", "dp"), None),
        P(("seq", "dp"), None),
        P(("seq", "dp"), None),
        P(("seq", "dp")),
        P(("seq", "dp")),
        P(("seq", "dp")),
        P(("seq", "dp"), None),
        P("dp", "seq", None),
        P("dp", "seq", None),
        P("dp", "seq", None),
        P("dp", None),
        P(("seq", "dp"), None),
        P("dp"),
        P(("seq", "dp")),
        P("dp", "seq", None),
        P(("seq", "dp"), None, None),
    )
    return jax.shard_map(
        on_device,
        mesh=mesh,
        in_specs=placed,
        out_specs=(
            P("dp", "seq", None),
            P(("seq", "dp"), None, None),
            P("dp", "seq", None),
            P(("seq", "dp"), None, None),
            P(("seq", "dp"), None),
            P(("seq", "dp"), None),
            P(("seq", "dp"), None),
            P(("seq", "dp"), None),
            P(("seq", "dp")),
            P(("seq", "dp")),
            P(("seq", "dp")),
            P(("seq", "dp"), None),
            P("dp", "seq", None),
            P("dp", "seq", None),
            P("dp", "seq", None),
        ),
        check_vma=False,
    )
```

```python
import functools

import jax
import jax.numpy as jnp
from jax import lax
from jax.experimental import pallas as pl
from jax.experimental.pallas import tpu as pltpu
from jax.sharding import PartitionSpec as P

MESH = pl.DeviceIdType.MESH

HEADS = 16
HEAD = 64
BUCKETS = 32


epsilon = 1e-06
masked = -1e30


def gather_kernel(dims, pieces, na, *refs):
    X, C, Z, Y = dims
    n = len(pieces)
    lsem, zs, zr, hs, hr, cs, cr = refs[2*na:]
    routes = [p[3] for p in pieces]
    ins = [refs[m].at[pl.ds(r0, nr)] for m, r0, nr, _ in pieces]
    class V:
        def __init__(self, ref, r0, nr): self.ref, self.r0, self.nr = ref, r0, nr
        @property
        def at(self): return self
        def __getitem__(self, k):
            k = k + (slice(None),) * (4 - len(k)) + (pl.ds(self.r0, self.nr),)
            return self.ref.at[k]
    outs = [V(refs[na + m], r0, nr) for m, r0, nr, _ in pieces]
    s = lax.axis_index("seq"); g = lax.axis_index("dp")
    x, c = s // C, lax.rem(s, C)
    z, y = g // Y, lax.rem(g, Y)
    def zdev(k): return (s, lax.rem(z + k, Z) * Y + y)
    ydev = (s, z * Y + (1 - y)); xdev = ((1 - x) * C + c, g); cdev = (x * C + 1 - c, g)
    bar = pltpu.get_barrier_semaphore()
    for d in [zdev(k) for k in range(1, Z)] + [ydev, xdev, cdev]:
        pl.semaphore_signal(bar, inc=1, device_id=d, device_id_type=MESH)
    pl.semaphore_wait(bar, Z + 2)
    def rc(src, dst, ss, rs, dev):
        cp = pltpu.make_async_remote_copy(src_ref=src, dst_ref=dst, send_sem=ss, recv_sem=rs, device_id=dev, device_id_type=MESH)
        cp.start(); return cp
    sends = []
    local = []; zc = []
    for m in range(n):
        lc = pltpu.make_async_copy(ins[m], outs[m].at[x, c, z, y], lsem.at[m]); lc.start(); local.append(lc)
        zc.append([rc(ins[m], outs[m].at[x, c, z, y], zs.at[m, k], zr.at[m, k], zdev(k)) for k in range(1, Z)])
    h = [[None, None] for _ in range(n)]
    cc = [[None]*3 for _ in range(n)]
    for t in range(n + 2):
        for stage in range(3):
            m = t - stage
            if not 0 <= m < n: continue
            o = outs[m]; route = routes[m]
            if stage == 0:
                local[m].wait()
                for q in zc[m]: q.wait_recv()
                mine = o.at[x, c, :, y]
                h[m][0] = rc(mine, mine, hs.at[m,0], hr.at[m,0], xdev if route == 0 else ydev)
                cc[m][0] = rc(mine, mine, cs.at[m,0], cr.at[m,0], cdev)
            elif stage == 1:
                h[m][0].wait_recv()
                if route == 0:
                    both = o.at[:, c, :, y]; got = o.at[1 - x, c, :, y]
                else:
                    both = o.at[x, c]; got = o.at[x, c, :, 1 - y]
                h[m][1] = rc(both, both, hs.at[m,1], hr.at[m,1], ydev if route == 0 else xdev)
                cc[m][1] = rc(got, got, cs.at[m,1], cr.at[m,1], cdev)
            else:
                h[m][1].wait_recv()
                got = o.at[:, c, :, 1 - y] if route == 0 else o.at[1 - x, c]
                cc[m][2] = rc(got, got, cs.at[m,2], cr.at[m,2], cdev)
    for m in range(n):
        for q in zc[m]: q.wait_send()
        for q in h[m]: q.wait_send()
        for q in cc[m]: q.wait()
def gather_all(arrays, pieces, dims, cid):
    X, C, Z, Y = dims; na = len(arrays); n = len(pieces)
    sem = pltpu.SemaphoreType.DMA
    return pl.pallas_call(functools.partial(gather_kernel, dims, pieces, na),
        out_shape=[jax.ShapeDtypeStruct((X, C, Z, Y) + a.shape, a.dtype) for a in arrays],
        in_specs=[pl.BlockSpec(memory_space=pl.ANY)] * na, out_specs=[pl.BlockSpec(memory_space=pl.ANY)] * na,
        scratch_shapes=[sem((n,)), sem((n, Z)), sem((n, Z)), sem((n, 2)), sem((n, 2)), sem((n, 3)), sem((n, 3))],
        compiler_params=pltpu.CompilerParams(collective_id=cid, has_side_effects=True))(*arrays)


EDGES = (-90, -63, -45, -31, -22, -15, -11, -7, -6, -5, -4, -3, -2, -1, 0, 1, 2, 3, 4, 5, 6, 7, 8, 12, 16, 23, 32, 46, 64, 91)
ORDER = (15, 14, 13, 12, 11, 10, 9, 8, 7, 6, 5, 4, 3, 2, 1, 0, 17, 18, 19, 20, 21, 22, 23, 24, 25, 26, 27, 28, 29, 30, 31)
FAR = (12, 16, 23, 32, 46, 64, 91)
def fill_buckets(out, q_col, k_row, length, base):
    r = k_row - q_col
    n = jnp.abs(r)
    far = jnp.full(r.shape, 8, jnp.int32)
    for e in FAR:
        far += (n >= e).astype(jnp.int32)
    b = jnp.where(n < 8, n, far) + jnp.where(r > 0, 16, 0)
    j = lax.broadcasted_iota(jnp.int32, r.shape, 1) + base
    out[...] = jnp.where(j < length, b, 32)
def dot(a, b, ca, cb):
    return lax.dot_general(a, b, (((ca,), (cb,)), ((), ())), preferred_element_type=jnp.float32)
def probs_of(qs, kk, tabs, bucket_ref, blocks):
    s = dot(qs, kk, 1, 1)
    t = [jnp.broadcast_to(tab, (128, 128)) for tab in tabs]
    bias = [jnp.concatenate([jnp.take_along_axis(x, bucket_ref[c], axis=1) for x in t], axis=0) for c in range(blocks)]
    s = s + (jnp.concatenate(bias, axis=1) if blocks > 1 else bias[0])
    p = jnp.exp(s - jnp.max(s, axis=1, keepdims=True))
    return p * (1.0 / jnp.sum(p, axis=1, keepdims=True))
def stack_heads(rows, first):
    return jnp.concatenate([jnp.where(first, rows, 0), jnp.where(first, 0, rows)], axis=0)
def attn_setup(nl, ns, blocks, ll, sl, lcol, lrow, scol, srow, lb, sb):
    me = lax.axis_index("seq")
    for b in range(nl):
        for c in range(blocks):
            fill_buckets(lb.at[b, c], lcol[b, me], lrow[b, c], ll[b], c * 128)
    for b in range(ns):
        fill_buckets(sb.at[b, 0], scol[b, 0], srow[b, 0], sl[b], 0)
def rows_of(long_ref, short_ref, t, nl, ns):
    if t == 0:
        return long_ref[...].reshape(nl * 128, -1)
    return short_ref[...].reshape(ns * 128, -1)
def rms_scale(mid):
    return lax.rsqrt(jnp.mean(mid * mid, axis=-1, keepdims=True) + epsilon)
def attn_fwd_kernel(nl, ns, blocks, experts, cap, ll, sl, q, k, v, kl, vl, tab, lcol, lrow, scol, srow,
                    xl, xsh, gl, gsh, wo, gain, rt, rrow, mixed, mid, xs, gs, logits, lb, sb, n2, gb):
    attn_setup(nl, ns, blocks, ll, sl, lcol, lrow, scol, srow, lb, sb)
    first = lax.broadcasted_iota(jnp.int32, (128, 128), 1) < 64
    @pl.loop(0, 8)
    def _(hp):
        cols = pl.ds(pl.multiple_of(hp * 128, 128), 128)
        for b in range(nl + ns):
            rows = pl.ds(b * 128, 128)
            n = blocks if b < nl else 1
            if b < nl:
                kk = kl[:, b, :, cols].reshape(n * 128, 128); vv = vl[:, b, :, cols].reshape(n * 128, 128)
            else:
                kk = k[rows, cols]; vv = v[rows, cols]
            p = probs_of(stack_heads(q[rows, cols], first), kk, (tab[2 * hp], tab[2 * hp + 1]), lb.at[b] if b < nl else sb.at[b - nl], n)
            out = dot(p.astype(jnp.bfloat16), vv, 1, 0)
            mixed[rows, cols] = jnp.where(first, out[:128], out[128:]).astype(jnp.bfloat16)
    f32, bf = jnp.float32, jnp.bfloat16
    tokens = q.shape[0]
    for t in range(2):
        rows = pl.ds(t * 256, 256)
        m = rows_of(xl, xsh, t, nl, ns).astype(f32) + jnp.dot(mixed[rows, :], wo[...], preferred_element_type=f32)
        mid[rows, :] = m
        n2[rows, :] = (m * rms_scale(m) * gain[...]).astype(bf)
        gb[rows, :] = rows_of(gl, gsh, t, nl, ns)
    logits[...] = dot(n2[...], rt[...], 1, 1)
    logit_t = dot(rt[...], n2[...], 1, 1)[:experts]
    e_iota = lax.broadcasted_iota(jnp.int32, (experts, tokens), 0)
    member = ((e_iota == rrow[0:1, :]) | (e_iota == rrow[1:2, :])).astype(f32)
    e = jnp.exp(logit_t - jnp.max(logit_t, axis=0, keepdims=True))
    p = e / jnp.sum(e, axis=0, keepdims=True)
    chosen = member * p
    before = (lax.broadcasted_iota(jnp.int32, (tokens, tokens), 0) < lax.broadcasted_iota(jnp.int32, (tokens, tokens), 1)).astype(f32).astype(bf)
    place = jnp.dot(member.astype(bf), before, preferred_element_type=f32)
    kept = (member > 0.5) & (place < cap)
    weight = jnp.where(kept, chosen / jnp.sum(chosen, axis=0, keepdims=True), 0.0)
    slot = jnp.where(kept, place.astype(jnp.int32), -1)
    s_iota = lax.broadcasted_iota(jnp.int32, (cap, tokens), 0)
    for i in range(experts):
        pick = (s_iota == slot[i:i + 1, :]).astype(f32)
        scale = jnp.sum(pick * weight[i:i + 1, :], axis=1, keepdims=True)
        pick = pick.astype(bf)
        xs[i] = jnp.dot(pick, n2[...], preferred_element_type=f32).astype(bf)
        gs[i] = (jnp.dot(pick, gb[...], preferred_element_type=f32) * scale).astype(bf)
def attn_bwd_kernel(nl, ns, blocks, experts, cap, ll, sl, q, k, v, kl, vl, tab, lcol, lrow, scol, srow,
                    eo, ri, mid, mixed, logits, rcol, gl, gsh, wo, gain, rt,
                    dq, dk, dv, dkl, dvl, seg, final, midg, wog, fgg, rtg, lb, sb, li, si, mg, bg, n2, lg, fin, bk, sh):
    f32, bf = jnp.float32, jnp.bfloat16
    tokens = q.shape[0]
    lane = lax.broadcasted_iota(jnp.int32, (tokens, 128), 1)
    member = ((lane == rcol[:, 0:1]) | (lane == rcol[:, 1:2])).astype(f32)
    after = (lax.broadcasted_iota(jnp.int32, (tokens, tokens), 1) < lax.broadcasted_iota(jnp.int32, (tokens, tokens), 0)).astype(f32).astype(bf)
    place = jnp.dot(after, member.astype(bf), preferred_element_type=f32)
    kept = (member > 0.5) & (place < cap)
    slot = jnp.where(kept, place.astype(jnp.int32), -1)
    lgt = jnp.where(lane < experts, logits[...], -1e30)
    ex = jnp.exp(lgt - jnp.max(lgt, axis=1, keepdims=True))
    p = ex / jnp.sum(ex, axis=1, keepdims=True)
    chosen = member * p
    both = jnp.sum(chosen, axis=1, keepdims=True)
    gate = chosen / both
    fg = jnp.zeros((1, q.shape[1]), f32)
    for t in range(2):
        at = slice(t * 256, t * 256 + 256)
        rows = pl.ds(t * 256, 256)
        g = rows_of(gl, gsh, t, nl, ns).astype(f32)
        m = mid[rows, :]
        fin[...] = m
        bk[...] = jnp.zeros_like(m)
        sh[...] = jnp.zeros_like(sh)
        s_iota = lax.broadcasted_iota(jnp.int32, (256, cap), 1)
        slot_t, weight_t, lane_t = slot[at], jnp.where(kept[at], gate[at], 0.0), lane[:256]
        @pl.loop(0, experts)
        def _(i):
            this = lane_t == i
            mine = jnp.sum(jnp.where(this, slot_t, 0), axis=1, keepdims=True)
            weight = jnp.sum(jnp.where(this, weight_t, 0.0), axis=1, keepdims=True)
            pick = (s_iota == mine).astype(f32).astype(bf)
            pair = jnp.dot(pick, eo[i], preferred_element_type=f32)
            fin[...] += weight * pair
            sh[...] = jnp.where(this, jnp.sum(rows_of(gl, gsh, t, nl, ns).astype(f32) * pair, axis=1, keepdims=True), sh[...])
            bk[...] += jnp.dot(pick, ri[i], preferred_element_type=f32)
        final[rows, :] = fin[...].astype(bf)
        share, back = sh[...], bk[...]
        mean = jnp.sum(share * gate[at], axis=1, keepdims=True)
        pg = member[at] * (share - mean) / both[at]
        lgrad = (p[at] * (pg - jnp.sum(p[at] * pg, axis=1, keepdims=True))).astype(bf)
        lg[rows, :] = lgrad
        r2 = rms_scale(m)
        u = m * r2
        n2[rows, :] = (u * gain[...]).astype(bf)
        back += jnp.dot(lgrad, rt[...], preferred_element_type=f32)
        fg += jnp.sum(back * u, axis=0, keepdims=True)
        w = back * gain[...]
        out = g + r2 * (w - u * jnp.mean(w * u, axis=-1, keepdims=True))
        midg[rows, :] = out
        bg[rows, :] = out.astype(bf)
        mg[rows, :] = dot(out.astype(bf), wo[...], 1, 1).astype(bf)
    fgg[...] = fg
    rtg[...] = dot(lg[...], n2[...], 0, 0)[:experts]
    wog[...] = dot(mixed[...], bg[...], 0, 0).astype(bf)
    attn_setup(nl, ns, blocks, ll, sl, lcol, lrow, scol, srow, lb, sb)
    me = lax.axis_index("seq")
    lane = lax.broadcasted_iota(jnp.int32, (128, 128), 1)
    edge = jnp.full((128, 128), 4096, jnp.int32)
    for i, e in enumerate(EDGES):
        edge = jnp.where(lane == i, e, edge)
    edge = jnp.where(lane > len(EDGES), -4096, edge)
    def places(out, q_col, k_col, k_first):
        t = lax.broadcasted_iota(jnp.int32, (128, 256), 1) + k_first
        below = jnp.sum((k_col < t).astype(jnp.int32), axis=0, keepdims=True)
        at = jnp.clip(q_col + edge - k_first, 0, 255)
        lo = jnp.take_along_axis(jnp.broadcast_to(below[:, :128], (128, 128)), at & 127, axis=1)
        hi = jnp.take_along_axis(jnp.broadcast_to(below[:, 128:], (128, 128)), at & 127, axis=1)
        out[...] = jnp.where(at < 128, lo, hi) - 1
    for b in range(nl):
        for c in range(blocks):
            places(li.at[b, c], lcol[b, me], lcol[b, c], lrow[b, c, 0, 0])
    for b in range(ns):
        places(si.at[b, 0], scol[b, 0], scol[b, 0], srow[b, 0, 0, 0])
    seg[...] = jnp.zeros_like(seg)
    first = lane < 64
    row = lax.broadcasted_iota(jnp.int32, (128, 128), 0)
    tri = jnp.where(row <= lane, 1.0, 0.0).astype(jnp.bfloat16)
    @pl.loop(0, 8)
    def _(hp):
        cols = pl.ds(pl.multiple_of(hp * 128, 128), 128)
        for b in range(nl + ns):
            rows = pl.ds(b * 128, 128)
            n = blocks if b < nl else 1
            if b < nl:
                kk = kl[:, b, :, cols].reshape(n * 128, 128); vv = vl[:, b, :, cols].reshape(n * 128, 128)
            else:
                kk = k[rows, cols]; vv = v[rows, cols]
            idx = li.at[b] if b < nl else si.at[b - nl]
            qs = stack_heads(q[rows, cols], first); gs = stack_heads(mg[rows, cols], first)
            p = probs_of(qs, kk, (tab[2 * hp], tab[2 * hp + 1]), lb.at[b] if b < nl else sb.at[b - nl], n)
            dp = dot(gs, vv, 1, 1)
            ds = (p * (dp - jnp.sum(p * dp, axis=1, keepdims=True))).astype(jnp.bfloat16)
            dqs = dot(ds, kk, 1, 0)
            dkt = dot(qs, ds, 0, 0)
            dvt = dot(gs, p.astype(jnp.bfloat16), 0, 0)
            sums = [0, 0]
            for c in range(n):
                pre = dot(ds[:, c * 128:(c + 1) * 128], tri, 1, 0)
                at = idx[c]
                for e in range(2):
                    sums[e] += jnp.where(at >= 0, jnp.take_along_axis(pre[e * 128:(e + 1) * 128], jnp.maximum(at, 0), axis=1), 0.0)
            for e in range(2):
                seg[2 * hp + e] += jnp.sum(sums[e], axis=0, keepdims=True)
            dq[rows, cols] = jnp.where(first, dqs[:128], dqs[128:]).astype(jnp.bfloat16)
            dkt = dkt.T.astype(jnp.bfloat16); dvt = dvt.T.astype(jnp.bfloat16)
            if b < nl:
                dkl[:, b, :, cols] = dkt.reshape(n, 128, 128); dvl[:, b, :, cols] = dvt.reshape(n, 128, 128)
            else:
                dk[pl.ds((b - nl) * 128, 128), cols] = dkt; dv[pl.ds((b - nl) * 128, 128), cols] = dvt
def attention(backward, nl, ns, blocks, experts, cap, arrays, tokens, width):
    sm, vm = pl.BlockSpec(memory_space=pltpu.SMEM), pl.BlockSpec(memory_space=pltpu.VMEM)
    bf, f32 = jnp.bfloat16, jnp.float32
    S = jax.ShapeDtypeStruct
    rows = S((tokens, width), bf)
    buckets = [pltpu.VMEM((nl, blocks, 128, 128), jnp.int32), pltpu.VMEM((ns, 1, 128, 128), jnp.int32)]
    row_buf = pltpu.VMEM((tokens, width), bf)
    if backward:
        short = S((ns * 128, width), bf)
        long = S((blocks, nl, 128, width), bf)
        outs = [rows, short, short, long, long, S((16, 1, 128), f32), rows, S((tokens, width), f32), S((width, width), bf),
                S((1, width), f32), S((experts, width), f32)]
        body = functools.partial(attn_bwd_kernel, nl, ns, blocks, experts, cap)
        scr = buckets * 2 + [row_buf] * 3 + [pltpu.VMEM((tokens, 128), bf)] + [pltpu.VMEM((256, width), f32)] * 2 + [pltpu.VMEM((256, 128), f32)]
    else:
        slots = S((experts, cap, width), bf)
        outs = [rows, S((tokens, width), f32), slots, slots, S((tokens, 128), f32)]
        body = functools.partial(attn_fwd_kernel, nl, ns, blocks, experts, cap); scr = buckets + [row_buf] * 2
    return pl.pallas_call(body, out_shape=outs, in_specs=[sm, sm] + [vm] * (len(arrays) - 2), out_specs=[vm] * len(outs),
        scratch_shapes=scr, compiler_params=pltpu.CompilerParams(vmem_limit_bytes=60 * 2**20))(*arrays)

def seq_places(C):
    s = lax.axis_index("seq"); g = lax.axis_index("dp")
    x, c = s // C, lax.rem(s, C)
    return s, x, c, ((1 - x) * C + c, g), (x * C + 1 - c, g)
def greet(devs):
    bar = pltpu.get_barrier_semaphore()
    for d in devs:
        pl.semaphore_signal(bar, inc=1, device_id=d, device_id_type=MESH)
    pl.semaphore_wait(bar, len(devs))
def remote(src, dst, ss, rs, dev):
    cp = pltpu.make_async_remote_copy(src_ref=src, dst_ref=dst, send_sem=ss, recv_sem=rs, device_id=dev, device_id_type=MESH)
    cp.start()
    return cp
def gelu_parts(v):
    c, a = 0.7978845608, 0.044715
    v2 = v * v
    t = jnp.tanh(c * v * (1.0 + a * v2))
    half = 0.5 * (1.0 + t)
    return v * half, half + 0.5 * v * (1.0 - t * t) * (c * (1.0 + 3.0 * a * v2))
RING, LAG = 6, 4
def expert_kernel(cap, per, order, todo, wcut, tile, whole_down, xs, gs, wgi, wui, wdi, eo_out, ri_out, grads, eo_h, ri_h,
                  wall, xr, gr, hall, lall, eo, ri, cb, ab, xb, ob,
                  lsem, xss, xrs, gss, grs, ess, ers, rss, rrs, wss, wrs, wls, css, crs, ass, ars, osem, free):
    dp = lax.axis_size("dp")
    f32, bf = jnp.float32, jnp.bfloat16
    s, x, c, xdev, cdev = seq_places(2)
    g = lax.axis_index("dp")
    def peer(k): return (s, g ^ k)
    greet([xdev, cdev] + [peer(k) for k in range(1, dp)])
    rows_w, ff = wgi.shape; width = xs.shape[2]
    piece = rows_w // wcut
    wx, wc, wl = [], [], []
    shared = ((wgi, 1), (wui, 2)) if whole_down else ((wgi, 1), (wui, 2), (wdi, 0))
    parts = [(src, m, h * piece) for h in range(wcut) for src, m in shared]
    for n, (src, m, r0) in enumerate(parts):
        a = src.at[pl.ds(r0, piece)]
        b = wall.at[m, x, c, pl.ds(r0, piece)]
        wx.append(remote(a, b, wss.at[n, 0], wrs.at[n, 0], xdev))
        wc.append(remote(a, b, wss.at[n, 1], wrs.at[n, 1], cdev))
        cp = pltpu.make_async_copy(a, b, wls.at[n]); cp.start(); wl.append(cp)
    if whole_down:
        cp = pltpu.make_async_copy(wdi, wall.at[0], wls.at[len(parts)]); cp.start(); wl.append(cp)
    sx, sg = {}, {}
    for k in [k for p in order for k in range(p * per, (p + 1) * per)]:
        at = pl.ds(k * cap, cap)
        if k == 0:
            sx[0] = pltpu.make_async_copy(xs.at[g], xr.at[at], lsem.at[0]); sx[0].start()
            sg[0] = pltpu.make_async_copy(gs.at[g], gr.at[at], lsem.at[1]); sg[0].start()
        else:
            sx[k] = remote(xs.at[g ^ k], xr.at[at], xss.at[k], xrs.at[k], peer(k))
            sg[k] = remote(gs.at[g ^ k], gr.at[at], gss.at[k], grs.at[k], peer(k))
    wf = []
    for n, (src, m, r0) in enumerate(parts):
        wx[n].wait_recv()
        b = wall.at[m, 1 - x, c, pl.ds(r0, piece)]
        wf.append(remote(b, b, wss.at[n, 2], wrs.at[n, 2], cdev))
    for cp in wl: cp.wait()
    for n in range(len(parts)):
        wc[n].wait_recv(); wf[n].wait_recv()
    ntile = ff // tile
    re, rr = {}, {}
    wide = 4 * rows_w
    for p in todo:
        ks = list(range(p * per, (p + 1) * per))
        for k in ks:
            if k == 0: sx[0].wait(); sg[0].wait()
            else: sx[k].wait_recv(); sg[k].wait_recv()
        rows = pl.ds(p * per * cap, per * cap)
        @pl.loop(0, ntile)
        def _(t):
            cols = pl.ds(pl.multiple_of(t * tile, 128), tile)
            w = lambda m: wall[m, :, :, :, cols].reshape(wide, tile)
            gp = jnp.dot(xr[rows, :], w(1), preferred_element_type=f32)
            up = jnp.dot(xr[rows, :], w(2), preferred_element_type=f32)
            hg = jnp.dot(gr[rows, :], w(0), preferred_element_type=f32)
            act, der = gelu_parts(gp)
            hall[0, rows, cols] = (act * up).astype(bf)
            hall[1, rows, cols] = (hg * up * der).astype(bf)
            hall[2, rows, cols] = (hg * act).astype(bf)
        @pl.loop(0, 4)
        def _(t):
            part = pl.ds(pl.multiple_of(t * rows_w, 128), rows_w)
            tx, tc = t // 2, lax.rem(t, 2)
            eo[:, part] = dot(hall[0, rows, :], wall[0, tx, tc], 1, 1).astype(bf)
            ri[:, part] = (dot(hall[1, rows, :], wall[1, tx, tc], 1, 1) + dot(hall[2, rows, :], wall[2, tx, tc], 1, 1)).astype(bf)
        keep = [pltpu.make_async_copy(eo, eo_h.at[rows], lsem.at[4]), pltpu.make_async_copy(ri, ri_h.at[rows], lsem.at[5])]
        for cp in keep: cp.start()
        for cp in keep: cp.wait()
        for k in ks:
            at = pl.ds(k * cap, cap)
            if k == 0:
                re[0] = pltpu.make_async_copy(eo_h.at[at], eo_out.at[g], lsem.at[2]); re[0].start()
                rr[0] = pltpu.make_async_copy(ri_h.at[at], ri_out.at[g], lsem.at[3]); rr[0].start()
            else:
                re[k] = remote(eo_h.at[at], eo_out.at[g], ess.at[k], ers.at[k], peer(k))
                rr[k] = remote(ri_h.at[at], ri_out.at[g], rss.at[k], rrs.at[k], peer(k))
    for n in range(len(parts)):
        wx[n].wait_send(); wc[n].wait_send(); wf[n].wait_send()
    total = dp * cap
    @pl.loop(0, total // 256)
    def _(t):
        at = pl.ds(pl.multiple_of(t * 256, 256), 256)
        lall[1, :, at] = xr[at, :].T
        lall[0, :, at] = gr[at, :].T
    nt = 3 * ntile
    def place(n):
        m = n // ntile
        return m, pl.ds(pl.multiple_of((n - m * ntile) * tile, 128), tile)
    def to_core(n):
        m, cols = place(n); r = lax.rem(n, RING)
        return pltpu.make_async_remote_copy(src_ref=wall.at[m, :, 1 - c, :, cols], dst_ref=cb.at[r], send_sem=css.at[r],
            recv_sem=crs.at[r], device_id=cdev, device_id_type=MESH)
    def to_chip(n):
        r = lax.rem(n, RING)
        return pltpu.make_async_remote_copy(src_ref=ab.at[r], dst_ref=xb.at[r], send_sem=ass.at[r],
            recv_sem=ars.at[r], device_id=xdev, device_id_type=MESH)
    def to_out(n):
        m, cols = place(n); r = lax.rem(n, 2)
        return pltpu.make_async_copy(ob.at[r], grads.at[m, :, cols], osem.at[r])
    @pl.loop(0, nt + LAG)
    def _(n):
        @pl.when(n < nt)
        def _():
            m, cols = place(n)
            res = jnp.dot(lall[jnp.minimum(m, 1)], hall[m, :, cols], preferred_element_type=f32)
            wall[m, :, :, :, cols] = res.astype(bf).reshape(2, 2, rows_w, tile)
            @pl.when(n >= RING)
            def _(): pl.semaphore_wait(free.at[0], 1)
            to_core(n).start()
        @pl.when((n >= 1) & (n <= nt))
        def _():
            i = n - 1
            m, cols = place(i); r = lax.rem(i, RING)
            to_core(i).wait_recv()
            @pl.when(i >= RING)
            def _():
                to_chip(i).wait_send()
                pl.semaphore_wait(free.at[1], 1)
            ab[r] = (wall[m, 1 - x, c, :, cols].astype(f32) + cb[r, 1 - x].astype(f32)).astype(bf)
            to_chip(i).start()
        @pl.when(n >= LAG)
        def _():
            j = n - LAG
            m, cols = place(j); r = lax.rem(j, RING)
            to_chip(j).wait_recv()
            to_core(j).wait_send()
            @pl.when(j >= 2)
            def _(): to_out(j).wait()
            ob[lax.rem(j, 2)] = wall[m, x, c, :, cols].astype(f32) + cb[r, x].astype(f32) + xb[r].astype(f32)
            to_out(j).start()
            @pl.when(j < nt - RING)
            def _():
                pl.semaphore_signal(free.at[0], inc=1, device_id=cdev, device_id_type=MESH)
                pl.semaphore_signal(free.at[1], inc=1, device_id=xdev, device_id_type=MESH)
    for j in range(nt - 2, nt): to_out(j).wait()
    for i in range(nt - RING, nt): to_chip(i).wait_send()
    for k in range(dp):
        if k == 0:
            re[0].wait(); rr[0].wait()
        else:
            sx[k].wait_send(); sg[k].wait_send(); re[k].wait(); rr[k].wait()
def expert_all(xs, gs, wg, wu, wd, seq, cid):
    dp, cap, width = xs.shape
    rows_w, ff = wg.shape; total = dp * cap
    whole_down = wd.shape[0] != rows_w
    if whole_down: wd = wd.reshape(seq // 2, 2, rows_w, ff)
    group = 320
    per = group // cap
    ng = dp // per
    order = [p for p in range(ng // 2, ng)] + [p for p in range(ng // 2 - 1, -1, -1)]
    todo = list(range(ng))
    sem = pltpu.SemaphoreType.DMA
    bf = jnp.bfloat16
    any_ = pl.BlockSpec(memory_space=pl.ANY)
    V = pltpu.VMEM
    tile = 256
    wcut = 2
    back = jax.ShapeDtypeStruct((dp, cap, width), bf)
    flat = jax.ShapeDtypeStruct((total, width), bf)
    return pl.pallas_call(functools.partial(expert_kernel, cap, per, order, todo, wcut, tile, whole_down),
        out_shape=[back, back, jax.ShapeDtypeStruct((3, rows_w, ff), jnp.float32), flat, flat],
        in_specs=[any_] * 5, out_specs=[any_] * 5,
        scratch_shapes=[V((3, seq // 2, 2, rows_w, ff), bf), V((total, width), bf), V((total, width), bf), V((3, total, ff), bf),
        V((2, width, total), bf), V((group, width), bf), V((group, width), bf),
        V((RING, seq // 2, rows_w, tile), bf), V((RING, rows_w, tile), bf), V((RING, rows_w, tile), bf), V((2, rows_w, tile), jnp.float32)]
        + [sem((6,))] + [sem((dp,))] * 8 + [sem((3 * wcut, 3))] * 2 + [sem((3 * wcut + 1,))] + [sem((RING,))] * 4 + [sem((2,)), pltpu.SemaphoreType.REGULAR((2,))],
        compiler_params=pltpu.CompilerParams(collective_id=cid, has_side_effects=True, vmem_limit_bytes=63 * 2**20))(xs, gs, wg, wu, wd)[:3]


def head_kernel(nl, ns, lx, sx, gain, wq, wk, wv, q, k, v, kl, vl, n1, lsem, ss, rs):
    f32, bf = jnp.float32, jnp.bfloat16
    s, x, c, xdev, cdev = seq_places(2)
    far = (1 - x) * 2 + c
    greet([xdev, cdev])
    half = nl * 128
    def norm(t):
        m = rows_of(lx, sx, t, nl, ns).astype(f32)
        n1[pl.ds(t * half, half), :] = (m * rms_scale(m) * gain[...]).astype(bf)
    def project(out, w, r0, nr):
        out[pl.ds(r0, nr), :] = jnp.dot(n1[pl.ds(r0, nr), :], w[...], preferred_element_type=f32).astype(bf)
    norm(0)
    local, a, b, f = [], [], [], []
    for m, (out, w, whole) in enumerate(((k, wk, kl), (v, wv, vl))):
        project(out, w, 0, half)
        for i in range(nl):
            n = m * nl + i
            src = out.at[pl.ds(i * 128, 128)]
            a.append(remote(src, whole.at[s, i], ss.at[n, 0], rs.at[n, 0], xdev))
            b.append(remote(src, whole.at[s, i], ss.at[n, 1], rs.at[n, 1], cdev))
            cp = pltpu.make_async_copy(src, whole.at[s, i], lsem.at[n]); cp.start(); local.append(cp)
    norm(1)
    project(k, wk, half, ns * 128)
    project(v, wv, half, ns * 128)
    project(q, wq, 0, half)
    project(q, wq, half, ns * 128)
    for m, whole in enumerate((kl, vl)):
        for i in range(nl):
            n = m * nl + i
            a[n].wait_recv()
            f.append(remote(whole.at[far, i], whole.at[far, i], ss.at[n, 2], rs.at[n, 2], cdev))
    for n in range(2 * nl):
        local[n].wait(); a[n].wait_send(); b[n].wait(); f[n].wait()
def head(nl, ns, seq, arrays, cid):
    tokens, width = (nl + ns) * 128, arrays[3].shape[1]
    S, sem, bf = jax.ShapeDtypeStruct, pltpu.SemaphoreType.DMA, jnp.bfloat16
    vm = pl.BlockSpec(memory_space=pltpu.VMEM)
    rows, long = S((tokens, width), bf), S((seq, nl, 128, width), bf)
    return pl.pallas_call(functools.partial(head_kernel, nl, ns), out_shape=[rows] * 3 + [long] * 2,
        in_specs=[vm] * 6, out_specs=[vm] * 5,
        scratch_shapes=[pltpu.VMEM((tokens, width), bf), sem((2 * nl,)), sem((2 * nl, 3)), sem((2 * nl, 3))],
        compiler_params=pltpu.CompilerParams(collective_id=cid, has_side_effects=True, vmem_limit_bytes=48 * 2**20))(*arrays)
def tail_kernel(dims, nl, ns, pieces, dq, dks, dvs, dkl, dvl, wog, lx, sx, gain, wq, wk, wv, midg, small_in,
                grad_in, og, qg, kg, vg, small, *refs):
    X, C, Z, Y = dims
    f32, bf = jnp.float32, jnp.bfloat16
    np_ = len(pieces)
    bufs = refs[:7 * np_]
    (gw, ka, va, n1, n1t, kcb, ka1, kb1, sacc, sbuf, cs, cr, hs, hr, zs, zr, kss, krs, sss, srs) = refs[7 * np_:]
    s = lax.axis_index("seq"); g = lax.axis_index("dp")
    x, c = s // C, lax.rem(s, C)
    z, y = g // Y, lax.rem(g, Y)
    def zdev(k): return (s, lax.rem(z + k, Z) * Y + y)
    ydev = (s, z * Y + (1 - y)); xdev = ((1 - x) * C + c, g); cdev = (x * C + 1 - c, g)
    greet([zdev(k) for k in range(1, Z)] + [ydev, xdev, cdev])
    half = nl * 128
    sources = [wog] + [gw.at[i] for i in range(3)]
    outs = [og, qg, kg, vg]
    first = {}; hh = {}; zz = {}
    def add(dst, a, b):
        dst[...] = (a.astype(f32) + b.astype(f32)).astype(dst.dtype)
    def send_core(i):
        m, r0, nr, route = pieces[i]
        first[i] = remote(sources[m].at[:, 1 - c, :, :, pl.ds(r0, nr)], bufs[7 * i], cs.at[i], cr.at[i], cdev)
    def stage(i, which):
        m, r0, nr, route = pieces[i]
        cb, a1, b1, a2, b2, a3, b3 = bufs[7 * i:7 * i + 7]
        if which == 0:
            first[i].wait_recv()
            add(a1, sources[m][:, c, :, :, pl.ds(r0, nr)], cb[...])
            src = a1.at[:, :, 1 - y] if route == 0 else a1.at[1 - x]
            hh[i, 0] = remote(src, b1, hs.at[i, 0], hr.at[i, 0], ydev if route == 0 else xdev)
        elif which == 1:
            hh[i, 0].wait_recv()
            add(a2, a1[:, :, y] if route == 0 else a1[x], b1[...])
            src = a2.at[1 - x] if route == 0 else a2.at[:, 1 - y]
            hh[i, 1] = remote(src, b2, hs.at[i, 1], hr.at[i, 1], xdev if route == 0 else ydev)
        elif which == 2:
            hh[i, 1].wait_recv()
            add(a3, a2[x] if route == 0 else a2[:, y], b2[...])
            zz[i] = [remote(a3.at[lax.rem(z + k, Z)], b3.at[k - 1], zs.at[i, k], zr.at[i, k], zdev(k)) for k in range(1, Z)]
        else:
            tot = a3[z].astype(f32)
            for k in range(1, Z):
                zz[i][k - 1].wait_recv()
                tot += b3[k - 1].astype(f32)
            outs[m][pl.ds(r0, nr), :] = tot
    mine = {m: [i for i, p in enumerate(pieces) if p[0] == m] for m in range(4)}
    def stages(m, which):
        for i in mine[m]:
            stage(i, which)
    def weight_grad(m, rows):
        quarter = n1t.shape[0] // (X * C)
        for xx in range(X):
            for cc in range(C):
                part = jnp.dot(n1t[pl.ds((xx * C + cc) * quarter, quarter), :], rows[...], preferred_element_type=f32)
                gw[m - 1, xx, cc] = part.astype(bf).reshape(gw.shape[3:])
        for i in mine[m]:
            send_core(i)
    kv = [(m, i) for m in range(2) for i in range(nl)]
    parts = (dkl, dvl)
    kf, kx = {}, {}
    for far in range(2):
        for n, (m, i) in enumerate(kv):
            at = (1 - x if far == 0 else x) * C + 1 - c
            kf[n, far] = remote(parts[m].at[at, i], kcb.at[n, far], kss.at[n, far], krs.at[n, far], cdev)
    for i in mine[0]:
        send_core(i)
    for n, (m, i) in enumerate(kv):
        kf[n, 0].wait_recv()
        add(ka1.at[n], parts[m][(1 - x) * C + c, i], kcb[n, 0])
        kx[n] = remote(ka1.at[n], kb1.at[n], kss.at[n, 2], krs.at[n, 2], xdev)
    for t in range(2):
        m = rows_of(lx, sx, t, nl, ns).astype(f32)
        nn = (m * rms_scale(m) * gain[...]).astype(bf)
        n1t[:, t * half:(t + 1) * half] = nn.T
    ka[pl.ds(half, ns * 128), :] = dks[...]
    va[pl.ds(half, ns * 128), :] = dvs[...]
    weight_grad(1, dq)
    stages(0, 0)
    for n, (m, i) in enumerate(kv):
        kf[n, 1].wait_recv(); kx[n].wait_recv()
        (ka, va)[m][pl.ds(i * 128, 128), :] = (parts[m][s, i].astype(f32) + kcb[n, 1].astype(f32) + kb1[n].astype(f32)).astype(bf)
    weight_grad(2, ka)
    stages(1, 0); stages(0, 1)
    weight_grad(3, va)
    stages(2, 0); stages(1, 1); stages(0, 2)
    ag = jnp.zeros((1, dq.shape[1]), f32)
    for t in range(2):
        rows = pl.ds(t * half, half)
        ng = dot(dq[rows, :], wq[...], 1, 1) + dot(ka[rows, :], wk[...], 1, 1) + dot(va[rows, :], wv[...], 1, 1)
        m = rows_of(lx, sx, t, nl, ns).astype(f32)
        r1 = rms_scale(m)
        u = m * r1
        ag += jnp.sum(ng * u, axis=0, keepdims=True)
        w = ng * gain[...]
        grad_in[rows, :] = midg[rows, :] + r1 * (w - u * jnp.mean(w * u, axis=-1, keepdims=True))
        if t == 0:
            stages(3, 0); stages(2, 1); stages(1, 2)
    is_gain = lax.broadcasted_iota(jnp.int32, small_in.shape, 0) == 0
    sacc[0] = jnp.where(is_gain, ag, small_in[...])
    sc = remote(sacc.at[0], sbuf.at[0], sss.at[0], srs.at[0], cdev)
    stages(0, 3); stages(3, 1); stages(2, 2)
    sc.wait_recv()
    sacc[1] = sacc[0] + sbuf[0]
    sx_ = remote(sacc.at[1], sbuf.at[1], sss.at[1], srs.at[1], xdev)
    stages(1, 3); stages(3, 2)
    sx_.wait_recv()
    sacc[2] = sacc[1] + sbuf[1]
    sy = remote(sacc.at[2], sbuf.at[2], sss.at[2], srs.at[2], ydev)
    stages(2, 3)
    sy.wait_recv()
    sacc[3] = sacc[2] + sbuf[2]
    sz = [remote(sacc.at[3], sbuf.at[2 + k], sss.at[2 + k], srs.at[2 + k], zdev(k)) for k in range(1, Z)]
    stages(3, 3)
    tot = sacc[3]
    for k in range(1, Z):
        sz[k - 1].wait_recv()
        tot += sbuf[2 + k]
    small[...] = tot
    for cp in [sc, sx_, sy] + sz + list(kx.values()) + list(kf.values()) + list(first.values()) + list(hh.values()) + [q for v in zz.values() for q in v]:
        cp.wait_send()
def tail(dims, nl, ns, pieces, arrays, cid):
    X, C, Z, Y = dims
    dq, wog, small_in = arrays[0], arrays[5], arrays[-1]
    tokens, width = dq.shape
    q = len(pieces)
    nr_all = width // (X * C * Z * Y)
    S, sem, bf, f32 = jax.ShapeDtypeStruct, pltpu.SemaphoreType.DMA, jnp.bfloat16, jnp.float32
    scr = []
    for m, r0, nr, route in pieces:
        h1 = (X, Z) if route == 0 else (Z, Y)
        for lead in ((X, Z, Y), (X, Z, Y), h1, h1, (Z,), (Z,), (Z - 1,)):
            scr.append(pltpu.VMEM(lead + (nr, width), bf))
    V = pltpu.VMEM
    kvn = 2 * nl
    scr += [V((3, X, C, Z, Y, nr_all, width), bf), V((tokens, width), bf), V((tokens, width), bf), V((8, 128), bf), V((width, tokens), bf),
            V((kvn, 2, 128, width), bf), V((kvn, 128, width), bf), V((kvn, 128, width), bf), V((4,) + small_in.shape, f32), V((Z + 2,) + small_in.shape, f32),
            sem((q,)), sem((q,)), sem((q, 2)), sem((q, 2)), sem((q, Z)), sem((q, Z)), sem((kvn, 3)), sem((kvn, 3)), sem((Z + 2,)), sem((Z + 2,))]
    vm = pl.BlockSpec(memory_space=pltpu.VMEM)
    part = S((nr_all, width), f32)
    outs = [S((tokens, width), f32)] + [part] * 4 + [S(small_in.shape, f32)]
    return pl.pallas_call(functools.partial(tail_kernel, dims, nl, ns, pieces), out_shape=outs,
        in_specs=[vm] * len(arrays), out_specs=[vm] * len(outs), scratch_shapes=scr,
        compiler_params=pltpu.CompilerParams(collective_id=cid, has_side_effects=True, vmem_limit_bytes=62 * 2**20))(*arrays)


def on_device(
    long_tokens,
    short_tokens,
    long_grad_out,
    short_grad_out,
    query_weight,
    key_weight,
    value_weight,
    output_weight,
    attn_gain,
    ffn_gain,
    rel_table,
    router_weight,
    gate_weight,
    up_weight,
    down_weight,
    long_positions,
    short_positions,
    long_lengths,
    short_lengths,
    long_routes,
    short_routes,
):
    long_items, quarter, model_width = long_tokens.shape
    short_items, short_len = (short_tokens.shape[0], short_tokens.shape[1])
    long_rows = long_items * quarter
    tokens = long_rows + short_items * short_len
    local_experts = gate_weight.shape[0]
    dp_size = lax.axis_size("dp")
    experts = local_experts * dp_size
    capacity = (5 * tokens + 2 * experts - 1) // (2 * experts)
    seq_size = lax.axis_size("seq")
    dims = (seq_size // 2, 2, dp_size // 2, 2)
    devices = seq_size * dp_size
    table_part, router_part = rel_table.shape[0], router_weight.size
    gain_part = attn_gain.shape[0]
    small_size = 2 * gain_part + table_part + router_part
    small = jnp.concatenate([attn_gain, ffn_gain, rel_table, router_weight.reshape(-1)])
    small = jnp.pad(small, (0, -small_size % 2048)).reshape(-1, 128)
    rows_part = query_weight.shape[0]
    cuts = 2 if rows_part % 32 == 0 else 1
    cut = rows_part // cuts
    pieces = tuple((m, h * cut, cut, (m + h) % 2) for m in range(4) for h in range(cuts))
    gathered = gather_all(
        (query_weight, key_weight, value_weight, output_weight, small),
        pieces[: 3 * cuts] + ((4, 0, small.shape[0], 0),) + pieces[3 * cuts :],
        dims,
        0,
    )
    small_all = gathered[4].reshape(devices, -1)
    attn_set = tuple(block.reshape(devices * rows_part, model_width) for block in gathered[:4]) + (
        small_all[:, :gain_part].reshape(-1),
        small_all[:, gain_part : 2 * gain_part].reshape(-1),
        small_all[:, 2 * gain_part : 2 * gain_part + table_part].reshape(-1),
        small_all[:, 2 * gain_part + table_part : small_size].reshape(model_width, experts),
    )
    gain_first = attn_set[4].astype(jnp.float32).reshape(1, model_width)
    queries, keys, values, long_keys, long_values = head(
        long_items,
        short_items,
        seq_size,
        (long_tokens, short_tokens, gain_first) + attn_set[:3],
        1,
    )
    table = attn_set[6].reshape(HEADS, 1, BUCKETS).astype(jnp.float32)
    table = jnp.pad(table, ((0, 0), (0, 0), (0, 128 - BUCKETS)), constant_values=masked)
    routes = jnp.concatenate([long_routes.reshape(-1, 2), short_routes.reshape(-1, 2)], 0)
    router_t = jnp.pad(attn_set[7].T, ((0, 128 - experts), (0, 0)))
    gain_second = attn_set[5].astype(jnp.float32).reshape(1, model_width)
    sizes = (long_items, short_items, seq_size, experts, capacity)
    attn_args = (
        long_lengths,
        short_lengths,
        queries,
        keys,
        values,
        long_keys,
        long_values,
        table,
        long_positions.reshape(long_items, seq_size, quarter, 1),
        long_positions.reshape(long_items, seq_size, 1, quarter),
        short_positions.reshape(short_items, 1, short_len, 1),
        short_positions.reshape(short_items, 1, 1, short_len),
    )
    tail_args = (long_grad_out, short_grad_out, attn_set[3], gain_second, router_t)
    mixed_all, resid_mid, outgoing, out_slots, logits = attention(
        False,
        *sizes,
        attn_args + (long_tokens, short_tokens) + tail_args + (routes.T,),
        tokens,
        model_width,
    )
    later_down, unused_keys = lax.optimization_barrier((down_weight[0], long_keys))
    down_full = lax.all_gather(later_down, "seq", axis=0, tiled=True)
    back_rows, returned_grad, expert_grads = expert_all(
        outgoing, out_slots, gate_weight[0], up_weight[0], down_full, seq_size, 4
    )
    (
        query_act,
        short_key,
        short_value,
        long_key,
        long_value,
        table_sums,
        final_low,
        middle_grad,
        output_local,
        ffn_gain_local,
        router_local,
    ) = attention(
        True,
        *sizes,
        attn_args
        + (back_rows, returned_grad, resid_mid, mixed_all, logits, routes)
        + tail_args,
        tokens,
        model_width,
    )
    long_out = final_low[:long_rows].reshape(long_items, quarter, model_width)
    short_out = final_low[long_rows:].reshape(short_items, short_len, model_width)
    down_grad, gate_grad, up_grad = (expert_grads[m : m + 1] for m in range(3))
    upto = table_sums.reshape(HEADS, 128)[:, : len(ORDER)]
    within = upto - jnp.pad(upto[:, :-1], ((0, 0), (1, 0)))
    table_local = jnp.stack(
        [
            within[:, ORDER.index(n)] if n in ORDER else jnp.zeros(HEADS, jnp.float32)
            for n in range(BUCKETS)
        ],
        1,
    ).reshape(1, -1)
    small_local = jnp.concatenate(
        [
            jnp.pad(ffn_gain_local, ((1, 0), (0, 0))),
            jnp.pad(table_local, ((0, 0), (0, model_width - table_local.shape[1]))),
            router_local,
        ],
        0,
    )
    small_local = jnp.pad(small_local, ((0, -small_local.shape[0] % 8), (0, 0)))
    whole = dims + (rows_part, model_width)
    grad_in, output_grad, query_grad, key_grad, value_grad, small_sum = tail(
        dims,
        long_items,
        short_items,
        pieces,
        (query_act, short_key, short_value, long_key, long_value, output_local.reshape(whole))
        + (long_tokens, short_tokens, gain_first)
        + attn_set[:3]
        + (middle_grad, small_local),
        2,
    )
    long_grad_in = grad_in[:long_rows].reshape(long_items, quarter, model_width)
    short_grad_in = grad_in[long_rows:].reshape(short_items, short_len, model_width)
    place = lax.axis_index("seq") * dp_size + lax.axis_index("dp")

    def own(row, count, size):
        return lax.dynamic_slice(small_sum, (row, place * size), (count, size))

    summed = (
        query_grad,
        key_grad,
        value_grad,
        output_grad,
        own(0, 1, gain_part)[0],
        own(1, 1, gain_part)[0],
        own(2, 1, table_part)[0],
        own(3, experts, rows_part).T,
    )
    return (
        long_out,
        short_out,
        long_grad_in,
        short_grad_in,
        summed[0],
        summed[1],
        summed[2],
        summed[3],
        summed[4],
        summed[5],
        summed[6],
        summed[7],
        gate_grad,
        up_grad,
        down_grad,
    )


def solution(mesh):
    placed = (
        P("dp", "seq", None),
        P(("seq", "dp"), None, None),
        P("dp", "seq", None),
        P(("seq", "dp"), None, None),
        P(("seq", "dp"), None),
        P(("seq", "dp"), None),
        P(("seq", "dp"), None),
        P(("seq", "dp"), None),
        P(("seq", "dp")),
        P(("seq", "dp")),
        P(("seq", "dp")),
        P(("seq", "dp"), None),
        P("dp", "seq", None),
        P("dp", "seq", None),
        P("dp", "seq", None),
        P("dp", None),
        P(("seq", "dp"), None),
        P("dp"),
        P(("seq", "dp")),
        P("dp", "seq", None),
        P(("seq", "dp"), None, None),
    )
    return jax.shard_map(
        on_device,
        mesh=mesh,
        in_specs=placed,
        out_specs=(
            P("dp", "seq", None),
            P(("seq", "dp"), None, None),
            P("dp", "seq", None),
            P(("seq", "dp"), None, None),
            P(("seq", "dp"), None),
            P(("seq", "dp"), None),
            P(("seq", "dp"), None),
            P(("seq", "dp"), None),
            P(("seq", "dp")),
            P(("seq", "dp")),
            P(("seq", "dp")),
            P(("seq", "dp"), None),
            P("dp", "seq", None),
            P("dp", "seq", None),
            P("dp", "seq", None),
        ),
        check_vma=False,
    )
```

```python
import functools

import jax
import jax.numpy as jnp
from jax import lax
from jax.experimental import pallas as pl
from jax.experimental.pallas import tpu as pltpu
from jax.sharding import PartitionSpec as P

MESH = pl.DeviceIdType.MESH

HEADS = 16
HEAD = 64
BUCKETS = 32


epsilon = 1e-06
masked = -1e30


def gather_kernel(dims, pieces, na, *refs):
    X, C, Z, Y = dims
    n = len(pieces)
    lsem, zs, zr, hs, hr, cs, cr = refs[2*na:]
    routes = [p[3] for p in pieces]
    ins = [refs[m].at[pl.ds(r0, nr)] for m, r0, nr, _ in pieces]
    class V:
        def __init__(self, ref, r0, nr): self.ref, self.r0, self.nr = ref, r0, nr
        @property
        def at(self): return self
        def __getitem__(self, k):
            k = k + (slice(None),) * (4 - len(k)) + (pl.ds(self.r0, self.nr),)
            return self.ref.at[k]
    outs = [V(refs[na + m], r0, nr) for m, r0, nr, _ in pieces]
    s = lax.axis_index("seq"); g = lax.axis_index("dp")
    x, c = s // C, lax.rem(s, C)
    z, y = g // Y, lax.rem(g, Y)
    def zdev(k): return (s, lax.rem(z + k, Z) * Y + y)
    ydev = (s, z * Y + (1 - y)); xdev = ((1 - x) * C + c, g); cdev = (x * C + 1 - c, g)
    bar = pltpu.get_barrier_semaphore()
    for d in [zdev(k) for k in range(1, Z)] + [ydev, xdev, cdev]:
        pl.semaphore_signal(bar, inc=1, device_id=d, device_id_type=MESH)
    pl.semaphore_wait(bar, Z + 2)
    def rc(src, dst, ss, rs, dev):
        cp = pltpu.make_async_remote_copy(src_ref=src, dst_ref=dst, send_sem=ss, recv_sem=rs, device_id=dev, device_id_type=MESH)
        cp.start(); return cp
    sends = []
    local = []; zc = []
    for m in range(n):
        lc = pltpu.make_async_copy(ins[m], outs[m].at[x, c, z, y], lsem.at[m]); lc.start(); local.append(lc)
        zc.append([rc(ins[m], outs[m].at[x, c, z, y], zs.at[m, k], zr.at[m, k], zdev(k)) for k in range(1, Z)])
    h = [[None, None] for _ in range(n)]
    cc = [[None]*3 for _ in range(n)]
    for t in range(n + 2):
        for stage in range(3):
            m = t - stage
            if not 0 <= m < n: continue
            o = outs[m]; route = routes[m]
            if stage == 0:
                local[m].wait()
                for q in zc[m]: q.wait_recv()
                mine = o.at[x, c, :, y]
                h[m][0] = rc(mine, mine, hs.at[m,0], hr.at[m,0], xdev if route == 0 else ydev)
                cc[m][0] = rc(mine, mine, cs.at[m,0], cr.at[m,0], cdev)
            elif stage == 1:
                h[m][0].wait_recv()
                if route == 0:
                    both = o.at[:, c, :, y]; got = o.at[1 - x, c, :, y]
                else:
                    both = o.at[x, c]; got = o.at[x, c, :, 1 - y]
                h[m][1] = rc(both, both, hs.at[m,1], hr.at[m,1], ydev if route == 0 else xdev)
                cc[m][1] = rc(got, got, cs.at[m,1], cr.at[m,1], cdev)
            else:
                h[m][1].wait_recv()
                got = o.at[:, c, :, 1 - y] if route == 0 else o.at[1 - x, c]
                cc[m][2] = rc(got, got, cs.at[m,2], cr.at[m,2], cdev)
    for m in range(n):
        for q in zc[m]: q.wait_send()
        for q in h[m]: q.wait_send()
        for q in cc[m]: q.wait()
def gather_all(arrays, pieces, dims, cid):
    X, C, Z, Y = dims; na = len(arrays); n = len(pieces)
    sem = pltpu.SemaphoreType.DMA
    return pl.pallas_call(functools.partial(gather_kernel, dims, pieces, na),
        out_shape=[jax.ShapeDtypeStruct((X, C, Z, Y) + a.shape, a.dtype) for a in arrays],
        in_specs=[pl.BlockSpec(memory_space=pl.ANY)] * na, out_specs=[pl.BlockSpec(memory_space=pl.ANY)] * na,
        scratch_shapes=[sem((n,)), sem((n, Z)), sem((n, Z)), sem((n, 2)), sem((n, 2)), sem((n, 3)), sem((n, 3))],
        compiler_params=pltpu.CompilerParams(collective_id=cid, has_side_effects=True))(*arrays)


def seq_places(C):
    s = lax.axis_index("seq"); g = lax.axis_index("dp")
    x, c = s // C, lax.rem(s, C)
    return s, x, c, ((1 - x) * C + c, g), (x * C + 1 - c, g)
def greet(devs):
    bar = pltpu.get_barrier_semaphore()
    for d in devs:
        pl.semaphore_signal(bar, inc=1, device_id=d, device_id_type=MESH)
    pl.semaphore_wait(bar, len(devs))
def remote(src, dst, ss, rs, dev):
    cp = pltpu.make_async_remote_copy(src_ref=src, dst_ref=dst, send_sem=ss, recv_sem=rs, device_id=dev, device_id_type=MESH)
    cp.start()
    return cp
EDGES = (-90, -63, -45, -31, -22, -15, -11, -7, -6, -5, -4, -3, -2, -1, 0, 1, 2, 3, 4, 5, 6, 7, 8, 12, 16, 23, 32, 46, 64, 91)
FAR = (12, 16, 23, 32, 46, 64, 91)
def fill_buckets(out, q_col, k_row, length, base):
    r = k_row - q_col
    n = jnp.abs(r)
    far = jnp.full(r.shape, 8, jnp.int32)
    for e in FAR:
        far += (n >= e).astype(jnp.int32)
    b = jnp.where(n < 8, n, far) + jnp.where(r > 0, 16, 0)
    j = lax.broadcasted_iota(jnp.int32, r.shape, 1) + base
    out[...] = jnp.where(j < length, b, 32)
def dot(a, b, ca, cb):
    return lax.dot_general(a, b, (((ca,), (cb,)), ((), ())), preferred_element_type=jnp.float32)
def probs_of(qs, kk, tabs, bucket_ref, blocks):
    s = dot(qs, kk, 1, 1)
    t = [jnp.broadcast_to(tab, (128, 128)) for tab in tabs]
    bias = [jnp.concatenate([jnp.take_along_axis(x, bucket_ref[c], axis=1) for x in t], axis=0) for c in range(blocks)]
    s = s + (jnp.concatenate(bias, axis=1) if blocks > 1 else bias[0])
    p = jnp.exp(s - jnp.max(s, axis=1, keepdims=True))
    return p * (1.0 / jnp.sum(p, axis=1, keepdims=True))
def stack_heads(rows, first):
    return jnp.concatenate([jnp.where(first, rows, 0), jnp.where(first, 0, rows)], axis=0)
def column_of(row):
    i = lax.broadcasted_iota(jnp.int32, (128, 128), 0)
    return jnp.sum(jnp.where(i == lax.broadcasted_iota(jnp.int32, (128, 128), 1), row, 0), axis=1, keepdims=True)
def row_of(col):
    i = lax.broadcasted_iota(jnp.int32, (128, 128), 0)
    return jnp.sum(jnp.where(i == lax.broadcasted_iota(jnp.int32, (128, 128), 1), col, 0), axis=0, keepdims=True)
def rows_of(long_ref, short_ref, t):
    ref = long_ref if t == 0 else short_ref
    return ref[...].reshape(ref.shape[0] * ref.shape[1], ref.shape[2])
def rms_scale(mid):
    return lax.rsqrt(jnp.mean(mid * mid, axis=-1, keepdims=True) + epsilon)
def item(b, nl, blocks, cols, k, v, kl, vl):
    rows = pl.ds(b * 128, 128)
    if b < nl:
        return rows, blocks, kl[:, b, :, cols].reshape(blocks * 128, 128), vl[:, b, :, cols].reshape(blocks * 128, 128)
    return rows, 1, k[rows, cols], v[rows, cols]
def mine_of(b, nl, long_ref, short_ref):
    return long_ref.at[b] if b < nl else short_ref.at[b - nl]
def attn_fwd_kernel(nl, ns, blocks, experts, cap, ll, sl, q, k, v, kl, vl, tab, lpos, spos,
                    xl, xsh, gl, gsh, wo, params, lr, sr, mixed, mid, xs, gs, logits, lb, sb, n2, gb):
    me = lax.axis_index("seq")
    for b in range(nl):
        own = column_of(lpos[b:b + 1, pl.ds(pl.multiple_of(me * 128, 128), 128)])
        for c in range(blocks):
            fill_buckets(lb.at[b, c], own, lpos[b:b + 1, c * 128:(c + 1) * 128], ll[b], c * 128)
    for b in range(ns):
        fill_buckets(sb.at[b, 0], column_of(spos[b:b + 1, :]), spos[b:b + 1, :], sl[b], 0)
    first = lax.broadcasted_iota(jnp.int32, (128, 128), 1) < 64
    @pl.loop(0, 8)
    def _(hp):
        cols = pl.ds(pl.multiple_of(hp * 128, 128), 128)
        for b in range(nl + ns):
            rows, n, kk, vv = item(b, nl, blocks, cols, k, v, kl, vl)
            p = probs_of(stack_heads(q[rows, cols], first), kk, (tab[2 * hp], tab[2 * hp + 1]), mine_of(b, nl, lb, sb), n)
            out = dot(p.astype(jnp.bfloat16), vv, 1, 0)
            mixed[rows, cols] = jnp.where(first, out[:128], out[128:]).astype(jnp.bfloat16)
    f32, bf = jnp.float32, jnp.bfloat16
    tokens = q.shape[0]
    gain = params[experts + 1:experts + 2, :].astype(f32)
    for t in range(2):
        rows = pl.ds(t * 256, 256)
        m = rows_of(xl, xsh, t).astype(f32) + jnp.dot(mixed[rows, :], wo[...], preferred_element_type=f32)
        mid[rows, :] = m
        n2[rows, :] = (m * rms_scale(m) * gain).astype(bf)
        gb[rows, :] = rows_of(gl, gsh, t)
    logits[...] = dot(n2[...], params[...], 1, 1)
    logit_t = dot(params[...], n2[...], 1, 1)[:experts]
    routes = [jnp.concatenate([row_of(ref[i, :, j:j + 1]) for ref in (lr, sr) for i in range(ref.shape[0])], axis=1) for j in range(2)]
    e_iota = lax.broadcasted_iota(jnp.int32, (experts, tokens), 0)
    member = ((e_iota == routes[0]) | (e_iota == routes[1])).astype(f32)
    e = jnp.exp(logit_t - jnp.max(logit_t, axis=0, keepdims=True))
    p = e / jnp.sum(e, axis=0, keepdims=True)
    chosen = member * p
    before = (lax.broadcasted_iota(jnp.int32, (tokens, tokens), 0) < lax.broadcasted_iota(jnp.int32, (tokens, tokens), 1)).astype(f32).astype(bf)
    place = jnp.dot(member.astype(bf), before, preferred_element_type=f32)
    kept = (member > 0.5) & (place < cap)
    weight = jnp.where(kept, chosen / jnp.sum(chosen, axis=0, keepdims=True), 0.0)
    slot = jnp.where(kept, place.astype(jnp.int32), -1)
    s_iota = lax.broadcasted_iota(jnp.int32, (cap, tokens), 0)
    for i in range(experts):
        pick = (s_iota == slot[i:i + 1, :]).astype(f32)
        scale = jnp.sum(pick * weight[i:i + 1, :], axis=1, keepdims=True)
        pick = pick.astype(bf)
        xs[i] = jnp.dot(pick, n2[...], preferred_element_type=f32).astype(bf)
        gs[i] = (jnp.dot(pick, gb[...], preferred_element_type=f32) * scale).astype(bf)
def post_kernel(nl, ns, blocks, experts, cap, lpos, spos, eo, ri, mid, mixed, logits, lr, sr, gl, gsh, wo, params, eg,
                lout, sout, midg, wog, small, mg, li, si, eg0, eg1, eg2, bg, n2, lg, fin, bk, sh, ev, sem):
    f32, bf = jnp.float32, jnp.bfloat16
    tokens = mid.shape[0]
    fetch = [pltpu.make_async_copy(eg.at[m], ev.at[m], sem.at[m]) for m in range(3)]
    copies = [pltpu.make_async_copy(ev.at[m], out.at[0], sem.at[m]) for m, out in enumerate((eg0, eg1, eg2))]
    for cp in fetch: cp.start()
    gain = params[experts + 1:experts + 2, :].astype(f32)
    lane = lax.broadcasted_iota(jnp.int32, (tokens, 128), 1)
    routes = jnp.concatenate([ref[i] for ref in (lr, sr) for i in range(ref.shape[0])], axis=0)
    member = ((lane == routes[:, 0:1]) | (lane == routes[:, 1:2])).astype(f32)
    after = (lax.broadcasted_iota(jnp.int32, (tokens, tokens), 1) < lax.broadcasted_iota(jnp.int32, (tokens, tokens), 0)).astype(f32).astype(bf)
    place = jnp.dot(after, member.astype(bf), preferred_element_type=f32)
    kept = (member > 0.5) & (place < cap)
    slot = jnp.where(kept, place.astype(jnp.int32), -1)
    lgt = jnp.where(lane < experts, logits[...], -1e30)
    ex = jnp.exp(lgt - jnp.max(lgt, axis=1, keepdims=True))
    p = ex / jnp.sum(ex, axis=1, keepdims=True)
    chosen = member * p
    both = jnp.sum(chosen, axis=1, keepdims=True)
    gate = chosen / both
    fg = jnp.zeros((1, mid.shape[1]), f32)
    for t in range(2):
        at = slice(t * 256, t * 256 + 256)
        rows = pl.ds(t * 256, 256)
        g = rows_of(gl, gsh, t).astype(f32)
        m = mid[rows, :]
        fin[...] = m
        bk[...] = jnp.zeros_like(m)
        sh[...] = jnp.zeros_like(sh)
        s_iota = lax.broadcasted_iota(jnp.int32, (256, cap), 1)
        slot_t, weight_t, lane_t = slot[at], jnp.where(kept[at], gate[at], 0.0), lane[:256]
        @pl.loop(0, experts)
        def _(i):
            this = lane_t == i
            mine = jnp.sum(jnp.where(this, slot_t, 0), axis=1, keepdims=True)
            weight = jnp.sum(jnp.where(this, weight_t, 0.0), axis=1, keepdims=True)
            pick = (s_iota == mine).astype(f32).astype(bf)
            pair = jnp.dot(pick, eo[i], preferred_element_type=f32)
            fin[...] += weight * pair
            sh[...] = jnp.where(this, jnp.sum(rows_of(gl, gsh, t).astype(f32) * pair, axis=1, keepdims=True), sh[...])
            bk[...] += jnp.dot(pick, ri[i], preferred_element_type=f32)
        (lout, sout)[t][...] = fin[...].astype(bf).reshape(lout.shape)
        share, back = sh[...], bk[...]
        mean = jnp.sum(share * gate[at], axis=1, keepdims=True)
        pg = member[at] * (share - mean) / both[at]
        lgrad = (p[at] * (pg - jnp.sum(p[at] * pg, axis=1, keepdims=True))).astype(bf)
        lg[rows, :] = lgrad
        r2 = rms_scale(m)
        u = m * r2
        n2[rows, :] = (u * gain).astype(bf)
        back += jnp.dot(lgrad, params[...], preferred_element_type=f32)
        fg += jnp.sum(back * u, axis=0, keepdims=True)
        w = back * gain
        out = g + r2 * (w - u * jnp.mean(w * u, axis=-1, keepdims=True))
        midg[rows, :] = out
        bg[rows, :] = out.astype(bf)
        mg[rows, :] = dot(out.astype(bf), wo[...], 1, 1).astype(bf)
    for m in range(3):
        fetch[m].wait()
        copies[m].start()
    small[...] = jnp.zeros_like(small)
    small[1:2, :] = fg
    small[2:2 + experts, :] = dot(lg[...], n2[...], 0, 0)[:experts]
    wog[...] = dot(mixed[...], bg[...], 0, 0).astype(bf).reshape(wog.shape)
    lane = lax.broadcasted_iota(jnp.int32, (128, 128), 1)
    edge = jnp.full((128, 128), 4096, jnp.int32)
    for i, e in enumerate(EDGES):
        edge = jnp.where(lane == i, e, edge)
    edge = jnp.where(lane > len(EDGES), -4096, edge)
    def places(out, q_col, k_row):
        k_first = k_row[:, 0:1]
        t = lax.broadcasted_iota(jnp.int32, (128, 256), 1) + k_first
        below = jnp.sum((column_of(k_row) < t).astype(jnp.int32), axis=0, keepdims=True)
        at = jnp.clip(q_col + edge - k_first, 0, 255)
        lo = jnp.take_along_axis(jnp.broadcast_to(below[:, :128], (128, 128)), at & 127, axis=1)
        hi = jnp.take_along_axis(jnp.broadcast_to(below[:, 128:], (128, 128)), at & 127, axis=1)
        out[...] = jnp.where(at < 128, lo, hi) - 1
    me = lax.axis_index("seq")
    for b in range(nl):
        own = column_of(lpos[b:b + 1, pl.ds(pl.multiple_of(me * 128, 128), 128)])
        for c in range(blocks):
            places(li.at[b, c], own, lpos[b:b + 1, c * 128:(c + 1) * 128])
    for b in range(ns):
        places(si.at[b, 0], column_of(spos[b:b + 1, :]), spos[b:b + 1, :])
    for cp in copies: cp.wait()
def attention(nl, ns, blocks, experts, cap, arrays, tokens, width):
    sm, vm = pl.BlockSpec(memory_space=pltpu.SMEM), pl.BlockSpec(memory_space=pltpu.VMEM)
    S, bf, f32 = jax.ShapeDtypeStruct, jnp.bfloat16, jnp.float32
    slots = S((experts, cap, width), bf)
    outs = [S((tokens, width), bf), S((tokens, width), f32), slots, slots, S((tokens, 128), f32),
            S((nl, blocks, 128, 128), jnp.int32), S((ns, 1, 128, 128), jnp.int32)]
    return pl.pallas_call(functools.partial(attn_fwd_kernel, nl, ns, blocks, experts, cap), out_shape=outs,
        in_specs=[sm, sm] + [vm] * (len(arrays) - 2), out_specs=[vm] * len(outs), scratch_shapes=[pltpu.VMEM((tokens, width), bf)] * 2,
        compiler_params=pltpu.CompilerParams(vmem_limit_bytes=60 * 2**20))(*arrays)
def small_rows(experts):
    return -(-(experts + 4) // 8) * 8
def post(nl, ns, blocks, experts, cap, whole, arrays, tokens, width):
    vm, hbm = pl.BlockSpec(memory_space=pltpu.VMEM), pl.BlockSpec(memory_space=pl.ANY)
    S, bf, f32 = jax.ShapeDtypeStruct, jnp.bfloat16, jnp.float32
    eg = arrays[-1]
    outs = [S((nl, 128, width), bf), S((ns, 128, width), bf), S((tokens, width), f32), S(whole, bf), S((small_rows(experts), width), f32), S((tokens, width), bf),
            S((nl, blocks, 128, 128), jnp.int32), S((ns, 1, 128, 128), jnp.int32)] + [S((1,) + eg.shape[1:], f32)] * 3
    V = pltpu.VMEM
    return pl.pallas_call(functools.partial(post_kernel, nl, ns, blocks, experts, cap), out_shape=outs,
        in_specs=[vm] * (len(arrays) - 1) + [hbm], out_specs=[vm] * (len(outs) - 3) + [hbm] * 3,
        scratch_shapes=[V((tokens, width), bf)] * 2 + [V((tokens, 128), bf)] + [V((256, width), f32)] * 2 + [V((256, 128), f32), V(eg.shape, f32), pltpu.SemaphoreType.DMA((3,))],
        compiler_params=pltpu.CompilerParams(vmem_limit_bytes=60 * 2**20))(*arrays)
def head_kernel(nl, ns, experts, lx, sx, params, wq, wk, wv, q, k, v, kl, vl, n1t, n1, lsem, ss, rs):
    f32, bf = jnp.float32, jnp.bfloat16
    s, x, c, xdev, cdev = seq_places(2)
    far = (1 - x) * 2 + c
    greet([xdev, cdev])
    half = nl * 128
    gain = params[experts:experts + 1, :].astype(f32)
    def norm(t):
        m = rows_of(lx, sx, t).astype(f32)
        n1[pl.ds(t * half, half), :] = (m * rms_scale(m) * gain).astype(bf)
    def project(out, w, r0, nr):
        out[pl.ds(r0, nr), :] = jnp.dot(n1[pl.ds(r0, nr), :], w[...], preferred_element_type=f32).astype(bf)
    norm(0)
    local, a, b, f = [], [], [], []
    for m, (out, w, whole) in enumerate(((k, wk, kl), (v, wv, vl))):
        project(out, w, 0, half)
        for i in range(nl):
            n = m * nl + i
            src = out.at[pl.ds(i * 128, 128)]
            a.append(remote(src, whole.at[s, i], ss.at[n, 0], rs.at[n, 0], xdev))
            b.append(remote(src, whole.at[s, i], ss.at[n, 1], rs.at[n, 1], cdev))
            cp = pltpu.make_async_copy(src, whole.at[s, i], lsem.at[n]); cp.start(); local.append(cp)
    norm(1)
    project(k, wk, half, ns * 128)
    project(v, wv, half, ns * 128)
    project(q, wq, 0, half)
    project(q, wq, half, ns * 128)
    for t in range(2):
        n1t[:, t * half:(t + 1) * half] = n1[pl.ds(t * half, half), :].T
    for m, whole in enumerate((kl, vl)):
        for i in range(nl):
            n = m * nl + i
            a[n].wait_recv()
            f.append(remote(whole.at[far, i], whole.at[far, i], ss.at[n, 2], rs.at[n, 2], cdev))
    for n in range(2 * nl):
        local[n].wait(); a[n].wait_send(); b[n].wait(); f[n].wait()
def head(nl, ns, seq, experts, arrays, cid):
    tokens, width = (nl + ns) * 128, arrays[3].shape[1]
    S, sem, bf = jax.ShapeDtypeStruct, pltpu.SemaphoreType.DMA, jnp.bfloat16
    vm = pl.BlockSpec(memory_space=pltpu.VMEM)
    rows, long = S((tokens, width), bf), S((seq, nl, 128, width), bf)
    return pl.pallas_call(functools.partial(head_kernel, nl, ns, experts), out_shape=[rows] * 3 + [long] * 2 + [S((width, tokens), bf)],
        in_specs=[vm] * 6, out_specs=[vm] * 6,
        scratch_shapes=[pltpu.VMEM((tokens, width), bf), sem((2 * nl,)), sem((2 * nl, 3)), sem((2 * nl, 3))],
        compiler_params=pltpu.CompilerParams(collective_id=cid, has_side_effects=True, vmem_limit_bytes=48 * 2**20))(*arrays)

def back_kernel(dims, nl, ns, experts, pieces, q, k, v, kl, vl, tab, lb, sb, li, si, mg, wog, n1t, lx, sx, params, wq, wk, wv, midg, small_in,
                lgrad, sgrad, og, qg, kg, vg, small, *refs):
    X, C, Z, Y = dims
    blocks = X * C
    f32, bf = jnp.float32, jnp.bfloat16
    np_ = len(pieces)
    bufs = refs[:4 * np_]
    (gw, dq, ka, va, dkl, dvl, kcb, ka1, kb1, seg, sacc, sbuf, cs, cr, hs, hr, zs, zr, kss, krs, sss, srs) = refs[4 * np_:]
    s = lax.axis_index("seq"); g = lax.axis_index("dp")
    x, c = s // C, lax.rem(s, C)
    z, y = g // Y, lax.rem(g, Y)
    def zdev(k): return (s, lax.rem(z + k, Z) * Y + y)
    ydev = (s, z * Y + (1 - y)); xdev = ((1 - x) * C + c, g); cdev = (x * C + 1 - c, g)
    greet([zdev(k) for k in range(1, Z)] + [ydev, xdev, cdev])
    half = nl * 128
    wide = 256
    nb = q.shape[1] // wide
    sources = [wog] + [gw.at[i] for i in range(3)]
    outs = [og, qg, kg, vg]
    first = {}; hh = {}; zz = {}
    def add(dst, a, b):
        dst[...] = (a.astype(f32) + b.astype(f32)).astype(dst.dtype)
    def send_core(i):
        m, c0, nc = pieces[i]
        first[i] = remote(sources[m].at[:, 1 - c, :, :, :, pl.ds(c0, nc)], bufs[4 * i], cs.at[i], cr.at[i], cdev)
    def stage(i, which):
        m, c0, nc = pieces[i]
        b0, b1, b2, b3 = bufs[4 * i:4 * i + 4]
        if which == 0:
            first[i].wait_recv()
            add(b0, sources[m][:, c, :, :, :, c0:c0 + nc], b0[...])
            hh[i, 0] = remote(b0.at[:, :, 1 - y], b1, hs.at[i, 0], hr.at[i, 0], ydev)
        elif which == 1:
            hh[i, 0].wait_recv()
            add(b1, b0[:, :, y], b1[...])
            hh[i, 1] = remote(b1.at[1 - x], b2, hs.at[i, 1], hr.at[i, 1], xdev)
        elif which == 2:
            hh[i, 1].wait_recv()
            add(b2, b1[x], b2[...])
            zz[i] = [remote(b2.at[lax.rem(z + k, Z)], b3.at[k - 1], zs.at[i, k], zr.at[i, k], zdev(k)) for k in range(1, Z)]
        else:
            tot = b2[z].astype(f32)
            for k in range(1, Z):
                zz[i][k - 1].wait_recv()
                tot += b3[k - 1].astype(f32)
            outs[m][:, c0:c0 + nc] = tot
    def piece(m, b):
        return [i for i, p in enumerate(pieces) if p[0] == m and (m == 0 or p[1] == b * wide)]
    def weight_grad(m, rows, b):
        cols = slice(b * wide, (b + 1) * wide)
        quarter = n1t.shape[0] // blocks
        for xx in range(X):
            for cc in range(C):
                part = jnp.dot(n1t[pl.ds((xx * C + cc) * quarter, quarter), :], rows[:, cols], preferred_element_type=f32)
                gw[m - 1, xx, cc, :, :, :, cols] = part.astype(bf).reshape(gw.shape[3:6] + (wide,))
        for i in piece(m, b):
            send_core(i)
    parts, wholes = (dkl, dvl), (ka, va)
    kf, kx = {}, {}
    def kv_core(b):
        cols = pl.ds(b * wide, wide)
        for far in range(2):
            for m in range(2):
                n = b * 2 + m
                at = (1 - x if far == 0 else x) * C + 1 - c
                kf[n, far] = remote(parts[m].at[at, :, :, cols], kcb.at[n, far], kss.at[n, far], krs.at[n, far], cdev)
    def kv_chip(b):
        for m in range(2):
            n = b * 2 + m
            kf[n, 0].wait_recv()
            add(ka1.at[n], parts[m][(1 - x) * C + c, :, :, b * wide:(b + 1) * wide], kcb[n, 0])
            kx[n] = remote(ka1.at[n], kb1.at[n], kss.at[n, 2], krs.at[n, 2], xdev)
    def kv_end(b):
        for m in range(2):
            n = b * 2 + m
            kf[n, 1].wait_recv(); kx[n].wait_recv()
            tot = parts[m][s, :, :, b * wide:(b + 1) * wide].astype(f32) + kcb[n, 1].astype(f32) + kb1[n].astype(f32)
            wholes[m][pl.ds(0, half), b * wide:(b + 1) * wide] = tot.astype(bf).reshape(half, wide)
        weight_grad(2, ka, b)
        weight_grad(3, va, b)
    def stages(which, b, *ms):
        for m in ms:
            for i in piece(m, b):
                stage(i, which)
    seg[...] = jnp.zeros_like(seg)
    lane = lax.broadcasted_iota(jnp.int32, (128, 128), 1)
    head_one = lane < 64
    tri = jnp.where(lax.broadcasted_iota(jnp.int32, (128, 128), 0) <= lane, 1.0, 0.0).astype(bf)
    def attend(b0):
        @pl.loop(0, wide // 128)
        def _(i):
            hp = b0 * (wide // 128) + i
            cols = pl.ds(pl.multiple_of(hp * 128, 128), 128)
            for b in range(nl + ns):
                rows, n, kk, vv = item(b, nl, blocks, cols, k, v, kl, vl)
                idx = mine_of(b, nl, li, si)
                qs = stack_heads(q[rows, cols], head_one); gs = stack_heads(mg[rows, cols], head_one)
                p = probs_of(qs, kk, (tab[2 * hp], tab[2 * hp + 1]), mine_of(b, nl, lb, sb), n)
                dp = dot(gs, vv, 1, 1)
                ds = (p * (dp - jnp.sum(p * dp, axis=1, keepdims=True))).astype(bf)
                dqs = dot(ds, kk, 1, 0)
                dkt = dot(qs, ds, 0, 0)
                dvt = dot(gs, p.astype(bf), 0, 0)
                sums = [0, 0]
                for c_ in range(n):
                    pre = dot(ds[:, c_ * 128:(c_ + 1) * 128], tri, 1, 0)
                    at = idx[c_]
                    for e in range(2):
                        sums[e] += jnp.where(at >= 0, jnp.take_along_axis(pre[e * 128:(e + 1) * 128], jnp.maximum(at, 0), axis=1), 0.0)
                for e in range(2):
                    seg[2 * hp + e] += jnp.sum(sums[e], axis=0, keepdims=True)
                dq[rows, cols] = jnp.where(head_one, dqs[:128], dqs[128:]).astype(bf)
                dkt = dkt.T.astype(bf); dvt = dvt.T.astype(bf)
                if b < nl:
                    dkl[:, b, :, cols] = dkt.reshape(n, 128, 128); dvl[:, b, :, cols] = dvt.reshape(n, 128, 128)
                else:
                    ka[rows, cols] = dkt; va[rows, cols] = dvt
    for i in piece(0, 0):
        send_core(i)
    attend(0)
    kv_core(0); weight_grad(1, dq, 0); stages(0, 0, 0)
    attend(1)
    kv_core(1); kv_chip(0); weight_grad(1, dq, 1); stages(0, 0, 1); stages(1, 0, 0)
    attend(2)
    kv_core(2); kv_chip(1); kv_end(0); weight_grad(1, dq, 2); stages(0, 1, 1); stages(1, 0, 1); stages(2, 0, 0)
    attend(3)
    kv_core(3); kv_chip(2); kv_end(1); weight_grad(1, dq, 3); stages(0, 0, 2, 3); stages(0, 2, 1); stages(1, 1, 1); stages(2, 0, 1)
    kv_chip(3); kv_end(2); stages(0, 1, 2, 3); stages(0, 3, 1); stages(1, 0, 2, 3); stages(1, 2, 1); stages(2, 1, 1); stages(3, 0, 0)
    kv_end(3); stages(0, 2, 2, 3); stages(1, 3, 1); stages(1, 1, 2, 3); stages(2, 2, 1); stages(2, 0, 2, 3); stages(3, 0, 1)
    gain = params[experts:experts + 1, :].astype(f32)
    ag = jnp.zeros((1, q.shape[1]), f32)
    for t in range(2):
        rows = pl.ds(t * half, half)
        ng = dot(dq[rows, :], wq[...], 1, 1) + dot(ka[rows, :], wk[...], 1, 1) + dot(va[rows, :], wv[...], 1, 1)
        m = rows_of(lx, sx, t).astype(f32)
        r1 = rms_scale(m)
        u = m * r1
        ag += jnp.sum(ng * u, axis=0, keepdims=True)
        w = ng * gain
        (lgrad, sgrad)[t][...] = (midg[rows, :] + r1 * (w - u * jnp.mean(w * u, axis=-1, keepdims=True))).reshape(lgrad.shape)
        if t == 0:
            stages(0, 3, 2, 3); stages(1, 2, 2, 3); stages(2, 3, 1); stages(2, 1, 2, 3); stages(3, 1, 1)
    sacc[0] = small_in[...]
    sacc[0, 0:1, :] = ag
    heads = seg.shape[0]
    spot = lax.broadcasted_iota(jnp.int32, (8, 128), 1)
    for h in range(heads):
        upto = jnp.broadcast_to(seg[h], (8, 128))
        within = upto - jnp.where(spot == 0, 0.0, pltpu.roll(upto, 1, 1))
        at = jnp.where(spot < 16, 15 - spot, jnp.minimum(spot - 1, 30))
        by_bucket = jnp.where((spot == 16) | (spot >= 32), 0.0, jnp.take_along_axis(within, at, axis=1))
        r = 2 + experts + h // 8
        sacc[0, r:r + 1, (h % 8) * 128:(h % 8 + 1) * 128] = by_bucket[0:1, :]
    sc = remote(sacc.at[0], sbuf.at[0], sss.at[0], srs.at[0], cdev)
    stages(1, 3, 2, 3); stages(2, 2, 2, 3); stages(3, 2, 1)
    sc.wait_recv()
    sacc[1] = sacc[0] + sbuf[0]
    sx_ = remote(sacc.at[1], sbuf.at[1], sss.at[1], srs.at[1], xdev)
    stages(2, 3, 2, 3); stages(3, 3, 1); stages(3, 0, 2, 3)
    sx_.wait_recv()
    sacc[2] = sacc[1] + sbuf[1]
    sy = remote(sacc.at[2], sbuf.at[2], sss.at[2], srs.at[2], ydev)
    stages(3, 1, 2, 3)
    sy.wait_recv()
    sacc[3] = sacc[2] + sbuf[2]
    sz = [remote(sacc.at[3], sbuf.at[2 + k], sss.at[2 + k], srs.at[2 + k], zdev(k)) for k in range(1, Z)]
    stages(3, 2, 2, 3); stages(3, 3, 2, 3)
    tot = sacc[3]
    for k in range(1, Z):
        sz[k - 1].wait_recv()
        tot += sbuf[2 + k]
    small[...] = tot
    for cp in [sc, sx_, sy] + sz + list(kx.values()) + list(kf.values()) + list(first.values()) + list(hh.values()) + [w for v_ in zz.values() for w in v_]:
        cp.wait_send()
def back(dims, nl, ns, experts, arrays, cid):
    X, C, Z, Y = dims
    q_, small_in = arrays[0], arrays[-1]
    tokens, width = q_.shape
    heads = arrays[5].shape[0]
    nr = width // (X * C * Z * Y)
    wide = 256
    pieces = tuple((0, h * 512, 512) for h in range(width // 512)) + tuple((m, b * wide, wide) for m in range(1, 4) for b in range(width // wide))
    n = len(pieces)
    S, sem, bf, f32 = jax.ShapeDtypeStruct, pltpu.SemaphoreType.DMA, jnp.bfloat16, jnp.float32
    V = pltpu.VMEM
    scr = [V(lead + (nr, nc), bf) for m, c0, nc in pieces for lead in ((X, Z, Y), (X, Z), (Z,), (Z - 1,))]
    kvn = 2 * (width // wide)
    long = V((X * C, nl, 128, width), bf)
    rows = V((tokens, width), bf)
    scr += [V((3, X, C, Z, Y, nr, width), bf), rows, rows, rows, long, long,
            V((kvn, 2, nl, 128, wide), bf), V((kvn, nl, 128, wide), bf), V((kvn, nl, 128, wide), bf), V((heads, 1, 128), f32),
            V((4,) + small_in.shape, f32), V((Z + 2,) + small_in.shape, f32),
            sem((n,)), sem((n,)), sem((n, 2)), sem((n, 2)), sem((n, Z)), sem((n, Z)), sem((kvn, 3)), sem((kvn, 3)), sem((Z + 2,)), sem((Z + 2,))]
    vm = pl.BlockSpec(memory_space=pltpu.VMEM)
    outs = [S((nl, 128, width), f32), S((ns, 128, width), f32)] + [S((nr, width), f32)] * 4 + [S(small_in.shape, f32)]
    return pl.pallas_call(functools.partial(back_kernel, dims, nl, ns, experts, pieces), out_shape=outs,
        in_specs=[vm] * len(arrays), out_specs=[vm] * len(outs), scratch_shapes=scr,
        compiler_params=pltpu.CompilerParams(collective_id=cid, has_side_effects=True, vmem_limit_bytes=63 * 2**20))(*arrays)

def gelu_parts(v):
    c, a = 0.7978845608, 0.044715
    v2 = v * v
    t = jnp.tanh(c * v * (1.0 + a * v2))
    half = 0.5 * (1.0 + t)
    return v * half, half + 0.5 * v * (1.0 - t * t) * (c * (1.0 + 3.0 * a * v2))
RING, LAG = 6, 4
def expert_kernel(cap, per, order, todo, wcut, tile, whole_down, xs, gs, wgi, wui, wdi, eo_out, ri_out, grads, eo_h, ri_h,
                  wall, xr, gr, hall, lall, eo, ri, cb, ab, xb, ob,
                  lsem, xss, xrs, gss, grs, ess, ers, rss, rrs, wss, wrs, wls, css, crs, ass, ars, osem, free):
    dp = lax.axis_size("dp")
    f32, bf = jnp.float32, jnp.bfloat16
    s, x, c, xdev, cdev = seq_places(2)
    g = lax.axis_index("dp")
    def peer(k): return (s, g ^ k)
    greet([xdev, cdev] + [peer(k) for k in range(1, dp)])
    rows_w, ff = wgi.shape; width = xs.shape[2]
    piece = rows_w // wcut
    wx, wc, wl = [], [], []
    shared = ((wgi, 1), (wui, 2)) if whole_down else ((wgi, 1), (wui, 2), (wdi, 0))
    parts = [(src, m, h * piece) for h in range(wcut) for src, m in shared]
    for n, (src, m, r0) in enumerate(parts):
        a = src.at[pl.ds(r0, piece)]
        b = wall.at[m, x, c, pl.ds(r0, piece)]
        wx.append(remote(a, b, wss.at[n, 0], wrs.at[n, 0], xdev))
        wc.append(remote(a, b, wss.at[n, 1], wrs.at[n, 1], cdev))
        cp = pltpu.make_async_copy(a, b, wls.at[n]); cp.start(); wl.append(cp)
    if whole_down:
        cp = pltpu.make_async_copy(wdi, wall.at[0], wls.at[len(parts)]); cp.start(); wl.append(cp)
    sx, sg = {}, {}
    for k in [k for p in order for k in range(p * per, (p + 1) * per)]:
        at = pl.ds(k * cap, cap)
        if k == 0:
            sx[0] = pltpu.make_async_copy(xs.at[g], xr.at[at], lsem.at[0]); sx[0].start()
            sg[0] = pltpu.make_async_copy(gs.at[g], gr.at[at], lsem.at[1]); sg[0].start()
        else:
            sx[k] = remote(xs.at[g ^ k], xr.at[at], xss.at[k], xrs.at[k], peer(k))
            sg[k] = remote(gs.at[g ^ k], gr.at[at], gss.at[k], grs.at[k], peer(k))
    wf = []
    for n, (src, m, r0) in enumerate(parts):
        wx[n].wait_recv()
        b = wall.at[m, 1 - x, c, pl.ds(r0, piece)]
        wf.append(remote(b, b, wss.at[n, 2], wrs.at[n, 2], cdev))
    for cp in wl: cp.wait()
    for n in range(len(parts)):
        wc[n].wait_recv(); wf[n].wait_recv()
    ntile = ff // tile
    re, rr = {}, {}
    wide = 4 * rows_w
    for p in todo:
        ks = list(range(p * per, (p + 1) * per))
        for k in ks:
            if k == 0: sx[0].wait(); sg[0].wait()
            else: sx[k].wait_recv(); sg[k].wait_recv()
        rows = pl.ds(p * per * cap, per * cap)
        @pl.loop(0, ntile)
        def _(t):
            cols = pl.ds(pl.multiple_of(t * tile, 128), tile)
            w = lambda m: wall[m, :, :, :, cols].reshape(wide, tile)
            gp = jnp.dot(xr[rows, :], w(1), preferred_element_type=f32)
            up = jnp.dot(xr[rows, :], w(2), preferred_element_type=f32)
            hg = jnp.dot(gr[rows, :], w(0), preferred_element_type=f32)
            act, der = gelu_parts(gp)
            hall[0, rows, cols] = (act * up).astype(bf)
            hall[1, rows, cols] = (hg * up * der).astype(bf)
            hall[2, rows, cols] = (hg * act).astype(bf)
        @pl.loop(0, 4)
        def _(t):
            part = pl.ds(pl.multiple_of(t * rows_w, 128), rows_w)
            tx, tc = t // 2, lax.rem(t, 2)
            eo[:, part] = dot(hall[0, rows, :], wall[0, tx, tc], 1, 1).astype(bf)
            ri[:, part] = (dot(hall[1, rows, :], wall[1, tx, tc], 1, 1) + dot(hall[2, rows, :], wall[2, tx, tc], 1, 1)).astype(bf)
        keep = [pltpu.make_async_copy(eo, eo_h.at[rows], lsem.at[4]), pltpu.make_async_copy(ri, ri_h.at[rows], lsem.at[5])]
        for cp in keep: cp.start()
        for cp in keep: cp.wait()
        for k in ks:
            at = pl.ds(k * cap, cap)
            if k == 0:
                re[0] = pltpu.make_async_copy(eo_h.at[at], eo_out.at[g], lsem.at[2]); re[0].start()
                rr[0] = pltpu.make_async_copy(ri_h.at[at], ri_out.at[g], lsem.at[3]); rr[0].start()
            else:
                re[k] = remote(eo_h.at[at], eo_out.at[g], ess.at[k], ers.at[k], peer(k))
                rr[k] = remote(ri_h.at[at], ri_out.at[g], rss.at[k], rrs.at[k], peer(k))
    for n in range(len(parts)):
        wx[n].wait_send(); wc[n].wait_send(); wf[n].wait_send()
    total = dp * cap
    @pl.loop(0, total // 256)
    def _(t):
        at = pl.ds(pl.multiple_of(t * 256, 256), 256)
        lall[1, :, at] = xr[at, :].T
        lall[0, :, at] = gr[at, :].T
    nt = 3 * ntile
    def place(n):
        m = n // ntile
        return m, pl.ds(pl.multiple_of((n - m * ntile) * tile, 128), tile)
    def to_core(n):
        m, cols = place(n); r = lax.rem(n, RING)
        return pltpu.make_async_remote_copy(src_ref=wall.at[m, :, 1 - c, :, cols], dst_ref=cb.at[r], send_sem=css.at[r],
            recv_sem=crs.at[r], device_id=cdev, device_id_type=MESH)
    def to_chip(n):
        r = lax.rem(n, RING)
        return pltpu.make_async_remote_copy(src_ref=ab.at[r], dst_ref=xb.at[r], send_sem=ass.at[r],
            recv_sem=ars.at[r], device_id=xdev, device_id_type=MESH)
    def to_out(n):
        m, cols = place(n); r = lax.rem(n, 2)
        return pltpu.make_async_copy(ob.at[r], grads.at[m, :, cols], osem.at[r])
    @pl.loop(0, nt + LAG)
    def _(n):
        @pl.when(n < nt)
        def _():
            m, cols = place(n)
            res = jnp.dot(lall[jnp.minimum(m, 1)], hall[m, :, cols], preferred_element_type=f32)
            wall[m, :, :, :, cols] = res.astype(bf).reshape(2, 2, rows_w, tile)
            @pl.when(n >= RING)
            def _(): pl.semaphore_wait(free.at[0], 1)
            to_core(n).start()
        @pl.when((n >= 1) & (n <= nt))
        def _():
            i = n - 1
            m, cols = place(i); r = lax.rem(i, RING)
            to_core(i).wait_recv()
            @pl.when(i >= RING)
            def _():
                to_chip(i).wait_send()
                pl.semaphore_wait(free.at[1], 1)
            ab[r] = (wall[m, 1 - x, c, :, cols].astype(f32) + cb[r, 1 - x].astype(f32)).astype(bf)
            to_chip(i).start()
        @pl.when(n >= LAG)
        def _():
            j = n - LAG
            m, cols = place(j); r = lax.rem(j, RING)
            to_chip(j).wait_recv()
            to_core(j).wait_send()
            @pl.when(j >= 2)
            def _(): to_out(j).wait()
            ob[lax.rem(j, 2)] = wall[m, x, c, :, cols].astype(f32) + cb[r, x].astype(f32) + xb[r].astype(f32)
            to_out(j).start()
            @pl.when(j < nt - RING)
            def _():
                pl.semaphore_signal(free.at[0], inc=1, device_id=cdev, device_id_type=MESH)
                pl.semaphore_signal(free.at[1], inc=1, device_id=xdev, device_id_type=MESH)
    for j in range(nt - 2, nt): to_out(j).wait()
    for i in range(nt - RING, nt): to_chip(i).wait_send()
    for k in range(dp):
        if k == 0:
            re[0].wait(); rr[0].wait()
        else:
            sx[k].wait_send(); sg[k].wait_send(); re[k].wait(); rr[k].wait()
def expert_all(xs, gs, wg, wu, wd, seq, cid):
    dp, cap, width = xs.shape
    rows_w, ff = wg.shape; total = dp * cap
    whole_down = wd.shape[0] != rows_w
    if whole_down: wd = wd.reshape(seq // 2, 2, rows_w, ff)
    group = 320
    per = group // cap
    ng = dp // per
    order = [p for p in range(ng // 2, ng)] + [p for p in range(ng // 2 - 1, -1, -1)]
    todo = list(range(ng))
    sem = pltpu.SemaphoreType.DMA
    bf = jnp.bfloat16
    any_ = pl.BlockSpec(memory_space=pl.ANY)
    V = pltpu.VMEM
    tile = 256
    wcut = 2
    back = jax.ShapeDtypeStruct((dp, cap, width), bf)
    flat = jax.ShapeDtypeStruct((total, width), bf)
    return pl.pallas_call(functools.partial(expert_kernel, cap, per, order, todo, wcut, tile, whole_down),
        out_shape=[back, back, jax.ShapeDtypeStruct((3, rows_w, ff), jnp.float32), flat, flat],
        in_specs=[any_] * 5, out_specs=[any_] * 5,
        scratch_shapes=[V((3, seq // 2, 2, rows_w, ff), bf), V((total, width), bf), V((total, width), bf), V((3, total, ff), bf),
        V((2, width, total), bf), V((group, width), bf), V((group, width), bf),
        V((RING, seq // 2, rows_w, tile), bf), V((RING, rows_w, tile), bf), V((RING, rows_w, tile), bf), V((2, rows_w, tile), jnp.float32)]
        + [sem((6,))] + [sem((dp,))] * 8 + [sem((3 * wcut, 3))] * 2 + [sem((3 * wcut + 1,))] + [sem((RING,))] * 4 + [sem((2,)), pltpu.SemaphoreType.REGULAR((2,))],
        compiler_params=pltpu.CompilerParams(collective_id=cid, has_side_effects=True, vmem_limit_bytes=63 * 2**20))(xs, gs, wg, wu, wd)[:3]


def on_device(
    long_tokens,
    short_tokens,
    long_grad_out,
    short_grad_out,
    query_weight,
    key_weight,
    value_weight,
    output_weight,
    attn_gain,
    ffn_gain,
    rel_table,
    router_weight,
    gate_weight,
    up_weight,
    down_weight,
    long_positions,
    short_positions,
    long_lengths,
    short_lengths,
    long_routes,
    short_routes,
):
    long_items, quarter, model_width = long_tokens.shape
    short_items, short_len = (short_tokens.shape[0], short_tokens.shape[1])
    long_rows = long_items * quarter
    tokens = long_rows + short_items * short_len
    local_experts = gate_weight.shape[0]
    dp_size = lax.axis_size("dp")
    experts = local_experts * dp_size
    capacity = (5 * tokens + 2 * experts - 1) // (2 * experts)
    seq_size = lax.axis_size("seq")
    dims = (seq_size // 2, 2, dp_size // 2, 2)
    devices = seq_size * dp_size
    table_part, gain_part = rel_table.shape[0], attn_gain.shape[0]
    small = jnp.concatenate([router_weight.T, attn_gain[None], ffn_gain[None]], 0)
    small = jnp.pad(small, ((0, 1), (0, 128 - gain_part)))
    table_row = jnp.pad(rel_table[None], ((experts + 2, 0), (0, 128 - table_part)))
    small = jnp.pad(small + table_row, ((0, -(experts + 3) % 16), (0, 0)))
    rows_part = query_weight.shape[0]
    cuts = 2 if rows_part % 32 == 0 else 1
    cut = rows_part // cuts
    pieces = tuple((m, h * cut, cut, (m + h) % 2) for m in range(4) for h in range(cuts))
    gathered = gather_all(
        (query_weight, key_weight, value_weight, output_weight, small),
        pieces[: 3 * cuts] + ((4, 0, small.shape[0], 0),) + pieces[3 * cuts :],
        dims,
        0,
    )
    query_all, key_all, value_all, output_all = (
        block.reshape(devices * rows_part, model_width) for block in gathered[:4]
    )
    small_all = gathered[4].reshape(devices, small.shape[0], 128)
    params = small_all[:, : experts + 2, :gain_part].transpose(1, 0, 2)
    params = jnp.pad(params.reshape(experts + 2, model_width), ((0, 126 - experts), (0, 0)))
    table = small_all[:, experts + 2, :table_part].reshape(HEADS, 1, BUCKETS).astype(jnp.float32)
    table = jnp.pad(table, ((0, 0), (0, 0), (0, 128 - BUCKETS)), constant_values=masked)
    queries, keys, values, long_keys, long_values, normed_t = head(
        long_items,
        short_items,
        seq_size,
        experts,
        (long_tokens, short_tokens, params, query_all, key_all, value_all),
        1,
    )
    sizes = (long_items, short_items, seq_size, experts, capacity)
    heads_args = (queries, keys, values, long_keys, long_values, table)
    places = (long_positions, short_positions)
    grads = (long_grad_out, short_grad_out, output_all, params)
    routes = (long_routes, short_routes)
    mixed, middle, outgoing, out_slots, logits, long_buckets, short_buckets = attention(
        *sizes,
        (long_lengths, short_lengths)
        + heads_args
        + places
        + (long_tokens, short_tokens)
        + grads
        + routes,
        tokens,
        model_width,
    )
    later_down, unused_keys = lax.optimization_barrier((down_weight[0], long_keys))
    down_full = lax.all_gather(later_down, "seq", axis=0, tiled=True)
    back_rows, back_grads, expert_grads = expert_all(
        outgoing, out_slots, gate_weight[0], up_weight[0], down_full, seq_size, 4
    )
    (
        long_out,
        short_out,
        middle_grad,
        output_local,
        small_local,
        mixed_grad,
        long_places,
        short_places,
        down_grad,
        gate_grad,
        up_grad,
    ) = post(
        *sizes,
        dims + (rows_part, model_width),
        places + (back_rows, back_grads, middle, mixed, logits) + routes + grads + (expert_grads,),
        tokens,
        model_width,
    )
    long_grad_in, short_grad_in, output_grad, query_grad, key_grad, value_grad, small_sum = back(
        dims,
        long_items,
        short_items,
        experts,
        heads_args
        + (long_buckets, short_buckets, long_places, short_places)
        + (mixed_grad, output_local, normed_t, long_tokens, short_tokens, params)
        + (query_all, key_all, value_all, middle_grad, small_local),
        2,
    )
    place = lax.axis_index("seq") * dp_size + lax.axis_index("dp")

    def own(row, column, size, count=1):
        return lax.dynamic_slice(small_sum, (row, column), (count, size))

    entry = place * table_part
    head_at = entry // BUCKETS
    table_grad = own(2 + experts + head_at // 8, head_at % 8 * 128 + entry % BUCKETS, table_part)
    summed = (
        query_grad,
        key_grad,
        value_grad,
        output_grad,
        own(0, place * gain_part, gain_part)[0],
        own(1, place * gain_part, gain_part)[0],
        table_grad[0],
        own(2, place * rows_part, rows_part, experts).T,
    )
    return (
        long_out,
        short_out,
        long_grad_in,
        short_grad_in,
        summed[0],
        summed[1],
        summed[2],
        summed[3],
        summed[4],
        summed[5],
        summed[6],
        summed[7],
        gate_grad,
        up_grad,
        down_grad,
    )


def solution(mesh):
    placed = (
        P("dp", "seq", None),
        P(("seq", "dp"), None, None),
        P("dp", "seq", None),
        P(("seq", "dp"), None, None),
        P(("seq", "dp"), None),
        P(("seq", "dp"), None),
        P(("seq", "dp"), None),
        P(("seq", "dp"), None),
        P(("seq", "dp")),
        P(("seq", "dp")),
        P(("seq", "dp")),
        P(("seq", "dp"), None),
        P("dp", "seq", None),
        P("dp", "seq", None),
        P("dp", "seq", None),
        P("dp", None),
        P(("seq", "dp"), None),
        P("dp"),
        P(("seq", "dp")),
        P("dp", "seq", None),
        P(("seq", "dp"), None, None),
    )
    return jax.shard_map(
        on_device,
        mesh=mesh,
        in_specs=placed,
        out_specs=(
            P("dp", "seq", None),
            P(("seq", "dp"), None, None),
            P("dp", "seq", None),
            P(("seq", "dp"), None, None),
            P(("seq", "dp"), None),
            P(("seq", "dp"), None),
            P(("seq", "dp"), None),
            P(("seq", "dp"), None),
            P(("seq", "dp")),
            P(("seq", "dp")),
            P(("seq", "dp")),
            P(("seq", "dp"), None),
            P("dp", "seq", None),
            P("dp", "seq", None),
            P("dp", "seq", None),
        ),
        check_vma=False,
    )
```

```python
import functools

import jax
import jax.numpy as jnp
from jax import lax
from jax.experimental import pallas as pl
from jax.experimental.pallas import tpu as pltpu
from jax.sharding import PartitionSpec as P

MESH = pl.DeviceIdType.MESH

HEADS = 16
HEAD = 64
BUCKETS = 32


epsilon = 1e-06
masked = -1e30


def seq_places(C):
    s = lax.axis_index("seq"); g = lax.axis_index("dp")
    x, c = s // C, lax.rem(s, C)
    return s, x, c, ((1 - x) * C + c, g), (x * C + 1 - c, g)
def greet(devs):
    bar = pltpu.get_barrier_semaphore()
    for d in devs:
        pl.semaphore_signal(bar, inc=1, device_id=d, device_id_type=MESH)
    pl.semaphore_wait(bar, len(devs))
def remote(src, dst, ss, rs, dev):
    cp = pltpu.make_async_remote_copy(src_ref=src, dst_ref=dst, send_sem=ss, recv_sem=rs, device_id=dev, device_id_type=MESH)
    cp.start()
    return cp
EDGES = (-90, -63, -45, -31, -22, -15, -11, -7, -6, -5, -4, -3, -2, -1, 0, 1, 2, 3, 4, 5, 6, 7, 8, 12, 16, 23, 32, 46, 64, 91)
FAR = (12, 16, 23, 32, 46, 64, 91)
def fill_buckets(out, q_col, k_row, length, base):
    r = k_row - q_col
    n = jnp.abs(r)
    far = jnp.full(r.shape, 8, jnp.int32)
    for e in FAR:
        far += (n >= e).astype(jnp.int32)
    b = jnp.where(n < 8, n, far) + jnp.where(r > 0, 16, 0)
    j = lax.broadcasted_iota(jnp.int32, r.shape, 1) + base
    out[...] = jnp.where(j < length, b, 32)
def dot(a, b, ca, cb):
    return lax.dot_general(a, b, (((ca,), (cb,)), ((), ())), preferred_element_type=jnp.float32)
def probs_of(qs, kk, tabs, bucket_ref, blocks):
    s = dot(qs, kk, 1, 1)
    t = [jnp.broadcast_to(tab, (128, 128)) for tab in tabs]
    bias = [jnp.concatenate([jnp.take_along_axis(x, bucket_ref[c], axis=1) for x in t], axis=0) for c in range(blocks)]
    s = s + (jnp.concatenate(bias, axis=1) if blocks > 1 else bias[0])
    p = jnp.exp(s - jnp.max(s, axis=1, keepdims=True))
    return p * (1.0 / jnp.sum(p, axis=1, keepdims=True))
def stack_heads(rows, first):
    return jnp.concatenate([jnp.where(first, rows, 0), jnp.where(first, 0, rows)], axis=0)
def column_of(row):
    i = lax.broadcasted_iota(jnp.int32, (128, 128), 0)
    return jnp.sum(jnp.where(i == lax.broadcasted_iota(jnp.int32, (128, 128), 1), row, 0), axis=1, keepdims=True)
def row_of(col):
    i = lax.broadcasted_iota(jnp.int32, (128, 128), 0)
    return jnp.sum(jnp.where(i == lax.broadcasted_iota(jnp.int32, (128, 128), 1), col, 0), axis=0, keepdims=True)
def rows_of(long_ref, short_ref, t):
    ref = long_ref if t == 0 else short_ref
    return ref[...].reshape(ref.shape[0] * ref.shape[1], ref.shape[2])
def rms_scale(mid):
    return lax.rsqrt(jnp.mean(mid * mid, axis=-1, keepdims=True) + epsilon)
def item(b, nl, blocks, cols, k, v, kl, vl):
    rows = pl.ds(b * 128, 128)
    if b < nl:
        return rows, blocks, kl[:, b, :, cols].reshape(blocks * 128, 128), vl[:, b, :, cols].reshape(blocks * 128, 128)
    short = pl.ds((b - nl) * 128, 128)
    return rows, 1, k[short, cols], v[short, cols]
def mine_of(b, nl, long_ref, short_ref):
    return long_ref.at[b] if b < nl else short_ref.at[b - nl]
def front_kernel(dims, nl, ns, experts, cap, pieces, table_part, gain_part, ll, sl, wk_in, wv_in, wq_in, wo_in, small_in, lpos, spos, xl, xsh, gl, gsh, lr, sr,
                 wk_out, wv_out, wq_out, wo_out, params, tab, q, ks, vs, kl, vl, n1t, mixed, mid, xs, gs, logits, lb, sb,
                 wall, sm, n1, n2, gb, zs, zr, hs, hr, cs, cr, kss, krs, osem):
    X, C, Z, Y = dims
    blocks = X * C
    f32, bf = jnp.float32, jnp.bfloat16
    s, x, c, xdev, cdev = seq_places(C)
    g = lax.axis_index("dp")
    z, y = g // Y, lax.rem(g, Y)
    def zdev(k): return (s, lax.rem(z + k, Z) * Y + y)
    ydev = (s, z * Y + (1 - y))
    tokens, width = q.shape
    half = nl * 128
    wide = 256
    nb = width // wide
    greet([zdev(k) for k in range(1, Z)] + [ydev, xdev, cdev])
    ins = (wk_in, wv_in, wq_in, wo_in)
    def part(i, *lead):
        m, r0, nr, route = pieces[i]
        if m == 4:
            return sm.at[lead + (slice(None),) * (4 - len(lead))]
        return wall.at[(m,) + lead + (slice(None),) * (4 - len(lead)) + (pl.ds(r0, nr),)]
    zc, h, cc = {}, {}, {}
    for i, (m, r0, nr, route) in enumerate(pieces):
        src = small_in if m == 4 else ins[m].at[pl.ds(r0, nr)]
        zc[i] = [remote(src, part(i, x, c, z, y), zs.at[i, k], zr.at[i, k], zdev(k)) for k in range(1, Z)]
    for m in range(4):
        wall[m, x, c, z, y] = ins[m][...]
    sm[x, c, z, y] = small_in[...]
    def gather_stage(i, stage):
        route = pieces[i][3]
        if stage == 0:
            for k in range(1, Z): zc[i][k - 1].wait_recv()
            mine = part(i, x, c, slice(None), y)
            h[i, 0] = remote(mine, mine, hs.at[i, 0], hr.at[i, 0], xdev if route == 0 else ydev)
            cc[i, 0] = remote(mine, mine, cs.at[i, 0], cr.at[i, 0], cdev)
        elif stage == 1:
            h[i, 0].wait_recv()
            if route == 0:
                both, got = part(i, slice(None), c, slice(None), y), part(i, 1 - x, c, slice(None), y)
            else:
                both, got = part(i, x, c), part(i, x, c, slice(None), 1 - y)
            h[i, 1] = remote(both, both, hs.at[i, 1], hr.at[i, 1], ydev if route == 0 else xdev)
            cc[i, 1] = remote(got, got, cs.at[i, 1], cr.at[i, 1], cdev)
        else:
            h[i, 1].wait_recv()
            got = part(i, slice(None), c, slice(None), 1 - y) if route == 0 else part(i, 1 - x, c)
            cc[i, 2] = remote(got, got, cs.at[i, 2], cr.at[i, 2], cdev)
    np_ = len(pieces)
    steps = [(t - st, st) for t in range(np_ + 2) for st in range(3) if 0 <= t - st < np_]
    done = [0]
    def gather_until(m):
        last = max(i for i, p in enumerate(pieces) if p[0] == m)
        while True:
            i, st = steps[done[0]]
            gather_stage(i, st)
            done[0] += 1
            if (i, st) == (last, 2): break
        for i, p in enumerate(pieces):
            if p[0] == m:
                for k in range(3): cc[i, k].wait_recv()
    kept_copies = []
    def keep(m, out):
        cp = pltpu.make_async_copy(wall.at[m], out, osem.at[m]); cp.start(); kept_copies.append(cp)
    def w_of(m):
        return wall[m].reshape(width, width)
    for b in range(nl):
        own = column_of(lpos[b:b + 1, pl.ds(pl.multiple_of(s * 128, 128), 128)])
        for k in range(blocks):
            fill_buckets(lb.at[b, k], own, lpos[b:b + 1, k * 128:(k + 1) * 128], ll[b], k * 128)
    for b in range(ns):
        fill_buckets(sb.at[b, 0], column_of(spos[b:b + 1, :]), spos[b:b + 1, :], sl[b], 0)
    gather_until(4)
    flat = sm[...].astype(f32).reshape(X * C * Z * Y, sm.shape[4], 128)
    per = 128 // gain_part
    def shifted(rows, n):
        return rows if n == 0 else pltpu.roll(rows, n, 1)
    chunks = []
    for k in range(width // 128):
        chunks.append(sum(shifted(flat[k * per + i], i * gain_part) for i in range(per)))
    found = jnp.concatenate(chunks, axis=1)
    params[...] = jnp.zeros_like(params)
    params[0:found.shape[0], :] = found.astype(bf)
    share = 32 // table_part
    lane8 = lax.broadcasted_iota(jnp.int32, (1, 128), 1)
    for hd in range(tab.shape[0]):
        rows = sum(shifted(flat[hd * share + i], i * table_part) for i in range(share))
        tab[hd] = jnp.where(lane8 < 32, rows[experts + 2:experts + 3, :], masked)
    gain = params[experts:experts + 1, :].astype(f32)
    for t in range(2):
        m = rows_of(xl, xsh, t).astype(f32)
        n1[pl.ds(t * half, half), :] = (m * rms_scale(m) * gain).astype(bf)
        gb[pl.ds(t * half, half), :] = rows_of(gl, gsh, t)
    wholes = (kl, vl)
    far = (1 - x) * C + c
    ka, kc, kf = {}, {}, {}
    def project(m, t):
        return jnp.dot(n1[pl.ds(t * half, half), :], w_of(m), preferred_element_type=f32).astype(bf)
    for m in range(2):
        gather_until(m)
        wholes[m][s] = project(m, 0).reshape(nl, 128, width)
        for b in range(nb):
            n = m * nb + b
            src = wholes[m].at[s, :, :, pl.ds(b * wide, wide)]
            ka[n] = remote(src, src, kss.at[n, 0], krs.at[n, 0], xdev)
            kc[n] = remote(src, src, kss.at[n, 1], krs.at[n, 1], cdev)
        keep(m, (wk_out, wv_out)[m])
    ks[...] = project(0, 1)
    vs[...] = project(1, 1)
    for t in range(2):
        n1t[:, t * half:(t + 1) * half] = n1[pl.ds(t * half, half), :].T
    gather_until(2)
    for t in range(2):
        q[pl.ds(t * half, half), :] = project(2, t)
    keep(2, wq_out)
    first = lax.broadcasted_iota(jnp.int32, (128, 128), 1) < 64
    for b0 in range(nb):
        for n in (b0, nb + b0):
            ka[n].wait_recv()
            got = wholes[n // nb].at[far, :, :, pl.ds(b0 * wide, wide)]
            kf[n] = remote(got, got, kss.at[n, 2], krs.at[n, 2], cdev)
        for n in (b0, nb + b0):
            kc[n].wait_recv(); kf[n].wait_recv()
        @pl.loop(0, wide // 128)
        def _(i):
            hp = b0 * (wide // 128) + i
            cols = pl.ds(pl.multiple_of(hp * 128, 128), 128)
            for b in range(nl + ns):
                rows, n, kk, vv = item(b, nl, blocks, cols, ks, vs, kl, vl)
                p = probs_of(stack_heads(q[rows, cols], first), kk, (tab[2 * hp], tab[2 * hp + 1]), mine_of(b, nl, lb, sb), n)
                out = dot(p.astype(bf), vv, 1, 0)
                mixed[rows, cols] = jnp.where(first, out[:128], out[128:]).astype(bf)
        if b0 == 0:
            gather_until(3)
            keep(3, wo_out)
    gain = params[experts + 1:experts + 2, :].astype(f32)
    for t in range(2):
        rows = pl.ds(t * 256, 256)
        m = rows_of(xl, xsh, t).astype(f32) + jnp.dot(mixed[rows, :], w_of(3), preferred_element_type=f32)
        mid[rows, :] = m
        n2[rows, :] = (m * rms_scale(m) * gain).astype(bf)
    logits[...] = dot(n2[...], params[...], 1, 1)
    logit_t = dot(params[...], n2[...], 1, 1)[:experts]
    routes = [jnp.concatenate([row_of(ref[i, :, j:j + 1]) for ref in (lr, sr) for i in range(ref.shape[0])], axis=1) for j in range(2)]
    e_iota = lax.broadcasted_iota(jnp.int32, (experts, tokens), 0)
    member = ((e_iota == routes[0]) | (e_iota == routes[1])).astype(f32)
    e = jnp.exp(logit_t - jnp.max(logit_t, axis=0, keepdims=True))
    p = e / jnp.sum(e, axis=0, keepdims=True)
    chosen = member * p
    before = (lax.broadcasted_iota(jnp.int32, (tokens, tokens), 0) < lax.broadcasted_iota(jnp.int32, (tokens, tokens), 1)).astype(f32).astype(bf)
    place = jnp.dot(member.astype(bf), before, preferred_element_type=f32)
    kept = (member > 0.5) & (place < cap)
    weight = jnp.where(kept, chosen / jnp.sum(chosen, axis=0, keepdims=True), 0.0)
    slot = jnp.where(kept, place.astype(jnp.int32), -1)
    s_iota = lax.broadcasted_iota(jnp.int32, (cap, tokens), 0)
    for i in range(experts):
        pick = (s_iota == slot[i:i + 1, :]).astype(f32)
        scale = jnp.sum(pick * weight[i:i + 1, :], axis=1, keepdims=True)
        pick = pick.astype(bf)
        xs[i] = jnp.dot(pick, n2[...], preferred_element_type=f32).astype(bf)
        gs[i] = (jnp.dot(pick, gb[...], preferred_element_type=f32) * scale).astype(bf)
    for cp in kept_copies: cp.wait()
    for group in (h, cc, ka, kc, kf):
        for cp in group.values(): cp.wait_send()
    for i in zc:
        for cp in zc[i]: cp.wait_send()
def post_kernel(nl, ns, blocks, experts, cap, lpos, spos, eo, ri, mid, mixed, logits, lr, sr, gl, gsh, wo, params, eg,
                lout, sout, midg, wog, small, mg, li, si, eg0, eg1, eg2, bg, n2, lg, fin, bk, sh, ev, sem):
    f32, bf = jnp.float32, jnp.bfloat16
    tokens = mid.shape[0]
    fetch = [pltpu.make_async_copy(eg.at[m], ev.at[m], sem.at[m]) for m in range(3)]
    copies = [pltpu.make_async_copy(ev.at[m], out.at[0], sem.at[m]) for m, out in enumerate((eg0, eg1, eg2))]
    for cp in fetch: cp.start()
    gain = params[experts + 1:experts + 2, :].astype(f32)
    lane = lax.broadcasted_iota(jnp.int32, (tokens, 128), 1)
    routes = jnp.concatenate([ref[i] for ref in (lr, sr) for i in range(ref.shape[0])], axis=0)
    member = ((lane == routes[:, 0:1]) | (lane == routes[:, 1:2])).astype(f32)
    after = (lax.broadcasted_iota(jnp.int32, (tokens, tokens), 1) < lax.broadcasted_iota(jnp.int32, (tokens, tokens), 0)).astype(f32).astype(bf)
    place = jnp.dot(after, member.astype(bf), preferred_element_type=f32)
    kept = (member > 0.5) & (place < cap)
    slot = jnp.where(kept, place.astype(jnp.int32), -1)
    lgt = jnp.where(lane < experts, logits[...], -1e30)
    ex = jnp.exp(lgt - jnp.max(lgt, axis=1, keepdims=True))
    p = ex / jnp.sum(ex, axis=1, keepdims=True)
    chosen = member * p
    both = jnp.sum(chosen, axis=1, keepdims=True)
    gate = chosen / both
    fg = jnp.zeros((1, mid.shape[1]), f32)
    for t in range(2):
        at = slice(t * 256, t * 256 + 256)
        rows = pl.ds(t * 256, 256)
        g = rows_of(gl, gsh, t).astype(f32)
        m = mid[rows, :]
        fin[...] = m
        bk[...] = jnp.zeros_like(m)
        sh[...] = jnp.zeros_like(sh)
        s_iota = lax.broadcasted_iota(jnp.int32, (256, cap), 1)
        slot_t, weight_t, lane_t = slot[at], jnp.where(kept[at], gate[at], 0.0), lane[:256]
        @pl.loop(0, experts)
        def _(i):
            this = lane_t == i
            mine = jnp.sum(jnp.where(this, slot_t, 0), axis=1, keepdims=True)
            weight = jnp.sum(jnp.where(this, weight_t, 0.0), axis=1, keepdims=True)
            pick = (s_iota == mine).astype(f32).astype(bf)
            pair = jnp.dot(pick, eo[i], preferred_element_type=f32)
            fin[...] += weight * pair
            sh[...] = jnp.where(this, jnp.sum(rows_of(gl, gsh, t).astype(f32) * pair, axis=1, keepdims=True), sh[...])
            bk[...] += jnp.dot(pick, ri[i], preferred_element_type=f32)
        (lout, sout)[t][...] = fin[...].astype(bf).reshape(lout.shape)
        share, back = sh[...], bk[...]
        mean = jnp.sum(share * gate[at], axis=1, keepdims=True)
        pg = member[at] * (share - mean) / both[at]
        lgrad = (p[at] * (pg - jnp.sum(p[at] * pg, axis=1, keepdims=True))).astype(bf)
        lg[rows, :] = lgrad
        r2 = rms_scale(m)
        u = m * r2
        n2[rows, :] = (u * gain).astype(bf)
        back += jnp.dot(lgrad, params[...], preferred_element_type=f32)
        fg += jnp.sum(back * u, axis=0, keepdims=True)
        w = back * gain
        out = g + r2 * (w - u * jnp.mean(w * u, axis=-1, keepdims=True))
        midg[rows, :] = out
        bg[rows, :] = out.astype(bf)
        mg[rows, :] = dot(out.astype(bf), wo[...], 1, 1).astype(bf)
    for m in range(3):
        fetch[m].wait()
        copies[m].start()
    small[...] = jnp.zeros_like(small)
    small[1:2, :] = fg
    small[2:2 + experts, :] = dot(lg[...], n2[...], 0, 0)[:experts]
    wog[...] = dot(mixed[...], bg[...], 0, 0).astype(bf).reshape(wog.shape)
    lane = lax.broadcasted_iota(jnp.int32, (128, 128), 1)
    edge = jnp.full((128, 128), 4096, jnp.int32)
    for i, e in enumerate(EDGES):
        edge = jnp.where(lane == i, e, edge)
    edge = jnp.where(lane > len(EDGES), -4096, edge)
    def places(out, q_col, k_row):
        k_first = k_row[:, 0:1]
        t = lax.broadcasted_iota(jnp.int32, (128, 256), 1) + k_first
        below = jnp.sum((column_of(k_row) < t).astype(jnp.int32), axis=0, keepdims=True)
        at = jnp.clip(q_col + edge - k_first, 0, 255)
        lo = jnp.take_along_axis(jnp.broadcast_to(below[:, :128], (128, 128)), at & 127, axis=1)
        hi = jnp.take_along_axis(jnp.broadcast_to(below[:, 128:], (128, 128)), at & 127, axis=1)
        out[...] = jnp.where(at < 128, lo, hi) - 1
    me = lax.axis_index("seq")
    for b in range(nl):
        own = column_of(lpos[b:b + 1, pl.ds(pl.multiple_of(me * 128, 128), 128)])
        for c in range(blocks):
            places(li.at[b, c], own, lpos[b:b + 1, c * 128:(c + 1) * 128])
    for b in range(ns):
        places(si.at[b, 0], column_of(spos[b:b + 1, :]), spos[b:b + 1, :])
    for cp in copies: cp.wait()
def front(dims, nl, ns, experts, cap, pieces, table_part, gain_part, arrays, tokens, width, heads, cid):
    X, C, Z, Y = dims
    sm, vm, hbm = pl.BlockSpec(memory_space=pltpu.SMEM), pl.BlockSpec(memory_space=pltpu.VMEM), pl.BlockSpec(memory_space=pl.ANY)
    S, V, sem, bf, f32 = jax.ShapeDtypeStruct, pltpu.VMEM, pltpu.SemaphoreType.DMA, jnp.bfloat16, jnp.float32
    rows_part, small_shape = arrays[2].shape[0], arrays[6].shape
    whole = dims + (rows_part, width)
    slots = S((experts, cap, width), bf)
    rows, short, long = S((tokens, width), bf), S((ns * 128, width), bf), S((X * C, nl, 128, width), bf)
    outs = [S(whole, bf)] * 4 + [S((128, width), bf), S((heads, 1, 128), f32), rows, short, short, long, long, S((width, tokens), bf), rows,
            S((tokens, width), f32), slots, slots, S((tokens, 128), f32), S((nl, X * C, 128, 128), jnp.int32), S((ns, 1, 128, 128), jnp.int32)]
    n, kvn = len(pieces), 2 * (width // 256)
    scr = [V((4,) + whole, bf), V(dims + small_shape, bf)] + [V((tokens, width), bf)] * 3
    scr += [sem((n, Z)), sem((n, Z)), sem((n, 2)), sem((n, 2)), sem((n, 3)), sem((n, 3)), sem((kvn, 3)), sem((kvn, 3)), sem((4,))]
    return pl.pallas_call(functools.partial(front_kernel, dims, nl, ns, experts, cap, pieces, table_part, gain_part), out_shape=outs,
        in_specs=[sm, sm] + [vm] * (len(arrays) - 2), out_specs=[hbm] * 4 + [vm] * (len(outs) - 4), scratch_shapes=scr,
        compiler_params=pltpu.CompilerParams(collective_id=cid, has_side_effects=True, vmem_limit_bytes=60 * 2**20))(*arrays)
def small_rows(experts):
    return -(-(experts + 4) // 8) * 8
def post(nl, ns, blocks, experts, cap, whole, arrays, tokens, width):
    vm, hbm = pl.BlockSpec(memory_space=pltpu.VMEM), pl.BlockSpec(memory_space=pl.ANY)
    S, bf, f32 = jax.ShapeDtypeStruct, jnp.bfloat16, jnp.float32
    eg = arrays[-1]
    outs = [S((nl, 128, width), bf), S((ns, 128, width), bf), S((tokens, width), f32), S(whole, bf), S((small_rows(experts), width), f32), S((tokens, width), bf),
            S((nl, blocks, 128, 128), jnp.int32), S((ns, 1, 128, 128), jnp.int32)] + [S((1,) + eg.shape[1:], f32)] * 3
    V = pltpu.VMEM
    return pl.pallas_call(functools.partial(post_kernel, nl, ns, blocks, experts, cap), out_shape=outs,
        in_specs=[vm] * (len(arrays) - 1) + [hbm], out_specs=[vm] * (len(outs) - 3) + [hbm] * 3,
        scratch_shapes=[V((tokens, width), bf)] * 2 + [V((tokens, 128), bf)] + [V((256, width), f32)] * 2 + [V((256, 128), f32), V(eg.shape, f32), pltpu.SemaphoreType.DMA((3,))],
        compiler_params=pltpu.CompilerParams(vmem_limit_bytes=60 * 2**20))(*arrays)
def back_kernel(dims, nl, ns, experts, pieces, q, k, v, kl, vl, tab, lb, sb, li, si, mg, wog, n1t, lx, sx, params, wq, wk, wv, midg, small_in,
                lgrad, sgrad, og, qg, kg, vg, small, *refs):
    X, C, Z, Y = dims
    blocks = X * C
    f32, bf = jnp.float32, jnp.bfloat16
    np_ = len(pieces)
    bufs = refs[:4 * np_]
    (gw, dq, ka, va, dkl, dvl, kcb, ka1, kb1, seg, sacc, sbuf, cs, cr, hs, hr, zs, zr, kss, krs, sss, srs) = refs[4 * np_:]
    s = lax.axis_index("seq"); g = lax.axis_index("dp")
    x, c = s // C, lax.rem(s, C)
    z, y = g // Y, lax.rem(g, Y)
    def zdev(k): return (s, lax.rem(z + k, Z) * Y + y)
    ydev = (s, z * Y + (1 - y)); xdev = ((1 - x) * C + c, g); cdev = (x * C + 1 - c, g)
    greet([zdev(k) for k in range(1, Z)] + [ydev, xdev, cdev])
    half = nl * 128
    wide = 256
    nb = q.shape[1] // wide
    sources = [wog] + [gw.at[i] for i in range(3)]
    outs = [og, qg, kg, vg]
    first = {}; hh = {}; zz = {}
    def add(dst, a, b):
        dst[...] = (a.astype(f32) + b.astype(f32)).astype(dst.dtype)
    def send_core(i):
        m, c0, nc = pieces[i]
        first[i] = remote(sources[m].at[:, 1 - c, :, :, :, pl.ds(c0, nc)], bufs[4 * i], cs.at[i], cr.at[i], cdev)
    def stage(i, which):
        m, c0, nc = pieces[i]
        b0, b1, b2, b3 = bufs[4 * i:4 * i + 4]
        if which == 0:
            first[i].wait_recv()
            add(b0, sources[m][:, c, :, :, :, c0:c0 + nc], b0[...])
            hh[i, 0] = remote(b0.at[:, :, 1 - y], b1, hs.at[i, 0], hr.at[i, 0], ydev)
        elif which == 1:
            hh[i, 0].wait_recv()
            add(b1, b0[:, :, y], b1[...])
            hh[i, 1] = remote(b1.at[1 - x], b2, hs.at[i, 1], hr.at[i, 1], xdev)
        elif which == 2:
            hh[i, 1].wait_recv()
            add(b2, b1[x], b2[...])
            zz[i] = [remote(b2.at[lax.rem(z + k, Z)], b3.at[k - 1], zs.at[i, k], zr.at[i, k], zdev(k)) for k in range(1, Z)]
        else:
            tot = b2[z].astype(f32)
            for k in range(1, Z):
                zz[i][k - 1].wait_recv()
                tot += b3[k - 1].astype(f32)
            outs[m][:, c0:c0 + nc] = tot
    def piece(m, b):
        return [i for i, p in enumerate(pieces) if p[0] == m and (m == 0 or p[1] == b * wide)]
    def weight_grad(m, rows, b):
        cols = slice(b * wide, (b + 1) * wide)
        quarter = n1t.shape[0] // blocks
        for xx in range(X):
            for cc in range(C):
                part = jnp.dot(n1t[pl.ds((xx * C + cc) * quarter, quarter), :], rows[:, cols], preferred_element_type=f32)
                gw[m - 1, xx, cc, :, :, :, cols] = part.astype(bf).reshape(gw.shape[3:6] + (wide,))
        for i in piece(m, b):
            send_core(i)
    parts, wholes = (dkl, dvl), (ka, va)
    kf, kx = {}, {}
    def kv_core(b):
        cols = pl.ds(b * wide, wide)
        for far in range(2):
            for m in range(2):
                n = b * 2 + m
                at = (1 - x if far == 0 else x) * C + 1 - c
                kf[n, far] = remote(parts[m].at[at, :, :, cols], kcb.at[n, far], kss.at[n, far], krs.at[n, far], cdev)
    def kv_chip(b):
        for m in range(2):
            n = b * 2 + m
            kf[n, 0].wait_recv()
            add(ka1.at[n], parts[m][(1 - x) * C + c, :, :, b * wide:(b + 1) * wide], kcb[n, 0])
            kx[n] = remote(ka1.at[n], kb1.at[n], kss.at[n, 2], krs.at[n, 2], xdev)
    def kv_end(b):
        for m in range(2):
            n = b * 2 + m
            kf[n, 1].wait_recv(); kx[n].wait_recv()
            tot = parts[m][s, :, :, b * wide:(b + 1) * wide].astype(f32) + kcb[n, 1].astype(f32) + kb1[n].astype(f32)
            wholes[m][pl.ds(0, half), b * wide:(b + 1) * wide] = tot.astype(bf).reshape(half, wide)
        weight_grad(2, ka, b)
        weight_grad(3, va, b)
    def stages(which, b, *ms):
        for m in ms:
            for i in piece(m, b):
                stage(i, which)
    seg[...] = jnp.zeros_like(seg)
    lane = lax.broadcasted_iota(jnp.int32, (128, 128), 1)
    head_one = lane < 64
    tri = jnp.where(lax.broadcasted_iota(jnp.int32, (128, 128), 0) <= lane, 1.0, 0.0).astype(bf)
    def attend(b0):
        @pl.loop(0, wide // 128)
        def _(i):
            hp = b0 * (wide // 128) + i
            cols = pl.ds(pl.multiple_of(hp * 128, 128), 128)
            for b in range(nl + ns):
                rows, n, kk, vv = item(b, nl, blocks, cols, k, v, kl, vl)
                idx = mine_of(b, nl, li, si)
                qs = stack_heads(q[rows, cols], head_one); gs = stack_heads(mg[rows, cols], head_one)
                p = probs_of(qs, kk, (tab[2 * hp], tab[2 * hp + 1]), mine_of(b, nl, lb, sb), n)
                dp = dot(gs, vv, 1, 1)
                ds = (p * (dp - jnp.sum(p * dp, axis=1, keepdims=True))).astype(bf)
                dqs = dot(ds, kk, 1, 0)
                dkt = dot(qs, ds, 0, 0)
                dvt = dot(gs, p.astype(bf), 0, 0)
                sums = [0, 0]
                for c_ in range(n):
                    pre = dot(ds[:, c_ * 128:(c_ + 1) * 128], tri, 1, 0)
                    at = idx[c_]
                    for e in range(2):
                        sums[e] += jnp.where(at >= 0, jnp.take_along_axis(pre[e * 128:(e + 1) * 128], jnp.maximum(at, 0), axis=1), 0.0)
                for e in range(2):
                    seg[2 * hp + e] += jnp.sum(sums[e], axis=0, keepdims=True)
                dq[rows, cols] = jnp.where(head_one, dqs[:128], dqs[128:]).astype(bf)
                dkt = dkt.T.astype(bf); dvt = dvt.T.astype(bf)
                if b < nl:
                    dkl[:, b, :, cols] = dkt.reshape(n, 128, 128); dvl[:, b, :, cols] = dvt.reshape(n, 128, 128)
                else:
                    ka[rows, cols] = dkt; va[rows, cols] = dvt
    for i in piece(0, 0):
        send_core(i)
    attend(0)
    kv_core(0); weight_grad(1, dq, 0); stages(0, 0, 0)
    attend(1)
    kv_core(1); kv_chip(0); weight_grad(1, dq, 1); stages(0, 0, 1); stages(1, 0, 0)
    attend(2)
    kv_core(2); kv_chip(1); kv_end(0); weight_grad(1, dq, 2); stages(0, 1, 1); stages(1, 0, 1); stages(2, 0, 0)
    attend(3)
    kv_core(3); kv_chip(2); kv_end(1); weight_grad(1, dq, 3); stages(0, 0, 2, 3); stages(0, 2, 1); stages(1, 1, 1); stages(2, 0, 1)
    kv_chip(3); kv_end(2); stages(0, 1, 2, 3); stages(0, 3, 1); stages(1, 0, 2, 3); stages(1, 2, 1); stages(2, 1, 1); stages(3, 0, 0)
    kv_end(3); stages(0, 2, 2, 3); stages(1, 3, 1); stages(1, 1, 2, 3); stages(2, 2, 1); stages(2, 0, 2, 3); stages(3, 0, 1)
    gain = params[experts:experts + 1, :].astype(f32)
    ag = jnp.zeros((1, q.shape[1]), f32)
    for t in range(2):
        rows = pl.ds(t * half, half)
        ng = dot(dq[rows, :], wq[...], 1, 1) + dot(ka[rows, :], wk[...], 1, 1) + dot(va[rows, :], wv[...], 1, 1)
        m = rows_of(lx, sx, t).astype(f32)
        r1 = rms_scale(m)
        u = m * r1
        ag += jnp.sum(ng * u, axis=0, keepdims=True)
        w = ng * gain
        (lgrad, sgrad)[t][...] = (midg[rows, :] + r1 * (w - u * jnp.mean(w * u, axis=-1, keepdims=True))).reshape(lgrad.shape)
        if t == 0:
            stages(0, 3, 2, 3); stages(1, 2, 2, 3); stages(2, 3, 1); stages(2, 1, 2, 3); stages(3, 1, 1)
    sacc[0] = small_in[...]
    sacc[0, 0:1, :] = ag
    heads = seg.shape[0]
    spot = lax.broadcasted_iota(jnp.int32, (8, 128), 1)
    for h in range(heads):
        upto = jnp.broadcast_to(seg[h], (8, 128))
        within = upto - jnp.where(spot == 0, 0.0, pltpu.roll(upto, 1, 1))
        at = jnp.where(spot < 16, 15 - spot, jnp.minimum(spot - 1, 30))
        by_bucket = jnp.where((spot == 16) | (spot >= 32), 0.0, jnp.take_along_axis(within, at, axis=1))
        r = 2 + experts + h // 8
        sacc[0, r:r + 1, (h % 8) * 128:(h % 8 + 1) * 128] = by_bucket[0:1, :]
    sc = remote(sacc.at[0], sbuf.at[0], sss.at[0], srs.at[0], cdev)
    stages(1, 3, 2, 3); stages(2, 2, 2, 3); stages(3, 2, 1)
    sc.wait_recv()
    sacc[1] = sacc[0] + sbuf[0]
    sx_ = remote(sacc.at[1], sbuf.at[1], sss.at[1], srs.at[1], xdev)
    stages(2, 3, 2, 3); stages(3, 3, 1); stages(3, 0, 2, 3)
    sx_.wait_recv()
    sacc[2] = sacc[1] + sbuf[1]
    sy = remote(sacc.at[2], sbuf.at[2], sss.at[2], srs.at[2], ydev)
    stages(3, 1, 2, 3)
    sy.wait_recv()
    sacc[3] = sacc[2] + sbuf[2]
    sz = [remote(sacc.at[3], sbuf.at[2 + k], sss.at[2 + k], srs.at[2 + k], zdev(k)) for k in range(1, Z)]
    stages(3, 2, 2, 3); stages(3, 3, 2, 3)
    tot = sacc[3]
    for k in range(1, Z):
        sz[k - 1].wait_recv()
        tot += sbuf[2 + k]
    small[...] = tot
    for cp in [sc, sx_, sy] + sz + list(kx.values()) + list(kf.values()) + list(first.values()) + list(hh.values()) + [w for v_ in zz.values() for w in v_]:
        cp.wait_send()
def back(dims, nl, ns, experts, arrays, cid):
    X, C, Z, Y = dims
    q_, small_in = arrays[0], arrays[-1]
    tokens, width = q_.shape
    heads = arrays[5].shape[0]
    nr = width // (X * C * Z * Y)
    wide = 256
    pieces = tuple((0, h * 512, 512) for h in range(width // 512)) + tuple((m, b * wide, wide) for m in range(1, 4) for b in range(width // wide))
    n = len(pieces)
    S, sem, bf, f32 = jax.ShapeDtypeStruct, pltpu.SemaphoreType.DMA, jnp.bfloat16, jnp.float32
    V = pltpu.VMEM
    scr = [V(lead + (nr, nc), bf) for m, c0, nc in pieces for lead in ((X, Z, Y), (X, Z), (Z,), (Z - 1,))]
    kvn = 2 * (width // wide)
    long = V((X * C, nl, 128, width), bf)
    rows = V((tokens, width), bf)
    scr += [V((3, X, C, Z, Y, nr, width), bf), rows, rows, rows, long, long,
            V((kvn, 2, nl, 128, wide), bf), V((kvn, nl, 128, wide), bf), V((kvn, nl, 128, wide), bf), V((heads, 1, 128), f32),
            V((4,) + small_in.shape, f32), V((Z + 2,) + small_in.shape, f32),
            sem((n,)), sem((n,)), sem((n, 2)), sem((n, 2)), sem((n, Z)), sem((n, Z)), sem((kvn, 3)), sem((kvn, 3)), sem((Z + 2,)), sem((Z + 2,))]
    vm = pl.BlockSpec(memory_space=pltpu.VMEM)
    outs = [S((nl, 128, width), f32), S((ns, 128, width), f32)] + [S((nr, width), f32)] * 4 + [S(small_in.shape, f32)]
    return pl.pallas_call(functools.partial(back_kernel, dims, nl, ns, experts, pieces), out_shape=outs,
        in_specs=[vm] * len(arrays), out_specs=[vm] * len(outs), scratch_shapes=scr,
        compiler_params=pltpu.CompilerParams(collective_id=cid, has_side_effects=True, vmem_limit_bytes=63 * 2**20))(*arrays)

def gelu_parts(v):
    c, a = 0.7978845608, 0.044715
    v2 = v * v
    h = 0.5 + 0.5 * jnp.tanh(v * (c + (c * a) * v2))
    act = v * h
    return act, h + act * (1.0 - h) * (2.0 * c + (6.0 * c * a) * v2)
RING, LAG = 6, 4
SEND_AT, JOIN_AT = 2, 3
def expert_kernel(cap, per, order, todo, wcut, tile, xs, gs, wgi, wui, wdi, eo_out, ri_out, grads, eo_h, ri_h,
                  wall, xr, gr, hall, lall, eo, ri, cb, ab, xb, ob,
                  lsem, xss, xrs, gss, grs, ess, ers, rss, rrs, wss, wrs, wls, css, crs, ass, ars, osem, free):
    dp = lax.axis_size("dp")
    f32, bf = jnp.float32, jnp.bfloat16
    s, x, c, xdev, cdev = seq_places(2)
    g = lax.axis_index("dp")
    def peer(k): return (s, g ^ k)
    greet([xdev, cdev] + [peer(k) for k in range(1, dp)])
    rows_w, ff = wgi.shape; width = xs.shape[2]
    wx, wc, wl, wf = [], [], [], []
    shared = ((wgi, 1), (wui, 2), (wdi, 0))
    parts = [(src, m, f0, nf) for f0, nf in wcut for src, m in shared]
    for n, (src, m, f0, nf) in enumerate(parts):
        a = src.at[:, pl.ds(f0, nf)]
        b = wall.at[m, x, c, :, pl.ds(f0, nf)]
        wx.append(remote(a, b, wss.at[n, 0], wrs.at[n, 0], xdev))
        wc.append(remote(a, b, wss.at[n, 1], wrs.at[n, 1], cdev))
        cp = pltpu.make_async_copy(a, b, wls.at[n]); cp.start(); wl.append(cp)
    sx, sg = {}, {}
    def dispatch(p):
        for k in range(p * per, (p + 1) * per):
            at = pl.ds(k * cap, cap)
            if k == 0:
                sx[0] = pltpu.make_async_copy(xs.at[g], xr.at[at], lsem.at[0]); sx[0].start()
                sg[0] = pltpu.make_async_copy(gs.at[g], gr.at[at], lsem.at[1]); sg[0].start()
            else:
                sx[k] = remote(xs.at[g ^ k], xr.at[at], xss.at[k], xrs.at[k], peer(k))
                sg[k] = remote(gs.at[g ^ k], gr.at[at], gss.at[k], grs.at[k], peer(k))
    for p in order[:-1]: dispatch(p)
    ntile = ff // tile
    re, rr = {}, {}
    wide = 4 * rows_w
    def sources(p): return list(range(p * per, (p + 1) * per))
    def arrive(p):
        for k in sources(p):
            if k == 0: sx[0].wait(); sg[0].wait()
            else: sx[k].wait_recv(); sg[k].wait_recv()
    def inner(p, t0, nt):
        rows = pl.ds(p * per * cap, per * cap)
        @pl.loop(t0, t0 + nt)
        def _(t):
            cols = pl.ds(pl.multiple_of(t * tile, 128), tile)
            w = lambda m: wall[m, :, :, :, cols].reshape(wide, tile)
            gp = jnp.dot(xr[rows, :], w(1), preferred_element_type=f32)
            up = jnp.dot(xr[rows, :], w(2), preferred_element_type=f32)
            hg = jnp.dot(gr[rows, :], w(0), preferred_element_type=f32)
            act, der = gelu_parts(gp)
            hall[0, rows, cols] = (act * up).astype(bf)
            hall[1, rows, cols] = (hg * up * der).astype(bf)
            hall[2, rows, cols] = (hg * act).astype(bf)
    def outer(p):
        rows = pl.ds(p * per * cap, per * cap)
        @pl.loop(0, 4)
        def _(t):
            part = pl.ds(pl.multiple_of(t * rows_w, 128), rows_w)
            tx, tc = t // 2, lax.rem(t, 2)
            eo[:, part] = dot(hall[0, rows, :], wall[0, tx, tc], 1, 1).astype(bf)
            ri[:, part] = (dot(hall[1, rows, :], wall[1, tx, tc], 1, 1) + dot(hall[2, rows, :], wall[2, tx, tc], 1, 1)).astype(bf)
        keep = [pltpu.make_async_copy(eo, eo_h.at[rows], lsem.at[4]), pltpu.make_async_copy(ri, ri_h.at[rows], lsem.at[5])]
        for cp in keep: cp.start()
        for cp in keep: cp.wait()
        for k in sources(p):
            at = pl.ds(k * cap, cap)
            if k == 0:
                re[0] = pltpu.make_async_copy(eo_h.at[at], eo_out.at[g], lsem.at[2]); re[0].start()
                rr[0] = pltpu.make_async_copy(ri_h.at[at], ri_out.at[g], lsem.at[3]); rr[0].start()
            else:
                re[k] = remote(eo_h.at[at], eo_out.at[g], ess.at[k], ers.at[k], peer(k))
                rr[k] = remote(ri_h.at[at], ri_out.at[g], rss.at[k], rrs.at[k], peer(k))
    early = list(todo[:-2])
    last = todo[-1]
    for i, (f0, nf) in enumerate(wcut):
        mine = range(3 * i, 3 * i + 3)
        for n in mine:
            wx[n].wait_recv()
            src, m, f0, nf = parts[n]
            b = wall.at[m, 1 - x, c, :, pl.ds(f0, nf)]
            wf.append(remote(b, b, wss.at[n, 2], wrs.at[n, 2], cdev))
        if i == SEND_AT: dispatch(last)
        if i == 0:
            for p in early: arrive(p)
        for n in mine:
            wl[n].wait(); wc[n].wait_recv(); wf[n].wait_recv()
        for p in early: inner(p, f0 // tile, nf // tile)
        if i == JOIN_AT:
            p = todo[-2]
            arrive(p)
            inner(p, 0, (f0 + nf) // tile)
            early.append(p)
    for p in early[::-1]: outer(p)
    arrive(last)
    inner(last, 0, ntile)
    outer(last)
    for n in range(len(parts)):
        wx[n].wait_send(); wc[n].wait_send(); wf[n].wait_send()
    total = dp * cap
    @pl.loop(0, total // 256)
    def _(t):
        at = pl.ds(pl.multiple_of(t * 256, 256), 256)
        lall[1, :, at] = xr[at, :].T
        lall[0, :, at] = gr[at, :].T
    nt = 3 * ntile
    def place(n):
        m = n // ntile
        return m, pl.ds(pl.multiple_of((n - m * ntile) * tile, 128), tile)
    def to_core(n):
        m, cols = place(n); r = lax.rem(n, RING)
        return pltpu.make_async_remote_copy(src_ref=wall.at[m, :, 1 - c, :, cols], dst_ref=cb.at[r], send_sem=css.at[r],
            recv_sem=crs.at[r], device_id=cdev, device_id_type=MESH)
    def to_chip(n):
        r = lax.rem(n, RING)
        return pltpu.make_async_remote_copy(src_ref=ab.at[r], dst_ref=xb.at[r], send_sem=ass.at[r],
            recv_sem=ars.at[r], device_id=xdev, device_id_type=MESH)
    def to_out(n):
        m, cols = place(n); r = lax.rem(n, 2)
        return pltpu.make_async_copy(ob.at[r], grads.at[m, :, cols], osem.at[r])
    @pl.loop(0, nt + LAG)
    def _(n):
        @pl.when(n < nt)
        def _():
            m, cols = place(n)
            res = jnp.dot(lall[jnp.minimum(m, 1)], hall[m, :, cols], preferred_element_type=f32)
            wall[m, :, :, :, cols] = res.astype(bf).reshape(2, 2, rows_w, tile)
            @pl.when(n >= RING)
            def _(): pl.semaphore_wait(free.at[0], 1)
            to_core(n).start()
        @pl.when((n >= 1) & (n <= nt))
        def _():
            i = n - 1
            m, cols = place(i); r = lax.rem(i, RING)
            to_core(i).wait_recv()
            @pl.when(i >= RING)
            def _():
                to_chip(i).wait_send()
                pl.semaphore_wait(free.at[1], 1)
            ab[r] = (wall[m, 1 - x, c, :, cols].astype(f32) + cb[r, 1 - x].astype(f32)).astype(bf)
            to_chip(i).start()
        @pl.when(n >= LAG)
        def _():
            j = n - LAG
            m, cols = place(j); r = lax.rem(j, RING)
            to_chip(j).wait_recv()
            to_core(j).wait_send()
            @pl.when(j >= 2)
            def _(): to_out(j).wait()
            ob[lax.rem(j, 2)] = wall[m, x, c, :, cols].astype(f32) + cb[r, x].astype(f32) + xb[r].astype(f32)
            to_out(j).start()
            @pl.when(j < nt - RING)
            def _():
                pl.semaphore_signal(free.at[0], inc=1, device_id=cdev, device_id_type=MESH)
                pl.semaphore_signal(free.at[1], inc=1, device_id=xdev, device_id_type=MESH)
    for j in range(nt - 2, nt): to_out(j).wait()
    for i in range(nt - RING, nt): to_chip(i).wait_send()
    for k in range(dp):
        if k == 0:
            re[0].wait(); rr[0].wait()
        else:
            sx[k].wait_send(); sg[k].wait_send(); re[k].wait(); rr[k].wait()
def expert_all(xs, gs, wg, wu, wd, seq, cid):
    dp, cap, width = xs.shape
    rows_w, ff = wg.shape; total = dp * cap
    group = 320
    per = group // cap
    ng = dp // per
    order = [ng - 2] + [p for p in range(ng - 3, -1, -1)] + [ng - 1]
    todo = list(range(ng))
    sem = pltpu.SemaphoreType.DMA
    bf = jnp.bfloat16
    any_ = pl.BlockSpec(memory_space=pl.ANY)
    V = pltpu.VMEM
    tile = 256
    wcut = tuple((f0, min(512, ff - f0)) for f0 in range(0, ff, 512))
    nw = 3 * len(wcut)
    back = jax.ShapeDtypeStruct((dp, cap, width), bf)
    flat = jax.ShapeDtypeStruct((total, width), bf)
    return pl.pallas_call(functools.partial(expert_kernel, cap, per, order, todo, wcut, tile),
        out_shape=[back, back, jax.ShapeDtypeStruct((3, rows_w, ff), jnp.float32), flat, flat],
        in_specs=[any_] * 5, out_specs=[any_] * 5,
        scratch_shapes=[V((3, seq // 2, 2, rows_w, ff), bf), V((total, width), bf), V((total, width), bf), V((3, total, ff), bf),
        V((2, width, total), bf), V((group, width), bf), V((group, width), bf),
        V((RING, seq // 2, rows_w, tile), bf), V((RING, rows_w, tile), bf), V((RING, rows_w, tile), bf), V((2, rows_w, tile), jnp.float32)]
        + [sem((6,))] + [sem((dp,))] * 8 + [sem((nw, 3))] * 2 + [sem((nw,))] + [sem((RING,))] * 4 + [sem((2,)), pltpu.SemaphoreType.REGULAR((2,))],
        compiler_params=pltpu.CompilerParams(collective_id=cid, has_side_effects=True, vmem_limit_bytes=63 * 2**20))(xs, gs, wg, wu, wd)[:3]


def on_device(
    long_tokens,
    short_tokens,
    long_grad_out,
    short_grad_out,
    query_weight,
    key_weight,
    value_weight,
    output_weight,
    attn_gain,
    ffn_gain,
    rel_table,
    router_weight,
    gate_weight,
    up_weight,
    down_weight,
    long_positions,
    short_positions,
    long_lengths,
    short_lengths,
    long_routes,
    short_routes,
):
    long_items, quarter, model_width = long_tokens.shape
    short_items, short_len = (short_tokens.shape[0], short_tokens.shape[1])
    long_rows = long_items * quarter
    tokens = long_rows + short_items * short_len
    local_experts = gate_weight.shape[0]
    dp_size = lax.axis_size("dp")
    experts = local_experts * dp_size
    capacity = (5 * tokens + 2 * experts - 1) // (2 * experts)
    seq_size = lax.axis_size("seq")
    dims = (seq_size // 2, 2, dp_size // 2, 2)
    devices = seq_size * dp_size
    table_part, gain_part = rel_table.shape[0], attn_gain.shape[0]
    small = jnp.concatenate([router_weight.T, attn_gain[None], ffn_gain[None]], 0)
    small = jnp.pad(small, ((0, 1), (0, 128 - gain_part)))
    table_row = jnp.pad(rel_table[None], ((experts + 2, 0), (0, 128 - table_part)))
    small = jnp.pad(small + table_row, ((0, -(experts + 3) % 16), (0, 0)))
    rows_part = query_weight.shape[0]
    cuts = 2 if rows_part % 32 == 0 else 1
    cut = rows_part // cuts
    pieces = tuple((m, h * cut, cut, (m + h) % 2) for m in range(4) for h in range(cuts))
    pieces = ((4, 0, small.shape[0], 0),) + pieces
    sizes = (long_items, short_items, seq_size, experts, capacity)
    places = (long_positions, short_positions)
    routes = (long_routes, short_routes)
    (
        key_all,
        value_all,
        query_all,
        output_all,
        params,
        table,
        queries,
        keys,
        values,
        long_keys,
        long_values,
        normed_t,
        mixed,
        middle,
        outgoing,
        out_slots,
        logits,
        long_buckets,
        short_buckets,
    ) = front(
        dims,
        long_items,
        short_items,
        experts,
        capacity,
        pieces,
        table_part,
        gain_part,
        (long_lengths, short_lengths, key_weight, value_weight, query_weight, output_weight, small)
        + places
        + (long_tokens, short_tokens, long_grad_out, short_grad_out)
        + routes,
        tokens,
        model_width,
        HEADS,
        0,
    )
    key_all, value_all, query_all, output_all = (
        block.reshape(devices * rows_part, model_width)
        for block in (key_all, value_all, query_all, output_all)
    )
    heads_args = (queries, keys, values, long_keys, long_values, table)
    grads = (long_grad_out, short_grad_out, output_all, params)
    back_rows, back_grads, expert_grads = expert_all(
        outgoing, out_slots, gate_weight[0], up_weight[0], down_weight[0], seq_size, 4
    )
    (
        long_out,
        short_out,
        middle_grad,
        output_local,
        small_local,
        mixed_grad,
        long_places,
        short_places,
        down_grad,
        gate_grad,
        up_grad,
    ) = post(
        *sizes,
        dims + (rows_part, model_width),
        places + (back_rows, back_grads, middle, mixed, logits) + routes + grads + (expert_grads,),
        tokens,
        model_width,
    )
    long_grad_in, short_grad_in, output_grad, query_grad, key_grad, value_grad, small_sum = back(
        dims,
        long_items,
        short_items,
        experts,
        heads_args
        + (long_buckets, short_buckets, long_places, short_places)
        + (mixed_grad, output_local, normed_t, long_tokens, short_tokens, params)
        + (query_all, key_all, value_all, middle_grad, small_local),
        2,
    )
    place = lax.axis_index("seq") * dp_size + lax.axis_index("dp")

    def own(row, column, size, count=1):
        return lax.dynamic_slice(small_sum, (row, column), (count, size))

    entry = place * table_part
    head_at = entry // BUCKETS
    table_grad = own(2 + experts + head_at // 8, head_at % 8 * 128 + entry % BUCKETS, table_part)
    summed = (
        query_grad,
        key_grad,
        value_grad,
        output_grad,
        own(0, place * gain_part, gain_part)[0],
        own(1, place * gain_part, gain_part)[0],
        table_grad[0],
        own(2, place * rows_part, rows_part, experts).T,
    )
    return (
        long_out,
        short_out,
        long_grad_in,
        short_grad_in,
        summed[0],
        summed[1],
        summed[2],
        summed[3],
        summed[4],
        summed[5],
        summed[6],
        summed[7],
        gate_grad,
        up_grad,
        down_grad,
    )


def solution(mesh):
    placed = (
        P("dp", "seq", None),
        P(("seq", "dp"), None, None),
        P("dp", "seq", None),
        P(("seq", "dp"), None, None),
        P(("seq", "dp"), None),
        P(("seq", "dp"), None),
        P(("seq", "dp"), None),
        P(("seq", "dp"), None),
        P(("seq", "dp")),
        P(("seq", "dp")),
        P(("seq", "dp")),
        P(("seq", "dp"), None),
        P("dp", "seq", None),
        P("dp", "seq", None),
        P("dp", "seq", None),
        P("dp", None),
        P(("seq", "dp"), None),
        P("dp"),
        P(("seq", "dp")),
        P("dp", "seq", None),
        P(("seq", "dp"), None, None),
    )
    return jax.shard_map(
        on_device,
        mesh=mesh,
        in_specs=placed,
        out_specs=(
            P("dp", "seq", None),
            P(("seq", "dp"), None, None),
            P("dp", "seq", None),
            P(("seq", "dp"), None, None),
            P(("seq", "dp"), None),
            P(("seq", "dp"), None),
            P(("seq", "dp"), None),
            P(("seq", "dp"), None),
            P(("seq", "dp")),
            P(("seq", "dp")),
            P(("seq", "dp")),
            P(("seq", "dp"), None),
            P("dp", "seq", None),
            P("dp", "seq", None),
            P("dp", "seq", None),
        ),
        check_vma=False,
    )
```

```python
import functools

import jax
import jax.numpy as jnp
from jax import lax
from jax.experimental import pallas as pl
from jax.experimental.pallas import tpu as pltpu
from jax.sharding import PartitionSpec as P

MESH = pl.DeviceIdType.MESH

HEADS = 16
HEAD = 64
BUCKETS = 32


epsilon = 1e-06
masked = -1e30


def seq_places(C):
    s = lax.axis_index("seq"); g = lax.axis_index("dp")
    x, c = s // C, lax.rem(s, C)
    return s, x, c, ((1 - x) * C + c, g), (x * C + 1 - c, g)
def greet(devs):
    bar = pltpu.get_barrier_semaphore()
    for d in devs:
        pl.semaphore_signal(bar, inc=1, device_id=d, device_id_type=MESH)
    pl.semaphore_wait(bar, len(devs))
def remote(src, dst, ss, rs, dev):
    cp = pltpu.make_async_remote_copy(src_ref=src, dst_ref=dst, send_sem=ss, recv_sem=rs, device_id=dev, device_id_type=MESH)
    cp.start()
    return cp
EDGES = (-90, -63, -45, -31, -22, -15, -11, -7, -6, -5, -4, -3, -2, -1, 0, 1, 2, 3, 4, 5, 6, 7, 8, 12, 16, 23, 32, 46, 64, 91)
FAR = (12, 16, 23, 32, 46, 64, 91)
def fill_buckets(out, q_col, k_row, length, base):
    r = k_row - q_col
    n = jnp.abs(r)
    far = jnp.full(r.shape, 8, jnp.int32)
    for e in FAR:
        far += (n >= e).astype(jnp.int32)
    b = jnp.where(n < 8, n, far) + jnp.where(r > 0, 16, 0)
    j = lax.broadcasted_iota(jnp.int32, r.shape, 1) + base
    out[...] = jnp.where(j < length, b, 32)
def dot(a, b, ca, cb):
    return lax.dot_general(a, b, (((ca,), (cb,)), ((), ())), preferred_element_type=jnp.float32)
def probs_of(qs, kk, tabs, bucket_ref, blocks):
    s = dot(qs, kk, 1, 1)
    t = [jnp.broadcast_to(tab, (128, 128)) for tab in tabs]
    bias = [jnp.concatenate([jnp.take_along_axis(x, bucket_ref[c], axis=1) for x in t], axis=0) for c in range(blocks)]
    s = s + (jnp.concatenate(bias, axis=1) if blocks > 1 else bias[0])
    p = jnp.exp(s - jnp.max(s, axis=1, keepdims=True))
    return p * (1.0 / jnp.sum(p, axis=1, keepdims=True))
def stack_heads(rows, first):
    return jnp.concatenate([jnp.where(first, rows, 0), jnp.where(first, 0, rows)], axis=0)
def column_of(row):
    i = lax.broadcasted_iota(jnp.int32, (128, 128), 0)
    return jnp.sum(jnp.where(i == lax.broadcasted_iota(jnp.int32, (128, 128), 1), row, 0), axis=1, keepdims=True)
def row_of(col):
    i = lax.broadcasted_iota(jnp.int32, (128, 128), 0)
    return jnp.sum(jnp.where(i == lax.broadcasted_iota(jnp.int32, (128, 128), 1), col, 0), axis=0, keepdims=True)
def rows_of(long_ref, short_ref, t):
    ref = long_ref if t == 0 else short_ref
    return ref[...].reshape(ref.shape[0] * ref.shape[1], ref.shape[2])
def rms_scale(mid):
    return lax.rsqrt(jnp.mean(mid * mid, axis=-1, keepdims=True) + epsilon)
def item(b, nl, blocks, cols, k, v, kl, vl):
    rows = pl.ds(b * 128, 128)
    if b < nl:
        return rows, blocks, kl[:, b, :, cols].reshape(blocks * 128, 128), vl[:, b, :, cols].reshape(blocks * 128, 128)
    short = pl.ds((b - nl) * 128, 128)
    return rows, 1, k[short, cols], v[short, cols]
def mine_of(b, nl, long_ref, short_ref):
    return long_ref.at[b] if b < nl else short_ref.at[b - nl]
def front_kernel(dims, nl, ns, experts, cap, pieces, table_part, gain_part, ll, sl, wk_in, wv_in, wq_in, wo_in, small_in, lpos, spos, xl, xsh, gl, gsh, lr, sr,
                 wk_out, wv_out, wq_out, wo_out, params, tab, q, ks, vs, kl, vl, n1t, mixed, mid, xs, gs, logits, lb, sb,
                 wall, sm, n1, n2, gb, zs, zr, hs, hr, cs, cr, kss, krs, osem):
    X, C, Z, Y = dims
    blocks = X * C
    f32, bf = jnp.float32, jnp.bfloat16
    s, x, c, xdev, cdev = seq_places(C)
    g = lax.axis_index("dp")
    z, y = g // Y, lax.rem(g, Y)
    def zdev(k): return (s, lax.rem(z + k, Z) * Y + y)
    ydev = (s, z * Y + (1 - y))
    tokens, width = q.shape
    half = nl * 128
    wide = 256
    nb = width // wide
    greet([zdev(k) for k in range(1, Z)] + [ydev, xdev, cdev])
    ins = (wk_in, wv_in, wq_in, wo_in)
    def part(i, *lead):
        m, r0, nr, route = pieces[i]
        if m == 4:
            return sm.at[lead + (slice(None),) * (4 - len(lead))]
        return wall.at[(m,) + lead + (slice(None),) * (4 - len(lead)) + (pl.ds(r0, nr),)]
    zc, h, cc = {}, {}, {}
    for i, (m, r0, nr, route) in enumerate(pieces):
        src = small_in if m == 4 else ins[m].at[pl.ds(r0, nr)]
        zc[i] = [remote(src, part(i, x, c, z, y), zs.at[i, k], zr.at[i, k], zdev(k)) for k in range(1, Z)]
    for m in range(4):
        wall[m, x, c, z, y] = ins[m][...]
    sm[x, c, z, y] = small_in[...]
    def gather_stage(i, stage):
        route = pieces[i][3]
        if stage == 0:
            for k in range(1, Z): zc[i][k - 1].wait_recv()
            mine = part(i, x, c, slice(None), y)
            h[i, 0] = remote(mine, mine, hs.at[i, 0], hr.at[i, 0], xdev if route == 0 else ydev)
            cc[i, 0] = remote(mine, mine, cs.at[i, 0], cr.at[i, 0], cdev)
        elif stage == 1:
            h[i, 0].wait_recv()
            if route == 0:
                both, got = part(i, slice(None), c, slice(None), y), part(i, 1 - x, c, slice(None), y)
            else:
                both, got = part(i, x, c), part(i, x, c, slice(None), 1 - y)
            h[i, 1] = remote(both, both, hs.at[i, 1], hr.at[i, 1], ydev if route == 0 else xdev)
            cc[i, 1] = remote(got, got, cs.at[i, 1], cr.at[i, 1], cdev)
        else:
            h[i, 1].wait_recv()
            got = part(i, slice(None), c, slice(None), 1 - y) if route == 0 else part(i, 1 - x, c)
            cc[i, 2] = remote(got, got, cs.at[i, 2], cr.at[i, 2], cdev)
    np_ = len(pieces)
    steps = [(t - st, st) for t in range(np_ + 2) for st in range(3) if 0 <= t - st < np_]
    done = [0]
    def gather_until(m):
        last = max(i for i, p in enumerate(pieces) if p[0] == m)
        while True:
            i, st = steps[done[0]]
            gather_stage(i, st)
            done[0] += 1
            if (i, st) == (last, 2): break
        for i, p in enumerate(pieces):
            if p[0] == m:
                for k in range(3): cc[i, k].wait_recv()
    kept_copies = []
    def keep(m, out):
        cp = pltpu.make_async_copy(wall.at[m], out, osem.at[m]); cp.start(); kept_copies.append(cp)
    def w_of(m):
        return wall[m].reshape(width, width)
    for b in range(nl):
        own = column_of(lpos[b:b + 1, pl.ds(pl.multiple_of(s * 128, 128), 128)])
        for k in range(blocks):
            fill_buckets(lb.at[b, k], own, lpos[b:b + 1, k * 128:(k + 1) * 128], ll[b], k * 128)
    for b in range(ns):
        fill_buckets(sb.at[b, 0], column_of(spos[b:b + 1, :]), spos[b:b + 1, :], sl[b], 0)
    gather_until(4)
    flat = sm[...].astype(f32).reshape(X * C * Z * Y, sm.shape[4], 128)
    per = 128 // gain_part
    def shifted(rows, n):
        return rows if n == 0 else pltpu.roll(rows, n, 1)
    chunks = []
    for k in range(width // 128):
        chunks.append(sum(shifted(flat[k * per + i], i * gain_part) for i in range(per)))
    found = jnp.concatenate(chunks, axis=1)
    params[...] = jnp.zeros_like(params)
    params[0:found.shape[0], :] = found.astype(bf)
    share = 32 // table_part
    lane8 = lax.broadcasted_iota(jnp.int32, (1, 128), 1)
    for hd in range(tab.shape[0]):
        rows = sum(shifted(flat[hd * share + i], i * table_part) for i in range(share))
        tab[hd] = jnp.where(lane8 < 32, rows[experts + 2:experts + 3, :], masked)
    gain = params[experts:experts + 1, :].astype(f32)
    for t in range(2):
        m = rows_of(xl, xsh, t).astype(f32)
        n1[pl.ds(t * half, half), :] = (m * rms_scale(m) * gain).astype(bf)
        gb[pl.ds(t * half, half), :] = rows_of(gl, gsh, t)
    wholes = (kl, vl)
    far = (1 - x) * C + c
    ka, kc, kf = {}, {}, {}
    def project(m, t):
        return jnp.dot(n1[pl.ds(t * half, half), :], w_of(m), preferred_element_type=f32).astype(bf)
    for m in range(2):
        gather_until(m)
        wholes[m][s] = project(m, 0).reshape(nl, 128, width)
        for b in range(nb):
            n = m * nb + b
            src = wholes[m].at[s, :, :, pl.ds(b * wide, wide)]
            ka[n] = remote(src, src, kss.at[n, 0], krs.at[n, 0], xdev)
            kc[n] = remote(src, src, kss.at[n, 1], krs.at[n, 1], cdev)
        keep(m, (wk_out, wv_out)[m])
    ks[...] = project(0, 1)
    vs[...] = project(1, 1)
    for t in range(2):
        n1t[:, t * half:(t + 1) * half] = n1[pl.ds(t * half, half), :].T
    gather_until(2)
    for t in range(2):
        q[pl.ds(t * half, half), :] = project(2, t)
    keep(2, wq_out)
    first = lax.broadcasted_iota(jnp.int32, (128, 128), 1) < 64
    for b0 in range(nb):
        for n in (b0, nb + b0):
            ka[n].wait_recv()
            got = wholes[n // nb].at[far, :, :, pl.ds(b0 * wide, wide)]
            kf[n] = remote(got, got, kss.at[n, 2], krs.at[n, 2], cdev)
        for n in (b0, nb + b0):
            kc[n].wait_recv(); kf[n].wait_recv()
        @pl.loop(0, wide // 128)
        def _(i):
            hp = b0 * (wide // 128) + i
            cols = pl.ds(pl.multiple_of(hp * 128, 128), 128)
            for b in range(nl + ns):
                rows, n, kk, vv = item(b, nl, blocks, cols, ks, vs, kl, vl)
                p = probs_of(stack_heads(q[rows, cols], first), kk, (tab[2 * hp], tab[2 * hp + 1]), mine_of(b, nl, lb, sb), n)
                out = dot(p.astype(bf), vv, 1, 0)
                mixed[rows, cols] = jnp.where(first, out[:128], out[128:]).astype(bf)
        if b0 == 0:
            gather_until(3)
            keep(3, wo_out)
    gain = params[experts + 1:experts + 2, :].astype(f32)
    for t in range(2):
        rows = pl.ds(t * 256, 256)
        m = rows_of(xl, xsh, t).astype(f32) + jnp.dot(mixed[rows, :], w_of(3), preferred_element_type=f32)
        mid[rows, :] = m
        n2[rows, :] = (m * rms_scale(m) * gain).astype(bf)
    logits[...] = dot(n2[...], params[...], 1, 1)
    logit_t = dot(params[...], n2[...], 1, 1)[:experts]
    routes = [jnp.concatenate([row_of(ref[i, :, j:j + 1]) for ref in (lr, sr) for i in range(ref.shape[0])], axis=1) for j in range(2)]
    e_iota = lax.broadcasted_iota(jnp.int32, (experts, tokens), 0)
    member = ((e_iota == routes[0]) | (e_iota == routes[1])).astype(f32)
    e = jnp.exp(logit_t - jnp.max(logit_t, axis=0, keepdims=True))
    p = e / jnp.sum(e, axis=0, keepdims=True)
    chosen = member * p
    before = (lax.broadcasted_iota(jnp.int32, (tokens, tokens), 0) < lax.broadcasted_iota(jnp.int32, (tokens, tokens), 1)).astype(f32).astype(bf)
    place = jnp.dot(member.astype(bf), before, preferred_element_type=f32)
    kept = (member > 0.5) & (place < cap)
    weight = jnp.where(kept, chosen / jnp.sum(chosen, axis=0, keepdims=True), 0.0)
    slot = jnp.where(kept, place.astype(jnp.int32), -1)
    s_iota = lax.broadcasted_iota(jnp.int32, (cap, tokens), 0)
    for i in range(experts):
        pick = (s_iota == slot[i:i + 1, :]).astype(f32)
        scale = jnp.sum(pick * weight[i:i + 1, :], axis=1, keepdims=True)
        pick = pick.astype(bf)
        xs[i] = jnp.dot(pick, n2[...], preferred_element_type=f32).astype(bf)
        gs[i] = (jnp.dot(pick, gb[...], preferred_element_type=f32) * scale).astype(bf)
    for cp in kept_copies: cp.wait()
    for group in (h, cc, ka, kc, kf):
        for cp in group.values(): cp.wait_send()
    for i in zc:
        for cp in zc[i]: cp.wait_send()
def post_kernel(nl, ns, blocks, experts, cap, lpos, spos, eo, ri, mid, mixed, logits, lr, sr, gl, gsh, wo, params, eg,
                lout, sout, midg, wog, small, mg, li, si, eg0, eg1, eg2, bg, n2, lg, fin, bk, sh, ev, sem):
    f32, bf = jnp.float32, jnp.bfloat16
    tokens = mid.shape[0]
    fetch = [pltpu.make_async_copy(eg.at[m], ev.at[m], sem.at[m]) for m in range(3)]
    copies = [pltpu.make_async_copy(ev.at[m], out.at[0], sem.at[m]) for m, out in enumerate((eg0, eg1, eg2))]
    for cp in fetch: cp.start()
    gain = params[experts + 1:experts + 2, :].astype(f32)
    lane = lax.broadcasted_iota(jnp.int32, (tokens, 128), 1)
    routes = jnp.concatenate([ref[i] for ref in (lr, sr) for i in range(ref.shape[0])], axis=0)
    member = ((lane == routes[:, 0:1]) | (lane == routes[:, 1:2])).astype(f32)
    after = (lax.broadcasted_iota(jnp.int32, (tokens, tokens), 1) < lax.broadcasted_iota(jnp.int32, (tokens, tokens), 0)).astype(f32).astype(bf)
    place = jnp.dot(after, member.astype(bf), preferred_element_type=f32)
    kept = (member > 0.5) & (place < cap)
    slot = jnp.where(kept, place.astype(jnp.int32), -1)
    lgt = jnp.where(lane < experts, logits[...], -1e30)
    ex = jnp.exp(lgt - jnp.max(lgt, axis=1, keepdims=True))
    p = ex / jnp.sum(ex, axis=1, keepdims=True)
    chosen = member * p
    both = jnp.sum(chosen, axis=1, keepdims=True)
    gate = chosen / both
    fg = jnp.zeros((1, mid.shape[1]), f32)
    for t in range(2):
        at = slice(t * 256, t * 256 + 256)
        rows = pl.ds(t * 256, 256)
        g = rows_of(gl, gsh, t).astype(f32)
        m = mid[rows, :]
        fin[...] = m
        bk[...] = jnp.zeros_like(m)
        sh[...] = jnp.zeros_like(sh)
        s_iota = lax.broadcasted_iota(jnp.int32, (256, cap), 1)
        slot_t, weight_t, lane_t = slot[at], jnp.where(kept[at], gate[at], 0.0), lane[:256]
        @pl.loop(0, experts)
        def _(i):
            this = lane_t == i
            mine = jnp.sum(jnp.where(this, slot_t, 0), axis=1, keepdims=True)
            weight = jnp.sum(jnp.where(this, weight_t, 0.0), axis=1, keepdims=True)
            pick = (s_iota == mine).astype(f32).astype(bf)
            pair = jnp.dot(pick, eo[i], preferred_element_type=f32)
            fin[...] += weight * pair
            sh[...] = jnp.where(this, jnp.sum(rows_of(gl, gsh, t).astype(f32) * pair, axis=1, keepdims=True), sh[...])
            bk[...] += jnp.dot(pick, ri[i], preferred_element_type=f32)
        (lout, sout)[t][...] = fin[...].astype(bf).reshape(lout.shape)
        share, back = sh[...], bk[...]
        mean = jnp.sum(share * gate[at], axis=1, keepdims=True)
        pg = member[at] * (share - mean) / both[at]
        lgrad = (p[at] * (pg - jnp.sum(p[at] * pg, axis=1, keepdims=True))).astype(bf)
        lg[rows, :] = lgrad
        r2 = rms_scale(m)
        u = m * r2
        n2[rows, :] = (u * gain).astype(bf)
        back += jnp.dot(lgrad, params[...], preferred_element_type=f32)
        fg += jnp.sum(back * u, axis=0, keepdims=True)
        w = back * gain
        out = g + r2 * (w - u * jnp.mean(w * u, axis=-1, keepdims=True))
        midg[rows, :] = out
        bg[rows, :] = out.astype(bf)
        mg[rows, :] = dot(out.astype(bf), wo[...], 1, 1).astype(bf)
    for m in range(3):
        fetch[m].wait()
        copies[m].start()
    small[...] = jnp.zeros_like(small)
    small[1:2, :] = fg
    small[2:2 + experts, :] = dot(lg[...], n2[...], 0, 0)[:experts]
    wog[...] = dot(mixed[...], bg[...], 0, 0).astype(bf).reshape(wog.shape)
    lane = lax.broadcasted_iota(jnp.int32, (128, 128), 1)
    edge = jnp.full((128, 128), 4096, jnp.int32)
    for i, e in enumerate(EDGES):
        edge = jnp.where(lane == i, e, edge)
    edge = jnp.where(lane > len(EDGES), -4096, edge)
    def places(out, q_col, k_row):
        k_first = k_row[:, 0:1]
        t = lax.broadcasted_iota(jnp.int32, (128, 256), 1) + k_first
        below = jnp.sum((column_of(k_row) < t).astype(jnp.int32), axis=0, keepdims=True)
        at = jnp.clip(q_col + edge - k_first, 0, 255)
        lo = jnp.take_along_axis(jnp.broadcast_to(below[:, :128], (128, 128)), at & 127, axis=1)
        hi = jnp.take_along_axis(jnp.broadcast_to(below[:, 128:], (128, 128)), at & 127, axis=1)
        out[...] = jnp.where(at < 128, lo, hi) - 1
    me = lax.axis_index("seq")
    for b in range(nl):
        own = column_of(lpos[b:b + 1, pl.ds(pl.multiple_of(me * 128, 128), 128)])
        for c in range(blocks):
            places(li.at[b, c], own, lpos[b:b + 1, c * 128:(c + 1) * 128])
    for b in range(ns):
        places(si.at[b, 0], column_of(spos[b:b + 1, :]), spos[b:b + 1, :])
    for cp in copies: cp.wait()
def front(dims, nl, ns, experts, cap, pieces, table_part, gain_part, arrays, tokens, width, heads, cid):
    X, C, Z, Y = dims
    sm, vm, hbm = pl.BlockSpec(memory_space=pltpu.SMEM), pl.BlockSpec(memory_space=pltpu.VMEM), pl.BlockSpec(memory_space=pl.ANY)
    S, V, sem, bf, f32 = jax.ShapeDtypeStruct, pltpu.VMEM, pltpu.SemaphoreType.DMA, jnp.bfloat16, jnp.float32
    rows_part, small_shape = arrays[2].shape[0], arrays[6].shape
    whole = dims + (rows_part, width)
    slots = S((experts, cap, width), bf)
    rows, short, long = S((tokens, width), bf), S((ns * 128, width), bf), S((X * C, nl, 128, width), bf)
    outs = [S(whole, bf)] * 4 + [S((128, width), bf), S((heads, 1, 128), f32), rows, short, short, long, long, S((width, tokens), bf), rows,
            S((tokens, width), f32), slots, slots, S((tokens, 128), f32), S((nl, X * C, 128, 128), jnp.int32), S((ns, 1, 128, 128), jnp.int32)]
    n, kvn = len(pieces), 2 * (width // 256)
    scr = [V((4,) + whole, bf), V(dims + small_shape, bf)] + [V((tokens, width), bf)] * 3
    scr += [sem((n, Z)), sem((n, Z)), sem((n, 2)), sem((n, 2)), sem((n, 3)), sem((n, 3)), sem((kvn, 3)), sem((kvn, 3)), sem((4,))]
    return pl.pallas_call(functools.partial(front_kernel, dims, nl, ns, experts, cap, pieces, table_part, gain_part), out_shape=outs,
        in_specs=[sm, sm] + [vm] * (len(arrays) - 2), out_specs=[hbm] * 4 + [vm] * (len(outs) - 4), scratch_shapes=scr,
        compiler_params=pltpu.CompilerParams(collective_id=cid, has_side_effects=True, vmem_limit_bytes=60 * 2**20))(*arrays)
def small_rows(experts):
    return -(-(experts + 4) // 8) * 8
def post(nl, ns, blocks, experts, cap, whole, arrays, tokens, width):
    vm, hbm = pl.BlockSpec(memory_space=pltpu.VMEM), pl.BlockSpec(memory_space=pl.ANY)
    S, bf, f32 = jax.ShapeDtypeStruct, jnp.bfloat16, jnp.float32
    eg = arrays[-1]
    outs = [S((nl, 128, width), bf), S((ns, 128, width), bf), S((tokens, width), f32), S(whole, bf), S((small_rows(experts), width), f32), S((tokens, width), bf),
            S((nl, blocks, 128, 128), jnp.int32), S((ns, 1, 128, 128), jnp.int32)] + [S((1,) + eg.shape[1:], f32)] * 3
    V = pltpu.VMEM
    return pl.pallas_call(functools.partial(post_kernel, nl, ns, blocks, experts, cap), out_shape=outs,
        in_specs=[vm] * (len(arrays) - 1) + [hbm], out_specs=[vm] * (len(outs) - 3) + [hbm] * 3,
        scratch_shapes=[V((tokens, width), bf)] * 2 + [V((tokens, 128), bf)] + [V((256, width), f32)] * 2 + [V((256, 128), f32), V(eg.shape, f32), pltpu.SemaphoreType.DMA((3,))],
        compiler_params=pltpu.CompilerParams(vmem_limit_bytes=60 * 2**20))(*arrays)
def back_kernel(dims, nl, ns, experts, pieces, q, k, v, kl, vl, tab, lb, sb, li, si, mg, wog, n1t, lx, sx, params, wq, wk, wv, midg, small_in,
                lgrad, sgrad, og, qg, kg, vg, small, *refs):
    X, C, Z, Y = dims
    blocks = X * C
    f32, bf = jnp.float32, jnp.bfloat16
    np_ = len(pieces)
    bufs = refs[:4 * np_]
    (gw, dq, ka, va, dkl, dvl, kcb, ka1, kb1, seg, sacc, sbuf, cs, cr, hs, hr, zs, zr, kss, krs, sss, srs) = refs[4 * np_:]
    s = lax.axis_index("seq"); g = lax.axis_index("dp")
    x, c = s // C, lax.rem(s, C)
    z, y = g // Y, lax.rem(g, Y)
    def zdev(k): return (s, lax.rem(z + k, Z) * Y + y)
    ydev = (s, z * Y + (1 - y)); xdev = ((1 - x) * C + c, g); cdev = (x * C + 1 - c, g)
    greet([zdev(k) for k in range(1, Z)] + [ydev, xdev, cdev])
    half = nl * 128
    wide = 256
    nb = q.shape[1] // wide
    sources = [wog] + [gw.at[i] for i in range(3)]
    outs = [og, qg, kg, vg]
    first = {}; hh = {}; zz = {}
    def add(dst, a, b):
        dst[...] = (a.astype(f32) + b.astype(f32)).astype(dst.dtype)
    def send_core(i):
        m, c0, nc = pieces[i]
        first[i] = remote(sources[m].at[:, 1 - c, :, :, :, pl.ds(c0, nc)], bufs[4 * i], cs.at[i], cr.at[i], cdev)
    def stage(i, which):
        m, c0, nc = pieces[i]
        b0, b1, b2, b3 = bufs[4 * i:4 * i + 4]
        if which == 0:
            first[i].wait_recv()
            add(b0, sources[m][:, c, :, :, :, c0:c0 + nc], b0[...])
            hh[i, 0] = remote(b0.at[:, :, 1 - y], b1, hs.at[i, 0], hr.at[i, 0], ydev)
        elif which == 1:
            hh[i, 0].wait_recv()
            add(b1, b0[:, :, y], b1[...])
            hh[i, 1] = remote(b1.at[1 - x], b2, hs.at[i, 1], hr.at[i, 1], xdev)
        elif which == 2:
            hh[i, 1].wait_recv()
            add(b2, b1[x], b2[...])
            zz[i] = [remote(b2.at[lax.rem(z + k, Z)], b3.at[k - 1], zs.at[i, k], zr.at[i, k], zdev(k)) for k in range(1, Z)]
        else:
            tot = b2[z].astype(f32)
            for k in range(1, Z):
                zz[i][k - 1].wait_recv()
                tot += b3[k - 1].astype(f32)
            outs[m][:, c0:c0 + nc] = tot
    def piece(m, b):
        return [i for i, p in enumerate(pieces) if p[0] == m and (m == 0 or p[1] == b * wide)]
    def weight_grad(m, rows, b):
        cols = slice(b * wide, (b + 1) * wide)
        quarter = n1t.shape[0] // blocks
        for xx in range(X):
            for cc in range(C):
                part = jnp.dot(n1t[pl.ds((xx * C + cc) * quarter, quarter), :], rows[:, cols], preferred_element_type=f32)
                gw[m - 1, xx, cc, :, :, :, cols] = part.astype(bf).reshape(gw.shape[3:6] + (wide,))
        for i in piece(m, b):
            send_core(i)
    parts, wholes = (dkl, dvl), (ka, va)
    kf, kx = {}, {}
    def kv_core(b):
        cols = pl.ds(b * wide, wide)
        for far in range(2):
            for m in range(2):
                n = b * 2 + m
                at = (1 - x if far == 0 else x) * C + 1 - c
                kf[n, far] = remote(parts[m].at[at, :, :, cols], kcb.at[n, far], kss.at[n, far], krs.at[n, far], cdev)
    def kv_chip(b):
        for m in range(2):
            n = b * 2 + m
            kf[n, 0].wait_recv()
            add(ka1.at[n], parts[m][(1 - x) * C + c, :, :, b * wide:(b + 1) * wide], kcb[n, 0])
            kx[n] = remote(ka1.at[n], kb1.at[n], kss.at[n, 2], krs.at[n, 2], xdev)
    def kv_end(b):
        for m in range(2):
            n = b * 2 + m
            kf[n, 1].wait_recv(); kx[n].wait_recv()
            tot = parts[m][s, :, :, b * wide:(b + 1) * wide].astype(f32) + kcb[n, 1].astype(f32) + kb1[n].astype(f32)
            wholes[m][pl.ds(0, half), b * wide:(b + 1) * wide] = tot.astype(bf).reshape(half, wide)
        weight_grad(2, ka, b)
        weight_grad(3, va, b)
    def stages(which, b, *ms):
        for m in ms:
            for i in piece(m, b):
                stage(i, which)
    seg[...] = jnp.zeros_like(seg)
    lane = lax.broadcasted_iota(jnp.int32, (128, 128), 1)
    head_one = lane < 64
    tri = jnp.where(lax.broadcasted_iota(jnp.int32, (128, 128), 0) <= lane, 1.0, 0.0).astype(bf)
    def attend(b0):
        @pl.loop(0, wide // 128)
        def _(i):
            hp = b0 * (wide // 128) + i
            cols = pl.ds(pl.multiple_of(hp * 128, 128), 128)
            for b in range(nl + ns):
                rows, n, kk, vv = item(b, nl, blocks, cols, k, v, kl, vl)
                idx = mine_of(b, nl, li, si)
                qs = stack_heads(q[rows, cols], head_one); gs = stack_heads(mg[rows, cols], head_one)
                p = probs_of(qs, kk, (tab[2 * hp], tab[2 * hp + 1]), mine_of(b, nl, lb, sb), n)
                dp = dot(gs, vv, 1, 1)
                ds = (p * (dp - jnp.sum(p * dp, axis=1, keepdims=True))).astype(bf)
                dqs = dot(ds, kk, 1, 0)
                dkt = dot(qs, ds, 0, 0)
                dvt = dot(gs, p.astype(bf), 0, 0)
                sums = [0, 0]
                for c_ in range(n):
                    pre = dot(ds[:, c_ * 128:(c_ + 1) * 128], tri, 1, 0)
                    at = idx[c_]
                    for e in range(2):
                        sums[e] += jnp.where(at >= 0, jnp.take_along_axis(pre[e * 128:(e + 1) * 128], jnp.maximum(at, 0), axis=1), 0.0)
                for e in range(2):
                    seg[2 * hp + e] += jnp.sum(sums[e], axis=0, keepdims=True)
                dq[rows, cols] = jnp.where(head_one, dqs[:128], dqs[128:]).astype(bf)
                dkt = dkt.T.astype(bf); dvt = dvt.T.astype(bf)
                if b < nl:
                    dkl[:, b, :, cols] = dkt.reshape(n, 128, 128); dvl[:, b, :, cols] = dvt.reshape(n, 128, 128)
                else:
                    ka[rows, cols] = dkt; va[rows, cols] = dvt
    for i in piece(0, 0):
        send_core(i)
    attend(0)
    kv_core(0); weight_grad(1, dq, 0); stages(0, 0, 0)
    attend(1)
    kv_core(1); kv_chip(0); weight_grad(1, dq, 1); stages(0, 0, 1); stages(1, 0, 0)
    attend(2)
    kv_core(2); kv_chip(1); kv_end(0); weight_grad(1, dq, 2); stages(0, 1, 1); stages(1, 0, 1); stages(2, 0, 0)
    attend(3)
    kv_core(3); kv_chip(2); kv_end(1); weight_grad(1, dq, 3); stages(0, 0, 2, 3); stages(0, 2, 1); stages(1, 1, 1); stages(2, 0, 1)
    kv_chip(3); kv_end(2); stages(0, 1, 2, 3); stages(0, 3, 1); stages(1, 0, 2, 3); stages(1, 2, 1); stages(2, 1, 1); stages(3, 0, 0)
    kv_end(3); stages(0, 2, 2, 3); stages(1, 3, 1); stages(1, 1, 2, 3); stages(2, 2, 1); stages(2, 0, 2, 3); stages(3, 0, 1)
    gain = params[experts:experts + 1, :].astype(f32)
    ag = jnp.zeros((1, q.shape[1]), f32)
    for t in range(2):
        rows = pl.ds(t * half, half)
        ng = dot(dq[rows, :], wq[...], 1, 1) + dot(ka[rows, :], wk[...], 1, 1) + dot(va[rows, :], wv[...], 1, 1)
        m = rows_of(lx, sx, t).astype(f32)
        r1 = rms_scale(m)
        u = m * r1
        ag += jnp.sum(ng * u, axis=0, keepdims=True)
        w = ng * gain
        (lgrad, sgrad)[t][...] = (midg[rows, :] + r1 * (w - u * jnp.mean(w * u, axis=-1, keepdims=True))).reshape(lgrad.shape)
        if t == 0:
            stages(0, 3, 2, 3); stages(1, 2, 2, 3); stages(2, 3, 1); stages(2, 1, 2, 3); stages(3, 1, 1)
    sacc[0] = small_in[...]
    sacc[0, 0:1, :] = ag
    heads = seg.shape[0]
    spot = lax.broadcasted_iota(jnp.int32, (8, 128), 1)
    for h in range(heads):
        upto = jnp.broadcast_to(seg[h], (8, 128))
        within = upto - jnp.where(spot == 0, 0.0, pltpu.roll(upto, 1, 1))
        at = jnp.where(spot < 16, 15 - spot, jnp.minimum(spot - 1, 30))
        by_bucket = jnp.where((spot == 16) | (spot >= 32), 0.0, jnp.take_along_axis(within, at, axis=1))
        r = 2 + experts + h // 8
        sacc[0, r:r + 1, (h % 8) * 128:(h % 8 + 1) * 128] = by_bucket[0:1, :]
    sc = remote(sacc.at[0], sbuf.at[0], sss.at[0], srs.at[0], cdev)
    stages(1, 3, 2, 3); stages(2, 2, 2, 3); stages(3, 2, 1)
    sc.wait_recv()
    sacc[1] = sacc[0] + sbuf[0]
    sx_ = remote(sacc.at[1], sbuf.at[1], sss.at[1], srs.at[1], xdev)
    stages(2, 3, 2, 3); stages(3, 3, 1); stages(3, 0, 2, 3)
    sx_.wait_recv()
    sacc[2] = sacc[1] + sbuf[1]
    sy = remote(sacc.at[2], sbuf.at[2], sss.at[2], srs.at[2], ydev)
    stages(3, 1, 2, 3)
    sy.wait_recv()
    sacc[3] = sacc[2] + sbuf[2]
    sz = [remote(sacc.at[3], sbuf.at[2 + k], sss.at[2 + k], srs.at[2 + k], zdev(k)) for k in range(1, Z)]
    stages(3, 2, 2, 3); stages(3, 3, 2, 3)
    tot = sacc[3]
    for k in range(1, Z):
        sz[k - 1].wait_recv()
        tot += sbuf[2 + k]
    small[...] = tot
    for cp in [sc, sx_, sy] + sz + list(kx.values()) + list(kf.values()) + list(first.values()) + list(hh.values()) + [w for v_ in zz.values() for w in v_]:
        cp.wait_send()
def back(dims, nl, ns, experts, arrays, cid):
    X, C, Z, Y = dims
    q_, small_in = arrays[0], arrays[-1]
    tokens, width = q_.shape
    heads = arrays[5].shape[0]
    nr = width // (X * C * Z * Y)
    wide = 256
    pieces = tuple((0, h * 512, 512) for h in range(width // 512)) + tuple((m, b * wide, wide) for m in range(1, 4) for b in range(width // wide))
    n = len(pieces)
    S, sem, bf, f32 = jax.ShapeDtypeStruct, pltpu.SemaphoreType.DMA, jnp.bfloat16, jnp.float32
    V = pltpu.VMEM
    scr = [V(lead + (nr, nc), bf) for m, c0, nc in pieces for lead in ((X, Z, Y), (X, Z), (Z,), (Z - 1,))]
    kvn = 2 * (width // wide)
    long = V((X * C, nl, 128, width), bf)
    rows = V((tokens, width), bf)
    scr += [V((3, X, C, Z, Y, nr, width), bf), rows, rows, rows, long, long,
            V((kvn, 2, nl, 128, wide), bf), V((kvn, nl, 128, wide), bf), V((kvn, nl, 128, wide), bf), V((heads, 1, 128), f32),
            V((4,) + small_in.shape, f32), V((Z + 2,) + small_in.shape, f32),
            sem((n,)), sem((n,)), sem((n, 2)), sem((n, 2)), sem((n, Z)), sem((n, Z)), sem((kvn, 3)), sem((kvn, 3)), sem((Z + 2,)), sem((Z + 2,))]
    vm = pl.BlockSpec(memory_space=pltpu.VMEM)
    outs = [S((nl, 128, width), f32), S((ns, 128, width), f32)] + [S((nr, width), f32)] * 4 + [S(small_in.shape, f32)]
    return pl.pallas_call(functools.partial(back_kernel, dims, nl, ns, experts, pieces), out_shape=outs,
        in_specs=[vm] * len(arrays), out_specs=[vm] * len(outs), scratch_shapes=scr,
        compiler_params=pltpu.CompilerParams(collective_id=cid, has_side_effects=True, vmem_limit_bytes=63 * 2**20))(*arrays)

def gelu_parts(v):
    c, a = 0.7978845608, 0.044715
    v2 = v * v
    h = 0.5 + 0.5 * jnp.tanh(v * (c + (c * a) * v2))
    act = v * h
    return act, h + act * (1.0 - h) * (2.0 * c + (6.0 * c * a) * v2)
RING, LAG = 6, 4
SEND_AT, JOIN_AT = 2, 3
def expert_kernel(cap, per, order, todo, wcut, tile, xs, gs, wgi, wui, wdi, eo_out, ri_out, grads, eo_h, ri_h,
                  wall, xr, gr, hall, lall, eo, ri, cb, ab, xb, ob,
                  lsem, xss, xrs, gss, grs, ess, ers, rss, rrs, wss, wrs, wls, css, crs, ass, ars, osem, free):
    dp = lax.axis_size("dp")
    f32, bf = jnp.float32, jnp.bfloat16
    s, x, c, xdev, cdev = seq_places(2)
    g = lax.axis_index("dp")
    def peer(k): return (s, g ^ k)
    greet([xdev, cdev] + [peer(k) for k in range(1, dp)])
    rows_w, ff = wgi.shape; width = xs.shape[2]
    wx, wc, wl, wf = [], [], [], []
    shared = ((wgi, 1), (wui, 2), (wdi, 0))
    parts = [(src, m, f0, nf) for f0, nf in wcut for src, m in shared]
    for n, (src, m, f0, nf) in enumerate(parts):
        a = src.at[:, pl.ds(f0, nf)]
        b = wall.at[m, x, c, :, pl.ds(f0, nf)]
        wx.append(remote(a, b, wss.at[n, 0], wrs.at[n, 0], xdev))
        wc.append(remote(a, b, wss.at[n, 1], wrs.at[n, 1], cdev))
        cp = pltpu.make_async_copy(a, b, wls.at[n]); cp.start(); wl.append(cp)
    sx, sg = {}, {}
    def dispatch(p):
        for k in range(p * per, (p + 1) * per):
            at = pl.ds(k * cap, cap)
            if k == 0:
                sx[0] = pltpu.make_async_copy(xs.at[g], xr.at[at], lsem.at[0]); sx[0].start()
                sg[0] = pltpu.make_async_copy(gs.at[g], gr.at[at], lsem.at[1]); sg[0].start()
            else:
                sx[k] = remote(xs.at[g ^ k], xr.at[at], xss.at[k], xrs.at[k], peer(k))
                sg[k] = remote(gs.at[g ^ k], gr.at[at], gss.at[k], grs.at[k], peer(k))
    for p in order[:-1]: dispatch(p)
    ntile = ff // tile
    re, rr = {}, {}
    wide = 4 * rows_w
    def sources(p): return list(range(p * per, (p + 1) * per))
    def arrive(p):
        for k in sources(p):
            if k == 0: sx[0].wait(); sg[0].wait()
            else: sx[k].wait_recv(); sg[k].wait_recv()
    def inner(p, t0, nt):
        rows = pl.ds(p * per * cap, per * cap)
        @pl.loop(t0, t0 + nt)
        def _(t):
            cols = pl.ds(pl.multiple_of(t * tile, 128), tile)
            w = lambda m: wall[m, :, :, :, cols].reshape(wide, tile)
            gp = jnp.dot(xr[rows, :], w(1), preferred_element_type=f32)
            up = jnp.dot(xr[rows, :], w(2), preferred_element_type=f32)
            hg = jnp.dot(gr[rows, :], w(0), preferred_element_type=f32)
            act, der = gelu_parts(gp)
            hall[0, rows, cols] = (act * up).astype(bf)
            hall[1, rows, cols] = (hg * up * der).astype(bf)
            hall[2, rows, cols] = (hg * act).astype(bf)
    def outer(p):
        rows = pl.ds(p * per * cap, per * cap)
        @pl.loop(0, 4)
        def _(t):
            part = pl.ds(pl.multiple_of(t * rows_w, 128), rows_w)
            tx, tc = t // 2, lax.rem(t, 2)
            eo[:, part] = dot(hall[0, rows, :], wall[0, tx, tc], 1, 1).astype(bf)
            ri[:, part] = (dot(hall[1, rows, :], wall[1, tx, tc], 1, 1) + dot(hall[2, rows, :], wall[2, tx, tc], 1, 1)).astype(bf)
        keep = [pltpu.make_async_copy(eo, eo_h.at[rows], lsem.at[4]), pltpu.make_async_copy(ri, ri_h.at[rows], lsem.at[5])]
        for cp in keep: cp.start()
        for cp in keep: cp.wait()
        for k in sources(p):
            at = pl.ds(k * cap, cap)
            if k == 0:
                re[0] = pltpu.make_async_copy(eo_h.at[at], eo_out.at[g], lsem.at[2]); re[0].start()
                rr[0] = pltpu.make_async_copy(ri_h.at[at], ri_out.at[g], lsem.at[3]); rr[0].start()
            else:
                re[k] = remote(eo_h.at[at], eo_out.at[g], ess.at[k], ers.at[k], peer(k))
                rr[k] = remote(ri_h.at[at], ri_out.at[g], rss.at[k], rrs.at[k], peer(k))
    early = list(todo[:-2])
    last = todo[-1]
    for i, (f0, nf) in enumerate(wcut):
        mine = range(3 * i, 3 * i + 3)
        for n in mine:
            wx[n].wait_recv()
            src, m, f0, nf = parts[n]
            b = wall.at[m, 1 - x, c, :, pl.ds(f0, nf)]
            wf.append(remote(b, b, wss.at[n, 2], wrs.at[n, 2], cdev))
        if i == SEND_AT: dispatch(last)
        if i == 0:
            for p in early: arrive(p)
        for n in mine:
            wl[n].wait(); wc[n].wait_recv(); wf[n].wait_recv()
        for p in early: inner(p, f0 // tile, nf // tile)
        if i == JOIN_AT:
            p = todo[-2]
            arrive(p)
            inner(p, 0, (f0 + nf) // tile)
            early.append(p)
    for p in early: outer(p)
    arrive(last)
    inner(last, 0, ntile)
    outer(last)
    for n in range(len(parts)):
        wx[n].wait_send(); wc[n].wait_send(); wf[n].wait_send()
    total = dp * cap
    @pl.loop(0, total // 256)
    def _(t):
        at = pl.ds(pl.multiple_of(t * 256, 256), 256)
        lall[1, :, at] = xr[at, :].T
        lall[0, :, at] = gr[at, :].T
    nt = 3 * ntile
    def place(n):
        m = n // ntile
        return m, pl.ds(pl.multiple_of((n - m * ntile) * tile, 128), tile)
    def to_core(n):
        m, cols = place(n); r = lax.rem(n, RING)
        return pltpu.make_async_remote_copy(src_ref=wall.at[m, :, 1 - c, :, cols], dst_ref=cb.at[r], send_sem=css.at[r],
            recv_sem=crs.at[r], device_id=cdev, device_id_type=MESH)
    def to_chip(n):
        r = lax.rem(n, RING)
        return pltpu.make_async_remote_copy(src_ref=ab.at[r], dst_ref=xb.at[r], send_sem=ass.at[r],
            recv_sem=ars.at[r], device_id=xdev, device_id_type=MESH)
    def to_out(n):
        m, cols = place(n); r = lax.rem(n, 2)
        return pltpu.make_async_copy(ob.at[r], grads.at[m, :, cols], osem.at[r])
    @pl.loop(0, nt + LAG)
    def _(n):
        @pl.when(n < nt)
        def _():
            m, cols = place(n)
            res = jnp.dot(lall[jnp.minimum(m, 1)], hall[m, :, cols], preferred_element_type=f32)
            wall[m, :, :, :, cols] = res.astype(bf).reshape(2, 2, rows_w, tile)
            @pl.when(n >= RING)
            def _(): pl.semaphore_wait(free.at[0], 1)
            to_core(n).start()
        @pl.when((n >= 1) & (n <= nt))
        def _():
            i = n - 1
            m, cols = place(i); r = lax.rem(i, RING)
            to_core(i).wait_recv()
            @pl.when(i >= RING)
            def _():
                to_chip(i).wait_send()
                pl.semaphore_wait(free.at[1], 1)
            ab[r] = (wall[m, 1 - x, c, :, cols].astype(f32) + cb[r, 1 - x].astype(f32)).astype(bf)
            to_chip(i).start()
        @pl.when(n >= LAG)
        def _():
            j = n - LAG
            m, cols = place(j); r = lax.rem(j, RING)
            to_chip(j).wait_recv()
            to_core(j).wait_send()
            @pl.when(j >= 2)
            def _(): to_out(j).wait()
            ob[lax.rem(j, 2)] = wall[m, x, c, :, cols].astype(f32) + cb[r, x].astype(f32) + xb[r].astype(f32)
            to_out(j).start()
            @pl.when(j < nt - RING)
            def _():
                pl.semaphore_signal(free.at[0], inc=1, device_id=cdev, device_id_type=MESH)
                pl.semaphore_signal(free.at[1], inc=1, device_id=xdev, device_id_type=MESH)
    for j in range(nt - 2, nt): to_out(j).wait()
    for i in range(nt - RING, nt): to_chip(i).wait_send()
    for k in range(dp):
        if k == 0:
            re[0].wait(); rr[0].wait()
        else:
            sx[k].wait_send(); sg[k].wait_send(); re[k].wait(); rr[k].wait()
def expert_all(xs, gs, wg, wu, wd, seq, cid):
    dp, cap, width = xs.shape
    rows_w, ff = wg.shape; total = dp * cap
    group = 320
    per = group // cap
    ng = dp // per
    order = [ng - 2] + [p for p in range(ng - 3, -1, -1)] + [ng - 1]
    todo = list(range(ng))
    sem = pltpu.SemaphoreType.DMA
    bf = jnp.bfloat16
    any_ = pl.BlockSpec(memory_space=pl.ANY)
    V = pltpu.VMEM
    tile = 256
    wcut = tuple((f0, min(512, ff - f0)) for f0 in range(0, ff, 512))
    nw = 3 * len(wcut)
    back = jax.ShapeDtypeStruct((dp, cap, width), bf)
    flat = jax.ShapeDtypeStruct((total, width), bf)
    return pl.pallas_call(functools.partial(expert_kernel, cap, per, order, todo, wcut, tile),
        out_shape=[back, back, jax.ShapeDtypeStruct((3, rows_w, ff), jnp.float32), flat, flat],
        in_specs=[any_] * 5, out_specs=[any_] * 5,
        scratch_shapes=[V((3, seq // 2, 2, rows_w, ff), bf), V((total, width), bf), V((total, width), bf), V((3, total, ff), bf),
        V((2, width, total), bf), V((group, width), bf), V((group, width), bf),
        V((RING, seq // 2, rows_w, tile), bf), V((RING, rows_w, tile), bf), V((RING, rows_w, tile), bf), V((2, rows_w, tile), jnp.float32)]
        + [sem((6,))] + [sem((dp,))] * 8 + [sem((nw, 3))] * 2 + [sem((nw,))] + [sem((RING,))] * 4 + [sem((2,)), pltpu.SemaphoreType.REGULAR((2,))],
        compiler_params=pltpu.CompilerParams(collective_id=cid, has_side_effects=True, vmem_limit_bytes=63 * 2**20))(xs, gs, wg, wu, wd)[:3]


def on_device(
    long_tokens,
    short_tokens,
    long_grad_out,
    short_grad_out,
    query_weight,
    key_weight,
    value_weight,
    output_weight,
    attn_gain,
    ffn_gain,
    rel_table,
    router_weight,
    gate_weight,
    up_weight,
    down_weight,
    long_positions,
    short_positions,
    long_lengths,
    short_lengths,
    long_routes,
    short_routes,
):
    long_items, quarter, model_width = long_tokens.shape
    short_items, short_len = (short_tokens.shape[0], short_tokens.shape[1])
    long_rows = long_items * quarter
    tokens = long_rows + short_items * short_len
    local_experts = gate_weight.shape[0]
    dp_size = lax.axis_size("dp")
    experts = local_experts * dp_size
    capacity = (5 * tokens + 2 * experts - 1) // (2 * experts)
    seq_size = lax.axis_size("seq")
    dims = (seq_size // 2, 2, dp_size // 2, 2)
    devices = seq_size * dp_size
    table_part, gain_part = rel_table.shape[0], attn_gain.shape[0]
    small = jnp.concatenate([router_weight.T, attn_gain[None], ffn_gain[None]], 0)
    small = jnp.pad(small, ((0, 1), (0, 128 - gain_part)))
    table_row = jnp.pad(rel_table[None], ((experts + 2, 0), (0, 128 - table_part)))
    small = jnp.pad(small + table_row, ((0, -(experts + 3) % 16), (0, 0)))
    rows_part = query_weight.shape[0]
    cuts = 2 if rows_part % 32 == 0 else 1
    cut = rows_part // cuts
    pieces = tuple((m, h * cut, cut, (m + h) % 2) for m in range(4) for h in range(cuts))
    pieces = ((4, 0, small.shape[0], 0),) + tuple(p[:3] + (0,) for p in pieces)
    sizes = (long_items, short_items, seq_size, experts, capacity)
    places = (long_positions, short_positions)
    routes = (long_routes, short_routes)
    (
        key_all,
        value_all,
        query_all,
        output_all,
        params,
        table,
        queries,
        keys,
        values,
        long_keys,
        long_values,
        normed_t,
        mixed,
        middle,
        outgoing,
        out_slots,
        logits,
        long_buckets,
        short_buckets,
    ) = front(
        dims,
        long_items,
        short_items,
        experts,
        capacity,
        pieces,
        table_part,
        gain_part,
        (long_lengths, short_lengths, key_weight, value_weight, query_weight, output_weight, small)
        + places
        + (long_tokens, short_tokens, long_grad_out, short_grad_out)
        + routes,
        tokens,
        model_width,
        HEADS,
        0,
    )
    key_all, value_all, query_all, output_all = (
        block.reshape(devices * rows_part, model_width)
        for block in (key_all, value_all, query_all, output_all)
    )
    heads_args = (queries, keys, values, long_keys, long_values, table)
    grads = (long_grad_out, short_grad_out, output_all, params)
    back_rows, back_grads, expert_grads = expert_all(
        outgoing, out_slots, gate_weight[0], up_weight[0], down_weight[0], seq_size, 4
    )
    (
        long_out,
        short_out,
        middle_grad,
        output_local,
        small_local,
        mixed_grad,
        long_places,
        short_places,
        down_grad,
        gate_grad,
        up_grad,
    ) = post(
        *sizes,
        dims + (rows_part, model_width),
        places + (back_rows, back_grads, middle, mixed, logits) + routes + grads + (expert_grads,),
        tokens,
        model_width,
    )
    long_grad_in, short_grad_in, output_grad, query_grad, key_grad, value_grad, small_sum = back(
        dims,
        long_items,
        short_items,
        experts,
        heads_args
        + (long_buckets, short_buckets, long_places, short_places)
        + (mixed_grad, output_local, normed_t, long_tokens, short_tokens, params)
        + (query_all, key_all, value_all, middle_grad, small_local),
        2,
    )
    place = lax.axis_index("seq") * dp_size + lax.axis_index("dp")

    def own(row, column, size, count=1):
        return lax.dynamic_slice(small_sum, (row, column), (count, size))

    entry = place * table_part
    head_at = entry // BUCKETS
    table_grad = own(2 + experts + head_at // 8, head_at % 8 * 128 + entry % BUCKETS, table_part)
    summed = (
        query_grad,
        key_grad,
        value_grad,
        output_grad,
        own(0, place * gain_part, gain_part)[0],
        own(1, place * gain_part, gain_part)[0],
        table_grad[0],
        own(2, place * rows_part, rows_part, experts).T,
    )
    return (
        long_out,
        short_out,
        long_grad_in,
        short_grad_in,
        summed[0],
        summed[1],
        summed[2],
        summed[3],
        summed[4],
        summed[5],
        summed[6],
        summed[7],
        gate_grad,
        up_grad,
        down_grad,
    )


def solution(mesh):
    placed = (
        P("dp", "seq", None),
        P(("seq", "dp"), None, None),
        P("dp", "seq", None),
        P(("seq", "dp"), None, None),
        P(("seq", "dp"), None),
        P(("seq", "dp"), None),
        P(("seq", "dp"), None),
        P(("seq", "dp"), None),
        P(("seq", "dp")),
        P(("seq", "dp")),
        P(("seq", "dp")),
        P(("seq", "dp"), None),
        P("dp", "seq", None),
        P("dp", "seq", None),
        P("dp", "seq", None),
        P("dp", None),
        P(("seq", "dp"), None),
        P("dp"),
        P(("seq", "dp")),
        P("dp", "seq", None),
        P(("seq", "dp"), None, None),
    )
    return jax.shard_map(
        on_device,
        mesh=mesh,
        in_specs=placed,
        out_specs=(
            P("dp", "seq", None),
            P(("seq", "dp"), None, None),
            P("dp", "seq", None),
            P(("seq", "dp"), None, None),
            P(("seq", "dp"), None),
            P(("seq", "dp"), None),
            P(("seq", "dp"), None),
            P(("seq", "dp"), None),
            P(("seq", "dp")),
            P(("seq", "dp")),
            P(("seq", "dp")),
            P(("seq", "dp"), None),
            P("dp", "seq", None),
            P("dp", "seq", None),
            P("dp", "seq", None),
        ),
        check_vma=False,
    )
```

```python
import functools

import jax
import jax.numpy as jnp
from jax import lax
from jax.experimental import pallas as pl
from jax.experimental.pallas import tpu as pltpu
from jax.sharding import PartitionSpec as P

MESH = pl.DeviceIdType.MESH

HEADS = 16
HEAD = 64
BUCKETS = 32


epsilon = 1e-06
masked = -1e30


def seq_places(C):
    s = lax.axis_index("seq"); g = lax.axis_index("dp")
    x, c = s // C, lax.rem(s, C)
    return s, x, c, ((1 - x) * C + c, g), (x * C + 1 - c, g)
def greet(devs):
    bar = pltpu.get_barrier_semaphore()
    for d in devs:
        pl.semaphore_signal(bar, inc=1, device_id=d, device_id_type=MESH)
    pl.semaphore_wait(bar, len(devs))
def remote(src, dst, ss, rs, dev):
    cp = pltpu.make_async_remote_copy(src_ref=src, dst_ref=dst, send_sem=ss, recv_sem=rs, device_id=dev, device_id_type=MESH)
    cp.start()
    return cp
EDGES = (-90, -63, -45, -31, -22, -15, -11, -7, -6, -5, -4, -3, -2, -1, 0, 1, 2, 3, 4, 5, 6, 7, 8, 12, 16, 23, 32, 46, 64, 91)
FAR = (12, 16, 23, 32, 46, 64, 91)
def fill_buckets(out, q_col, k_row, length, base):
    r = k_row - q_col
    n = jnp.abs(r)
    far = jnp.full(r.shape, 8, jnp.int32)
    for e in FAR:
        far += (n >= e).astype(jnp.int32)
    b = jnp.where(n < 8, n, far) + jnp.where(r > 0, 16, 0)
    j = lax.broadcasted_iota(jnp.int32, r.shape, 1) + base
    out[...] = jnp.where(j < length, b, 32)
def dot(a, b, ca, cb):
    return lax.dot_general(a, b, (((ca,), (cb,)), ((), ())), preferred_element_type=jnp.float32)
def probs_of(qs, kk, tabs, bucket_ref, blocks):
    s = dot(qs, kk, 1, 1)
    t = [jnp.broadcast_to(tab, (128, 128)) for tab in tabs]
    bias = [jnp.concatenate([jnp.take_along_axis(x, bucket_ref[c], axis=1) for x in t], axis=0) for c in range(blocks)]
    s = s + (jnp.concatenate(bias, axis=1) if blocks > 1 else bias[0])
    p = jnp.exp(s - jnp.max(s, axis=1, keepdims=True))
    return p * (1.0 / jnp.sum(p, axis=1, keepdims=True))
def stack_heads(rows, first):
    return jnp.concatenate([jnp.where(first, rows, 0), jnp.where(first, 0, rows)], axis=0)
def column_of(row):
    i = lax.broadcasted_iota(jnp.int32, (128, 128), 0)
    return jnp.sum(jnp.where(i == lax.broadcasted_iota(jnp.int32, (128, 128), 1), row, 0), axis=1, keepdims=True)
def row_of(col):
    i = lax.broadcasted_iota(jnp.int32, (128, 128), 0)
    return jnp.sum(jnp.where(i == lax.broadcasted_iota(jnp.int32, (128, 128), 1), col, 0), axis=0, keepdims=True)
def rows_of(long_ref, short_ref, t):
    ref = long_ref if t == 0 else short_ref
    return ref[...].reshape(ref.shape[0] * ref.shape[1], ref.shape[2])
def rms_scale(mid):
    return lax.rsqrt(jnp.mean(mid * mid, axis=-1, keepdims=True) + epsilon)
def item(b, nl, blocks, cols, k, v, kl, vl):
    rows = pl.ds(b * 128, 128)
    if b < nl:
        return rows, blocks, kl[:, b, :, cols].reshape(blocks * 128, 128), vl[:, b, :, cols].reshape(blocks * 128, 128)
    short = pl.ds((b - nl) * 128, 128)
    return rows, 1, k[short, cols], v[short, cols]
def mine_of(b, nl, long_ref, short_ref):
    return long_ref.at[b] if b < nl else short_ref.at[b - nl]
def front_kernel(dims, nl, ns, experts, cap, pieces, table_part, gain_part, ll, sl, wk_in, wv_in, wq_in, wo_in, small_in, lpos, spos, xl, xsh, gl, gsh, lr, sr,
                 wk_out, wv_out, wq_out, wo_out, params, tab, q, ks, vs, kl, vl, n1t, mixed, mid, xs, gs, logits, lb, sb,
                 wall, sm, n1, n2, gb, zs, zr, hs, hr, cs, cr, kss, krs, osem):
    X, C, Z, Y = dims
    blocks = X * C
    f32, bf = jnp.float32, jnp.bfloat16
    s, x, c, xdev, cdev = seq_places(C)
    g = lax.axis_index("dp")
    z, y = g // Y, lax.rem(g, Y)
    def zdev(k): return (s, lax.rem(z + k, Z) * Y + y)
    ydev = (s, z * Y + (1 - y))
    tokens, width = q.shape
    half = nl * 128
    wide = 256
    nb = width // wide
    greet([zdev(k) for k in range(1, Z)] + [ydev, xdev, cdev])
    ins = (wk_in, wv_in, wq_in, wo_in)
    def part(i, *lead):
        m, r0, nr, route = pieces[i]
        if m == 4:
            return sm.at[lead + (slice(None),) * (4 - len(lead))]
        return wall.at[(m,) + lead + (slice(None),) * (4 - len(lead)) + (pl.ds(r0, nr),)]
    zc, h, cc = {}, {}, {}
    for i, (m, r0, nr, route) in enumerate(pieces):
        src = small_in if m == 4 else ins[m].at[pl.ds(r0, nr)]
        zc[i] = [remote(src, part(i, x, c, z, y), zs.at[i, k], zr.at[i, k], zdev(k)) for k in range(1, Z)]
    for m in range(4):
        wall[m, x, c, z, y] = ins[m][...]
    sm[x, c, z, y] = small_in[...]
    def gather_stage(i, stage):
        route = pieces[i][3]
        if stage == 0:
            for k in range(1, Z): zc[i][k - 1].wait_recv()
            mine = part(i, x, c, slice(None), y)
            h[i, 0] = remote(mine, mine, hs.at[i, 0], hr.at[i, 0], xdev if route == 0 else ydev)
            cc[i, 0] = remote(mine, mine, cs.at[i, 0], cr.at[i, 0], cdev)
        elif stage == 1:
            h[i, 0].wait_recv()
            if route == 0:
                both, got = part(i, slice(None), c, slice(None), y), part(i, 1 - x, c, slice(None), y)
            else:
                both, got = part(i, x, c), part(i, x, c, slice(None), 1 - y)
            h[i, 1] = remote(both, both, hs.at[i, 1], hr.at[i, 1], ydev if route == 0 else xdev)
            cc[i, 1] = remote(got, got, cs.at[i, 1], cr.at[i, 1], cdev)
        else:
            h[i, 1].wait_recv()
            got = part(i, slice(None), c, slice(None), 1 - y) if route == 0 else part(i, 1 - x, c)
            cc[i, 2] = remote(got, got, cs.at[i, 2], cr.at[i, 2], cdev)
    np_ = len(pieces)
    steps = [(t - st, st) for t in range(np_ + 2) for st in range(3) if 0 <= t - st < np_]
    done = [0]
    def gather_until(m):
        last = max(i for i, p in enumerate(pieces) if p[0] == m)
        while True:
            i, st = steps[done[0]]
            gather_stage(i, st)
            done[0] += 1
            if (i, st) == (last, 2): break
        for i, p in enumerate(pieces):
            if p[0] == m:
                for k in range(3): cc[i, k].wait_recv()
    kept_copies = []
    def keep(m, out):
        cp = pltpu.make_async_copy(wall.at[m], out, osem.at[m]); cp.start(); kept_copies.append(cp)
    def w_of(m):
        return wall[m].reshape(width, width)
    for b in range(nl):
        own = column_of(lpos[b:b + 1, pl.ds(pl.multiple_of(s * 128, 128), 128)])
        for k in range(blocks):
            fill_buckets(lb.at[b, k], own, lpos[b:b + 1, k * 128:(k + 1) * 128], ll[b], k * 128)
    for b in range(ns):
        fill_buckets(sb.at[b, 0], column_of(spos[b:b + 1, :]), spos[b:b + 1, :], sl[b], 0)
    gather_until(4)
    flat = sm[...].astype(f32).reshape(X * C * Z * Y, sm.shape[4], 128)
    per = 128 // gain_part
    def shifted(rows, n):
        return rows if n == 0 else pltpu.roll(rows, n, 1)
    chunks = []
    for k in range(width // 128):
        chunks.append(sum(shifted(flat[k * per + i], i * gain_part) for i in range(per)))
    found = jnp.concatenate(chunks, axis=1)
    params[...] = jnp.zeros_like(params)
    params[0:found.shape[0], :] = found.astype(bf)
    share = 32 // table_part
    lane8 = lax.broadcasted_iota(jnp.int32, (1, 128), 1)
    for hd in range(tab.shape[0]):
        rows = sum(shifted(flat[hd * share + i], i * table_part) for i in range(share))
        tab[hd] = jnp.where(lane8 < 32, rows[experts + 2:experts + 3, :], masked)
    gain = params[experts:experts + 1, :].astype(f32)
    for t in range(2):
        m = rows_of(xl, xsh, t).astype(f32)
        n1[pl.ds(t * half, half), :] = (m * rms_scale(m) * gain).astype(bf)
        gb[pl.ds(t * half, half), :] = rows_of(gl, gsh, t)
    wholes = (kl, vl)
    far = (1 - x) * C + c
    ka, kc, kf = {}, {}, {}
    def project(m, t):
        return jnp.dot(n1[pl.ds(t * half, half), :], w_of(m), preferred_element_type=f32).astype(bf)
    for m in range(2):
        gather_until(m)
        wholes[m][s] = project(m, 0).reshape(nl, 128, width)
        for b in range(nb):
            n = m * nb + b
            src = wholes[m].at[s, :, :, pl.ds(b * wide, wide)]
            ka[n] = remote(src, src, kss.at[n, 0], krs.at[n, 0], xdev)
            kc[n] = remote(src, src, kss.at[n, 1], krs.at[n, 1], cdev)
        keep(m, (wk_out, wv_out)[m])
    ks[...] = project(0, 1)
    vs[...] = project(1, 1)
    for t in range(2):
        n1t[:, t * half:(t + 1) * half] = n1[pl.ds(t * half, half), :].T
    gather_until(2)
    for t in range(2):
        q[pl.ds(t * half, half), :] = project(2, t)
    keep(2, wq_out)
    first = lax.broadcasted_iota(jnp.int32, (128, 128), 1) < 64
    for b0 in range(nb):
        for n in (b0, nb + b0):
            ka[n].wait_recv()
            got = wholes[n // nb].at[far, :, :, pl.ds(b0 * wide, wide)]
            kf[n] = remote(got, got, kss.at[n, 2], krs.at[n, 2], cdev)
        for n in (b0, nb + b0):
            kc[n].wait_recv(); kf[n].wait_recv()
        @pl.loop(0, wide // 128)
        def _(i):
            hp = b0 * (wide // 128) + i
            cols = pl.ds(pl.multiple_of(hp * 128, 128), 128)
            for b in range(nl + ns):
                rows, n, kk, vv = item(b, nl, blocks, cols, ks, vs, kl, vl)
                p = probs_of(stack_heads(q[rows, cols], first), kk, (tab[2 * hp], tab[2 * hp + 1]), mine_of(b, nl, lb, sb), n)
                out = dot(p.astype(bf), vv, 1, 0)
                mixed[rows, cols] = jnp.where(first, out[:128], out[128:]).astype(bf)
        if b0 == 0:
            gather_until(3)
            keep(3, wo_out)
    gain = params[experts + 1:experts + 2, :].astype(f32)
    for t in range(2):
        rows = pl.ds(t * 256, 256)
        m = rows_of(xl, xsh, t).astype(f32) + jnp.dot(mixed[rows, :], w_of(3), preferred_element_type=f32)
        mid[rows, :] = m
        n2[rows, :] = (m * rms_scale(m) * gain).astype(bf)
    logits[...] = dot(n2[...], params[...], 1, 1)
    logit_t = dot(params[...], n2[...], 1, 1)[:experts]
    routes = [jnp.concatenate([row_of(ref[i, :, j:j + 1]) for ref in (lr, sr) for i in range(ref.shape[0])], axis=1) for j in range(2)]
    e_iota = lax.broadcasted_iota(jnp.int32, (experts, tokens), 0)
    member = ((e_iota == routes[0]) | (e_iota == routes[1])).astype(f32)
    e = jnp.exp(logit_t - jnp.max(logit_t, axis=0, keepdims=True))
    p = e / jnp.sum(e, axis=0, keepdims=True)
    chosen = member * p
    before = (lax.broadcasted_iota(jnp.int32, (tokens, tokens), 0) < lax.broadcasted_iota(jnp.int32, (tokens, tokens), 1)).astype(f32).astype(bf)
    place = jnp.dot(member.astype(bf), before, preferred_element_type=f32)
    kept = (member > 0.5) & (place < cap)
    weight = jnp.where(kept, chosen / jnp.sum(chosen, axis=0, keepdims=True), 0.0)
    slot = jnp.where(kept, place.astype(jnp.int32), -1)
    s_iota = lax.broadcasted_iota(jnp.int32, (cap, tokens), 0)
    for i in range(experts):
        pick = (s_iota == slot[i:i + 1, :]).astype(f32)
        scale = jnp.sum(pick * weight[i:i + 1, :], axis=1, keepdims=True)
        pick = pick.astype(bf)
        xs[i] = jnp.dot(pick, n2[...], preferred_element_type=f32).astype(bf)
        gs[i] = (jnp.dot(pick, gb[...], preferred_element_type=f32) * scale).astype(bf)
    for cp in kept_copies: cp.wait()
    for group in (h, cc, ka, kc, kf):
        for cp in group.values(): cp.wait_send()
    for i in zc:
        for cp in zc[i]: cp.wait_send()
def post_kernel(nl, ns, blocks, experts, cap, lpos, spos, eo, ri, mid, mixed, logits, lr, sr, gl, gsh, wo, params, eg,
                lout, sout, midg, wog, small, mg, li, si, eg0, eg1, eg2, bg, n2, lg, ev, sem):
    f32, bf = jnp.float32, jnp.bfloat16
    tokens = mid.shape[0]
    fetch = [pltpu.make_async_copy(eg.at[m], ev.at[m], sem.at[m]) for m in range(3)]
    copies = [pltpu.make_async_copy(ev.at[m], out.at[0], sem.at[m]) for m, out in enumerate((eg0, eg1, eg2))]
    for cp in fetch: cp.start()
    gain = params[experts + 1:experts + 2, :].astype(f32)
    lane = lax.broadcasted_iota(jnp.int32, (tokens, 128), 1)
    routes = jnp.concatenate([ref[i] for ref in (lr, sr) for i in range(ref.shape[0])], axis=0)
    member = ((lane == routes[:, 0:1]) | (lane == routes[:, 1:2])).astype(f32)
    after = (lax.broadcasted_iota(jnp.int32, (tokens, tokens), 1) < lax.broadcasted_iota(jnp.int32, (tokens, tokens), 0)).astype(f32).astype(bf)
    place = jnp.dot(after, member.astype(bf), preferred_element_type=f32)
    kept = (member > 0.5) & (place < cap)
    slot = jnp.where(kept, place.astype(jnp.int32), -1)
    lgt = jnp.where(lane < experts, logits[...], -1e30)
    ex = jnp.exp(lgt - jnp.max(lgt, axis=1, keepdims=True))
    p = ex / jnp.sum(ex, axis=1, keepdims=True)
    chosen = member * p
    both = jnp.sum(chosen, axis=1, keepdims=True)
    gate = chosen / both
    fg = jnp.zeros((1, mid.shape[1]), f32)
    for t in range(2):
        at = slice(t * 256, t * 256 + 256)
        rows = pl.ds(t * 256, 256)
        g = rows_of(gl, gsh, t).astype(f32)
        m = mid[rows, :]
        s_iota = lax.broadcasted_iota(jnp.int32, (256, experts * cap), 1)
        fin, back, mean, shares = m, 0.0, 0.0, []
        for j in range(2):
            this = lane[at] == routes[at, j:j + 1]
            place_j = jnp.sum(jnp.where(this, slot[at], 0), axis=1, keepdims=True)
            gate_j = jnp.sum(jnp.where(this, gate[at], 0.0), axis=1, keepdims=True)
            index = jnp.where(place_j >= 0, routes[at, j:j + 1] * cap + place_j, -1)
            pick = (s_iota == index).astype(f32).astype(bf)
            pair = jnp.dot(pick, eo[...], preferred_element_type=f32)
            back += jnp.dot(pick, ri[...], preferred_element_type=f32)
            fin += jnp.where(place_j >= 0, gate_j, 0.0) * pair
            share_j = jnp.sum(g * pair, axis=1, keepdims=True)
            mean += share_j * gate_j
            shares.append(jnp.where(this, share_j, 0.0))
        (lout, sout)[t][...] = fin.astype(bf).reshape(lout.shape)
        pg = member[at] * (shares[0] + shares[1] - mean) / both[at]
        lgrad = (p[at] * (pg - jnp.sum(p[at] * pg, axis=1, keepdims=True))).astype(bf)
        lg[rows, :] = lgrad
        r2 = rms_scale(m)
        u = m * r2
        n2[rows, :] = (u * gain).astype(bf)
        back += jnp.dot(lgrad, params[...], preferred_element_type=f32)
        fg += jnp.sum(back * u, axis=0, keepdims=True)
        w = back * gain
        out = g + r2 * (w - u * jnp.mean(w * u, axis=-1, keepdims=True))
        midg[rows, :] = out
        bg[rows, :] = out.astype(bf)
        mg[rows, :] = dot(out.astype(bf), wo[...], 1, 1).astype(bf)
    for m in range(3):
        fetch[m].wait()
        copies[m].start()
    small[...] = jnp.zeros_like(small)
    small[1:2, :] = fg
    small[2:2 + experts, :] = dot(lg[...], n2[...], 0, 0)[:experts]
    wog[...] = dot(mixed[...], bg[...], 0, 0).astype(bf).reshape(wog.shape)
    lane = lax.broadcasted_iota(jnp.int32, (128, 128), 1)
    edge = jnp.full((128, 128), 4096, jnp.int32)
    for i, e in enumerate(EDGES):
        edge = jnp.where(lane == i, e, edge)
    edge = jnp.where(lane > len(EDGES), -4096, edge)
    def places(out, q_col, k_row):
        k_first = k_row[:, 0:1]
        t = lax.broadcasted_iota(jnp.int32, (128, 256), 1) + k_first
        below = jnp.sum((column_of(k_row) < t).astype(jnp.int32), axis=0, keepdims=True)
        at = jnp.clip(q_col + edge - k_first, 0, 255)
        lo = jnp.take_along_axis(jnp.broadcast_to(below[:, :128], (128, 128)), at & 127, axis=1)
        hi = jnp.take_along_axis(jnp.broadcast_to(below[:, 128:], (128, 128)), at & 127, axis=1)
        out[...] = jnp.where(at < 128, lo, hi) - 1
    me = lax.axis_index("seq")
    for b in range(nl):
        own = column_of(lpos[b:b + 1, pl.ds(pl.multiple_of(me * 128, 128), 128)])
        for c in range(blocks):
            places(li.at[b, c], own, lpos[b:b + 1, c * 128:(c + 1) * 128])
    for b in range(ns):
        places(si.at[b, 0], column_of(spos[b:b + 1, :]), spos[b:b + 1, :])
    for cp in copies: cp.wait()
def front(dims, nl, ns, experts, cap, pieces, table_part, gain_part, arrays, tokens, width, heads, cid):
    X, C, Z, Y = dims
    sm, vm, hbm = pl.BlockSpec(memory_space=pltpu.SMEM), pl.BlockSpec(memory_space=pltpu.VMEM), pl.BlockSpec(memory_space=pl.ANY)
    S, V, sem, bf, f32 = jax.ShapeDtypeStruct, pltpu.VMEM, pltpu.SemaphoreType.DMA, jnp.bfloat16, jnp.float32
    rows_part, small_shape = arrays[2].shape[0], arrays[6].shape
    whole = dims + (rows_part, width)
    slots = S((experts, cap, width), bf)
    rows, short, long = S((tokens, width), bf), S((ns * 128, width), bf), S((X * C, nl, 128, width), bf)
    outs = [S(whole, bf)] * 4 + [S((128, width), bf), S((heads, 1, 128), f32), rows, short, short, long, long, S((width, tokens), bf), rows,
            S((tokens, width), f32), slots, slots, S((tokens, 128), f32), S((nl, X * C, 128, 128), jnp.int32), S((ns, 1, 128, 128), jnp.int32)]
    n, kvn = len(pieces), 2 * (width // 256)
    scr = [V((4,) + whole, bf), V(dims + small_shape, bf)] + [V((tokens, width), bf)] * 3
    scr += [sem((n, Z)), sem((n, Z)), sem((n, 2)), sem((n, 2)), sem((n, 3)), sem((n, 3)), sem((kvn, 3)), sem((kvn, 3)), sem((4,))]
    return pl.pallas_call(functools.partial(front_kernel, dims, nl, ns, experts, cap, pieces, table_part, gain_part), out_shape=outs,
        in_specs=[sm, sm] + [vm] * (len(arrays) - 2), out_specs=[hbm] * 4 + [vm] * (len(outs) - 4), scratch_shapes=scr,
        compiler_params=pltpu.CompilerParams(collective_id=cid, has_side_effects=True, vmem_limit_bytes=60 * 2**20))(*arrays)
def small_rows(experts):
    return -(-(experts + 4) // 8) * 8
def post(nl, ns, blocks, experts, cap, whole, arrays, tokens, width):
    vm, hbm = pl.BlockSpec(memory_space=pltpu.VMEM), pl.BlockSpec(memory_space=pl.ANY)
    S, bf, f32 = jax.ShapeDtypeStruct, jnp.bfloat16, jnp.float32
    eg = arrays[-1]
    outs = [S((nl, 128, width), bf), S((ns, 128, width), bf), S((tokens, width), f32), S(whole, bf), S((small_rows(experts), width), f32), S((tokens, width), bf),
            S((nl, blocks, 128, 128), jnp.int32), S((ns, 1, 128, 128), jnp.int32)] + [S((1,) + eg.shape[1:], f32)] * 3
    V = pltpu.VMEM
    return pl.pallas_call(functools.partial(post_kernel, nl, ns, blocks, experts, cap), out_shape=outs,
        in_specs=[vm] * (len(arrays) - 1) + [hbm], out_specs=[vm] * (len(outs) - 3) + [hbm] * 3,
        scratch_shapes=[V((tokens, width), bf)] * 2 + [V((tokens, 128), bf), V(eg.shape, f32), pltpu.SemaphoreType.DMA((3,))],
        compiler_params=pltpu.CompilerParams(vmem_limit_bytes=60 * 2**20))(*arrays)
def back_kernel(dims, nl, ns, experts, pieces, q, k, v, kl, vl, tab, lb, sb, li, si, mg, wog, n1t, lx_in, sx_in, params, wq_in, wk_in, wv_in, midg_in, small_in,
                lgrad, sgrad, og, qg, kg, vg, small, *refs):
    X, C, Z, Y = dims
    blocks = X * C
    f32, bf = jnp.float32, jnp.bfloat16
    np_ = len(pieces)
    bufs = refs[:4 * np_]
    (gw, dq, ka, va, dkl, dvl, kcb, ka1, kb1, seg, sacc, sbuf, lx, sx, wq, wk, wv, midg, cs, cr, hs, hr, zs, zr, kss, krs, sss, srs, fs) = refs[4 * np_:]
    late = [pltpu.make_async_copy(a, b, fs.at[i]) for i, (a, b) in enumerate(((lx_in, lx), (sx_in, sx), (wq_in, wq), (wk_in, wk), (wv_in, wv), (midg_in, midg)))]
    for cp in late: cp.start()
    s = lax.axis_index("seq"); g = lax.axis_index("dp")
    x, c = s // C, lax.rem(s, C)
    z, y = g // Y, lax.rem(g, Y)
    def zdev(k): return (s, lax.rem(z + k, Z) * Y + y)
    ydev = (s, z * Y + (1 - y)); xdev = ((1 - x) * C + c, g); cdev = (x * C + 1 - c, g)
    greet([zdev(k) for k in range(1, Z)] + [ydev, xdev, cdev])
    half = nl * 128
    wide = 256
    nb = q.shape[1] // wide
    sources = [wog] + [gw.at[i] for i in range(3)]
    outs = [og, qg, kg, vg]
    first = {}; hh = {}; zz = {}
    def add(dst, a, b):
        dst[...] = (a.astype(f32) + b.astype(f32)).astype(dst.dtype)
    def send_core(i):
        m, c0, nc, route = pieces[i]
        first[i] = remote(sources[m].at[:, 1 - c, :, :, :, pl.ds(c0, nc)], bufs[4 * i], cs.at[i], cr.at[i], cdev)
    def stage(i, which):
        m, c0, nc, route = pieces[i]
        b0, b1, b2, b3 = bufs[4 * i:4 * i + 4]
        if which == 0:
            first[i].wait_recv()
            add(b0, sources[m][:, c, :, :, :, c0:c0 + nc], b0[...])
            src = b0.at[:, :, 1 - y] if route == 0 else b0.at[1 - x]
            hh[i, 0] = remote(src, b1, hs.at[i, 0], hr.at[i, 0], ydev if route == 0 else xdev)
        elif which == 1:
            hh[i, 0].wait_recv()
            add(b1, b0[:, :, y] if route == 0 else b0[x], b1[...])
            src = b1.at[1 - x] if route == 0 else b1.at[:, 1 - y]
            hh[i, 1] = remote(src, b2, hs.at[i, 1], hr.at[i, 1], xdev if route == 0 else ydev)
        elif which == 2:
            hh[i, 1].wait_recv()
            add(b2, b1[x] if route == 0 else b1[:, y], b2[...])
            zz[i] = [remote(b2.at[lax.rem(z + k, Z)], b3.at[k - 1], zs.at[i, k], zr.at[i, k], zdev(k)) for k in range(1, Z)]
        else:
            tot = b2[z].astype(f32)
            for k in range(1, Z):
                zz[i][k - 1].wait_recv()
                tot += b3[k - 1].astype(f32)
            outs[m][:, c0:c0 + nc] = tot
    def piece(m, b):
        return [i for i, p in enumerate(pieces) if p[0] == m and (m == 0 or p[1] == b * wide)]
    def weight_grad(m, rows, b):
        cols = slice(b * wide, (b + 1) * wide)
        quarter = n1t.shape[0] // blocks
        for xx in range(X):
            for cc in range(C):
                part = jnp.dot(n1t[pl.ds((xx * C + cc) * quarter, quarter), :], rows[:, cols], preferred_element_type=f32)
                gw[m - 1, xx, cc, :, :, :, cols] = part.astype(bf).reshape(gw.shape[3:6] + (wide,))
        for i in piece(m, b):
            send_core(i)
    parts, wholes = (dkl, dvl), (ka, va)
    kf, kx = {}, {}
    def kv_core(b):
        cols = pl.ds(b * wide, wide)
        for far in range(2):
            for m in range(2):
                n = b * 2 + m
                at = (1 - x if far == 0 else x) * C + 1 - c
                kf[n, far] = remote(parts[m].at[at, :, :, cols], kcb.at[n, far], kss.at[n, far], krs.at[n, far], cdev)
    def kv_chip(b):
        for m in range(2):
            n = b * 2 + m
            kf[n, 0].wait_recv()
            add(ka1.at[n], parts[m][(1 - x) * C + c, :, :, b * wide:(b + 1) * wide], kcb[n, 0])
            kx[n] = remote(ka1.at[n], kb1.at[n], kss.at[n, 2], krs.at[n, 2], xdev)
    def kv_end(b):
        for m in range(2):
            n = b * 2 + m
            kf[n, 1].wait_recv(); kx[n].wait_recv()
            tot = parts[m][s, :, :, b * wide:(b + 1) * wide].astype(f32) + kcb[n, 1].astype(f32) + kb1[n].astype(f32)
            wholes[m][pl.ds(0, half), b * wide:(b + 1) * wide] = tot.astype(bf).reshape(half, wide)
        weight_grad(2, ka, b)
        weight_grad(3, va, b)
    def stages(which, b, *ms):
        for m in ms:
            for i in piece(m, b):
                stage(i, which)
    seg[...] = jnp.zeros_like(seg)
    lane = lax.broadcasted_iota(jnp.int32, (128, 128), 1)
    head_one = lane < 64
    tri = jnp.where(lax.broadcasted_iota(jnp.int32, (128, 128), 0) <= lane, 1.0, 0.0).astype(bf)
    def attend(b0):
        @pl.loop(0, wide // 128)
        def _(i):
            hp = b0 * (wide // 128) + i
            cols = pl.ds(pl.multiple_of(hp * 128, 128), 128)
            for b in range(nl + ns):
                rows, n, kk, vv = item(b, nl, blocks, cols, k, v, kl, vl)
                idx = mine_of(b, nl, li, si)
                qs = stack_heads(q[rows, cols], head_one); gs = stack_heads(mg[rows, cols], head_one)
                p = probs_of(qs, kk, (tab[2 * hp], tab[2 * hp + 1]), mine_of(b, nl, lb, sb), n)
                dp = dot(gs, vv, 1, 1)
                ds = (p * (dp - jnp.sum(p * dp, axis=1, keepdims=True))).astype(bf)
                dqs = dot(ds, kk, 1, 0)
                dkt = dot(qs, ds, 0, 0)
                dvt = dot(gs, p.astype(bf), 0, 0)
                sums = [0, 0]
                for c_ in range(n):
                    pre = dot(ds[:, c_ * 128:(c_ + 1) * 128], tri, 1, 0)
                    at = idx[c_]
                    for e in range(2):
                        sums[e] += jnp.where(at >= 0, jnp.take_along_axis(pre[e * 128:(e + 1) * 128], jnp.maximum(at, 0), axis=1), 0.0)
                for e in range(2):
                    seg[2 * hp + e] += jnp.sum(sums[e], axis=0, keepdims=True)
                dq[rows, cols] = jnp.where(head_one, dqs[:128], dqs[128:]).astype(bf)
                dkt = dkt.T.astype(bf); dvt = dvt.T.astype(bf)
                if b < nl:
                    dkl[:, b, :, cols] = dkt.reshape(n, 128, 128); dvl[:, b, :, cols] = dvt.reshape(n, 128, 128)
                else:
                    ka[rows, cols] = dkt; va[rows, cols] = dvt
    for i in piece(0, 0):
        send_core(i)
    attend(0)
    kv_core(0); weight_grad(1, dq, 0); stages(0, 0, 0)
    attend(1)
    kv_core(1); kv_chip(0); weight_grad(1, dq, 1); stages(0, 0, 1); stages(1, 0, 0)
    attend(2)
    kv_core(2); kv_chip(1); kv_end(0); weight_grad(1, dq, 2); stages(0, 1, 1); stages(1, 0, 1); stages(2, 0, 0)
    attend(3)
    kv_core(3); kv_chip(2); kv_end(1); weight_grad(1, dq, 3); stages(0, 0, 2, 3); stages(0, 2, 1); stages(1, 1, 1); stages(2, 0, 1)
    kv_chip(3); kv_end(2); stages(0, 1, 2, 3); stages(0, 3, 1); stages(1, 0, 2, 3); stages(1, 2, 1); stages(2, 1, 1); stages(3, 0, 0)
    kv_end(3); stages(0, 2, 2, 3); stages(1, 3, 1); stages(1, 1, 2, 3); stages(2, 2, 1); stages(2, 0, 2, 3); stages(3, 0, 1)
    for cp in late: cp.wait()
    gain = params[experts:experts + 1, :].astype(f32)
    ag = jnp.zeros((1, q.shape[1]), f32)
    for t in range(2):
        rows = pl.ds(t * half, half)
        ng = dot(dq[rows, :], wq[...], 1, 1) + dot(ka[rows, :], wk[...], 1, 1) + dot(va[rows, :], wv[...], 1, 1)
        m = rows_of(lx, sx, t).astype(f32)
        r1 = rms_scale(m)
        u = m * r1
        ag += jnp.sum(ng * u, axis=0, keepdims=True)
        w = ng * gain
        (lgrad, sgrad)[t][...] = (midg[rows, :] + r1 * (w - u * jnp.mean(w * u, axis=-1, keepdims=True))).reshape(lgrad.shape)
        if t == 0:
            stages(0, 3, 2, 3); stages(1, 2, 2, 3); stages(2, 3, 1); stages(2, 1, 2, 3); stages(3, 1, 1)
    sacc[0] = small_in[...]
    sacc[0, 0:1, :] = ag
    heads = seg.shape[0]
    spot = lax.broadcasted_iota(jnp.int32, (8, 128), 1)
    for h in range(heads):
        upto = jnp.broadcast_to(seg[h], (8, 128))
        within = upto - jnp.where(spot == 0, 0.0, pltpu.roll(upto, 1, 1))
        at = jnp.where(spot < 16, 15 - spot, jnp.minimum(spot - 1, 30))
        by_bucket = jnp.where((spot == 16) | (spot >= 32), 0.0, jnp.take_along_axis(within, at, axis=1))
        r = 2 + experts + h // 8
        sacc[0, r:r + 1, (h % 8) * 128:(h % 8 + 1) * 128] = by_bucket[0:1, :]
    sc = remote(sacc.at[0], sbuf.at[0], sss.at[0], srs.at[0], cdev)
    stages(1, 3, 2, 3); stages(2, 2, 2, 3); stages(3, 2, 1)
    sc.wait_recv()
    sacc[1] = sacc[0] + sbuf[0]
    sx_ = remote(sacc.at[1], sbuf.at[1], sss.at[1], srs.at[1], xdev)
    stages(2, 3, 2, 3); stages(3, 3, 1); stages(3, 0, 2, 3)
    sx_.wait_recv()
    sacc[2] = sacc[1] + sbuf[1]
    sy = remote(sacc.at[2], sbuf.at[2], sss.at[2], srs.at[2], ydev)
    stages(3, 1, 2, 3)
    sy.wait_recv()
    sacc[3] = sacc[2] + sbuf[2]
    sz = [remote(sacc.at[3], sbuf.at[2 + k], sss.at[2 + k], srs.at[2 + k], zdev(k)) for k in range(1, Z)]
    stages(3, 2, 2, 3); stages(3, 3, 2, 3)
    tot = sacc[3]
    for k in range(1, Z):
        sz[k - 1].wait_recv()
        tot += sbuf[2 + k]
    small[...] = tot
    for cp in [sc, sx_, sy] + sz + list(kx.values()) + list(kf.values()) + list(first.values()) + list(hh.values()) + [w for v_ in zz.values() for w in v_]:
        cp.wait_send()
LATE = (13, 14, 16, 17, 18, 19)
def back(dims, nl, ns, experts, arrays, cid):
    X, C, Z, Y = dims
    q_, small_in = arrays[0], arrays[-1]
    tokens, width = q_.shape
    heads = arrays[5].shape[0]
    nr = width // (X * C * Z * Y)
    wide = 256
    pieces = tuple((0, h * 512, 512, 1) for h in range(width // 512)) + tuple(
        (m, b * wide, wide, 1 if m == 3 and b >= 2 else 0) for m in range(1, 4) for b in range(width // wide))
    n = len(pieces)
    S, sem, bf, f32 = jax.ShapeDtypeStruct, pltpu.SemaphoreType.DMA, jnp.bfloat16, jnp.float32
    V = pltpu.VMEM
    scr = [V(lead + (nr, nc), bf) for m, c0, nc, route in pieces for lead in ((X, Z, Y), (Z, Y) if route else (X, Z), (Z,), (Z - 1,))]
    kvn = 2 * (width // wide)
    long = V((X * C, nl, 128, width), bf)
    rows = V((tokens, width), bf)
    scr += [V((3, X, C, Z, Y, nr, width), bf), rows, rows, rows, long, long,
            V((kvn, 2, nl, 128, wide), bf), V((kvn, nl, 128, wide), bf), V((kvn, nl, 128, wide), bf), V((heads, 1, 128), f32),
            V((4,) + small_in.shape, f32), V((Z + 2,) + small_in.shape, f32)] + [V(arrays[i].shape, arrays[i].dtype) for i in LATE] + [
            sem((n,)), sem((n,)), sem((n, 2)), sem((n, 2)), sem((n, Z)), sem((n, Z)), sem((kvn, 3)), sem((kvn, 3)), sem((Z + 2,)), sem((Z + 2,)), sem((len(LATE),))]
    vm = pl.BlockSpec(memory_space=pltpu.VMEM)
    outs = [S((nl, 128, width), f32), S((ns, 128, width), f32)] + [S((nr, width), f32)] * 4 + [S(small_in.shape, f32)]
    return pl.pallas_call(functools.partial(back_kernel, dims, nl, ns, experts, pieces), out_shape=outs,
        in_specs=[pl.BlockSpec(memory_space=pl.ANY) if i in LATE else vm for i in range(len(arrays))], out_specs=[vm] * len(outs), scratch_shapes=scr,
        compiler_params=pltpu.CompilerParams(collective_id=cid, has_side_effects=True, vmem_limit_bytes=63 * 2**20))(*arrays)

def gelu_parts(v):
    c, a = 0.7978845608, 0.044715
    v2 = v * v
    h = 0.5 + 0.5 * jnp.tanh(v * (c + (c * a) * v2))
    act = v * h
    return act, h + act * (1.0 - h) * (2.0 * c + (6.0 * c * a) * v2)
RING, LAG = 6, 4
SEND_AT, JOIN_AT = 2, 3
def expert_kernel(cap, per, order, todo, wcut, tile, xs, gs, wgi, wui, wdi, eo_out, ri_out, grads, eo_h, ri_h,
                  wall, xr, gr, hall, lall, eo, ri, cb, ab, xb, ob,
                  lsem, xss, xrs, gss, grs, ess, ers, rss, rrs, wss, wrs, wls, css, crs, ass, ars, osem, free):
    dp = lax.axis_size("dp")
    f32, bf = jnp.float32, jnp.bfloat16
    s, x, c, xdev, cdev = seq_places(2)
    g = lax.axis_index("dp")
    def peer(k): return (s, g ^ k)
    greet([xdev, cdev] + [peer(k) for k in range(1, dp)])
    rows_w, ff = wgi.shape; width = xs.shape[2]
    wx, wc, wl, wf = [], [], [], []
    shared = ((wgi, 1), (wui, 2), (wdi, 0))
    parts = [(src, m, f0, nf) for f0, nf in wcut for src, m in shared]
    for n, (src, m, f0, nf) in enumerate(parts):
        a = src.at[:, pl.ds(f0, nf)]
        b = wall.at[m, x, c, :, pl.ds(f0, nf)]
        wx.append(remote(a, b, wss.at[n, 0], wrs.at[n, 0], xdev))
        wc.append(remote(a, b, wss.at[n, 1], wrs.at[n, 1], cdev))
        cp = pltpu.make_async_copy(a, b, wls.at[n]); cp.start(); wl.append(cp)
    sx, sg = {}, {}
    def dispatch(p):
        for k in range(p * per, (p + 1) * per):
            at = pl.ds(k * cap, cap)
            if k == 0:
                sx[0] = pltpu.make_async_copy(xs.at[g], xr.at[at], lsem.at[0]); sx[0].start()
                sg[0] = pltpu.make_async_copy(gs.at[g], gr.at[at], lsem.at[1]); sg[0].start()
            else:
                sx[k] = remote(xs.at[g ^ k], xr.at[at], xss.at[k], xrs.at[k], peer(k))
                sg[k] = remote(gs.at[g ^ k], gr.at[at], gss.at[k], grs.at[k], peer(k))
    for p in order[:-1]: dispatch(p)
    ntile = ff // tile
    re, rr = {}, {}
    wide = 4 * rows_w
    def sources(p): return list(range(p * per, (p + 1) * per))
    def arrive(p):
        for k in sources(p):
            if k == 0: sx[0].wait(); sg[0].wait()
            else: sx[k].wait_recv(); sg[k].wait_recv()
    def inner(p, t0, nt):
        rows = pl.ds(p * per * cap, per * cap)
        @pl.loop(t0, t0 + nt)
        def _(t):
            cols = pl.ds(pl.multiple_of(t * tile, 128), tile)
            w = lambda m: wall[m, :, :, :, cols].reshape(wide, tile)
            gp = jnp.dot(xr[rows, :], w(1), preferred_element_type=f32)
            up = jnp.dot(xr[rows, :], w(2), preferred_element_type=f32)
            hg = jnp.dot(gr[rows, :], w(0), preferred_element_type=f32)
            act, der = gelu_parts(gp)
            hall[0, rows, cols] = (act * up).astype(bf)
            hall[1, rows, cols] = (hg * up * der).astype(bf)
            hall[2, rows, cols] = (hg * act).astype(bf)
    def outer(p):
        rows = pl.ds(p * per * cap, per * cap)
        @pl.loop(0, 4)
        def _(t):
            part = pl.ds(pl.multiple_of(t * rows_w, 128), rows_w)
            tx, tc = t // 2, lax.rem(t, 2)
            eo[:, part] = dot(hall[0, rows, :], wall[0, tx, tc], 1, 1).astype(bf)
            ri[:, part] = (dot(hall[1, rows, :], wall[1, tx, tc], 1, 1) + dot(hall[2, rows, :], wall[2, tx, tc], 1, 1)).astype(bf)
        keep = [pltpu.make_async_copy(eo, eo_h.at[rows], lsem.at[4]), pltpu.make_async_copy(ri, ri_h.at[rows], lsem.at[5])]
        for cp in keep: cp.start()
        for cp in keep: cp.wait()
        for k in sources(p):
            at = pl.ds(k * cap, cap)
            if k == 0:
                re[0] = pltpu.make_async_copy(eo_h.at[at], eo_out.at[g], lsem.at[2]); re[0].start()
                rr[0] = pltpu.make_async_copy(ri_h.at[at], ri_out.at[g], lsem.at[3]); rr[0].start()
            else:
                re[k] = remote(eo_h.at[at], eo_out.at[g], ess.at[k], ers.at[k], peer(k))
                rr[k] = remote(ri_h.at[at], ri_out.at[g], rss.at[k], rrs.at[k], peer(k))
    early = list(todo[:-2])
    last = todo[-1]
    for i, (f0, nf) in enumerate(wcut):
        mine = range(3 * i, 3 * i + 3)
        for n in mine:
            wx[n].wait_recv()
            src, m, f0, nf = parts[n]
            b = wall.at[m, 1 - x, c, :, pl.ds(f0, nf)]
            wf.append(remote(b, b, wss.at[n, 2], wrs.at[n, 2], cdev))
        if i == SEND_AT: dispatch(last)
        if i == 0:
            for p in early: arrive(p)
        for n in mine:
            wl[n].wait(); wc[n].wait_recv(); wf[n].wait_recv()
        for p in early: inner(p, f0 // tile, nf // tile)
        if i == JOIN_AT:
            p = todo[-2]
            arrive(p)
            inner(p, 0, (f0 + nf) // tile)
            early.append(p)
    for p in early: outer(p)
    arrive(last)
    inner(last, 0, ntile)
    outer(last)
    for n in range(len(parts)):
        wx[n].wait_send(); wc[n].wait_send(); wf[n].wait_send()
    total = dp * cap
    @pl.loop(0, total // 256)
    def _(t):
        at = pl.ds(pl.multiple_of(t * 256, 256), 256)
        lall[1, :, at] = xr[at, :].T
        lall[0, :, at] = gr[at, :].T
    nt = 3 * ntile
    def place(n):
        m = n // ntile
        return m, pl.ds(pl.multiple_of((n - m * ntile) * tile, 128), tile)
    def to_core(n):
        m, cols = place(n); r = lax.rem(n, RING)
        return pltpu.make_async_remote_copy(src_ref=wall.at[m, :, 1 - c, :, cols], dst_ref=cb.at[r], send_sem=css.at[r],
            recv_sem=crs.at[r], device_id=cdev, device_id_type=MESH)
    def to_chip(n):
        r = lax.rem(n, RING)
        return pltpu.make_async_remote_copy(src_ref=ab.at[r], dst_ref=xb.at[r], send_sem=ass.at[r],
            recv_sem=ars.at[r], device_id=xdev, device_id_type=MESH)
    def to_out(n):
        m, cols = place(n); r = lax.rem(n, 2)
        return pltpu.make_async_copy(ob.at[r], grads.at[m, :, cols], osem.at[r])
    @pl.loop(0, nt + LAG)
    def _(n):
        @pl.when(n < nt)
        def _():
            m, cols = place(n)
            res = jnp.dot(lall[jnp.minimum(m, 1)], hall[m, :, cols], preferred_element_type=f32)
            wall[m, :, :, :, cols] = res.astype(bf).reshape(2, 2, rows_w, tile)
            @pl.when(n >= RING)
            def _(): pl.semaphore_wait(free.at[0], 1)
            to_core(n).start()
        @pl.when((n >= 1) & (n <= nt))
        def _():
            i = n - 1
            m, cols = place(i); r = lax.rem(i, RING)
            to_core(i).wait_recv()
            @pl.when(i >= RING)
            def _():
                to_chip(i).wait_send()
                pl.semaphore_wait(free.at[1], 1)
            ab[r] = (wall[m, 1 - x, c, :, cols].astype(f32) + cb[r, 1 - x].astype(f32)).astype(bf)
            to_chip(i).start()
        @pl.when(n >= LAG)
        def _():
            j = n - LAG
            m, cols = place(j); r = lax.rem(j, RING)
            to_chip(j).wait_recv()
            to_core(j).wait_send()
            @pl.when(j >= 2)
            def _(): to_out(j).wait()
            ob[lax.rem(j, 2)] = wall[m, x, c, :, cols].astype(f32) + cb[r, x].astype(f32) + xb[r].astype(f32)
            to_out(j).start()
            @pl.when(j < nt - RING)
            def _():
                pl.semaphore_signal(free.at[0], inc=1, device_id=cdev, device_id_type=MESH)
                pl.semaphore_signal(free.at[1], inc=1, device_id=xdev, device_id_type=MESH)
    for j in range(nt - 2, nt): to_out(j).wait()
    for i in range(nt - RING, nt): to_chip(i).wait_send()
    for k in range(dp):
        if k == 0:
            re[0].wait(); rr[0].wait()
        else:
            sx[k].wait_send(); sg[k].wait_send(); re[k].wait(); rr[k].wait()
def expert_all(xs, gs, wg, wu, wd, seq, cid):
    dp, cap, width = xs.shape
    rows_w, ff = wg.shape; total = dp * cap
    group = 320
    per = group // cap
    ng = dp // per
    order = [ng - 2] + [p for p in range(ng - 3, -1, -1)] + [ng - 1]
    todo = list(range(ng))
    sem = pltpu.SemaphoreType.DMA
    bf = jnp.bfloat16
    any_ = pl.BlockSpec(memory_space=pl.ANY)
    V = pltpu.VMEM
    tile = 256
    wcut = tuple((f0, min(512, ff - f0)) for f0 in range(0, ff, 512))
    nw = 3 * len(wcut)
    back = jax.ShapeDtypeStruct((dp, cap, width), bf)
    flat = jax.ShapeDtypeStruct((total, width), bf)
    return pl.pallas_call(functools.partial(expert_kernel, cap, per, order, todo, wcut, tile),
        out_shape=[back, back, jax.ShapeDtypeStruct((3, rows_w, ff), jnp.float32), flat, flat],
        in_specs=[any_] * 5, out_specs=[any_] * 5,
        scratch_shapes=[V((3, seq // 2, 2, rows_w, ff), bf), V((total, width), bf), V((total, width), bf), V((3, total, ff), bf),
        V((2, width, total), bf), V((group, width), bf), V((group, width), bf),
        V((RING, seq // 2, rows_w, tile), bf), V((RING, rows_w, tile), bf), V((RING, rows_w, tile), bf), V((2, rows_w, tile), jnp.float32)]
        + [sem((6,))] + [sem((dp,))] * 8 + [sem((nw, 3))] * 2 + [sem((nw,))] + [sem((RING,))] * 4 + [sem((2,)), pltpu.SemaphoreType.REGULAR((2,))],
        compiler_params=pltpu.CompilerParams(collective_id=cid, has_side_effects=True, vmem_limit_bytes=63 * 2**20))(xs, gs, wg, wu, wd)[:3]


def on_device(
    long_tokens,
    short_tokens,
    long_grad_out,
    short_grad_out,
    query_weight,
    key_weight,
    value_weight,
    output_weight,
    attn_gain,
    ffn_gain,
    rel_table,
    router_weight,
    gate_weight,
    up_weight,
    down_weight,
    long_positions,
    short_positions,
    long_lengths,
    short_lengths,
    long_routes,
    short_routes,
):
    long_items, quarter, model_width = long_tokens.shape
    short_items, short_len = (short_tokens.shape[0], short_tokens.shape[1])
    long_rows = long_items * quarter
    tokens = long_rows + short_items * short_len
    local_experts = gate_weight.shape[0]
    dp_size = lax.axis_size("dp")
    experts = local_experts * dp_size
    capacity = (5 * tokens + 2 * experts - 1) // (2 * experts)
    seq_size = lax.axis_size("seq")
    dims = (seq_size // 2, 2, dp_size // 2, 2)
    devices = seq_size * dp_size
    table_part, gain_part = rel_table.shape[0], attn_gain.shape[0]
    small = jnp.concatenate([router_weight.T, attn_gain[None], ffn_gain[None]], 0)
    small = jnp.pad(small, ((0, 1), (0, 128 - gain_part)))
    table_row = jnp.pad(rel_table[None], ((experts + 2, 0), (0, 128 - table_part)))
    small = jnp.pad(small + table_row, ((0, -(experts + 3) % 16), (0, 0)))
    rows_part = query_weight.shape[0]
    cuts = 2 if rows_part % 32 == 0 else 1
    cut = rows_part // cuts
    pieces = tuple((m, h * cut, cut, (m + h) % 2) for m in range(4) for h in range(cuts))
    pieces = ((4, 0, small.shape[0], 0),) + tuple(p[:3] + (0,) for p in pieces)
    sizes = (long_items, short_items, seq_size, experts, capacity)
    places = (long_positions, short_positions)
    routes = (long_routes, short_routes)
    (
        key_all,
        value_all,
        query_all,
        output_all,
        params,
        table,
        queries,
        keys,
        values,
        long_keys,
        long_values,
        normed_t,
        mixed,
        middle,
        outgoing,
        out_slots,
        logits,
        long_buckets,
        short_buckets,
    ) = front(
        dims,
        long_items,
        short_items,
        experts,
        capacity,
        pieces,
        table_part,
        gain_part,
        (long_lengths, short_lengths, key_weight, value_weight, query_weight, output_weight, small)
        + places
        + (long_tokens, short_tokens, long_grad_out, short_grad_out)
        + routes,
        tokens,
        model_width,
        HEADS,
        0,
    )
    key_all, value_all, query_all, output_all = (
        block.reshape(devices * rows_part, model_width)
        for block in (key_all, value_all, query_all, output_all)
    )
    heads_args = (queries, keys, values, long_keys, long_values, table)
    grads = (long_grad_out, short_grad_out, output_all, params)
    back_rows, back_grads, expert_grads = expert_all(
        outgoing, out_slots, gate_weight[0], up_weight[0], down_weight[0], seq_size, 4
    )
    (
        long_out,
        short_out,
        middle_grad,
        output_local,
        small_local,
        mixed_grad,
        long_places,
        short_places,
        down_grad,
        gate_grad,
        up_grad,
    ) = post(
        *sizes,
        dims + (rows_part, model_width),
        places
        + tuple(block.reshape(-1, model_width) for block in (back_rows, back_grads))
        + (middle, mixed, logits) + routes + grads + (expert_grads,),
        tokens,
        model_width,
    )
    long_grad_in, short_grad_in, output_grad, query_grad, key_grad, value_grad, small_sum = back(
        dims,
        long_items,
        short_items,
        experts,
        heads_args
        + (long_buckets, short_buckets, long_places, short_places)
        + (mixed_grad, output_local, normed_t, long_tokens, short_tokens, params)
        + (query_all, key_all, value_all, middle_grad, small_local),
        2,
    )
    place = lax.axis_index("seq") * dp_size + lax.axis_index("dp")

    def own(row, column, size, count=1):
        return lax.dynamic_slice(small_sum, (row, column), (count, size))

    entry = place * table_part
    head_at = entry // BUCKETS
    table_grad = own(2 + experts + head_at // 8, head_at % 8 * 128 + entry % BUCKETS, table_part)
    summed = (
        query_grad,
        key_grad,
        value_grad,
        output_grad,
        own(0, place * gain_part, gain_part)[0],
        own(1, place * gain_part, gain_part)[0],
        table_grad[0],
        own(2, place * rows_part, rows_part, experts).T,
    )
    return (
        long_out,
        short_out,
        long_grad_in,
        short_grad_in,
        summed[0],
        summed[1],
        summed[2],
        summed[3],
        summed[4],
        summed[5],
        summed[6],
        summed[7],
        gate_grad,
        up_grad,
        down_grad,
    )


def solution(mesh):
    placed = (
        P("dp", "seq", None),
        P(("seq", "dp"), None, None),
        P("dp", "seq", None),
        P(("seq", "dp"), None, None),
        P(("seq", "dp"), None),
        P(("seq", "dp"), None),
        P(("seq", "dp"), None),
        P(("seq", "dp"), None),
        P(("seq", "dp")),
        P(("seq", "dp")),
        P(("seq", "dp")),
        P(("seq", "dp"), None),
        P("dp", "seq", None),
        P("dp", "seq", None),
        P("dp", "seq", None),
        P("dp", None),
        P(("seq", "dp"), None),
        P("dp"),
        P(("seq", "dp")),
        P("dp", "seq", None),
        P(("seq", "dp"), None, None),
    )
    return jax.shard_map(
        on_device,
        mesh=mesh,
        in_specs=placed,
        out_specs=(
            P("dp", "seq", None),
            P(("seq", "dp"), None, None),
            P("dp", "seq", None),
            P(("seq", "dp"), None, None),
            P(("seq", "dp"), None),
            P(("seq", "dp"), None),
            P(("seq", "dp"), None),
            P(("seq", "dp"), None),
            P(("seq", "dp")),
            P(("seq", "dp")),
            P(("seq", "dp")),
            P(("seq", "dp"), None),
            P("dp", "seq", None),
            P("dp", "seq", None),
            P("dp", "seq", None),
        ),
        check_vma=False,
    )
```

```python
import functools

import jax
import jax.numpy as jnp
from jax import lax
from jax.experimental import pallas as pl
from jax.experimental.pallas import tpu as pltpu
from jax.sharding import PartitionSpec as P

MESH = pl.DeviceIdType.MESH

HEADS = 16
HEAD = 64
BUCKETS = 32


epsilon = 1e-06
masked = -1e30


def seq_places(C):
    s = lax.axis_index("seq"); g = lax.axis_index("dp")
    x, c = s // C, lax.rem(s, C)
    return s, x, c, ((1 - x) * C + c, g), (x * C + 1 - c, g)
def greet(devs):
    bar = pltpu.get_barrier_semaphore()
    for d in devs:
        pl.semaphore_signal(bar, inc=1, device_id=d, device_id_type=MESH)
    pl.semaphore_wait(bar, len(devs))
def remote(src, dst, ss, rs, dev):
    cp = pltpu.make_async_remote_copy(src_ref=src, dst_ref=dst, send_sem=ss, recv_sem=rs, device_id=dev, device_id_type=MESH)
    cp.start()
    return cp
EDGES = (-90, -63, -45, -31, -22, -15, -11, -7, -6, -5, -4, -3, -2, -1, 0, 1, 2, 3, 4, 5, 6, 7, 8, 12, 16, 23, 32, 46, 64, 91)
FAR = (12, 16, 23, 32, 46, 64, 91)
def fill_buckets(out, q_col, k_row, length, base):
    r = k_row - q_col
    n = jnp.abs(r)
    far = jnp.full(r.shape, 8, jnp.int32)
    for e in FAR:
        far += (n >= e).astype(jnp.int32)
    b = jnp.where(n < 8, n, far) + jnp.where(r > 0, 16, 0)
    j = lax.broadcasted_iota(jnp.int32, r.shape, 1) + base
    out[...] = jnp.where(j < length, b, 32)
def dot(a, b, ca, cb):
    return lax.dot_general(a, b, (((ca,), (cb,)), ((), ())), preferred_element_type=jnp.float32)
def probs_of(qs, kk, tabs, bucket_ref, blocks):
    s = dot(qs, kk, 1, 1)
    t = [jnp.broadcast_to(tab, (128, 128)) for tab in tabs]
    bias = [jnp.concatenate([jnp.take_along_axis(x, bucket_ref[c], axis=1) for x in t], axis=0) for c in range(blocks)]
    s = s + (jnp.concatenate(bias, axis=1) if blocks > 1 else bias[0])
    p = jnp.exp(s - jnp.max(s, axis=1, keepdims=True))
    return p * (1.0 / jnp.sum(p, axis=1, keepdims=True))
def stack_heads(rows, first):
    return jnp.concatenate([jnp.where(first, rows, 0), jnp.where(first, 0, rows)], axis=0)
def column_of(row):
    i = lax.broadcasted_iota(jnp.int32, (128, 128), 0)
    return jnp.sum(jnp.where(i == lax.broadcasted_iota(jnp.int32, (128, 128), 1), row, 0), axis=1, keepdims=True)
def rows_of(long_ref, short_ref, t):
    ref = long_ref if t == 0 else short_ref
    return ref[...].reshape(ref.shape[0] * ref.shape[1], ref.shape[2])
def rms_scale(mid):
    return lax.rsqrt(jnp.mean(mid * mid, axis=-1, keepdims=True) + epsilon)
def item(b, nl, blocks, cols, k, v, kl, vl):
    rows = pl.ds(b * 128, 128)
    if b < nl:
        return rows, blocks, kl[:, b, :, cols].reshape(blocks * 128, 128), vl[:, b, :, cols].reshape(blocks * 128, 128)
    short = pl.ds((b - nl) * 128, 128)
    return rows, 1, k[short, cols], v[short, cols]
def mine_of(b, nl, long_ref, short_ref):
    return long_ref.at[b] if b < nl else short_ref.at[b - nl]
def front_kernel(dims, nl, ns, experts, cap, pieces, table_part, gain_part, ll, sl, wk_in, wv_in, wq_in, wo_in, small_in, lpos, spos, xl, xsh, gl, gsh, lr, sr,
                 wk_out, wv_out, wq_out, wo_out, params, tab, q, ks, vs, kl, vl, n1t, mixed, mid, xs, gs, logits, lb, sb,
                 wall, sm, n1, n2, gb, zs, zr, hs, hr, cs, cr, kss, krs, osem):
    X, C, Z, Y = dims
    blocks = X * C
    f32, bf = jnp.float32, jnp.bfloat16
    s, x, c, xdev, cdev = seq_places(C)
    g = lax.axis_index("dp")
    z, y = g // Y, lax.rem(g, Y)
    def zdev(k): return (s, lax.rem(z + k, Z) * Y + y)
    ydev = (s, z * Y + (1 - y))
    tokens, width = q.shape
    half = nl * 128
    wide = 256
    nb = width // wide
    greet([zdev(k) for k in range(1, Z)] + [ydev, xdev, cdev])
    ins = (wk_in, wv_in, wq_in, wo_in)
    def part(i, *lead):
        m, r0, nr, route = pieces[i]
        if m == 4:
            return sm.at[lead + (slice(None),) * (4 - len(lead))]
        return wall.at[(m,) + lead + (slice(None),) * (4 - len(lead)) + (pl.ds(r0, nr),)]
    zc, h, cc = {}, {}, {}
    for i, (m, r0, nr, route) in enumerate(pieces):
        src = small_in if m == 4 else ins[m].at[pl.ds(r0, nr)]
        zc[i] = [remote(src, part(i, x, c, z, y), zs.at[i, k], zr.at[i, k], zdev(k)) for k in range(1, Z)]
    for m in range(4):
        wall[m, x, c, z, y] = ins[m][...]
    sm[x, c, z, y] = small_in[...]
    def gather_stage(i, stage):
        route = pieces[i][3]
        if stage == 0:
            for k in range(1, Z): zc[i][k - 1].wait_recv()
            mine = part(i, x, c, slice(None), y)
            h[i, 0] = remote(mine, mine, hs.at[i, 0], hr.at[i, 0], xdev if route == 0 else ydev)
            cc[i, 0] = remote(mine, mine, cs.at[i, 0], cr.at[i, 0], cdev)
        elif stage == 1:
            h[i, 0].wait_recv()
            if route == 0:
                both, got = part(i, slice(None), c, slice(None), y), part(i, 1 - x, c, slice(None), y)
            else:
                both, got = part(i, x, c), part(i, x, c, slice(None), 1 - y)
            h[i, 1] = remote(both, both, hs.at[i, 1], hr.at[i, 1], ydev if route == 0 else xdev)
            cc[i, 1] = remote(got, got, cs.at[i, 1], cr.at[i, 1], cdev)
        else:
            h[i, 1].wait_recv()
            got = part(i, slice(None), c, slice(None), 1 - y) if route == 0 else part(i, 1 - x, c)
            cc[i, 2] = remote(got, got, cs.at[i, 2], cr.at[i, 2], cdev)
    np_ = len(pieces)
    steps = [(t - st, st) for t in range(np_ + 2) for st in range(3) if 0 <= t - st < np_]
    done = [0]
    def gather_until(m):
        last = max(i for i, p in enumerate(pieces) if p[0] == m)
        while True:
            i, st = steps[done[0]]
            gather_stage(i, st)
            done[0] += 1
            if (i, st) == (last, 2): break
        for i, p in enumerate(pieces):
            if p[0] == m:
                for k in range(3): cc[i, k].wait_recv()
    kept_copies = []
    def keep(m, out):
        cp = pltpu.make_async_copy(wall.at[m], out, osem.at[m]); cp.start(); kept_copies.append(cp)
    def w_of(m):
        return wall[m].reshape(width, width)
    for b in range(nl):
        own = column_of(lpos[b:b + 1, pl.ds(pl.multiple_of(s * 128, 128), 128)])
        for k in range(blocks):
            fill_buckets(lb.at[b, k], own, lpos[b:b + 1, k * 128:(k + 1) * 128], ll[b], k * 128)
    for b in range(ns):
        fill_buckets(sb.at[b, 0], column_of(spos[b:b + 1, :]), spos[b:b + 1, :], sl[b], 0)
    gather_until(4)
    flat = sm[...].astype(f32).reshape(X * C * Z * Y, sm.shape[4], 128)
    per = 128 // gain_part
    def shifted(rows, n):
        return rows if n == 0 else pltpu.roll(rows, n, 1)
    chunks = []
    for k in range(width // 128):
        chunks.append(sum(shifted(flat[k * per + i], i * gain_part) for i in range(per)))
    found = jnp.concatenate(chunks, axis=1)
    params[...] = jnp.zeros_like(params)
    params[0:found.shape[0], :] = found.astype(bf)
    share = 32 // table_part
    lane8 = lax.broadcasted_iota(jnp.int32, (1, 128), 1)
    for hd in range(tab.shape[0]):
        rows = sum(shifted(flat[hd * share + i], i * table_part) for i in range(share))
        tab[hd] = jnp.where(lane8 < 32, rows[experts + 2:experts + 3, :], masked)
    gain = params[experts:experts + 1, :].astype(f32)
    for t in range(2):
        m = rows_of(xl, xsh, t).astype(f32)
        n1[pl.ds(t * half, half), :] = (m * rms_scale(m) * gain).astype(bf)
        gb[pl.ds(t * half, half), :] = rows_of(gl, gsh, t)
    wholes = (kl, vl)
    far = (1 - x) * C + c
    ka, kc, kf = {}, {}, {}
    def project(m, t):
        return jnp.dot(n1[pl.ds(t * half, half), :], w_of(m), preferred_element_type=f32).astype(bf)
    for m in range(2):
        gather_until(m)
        wholes[m][s] = project(m, 0).reshape(nl, 128, width)
        for b in range(nb):
            n = m * nb + b
            src = wholes[m].at[s, :, :, pl.ds(b * wide, wide)]
            ka[n] = remote(src, src, kss.at[n, 0], krs.at[n, 0], xdev)
            kc[n] = remote(src, src, kss.at[n, 1], krs.at[n, 1], cdev)
        keep(m, (wk_out, wv_out)[m])
    ks[...] = project(0, 1)
    vs[...] = project(1, 1)
    for t in range(2):
        n1t[:, t * half:(t + 1) * half] = n1[pl.ds(t * half, half), :].T
    gather_until(2)
    for t in range(2):
        q[pl.ds(t * half, half), :] = project(2, t)
    keep(2, wq_out)
    first = lax.broadcasted_iota(jnp.int32, (128, 128), 1) < 64
    for b0 in range(nb):
        for n in (b0, nb + b0):
            ka[n].wait_recv()
            got = wholes[n // nb].at[far, :, :, pl.ds(b0 * wide, wide)]
            kf[n] = remote(got, got, kss.at[n, 2], krs.at[n, 2], cdev)
        for n in (b0, nb + b0):
            kc[n].wait_recv(); kf[n].wait_recv()
        @pl.loop(0, wide // 128)
        def _(i):
            hp = b0 * (wide // 128) + i
            cols = pl.ds(pl.multiple_of(hp * 128, 128), 128)
            for b in range(nl + ns):
                rows, n, kk, vv = item(b, nl, blocks, cols, ks, vs, kl, vl)
                p = probs_of(stack_heads(q[rows, cols], first), kk, (tab[2 * hp], tab[2 * hp + 1]), mine_of(b, nl, lb, sb), n)
                out = dot(p.astype(bf), vv, 1, 0)
                mixed[rows, cols] = jnp.where(first, out[:128], out[128:]).astype(bf)
        if b0 == 0:
            gather_until(3)
            keep(3, wo_out)
    gain = params[experts + 1:experts + 2, :].astype(f32)
    for t in range(2):
        rows = pl.ds(t * 256, 256)
        m = rows_of(xl, xsh, t).astype(f32) + jnp.dot(mixed[rows, :], w_of(3), preferred_element_type=f32)
        mid[rows, :] = m
        n2[rows, :] = (m * rms_scale(m) * gain).astype(bf)
    logits[...] = dot(n2[...], params[...], 1, 1)
    logit_t = dot(params[...], n2[...], 1, 1)[:experts]
    routes = [jnp.concatenate([ref[i, j:j + 1, :] for ref in (lr, sr) for i in range(ref.shape[0])], axis=1) for j in range(2)]
    e_iota = lax.broadcasted_iota(jnp.int32, (experts, tokens), 0)
    member = ((e_iota == routes[0]) | (e_iota == routes[1])).astype(f32)
    e = jnp.exp(logit_t - jnp.max(logit_t, axis=0, keepdims=True))
    p = e / jnp.sum(e, axis=0, keepdims=True)
    chosen = member * p
    before = (lax.broadcasted_iota(jnp.int32, (tokens, tokens), 0) < lax.broadcasted_iota(jnp.int32, (tokens, tokens), 1)).astype(f32).astype(bf)
    place = jnp.dot(member.astype(bf), before, preferred_element_type=f32)
    kept = (member > 0.5) & (place < cap)
    weight = jnp.where(kept, chosen / jnp.sum(chosen, axis=0, keepdims=True), 0.0)
    slot = jnp.where(kept, place.astype(jnp.int32), -1)
    s_iota = lax.broadcasted_iota(jnp.int32, (cap, tokens), 0)
    for i in range(experts):
        pick = (s_iota == slot[i:i + 1, :]).astype(f32)
        scale = jnp.sum(pick * weight[i:i + 1, :], axis=1, keepdims=True)
        pick = pick.astype(bf)
        xs[i] = jnp.dot(pick, n2[...], preferred_element_type=f32).astype(bf)
        gs[i] = (jnp.dot(pick, gb[...], preferred_element_type=f32) * scale).astype(bf)
    for cp in kept_copies: cp.wait()
    for group in (h, cc, ka, kc, kf):
        for cp in group.values(): cp.wait_send()
    for i in zc:
        for cp in zc[i]: cp.wait_send()
def post_kernel(nl, ns, blocks, experts, cap, lpos, spos, eo, ri, mid, mixed, logits, lr, sr, gl, gsh, wo, params, eg,
                lout, sout, midg, wog, small, mg, li, si, eg0, eg1, eg2, bg, n2, lg, ev, sem):
    f32, bf = jnp.float32, jnp.bfloat16
    tokens = mid.shape[0]
    fetch = [pltpu.make_async_copy(eg.at[m], ev.at[m], sem.at[m]) for m in range(3)]
    copies = [pltpu.make_async_copy(ev.at[m], out.at[0], sem.at[m]) for m, out in enumerate((eg0, eg1, eg2))]
    for cp in fetch: cp.start()
    gain = params[experts + 1:experts + 2, :].astype(f32)
    lane = lax.broadcasted_iota(jnp.int32, (tokens, 128), 1)
    routes = [jnp.concatenate([column_of(ref[i, j:j + 1, :]) for ref in (lr, sr) for i in range(ref.shape[0])], axis=0) for j in range(2)]
    member = ((lane == routes[0]) | (lane == routes[1])).astype(f32)
    after = (lax.broadcasted_iota(jnp.int32, (tokens, tokens), 1) < lax.broadcasted_iota(jnp.int32, (tokens, tokens), 0)).astype(f32).astype(bf)
    place = jnp.dot(after, member.astype(bf), preferred_element_type=f32)
    kept = (member > 0.5) & (place < cap)
    slot = jnp.where(kept, place.astype(jnp.int32), -1)
    lgt = jnp.where(lane < experts, logits[...], -1e30)
    ex = jnp.exp(lgt - jnp.max(lgt, axis=1, keepdims=True))
    p = ex / jnp.sum(ex, axis=1, keepdims=True)
    chosen = member * p
    both = jnp.sum(chosen, axis=1, keepdims=True)
    gate = chosen / both
    fg = jnp.zeros((1, mid.shape[1]), f32)
    for t in range(2):
        at = slice(t * 256, t * 256 + 256)
        rows = pl.ds(t * 256, 256)
        g = rows_of(gl, gsh, t).astype(f32)
        m = mid[rows, :]
        s_iota = lax.broadcasted_iota(jnp.int32, (256, experts * cap), 1)
        fin, back, mean, shares = m, 0.0, 0.0, []
        for j in range(2):
            this = lane[at] == routes[j][at]
            place_j = jnp.sum(jnp.where(this, slot[at], 0), axis=1, keepdims=True)
            gate_j = jnp.sum(jnp.where(this, gate[at], 0.0), axis=1, keepdims=True)
            index = jnp.where(place_j >= 0, routes[j][at] * cap + place_j, -1)
            pick = (s_iota == index).astype(f32).astype(bf)
            pair = jnp.dot(pick, eo[...], preferred_element_type=f32)
            back += jnp.dot(pick, ri[...], preferred_element_type=f32)
            fin += jnp.where(place_j >= 0, gate_j, 0.0) * pair
            share_j = jnp.sum(g * pair, axis=1, keepdims=True)
            mean += share_j * gate_j
            shares.append(jnp.where(this, share_j, 0.0))
        (lout, sout)[t][...] = fin.astype(bf).reshape(lout.shape)
        pg = member[at] * (shares[0] + shares[1] - mean) / both[at]
        lgrad = (p[at] * (pg - jnp.sum(p[at] * pg, axis=1, keepdims=True))).astype(bf)
        lg[rows, :] = lgrad
        r2 = rms_scale(m)
        u = m * r2
        n2[rows, :] = (u * gain).astype(bf)
        back += jnp.dot(lgrad, params[...], preferred_element_type=f32)
        fg += jnp.sum(back * u, axis=0, keepdims=True)
        w = back * gain
        out = g + r2 * (w - u * jnp.mean(w * u, axis=-1, keepdims=True))
        midg[rows, :] = out
        bg[rows, :] = out.astype(bf)
        mg[rows, :] = dot(out.astype(bf), wo[...], 1, 1).astype(bf)
    for m in range(3):
        fetch[m].wait()
        copies[m].start()
    small[...] = jnp.zeros_like(small)
    small[1:2, :] = fg
    small[2:2 + experts, :] = dot(lg[...], n2[...], 0, 0)[:experts]
    wog[...] = dot(mixed[...], bg[...], 0, 0).astype(bf).reshape(wog.shape)
    lane = lax.broadcasted_iota(jnp.int32, (128, 128), 1)
    edge = jnp.full((128, 128), 4096, jnp.int32)
    for i, e in enumerate(EDGES):
        edge = jnp.where(lane == i, e, edge)
    edge = jnp.where(lane > len(EDGES), -4096, edge)
    def places(out, q_col, k_row):
        k_first = k_row[:, 0:1]
        t = lax.broadcasted_iota(jnp.int32, (128, 256), 1) + k_first
        below = jnp.sum((column_of(k_row) < t).astype(jnp.int32), axis=0, keepdims=True)
        at = jnp.clip(q_col + edge - k_first, 0, 255)
        lo = jnp.take_along_axis(jnp.broadcast_to(below[:, :128], (128, 128)), at & 127, axis=1)
        hi = jnp.take_along_axis(jnp.broadcast_to(below[:, 128:], (128, 128)), at & 127, axis=1)
        out[...] = jnp.where(at < 128, lo, hi) - 1
    me = lax.axis_index("seq")
    for b in range(nl):
        own = column_of(lpos[b:b + 1, pl.ds(pl.multiple_of(me * 128, 128), 128)])
        for c in range(blocks):
            places(li.at[b, c], own, lpos[b:b + 1, c * 128:(c + 1) * 128])
    for b in range(ns):
        places(si.at[b, 0], column_of(spos[b:b + 1, :]), spos[b:b + 1, :])
    for cp in copies: cp.wait()
def front(dims, nl, ns, experts, cap, pieces, table_part, gain_part, arrays, tokens, width, heads, cid):
    X, C, Z, Y = dims
    sm, vm, hbm = pl.BlockSpec(memory_space=pltpu.SMEM), pl.BlockSpec(memory_space=pltpu.VMEM), pl.BlockSpec(memory_space=pl.ANY)
    S, V, sem, bf, f32 = jax.ShapeDtypeStruct, pltpu.VMEM, pltpu.SemaphoreType.DMA, jnp.bfloat16, jnp.float32
    rows_part, small_shape = arrays[2].shape[0], arrays[6].shape
    whole = dims + (rows_part, width)
    slots = S((experts, cap, width), bf)
    rows, short, long = S((tokens, width), bf), S((ns * 128, width), bf), S((X * C, nl, 128, width), bf)
    outs = [S(whole, bf)] * 4 + [S((128, width), bf), S((heads, 1, 128), f32), rows, short, short, long, long, S((width, tokens), bf), rows,
            S((tokens, width), f32), slots, slots, S((tokens, 128), f32), S((nl, X * C, 128, 128), jnp.int32), S((ns, 1, 128, 128), jnp.int32)]
    n, kvn = len(pieces), 2 * (width // 256)
    scr = [V((4,) + whole, bf), V(dims + small_shape, bf)] + [V((tokens, width), bf)] * 3
    scr += [sem((n, Z)), sem((n, Z)), sem((n, 2)), sem((n, 2)), sem((n, 3)), sem((n, 3)), sem((kvn, 3)), sem((kvn, 3)), sem((4,))]
    return pl.pallas_call(functools.partial(front_kernel, dims, nl, ns, experts, cap, pieces, table_part, gain_part), out_shape=outs,
        in_specs=[sm, sm] + [vm] * (len(arrays) - 2), out_specs=[hbm] * 4 + [vm] * (len(outs) - 4), scratch_shapes=scr,
        compiler_params=pltpu.CompilerParams(collective_id=cid, has_side_effects=True, vmem_limit_bytes=60 * 2**20))(*arrays)
def small_rows(experts):
    return -(-(experts + 4) // 8) * 8
def post(nl, ns, blocks, experts, cap, whole, arrays, tokens, width):
    vm, hbm = pl.BlockSpec(memory_space=pltpu.VMEM), pl.BlockSpec(memory_space=pl.ANY)
    S, bf, f32 = jax.ShapeDtypeStruct, jnp.bfloat16, jnp.float32
    eg = arrays[-1]
    outs = [S((nl, 128, width), bf), S((ns, 128, width), bf), S((tokens, width), f32), S(whole, bf), S((small_rows(experts), width), f32), S((tokens, width), bf),
            S((nl, blocks, 128, 128), jnp.int32), S((ns, 1, 128, 128), jnp.int32)] + [S((1,) + eg.shape[1:], f32)] * 3
    V = pltpu.VMEM
    return pl.pallas_call(functools.partial(post_kernel, nl, ns, blocks, experts, cap), out_shape=outs,
        in_specs=[vm] * (len(arrays) - 1) + [hbm], out_specs=[vm] * (len(outs) - 3) + [hbm] * 3,
        scratch_shapes=[V((tokens, width), bf)] * 2 + [V((tokens, 128), bf), V(eg.shape, f32), pltpu.SemaphoreType.DMA((3,))],
        compiler_params=pltpu.CompilerParams(vmem_limit_bytes=60 * 2**20))(*arrays)
def back_kernel(dims, nl, ns, experts, pieces, q, k, v, kl, vl, tab, lb, sb, li, si, mg, wog, n1t, lx_in, sx_in, params, wq_in, wk_in, wv_in, midg_in, small_in,
                lgrad, sgrad, og, qg, kg, vg, small, *refs):
    X, C, Z, Y = dims
    blocks = X * C
    f32, bf = jnp.float32, jnp.bfloat16
    np_ = len(pieces)
    bufs = refs[:4 * np_]
    (gw, dq, ka, va, dkl, dvl, kcb, ka1, kb1, seg, sacc, sbuf, lx, sx, wq, wk, wv, midg, cs, cr, hs, hr, zs, zr, kss, krs, sss, srs, fs) = refs[4 * np_:]
    late = [pltpu.make_async_copy(a, b, fs.at[i]) for i, (a, b) in enumerate(((lx_in, lx), (sx_in, sx), (wq_in, wq), (wk_in, wk), (wv_in, wv), (midg_in, midg)))]
    for cp in late: cp.start()
    s = lax.axis_index("seq"); g = lax.axis_index("dp")
    x, c = s // C, lax.rem(s, C)
    z, y = g // Y, lax.rem(g, Y)
    def zdev(k): return (s, lax.rem(z + k, Z) * Y + y)
    ydev = (s, z * Y + (1 - y)); xdev = ((1 - x) * C + c, g); cdev = (x * C + 1 - c, g)
    greet([zdev(k) for k in range(1, Z)] + [ydev, xdev, cdev])
    half = nl * 128
    wide = 256
    nb = q.shape[1] // wide
    sources = [wog] + [gw.at[i] for i in range(3)]
    outs = [og, qg, kg, vg]
    first = {}; hh = {}; zz = {}
    def add(dst, a, b):
        dst[...] = (a.astype(f32) + b.astype(f32)).astype(dst.dtype)
    def send_core(i):
        m, c0, nc, route = pieces[i]
        first[i] = remote(sources[m].at[:, 1 - c, :, :, :, pl.ds(c0, nc)], bufs[4 * i], cs.at[i], cr.at[i], cdev)
    def stage(i, which):
        m, c0, nc, route = pieces[i]
        b0, b1, b2, b3 = bufs[4 * i:4 * i + 4]
        if which == 0:
            first[i].wait_recv()
            add(b0, sources[m][:, c, :, :, :, c0:c0 + nc], b0[...])
            src = b0.at[:, :, 1 - y] if route == 0 else b0.at[1 - x]
            hh[i, 0] = remote(src, b1, hs.at[i, 0], hr.at[i, 0], ydev if route == 0 else xdev)
        elif which == 1:
            hh[i, 0].wait_recv()
            add(b1, b0[:, :, y] if route == 0 else b0[x], b1[...])
            src = b1.at[1 - x] if route == 0 else b1.at[:, 1 - y]
            hh[i, 1] = remote(src, b2, hs.at[i, 1], hr.at[i, 1], xdev if route == 0 else ydev)
        elif which == 2:
            hh[i, 1].wait_recv()
            add(b2, b1[x] if route == 0 else b1[:, y], b2[...])
            zz[i] = [remote(b2.at[lax.rem(z + k, Z)], b3.at[k - 1], zs.at[i, k], zr.at[i, k], zdev(k)) for k in range(1, Z)]
        else:
            tot = b2[z].astype(f32)
            for k in range(1, Z):
                zz[i][k - 1].wait_recv()
                tot += b3[k - 1].astype(f32)
            outs[m][:, c0:c0 + nc] = tot
    def piece(m, b):
        return [i for i, p in enumerate(pieces) if p[0] == m and (m == 0 or p[1] == b * wide)]
    def weight_grad(m, rows, b):
        cols = slice(b * wide, (b + 1) * wide)
        quarter = n1t.shape[0] // blocks
        for xx in range(X):
            for cc in range(C):
                part = jnp.dot(n1t[pl.ds((xx * C + cc) * quarter, quarter), :], rows[:, cols], preferred_element_type=f32)
                gw[m - 1, xx, cc, :, :, :, cols] = part.astype(bf).reshape(gw.shape[3:6] + (wide,))
        for i in piece(m, b):
            send_core(i)
    parts, wholes = (dkl, dvl), (ka, va)
    kf, kx = {}, {}
    def kv_core(b):
        cols = pl.ds(b * wide, wide)
        for far in range(2):
            for m in range(2):
                n = b * 2 + m
                at = (1 - x if far == 0 else x) * C + 1 - c
                kf[n, far] = remote(parts[m].at[at, :, :, cols], kcb.at[n, far], kss.at[n, far], krs.at[n, far], cdev)
    def kv_chip(b):
        for m in range(2):
            n = b * 2 + m
            kf[n, 0].wait_recv()
            add(ka1.at[n], parts[m][(1 - x) * C + c, :, :, b * wide:(b + 1) * wide], kcb[n, 0])
            kx[n] = remote(ka1.at[n], kb1.at[n], kss.at[n, 2], krs.at[n, 2], xdev)
    def kv_end(b):
        for m in range(2):
            n = b * 2 + m
            kf[n, 1].wait_recv(); kx[n].wait_recv()
            tot = parts[m][s, :, :, b * wide:(b + 1) * wide].astype(f32) + kcb[n, 1].astype(f32) + kb1[n].astype(f32)
            wholes[m][pl.ds(0, half), b * wide:(b + 1) * wide] = tot.astype(bf).reshape(half, wide)
        weight_grad(2, ka, b)
        weight_grad(3, va, b)
    def stages(which, b, *ms):
        for m in ms:
            for i in piece(m, b):
                stage(i, which)
    seg[...] = jnp.zeros_like(seg)
    lane = lax.broadcasted_iota(jnp.int32, (128, 128), 1)
    head_one = lane < 64
    tri = jnp.where(lax.broadcasted_iota(jnp.int32, (128, 128), 0) <= lane, 1.0, 0.0).astype(bf)
    def attend(b0):
        @pl.loop(0, wide // 128)
        def _(i):
            hp = b0 * (wide // 128) + i
            cols = pl.ds(pl.multiple_of(hp * 128, 128), 128)
            for b in range(nl + ns):
                rows, n, kk, vv = item(b, nl, blocks, cols, k, v, kl, vl)
                idx = mine_of(b, nl, li, si)
                qs = stack_heads(q[rows, cols], head_one); gs = stack_heads(mg[rows, cols], head_one)
                p = probs_of(qs, kk, (tab[2 * hp], tab[2 * hp + 1]), mine_of(b, nl, lb, sb), n)
                dp = dot(gs, vv, 1, 1)
                ds = (p * (dp - jnp.sum(p * dp, axis=1, keepdims=True))).astype(bf)
                dqs = dot(ds, kk, 1, 0)
                dkt = dot(qs, ds, 0, 0)
                dvt = dot(gs, p.astype(bf), 0, 0)
                sums = [0, 0]
                for c_ in range(n):
                    pre = dot(ds[:, c_ * 128:(c_ + 1) * 128], tri, 1, 0)
                    at = idx[c_]
                    for e in range(2):
                        sums[e] += jnp.where(at >= 0, jnp.take_along_axis(pre[e * 128:(e + 1) * 128], jnp.maximum(at, 0), axis=1), 0.0)
                for e in range(2):
                    seg[2 * hp + e] += jnp.sum(sums[e], axis=0, keepdims=True)
                dq[rows, cols] = jnp.where(head_one, dqs[:128], dqs[128:]).astype(bf)
                dkt = dkt.T.astype(bf); dvt = dvt.T.astype(bf)
                if b < nl:
                    dkl[:, b, :, cols] = dkt.reshape(n, 128, 128); dvl[:, b, :, cols] = dvt.reshape(n, 128, 128)
                else:
                    ka[rows, cols] = dkt; va[rows, cols] = dvt
    for i in piece(0, 0):
        send_core(i)
    attend(0)
    kv_core(0); weight_grad(1, dq, 0); stages(0, 0, 0)
    attend(1)
    kv_core(1); kv_chip(0); weight_grad(1, dq, 1); stages(0, 0, 1); stages(1, 0, 0)
    attend(2)
    kv_core(2); kv_chip(1); kv_end(0); weight_grad(1, dq, 2); stages(0, 1, 1); stages(1, 0, 1); stages(2, 0, 0)
    attend(3)
    kv_core(3); kv_chip(2); kv_end(1); kv_chip(3); weight_grad(1, dq, 3); stages(0, 0, 2, 3); stages(0, 2, 1); stages(1, 1, 1); stages(2, 0, 1)
    kv_end(2); stages(0, 1, 2, 3); stages(0, 3, 1); stages(1, 0, 2, 3); stages(1, 2, 1); stages(2, 1, 1); stages(3, 0, 0)
    kv_end(3); stages(0, 2, 2, 3); stages(1, 3, 1); stages(1, 1, 2, 3); stages(2, 2, 1); stages(2, 0, 2, 3); stages(3, 0, 1)
    for cp in late: cp.wait()
    gain = params[experts:experts + 1, :].astype(f32)
    ag = jnp.zeros((1, q.shape[1]), f32)
    for t in range(2):
        rows = pl.ds(t * half, half)
        ng = dot(dq[rows, :], wq[...], 1, 1) + dot(ka[rows, :], wk[...], 1, 1) + dot(va[rows, :], wv[...], 1, 1)
        m = rows_of(lx, sx, t).astype(f32)
        r1 = rms_scale(m)
        u = m * r1
        ag += jnp.sum(ng * u, axis=0, keepdims=True)
        w = ng * gain
        (lgrad, sgrad)[t][...] = (midg[rows, :] + r1 * (w - u * jnp.mean(w * u, axis=-1, keepdims=True))).reshape(lgrad.shape)
        if t == 0:
            stages(0, 3, 2, 3); stages(1, 2, 2, 3); stages(2, 3, 1); stages(2, 1, 2, 3); stages(3, 1, 1)
    sacc[0] = small_in[...]
    sacc[0, 0:1, :] = ag
    heads = seg.shape[0]
    spot = lax.broadcasted_iota(jnp.int32, (8, 128), 1)
    for h in range(heads):
        upto = jnp.broadcast_to(seg[h], (8, 128))
        within = upto - jnp.where(spot == 0, 0.0, pltpu.roll(upto, 1, 1))
        at = jnp.where(spot < 16, 15 - spot, jnp.minimum(spot - 1, 30))
        by_bucket = jnp.where((spot == 16) | (spot >= 32), 0.0, jnp.take_along_axis(within, at, axis=1))
        r = 2 + experts + h // 8
        sacc[0, r:r + 1, (h % 8) * 128:(h % 8 + 1) * 128] = by_bucket[0:1, :]
    sc = remote(sacc.at[0], sbuf.at[0], sss.at[0], srs.at[0], cdev)
    stages(1, 3, 2, 3); stages(2, 2, 2, 3); stages(3, 2, 1)
    sc.wait_recv()
    sacc[1] = sacc[0] + sbuf[0]
    sx_ = remote(sacc.at[1], sbuf.at[1], sss.at[1], srs.at[1], xdev)
    stages(2, 3, 2, 3); stages(3, 3, 1); stages(3, 0, 2, 3)
    sx_.wait_recv()
    sacc[2] = sacc[1] + sbuf[1]
    sy = remote(sacc.at[2], sbuf.at[2], sss.at[2], srs.at[2], ydev)
    stages(3, 1, 2, 3)
    sy.wait_recv()
    sacc[3] = sacc[2] + sbuf[2]
    sz = [remote(sacc.at[3], sbuf.at[2 + k], sss.at[2 + k], srs.at[2 + k], zdev(k)) for k in range(1, Z)]
    stages(3, 2, 2, 3); stages(3, 3, 2, 3)
    tot = sacc[3]
    for k in range(1, Z):
        sz[k - 1].wait_recv()
        tot += sbuf[2 + k]
    small[...] = tot
    for cp in [sc, sx_, sy] + sz + list(kx.values()) + list(kf.values()) + list(first.values()) + list(hh.values()) + [w for v_ in zz.values() for w in v_]:
        cp.wait_send()
LATE = (13, 14, 16, 17, 18, 19)
def back(dims, nl, ns, experts, arrays, cid):
    X, C, Z, Y = dims
    q_, small_in = arrays[0], arrays[-1]
    tokens, width = q_.shape
    heads = arrays[5].shape[0]
    nr = width // (X * C * Z * Y)
    wide = 256
    pieces = tuple((0, h * 512, 512, 1) for h in range(width // 512)) + tuple(
        (m, b * wide, wide, 1 if m == 3 and b >= 2 else 0) for m in range(1, 4) for b in range(width // wide))
    n = len(pieces)
    S, sem, bf, f32 = jax.ShapeDtypeStruct, pltpu.SemaphoreType.DMA, jnp.bfloat16, jnp.float32
    V = pltpu.VMEM
    scr = [V(lead + (nr, nc), bf) for m, c0, nc, route in pieces for lead in ((X, Z, Y), (Z, Y) if route else (X, Z), (Z,), (Z - 1,))]
    kvn = 2 * (width // wide)
    long = V((X * C, nl, 128, width), bf)
    rows = V((tokens, width), bf)
    scr += [V((3, X, C, Z, Y, nr, width), bf), rows, rows, rows, long, long,
            V((kvn, 2, nl, 128, wide), bf), V((kvn, nl, 128, wide), bf), V((kvn, nl, 128, wide), bf), V((heads, 1, 128), f32),
            V((4,) + small_in.shape, f32), V((Z + 2,) + small_in.shape, f32)] + [V(arrays[i].shape, arrays[i].dtype) for i in LATE] + [
            sem((n,)), sem((n,)), sem((n, 2)), sem((n, 2)), sem((n, Z)), sem((n, Z)), sem((kvn, 3)), sem((kvn, 3)), sem((Z + 2,)), sem((Z + 2,)), sem((len(LATE),))]
    vm = pl.BlockSpec(memory_space=pltpu.VMEM)
    outs = [S((nl, 128, width), f32), S((ns, 128, width), f32)] + [S((nr, width), f32)] * 4 + [S(small_in.shape, f32)]
    return pl.pallas_call(functools.partial(back_kernel, dims, nl, ns, experts, pieces), out_shape=outs,
        in_specs=[pl.BlockSpec(memory_space=pl.ANY) if i in LATE else vm for i in range(len(arrays))], out_specs=[vm] * len(outs), scratch_shapes=scr,
        compiler_params=pltpu.CompilerParams(collective_id=cid, has_side_effects=True, vmem_limit_bytes=63 * 2**20))(*arrays)

def gelu_parts(v):
    c, a = 0.7978845608, 0.044715
    v2 = v * v
    h = 0.5 + 0.5 * jnp.tanh(v * (c + (c * a) * v2))
    act = v * h
    return act, h + act * (1.0 - h) * (2.0 * c + (6.0 * c * a) * v2)
RING, LAG = 6, 4
SEND_AT, JOIN_AT = 2, 3
def expert_kernel(cap, per, order, todo, wcut, tile, xs, gs, wgi, wui, wdi, eo_out, ri_out, grads, eo_h, ri_h,
                  wall, xr, gr, hall, lall, eo, ri, cb, ab, xb, ob,
                  lsem, xss, xrs, gss, grs, ess, ers, rss, rrs, wss, wrs, wls, css, crs, ass, ars, osem, free):
    dp = lax.axis_size("dp")
    f32, bf = jnp.float32, jnp.bfloat16
    s, x, c, xdev, cdev = seq_places(2)
    g = lax.axis_index("dp")
    def peer(k): return (s, g ^ k)
    greet([xdev, cdev] + [peer(k) for k in range(1, dp)])
    rows_w, ff = wgi.shape; width = xs.shape[2]
    wx, wc, wl, wf = [], [], [], []
    shared = ((wgi, 1), (wui, 2), (wdi, 0))
    parts = [(src, m, f0, nf) for f0, nf in wcut for src, m in shared]
    for n, (src, m, f0, nf) in enumerate(parts):
        a = src.at[:, pl.ds(f0, nf)]
        b = wall.at[m, x, c, :, pl.ds(f0, nf)]
        wx.append(remote(a, b, wss.at[n, 0], wrs.at[n, 0], xdev))
        wc.append(remote(a, b, wss.at[n, 1], wrs.at[n, 1], cdev))
        cp = pltpu.make_async_copy(a, b, wls.at[n]); cp.start(); wl.append(cp)
    sx, sg = {}, {}
    def dispatch(p):
        for k in range(p * per, (p + 1) * per):
            at = pl.ds(k * cap, cap)
            if k == 0:
                sx[0] = pltpu.make_async_copy(xs.at[g], xr.at[at], lsem.at[0]); sx[0].start()
                sg[0] = pltpu.make_async_copy(gs.at[g], gr.at[at], lsem.at[1]); sg[0].start()
            else:
                sx[k] = remote(xs.at[g ^ k], xr.at[at], xss.at[k], xrs.at[k], peer(k))
                sg[k] = remote(gs.at[g ^ k], gr.at[at], gss.at[k], grs.at[k], peer(k))
    for p in order[:-1]: dispatch(p)
    ntile = ff // tile
    re, rr = {}, {}
    wide = 4 * rows_w
    def sources(p): return list(range(p * per, (p + 1) * per))
    def arrive(p):
        for k in sources(p):
            if k == 0: sx[0].wait(); sg[0].wait()
            else: sx[k].wait_recv(); sg[k].wait_recv()
    def inner(p, t0, nt):
        rows = pl.ds(p * per * cap, per * cap)
        @pl.loop(t0, t0 + nt)
        def _(t):
            cols = pl.ds(pl.multiple_of(t * tile, 128), tile)
            w = lambda m: wall[m, :, :, :, cols].reshape(wide, tile)
            gp = jnp.dot(xr[rows, :], w(1), preferred_element_type=f32)
            up = jnp.dot(xr[rows, :], w(2), preferred_element_type=f32)
            hg = jnp.dot(gr[rows, :], w(0), preferred_element_type=f32)
            act, der = gelu_parts(gp)
            hall[0, rows, cols] = (act * up).astype(bf)
            hall[1, rows, cols] = (hg * up * der).astype(bf)
            hall[2, rows, cols] = (hg * act).astype(bf)
    def outer(p):
        rows = pl.ds(p * per * cap, per * cap)
        @pl.loop(0, 4)
        def _(t):
            part = pl.ds(pl.multiple_of(t * rows_w, 128), rows_w)
            tx, tc = t // 2, lax.rem(t, 2)
            eo[:, part] = dot(hall[0, rows, :], wall[0, tx, tc], 1, 1).astype(bf)
            ri[:, part] = (dot(hall[1, rows, :], wall[1, tx, tc], 1, 1) + dot(hall[2, rows, :], wall[2, tx, tc], 1, 1)).astype(bf)
        keep = [pltpu.make_async_copy(eo, eo_h.at[rows], lsem.at[4]), pltpu.make_async_copy(ri, ri_h.at[rows], lsem.at[5])]
        for cp in keep: cp.start()
        for cp in keep: cp.wait()
        for k in sources(p):
            at = pl.ds(k * cap, cap)
            if k == 0:
                re[0] = pltpu.make_async_copy(eo_h.at[at], eo_out.at[g], lsem.at[2]); re[0].start()
                rr[0] = pltpu.make_async_copy(ri_h.at[at], ri_out.at[g], lsem.at[3]); rr[0].start()
            else:
                re[k] = remote(eo_h.at[at], eo_out.at[g], ess.at[k], ers.at[k], peer(k))
                rr[k] = remote(ri_h.at[at], ri_out.at[g], rss.at[k], rrs.at[k], peer(k))
    early = list(todo[:-2])
    last = todo[-1]
    for i, (f0, nf) in enumerate(wcut):
        mine = range(3 * i, 3 * i + 3)
        for n in mine:
            wx[n].wait_recv()
            src, m, f0, nf = parts[n]
            b = wall.at[m, 1 - x, c, :, pl.ds(f0, nf)]
            wf.append(remote(b, b, wss.at[n, 2], wrs.at[n, 2], cdev))
        if i == SEND_AT: dispatch(last)
        if i == 0:
            for p in early: arrive(p)
        for n in mine:
            wl[n].wait(); wc[n].wait_recv(); wf[n].wait_recv()
        for p in early: inner(p, f0 // tile, nf // tile)
        if i == JOIN_AT:
            p = todo[-2]
            arrive(p)
            inner(p, 0, (f0 + nf) // tile)
            early.append(p)
    for p in early: outer(p)
    arrive(last)
    inner(last, 0, ntile)
    outer(last)
    for n in range(len(parts)):
        wx[n].wait_send(); wc[n].wait_send(); wf[n].wait_send()
    total = dp * cap
    @pl.loop(0, total // 256)
    def _(t):
        at = pl.ds(pl.multiple_of(t * 256, 256), 256)
        lall[1, :, at] = xr[at, :].T
        lall[0, :, at] = gr[at, :].T
    nt = 3 * ntile
    def place(n):
        m = n // ntile
        return m, pl.ds(pl.multiple_of((n - m * ntile) * tile, 128), tile)
    def to_core(n):
        m, cols = place(n); r = lax.rem(n, RING)
        return pltpu.make_async_remote_copy(src_ref=wall.at[m, :, 1 - c, :, cols], dst_ref=cb.at[r], send_sem=css.at[r],
            recv_sem=crs.at[r], device_id=cdev, device_id_type=MESH)
    def to_chip(n):
        r = lax.rem(n, RING)
        return pltpu.make_async_remote_copy(src_ref=ab.at[r], dst_ref=xb.at[r], send_sem=ass.at[r],
            recv_sem=ars.at[r], device_id=xdev, device_id_type=MESH)
    def to_out(n):
        m, cols = place(n); r = lax.rem(n, 2)
        return pltpu.make_async_copy(ob.at[r], grads.at[m, :, cols], osem.at[r])
    @pl.loop(0, nt + LAG)
    def _(n):
        @pl.when(n < nt)
        def _():
            m, cols = place(n)
            res = jnp.dot(lall[jnp.minimum(m, 1)], hall[m, :, cols], preferred_element_type=f32)
            wall[m, :, :, :, cols] = res.astype(bf).reshape(2, 2, rows_w, tile)
            @pl.when(n >= RING)
            def _(): pl.semaphore_wait(free.at[0], 1)
            to_core(n).start()
        @pl.when((n >= 1) & (n <= nt))
        def _():
            i = n - 1
            m, cols = place(i); r = lax.rem(i, RING)
            to_core(i).wait_recv()
            @pl.when(i >= RING)
            def _():
                to_chip(i).wait_send()
                pl.semaphore_wait(free.at[1], 1)
            ab[r] = (wall[m, 1 - x, c, :, cols].astype(f32) + cb[r, 1 - x].astype(f32)).astype(bf)
            to_chip(i).start()
        @pl.when(n >= LAG)
        def _():
            j = n - LAG
            m, cols = place(j); r = lax.rem(j, RING)
            to_chip(j).wait_recv()
            to_core(j).wait_send()
            @pl.when(j >= 2)
            def _(): to_out(j).wait()
            ob[lax.rem(j, 2)] = wall[m, x, c, :, cols].astype(f32) + cb[r, x].astype(f32) + xb[r].astype(f32)
            to_out(j).start()
            @pl.when(j < nt - RING)
            def _():
                pl.semaphore_signal(free.at[0], inc=1, device_id=cdev, device_id_type=MESH)
                pl.semaphore_signal(free.at[1], inc=1, device_id=xdev, device_id_type=MESH)
    for j in range(nt - 2, nt): to_out(j).wait()
    for i in range(nt - RING, nt): to_chip(i).wait_send()
    for k in range(dp):
        if k == 0:
            re[0].wait(); rr[0].wait()
        else:
            sx[k].wait_send(); sg[k].wait_send(); re[k].wait(); rr[k].wait()
def expert_all(xs, gs, wg, wu, wd, seq, cid):
    dp, cap, width = xs.shape
    rows_w, ff = wg.shape; total = dp * cap
    group = 320
    per = group // cap
    ng = dp // per
    order = [ng - 2] + [p for p in range(ng - 3, -1, -1)] + [ng - 1]
    todo = list(range(ng))
    sem = pltpu.SemaphoreType.DMA
    bf = jnp.bfloat16
    any_ = pl.BlockSpec(memory_space=pl.ANY)
    V = pltpu.VMEM
    tile = 256
    wcut = tuple((f0, min(512, ff - f0)) for f0 in range(0, ff, 512))
    nw = 3 * len(wcut)
    back = jax.ShapeDtypeStruct((dp, cap, width), bf)
    flat = jax.ShapeDtypeStruct((total, width), bf)
    return pl.pallas_call(functools.partial(expert_kernel, cap, per, order, todo, wcut, tile),
        out_shape=[back, back, jax.ShapeDtypeStruct((3, rows_w, ff), jnp.float32), flat, flat],
        in_specs=[any_] * 5, out_specs=[any_] * 5,
        scratch_shapes=[V((3, seq // 2, 2, rows_w, ff), bf), V((total, width), bf), V((total, width), bf), V((3, total, ff), bf),
        V((2, width, total), bf), V((group, width), bf), V((group, width), bf),
        V((RING, seq // 2, rows_w, tile), bf), V((RING, rows_w, tile), bf), V((RING, rows_w, tile), bf), V((2, rows_w, tile), jnp.float32)]
        + [sem((6,))] + [sem((dp,))] * 8 + [sem((nw, 3))] * 2 + [sem((nw,))] + [sem((RING,))] * 4 + [sem((2,)), pltpu.SemaphoreType.REGULAR((2,))],
        compiler_params=pltpu.CompilerParams(collective_id=cid, has_side_effects=True, vmem_limit_bytes=63 * 2**20))(xs, gs, wg, wu, wd)[:3]


def on_device(
    long_tokens,
    short_tokens,
    long_grad_out,
    short_grad_out,
    query_weight,
    key_weight,
    value_weight,
    output_weight,
    attn_gain,
    ffn_gain,
    rel_table,
    router_weight,
    gate_weight,
    up_weight,
    down_weight,
    long_positions,
    short_positions,
    long_lengths,
    short_lengths,
    long_routes,
    short_routes,
):
    long_items, quarter, model_width = long_tokens.shape
    short_items, short_len = (short_tokens.shape[0], short_tokens.shape[1])
    long_rows = long_items * quarter
    tokens = long_rows + short_items * short_len
    local_experts = gate_weight.shape[0]
    dp_size = lax.axis_size("dp")
    experts = local_experts * dp_size
    capacity = (5 * tokens + 2 * experts - 1) // (2 * experts)
    seq_size = lax.axis_size("seq")
    dims = (seq_size // 2, 2, dp_size // 2, 2)
    devices = seq_size * dp_size
    table_part, gain_part = rel_table.shape[0], attn_gain.shape[0]
    small = jnp.concatenate([router_weight.T, attn_gain[None], ffn_gain[None]], 0)
    small = jnp.pad(small, ((0, 1), (0, 128 - gain_part)))
    table_row = jnp.pad(rel_table[None], ((experts + 2, 0), (0, 128 - table_part)))
    small = jnp.pad(small + table_row, ((0, -(experts + 3) % 16), (0, 0)))
    rows_part = query_weight.shape[0]
    cuts = 2 if rows_part % 32 == 0 else 1
    cut = rows_part // cuts
    pieces = tuple((m, h * cut, cut, (m + h) % 2) for m in range(4) for h in range(cuts))
    pieces = ((4, 0, small.shape[0], 0),) + tuple(p[:3] + (0,) for p in pieces)
    sizes = (long_items, short_items, seq_size, experts, capacity)
    places = (long_positions, short_positions)
    routes = (long_routes.swapaxes(1, 2), short_routes.swapaxes(1, 2))
    (
        key_all,
        value_all,
        query_all,
        output_all,
        params,
        table,
        queries,
        keys,
        values,
        long_keys,
        long_values,
        normed_t,
        mixed,
        middle,
        outgoing,
        out_slots,
        logits,
        long_buckets,
        short_buckets,
    ) = front(
        dims,
        long_items,
        short_items,
        experts,
        capacity,
        pieces,
        table_part,
        gain_part,
        (long_lengths, short_lengths, key_weight, value_weight, query_weight, output_weight, small)
        + places
        + (long_tokens, short_tokens, long_grad_out, short_grad_out)
        + routes,
        tokens,
        model_width,
        HEADS,
        0,
    )
    key_all, value_all, query_all, output_all = (
        block.reshape(devices * rows_part, model_width)
        for block in (key_all, value_all, query_all, output_all)
    )
    heads_args = (queries, keys, values, long_keys, long_values, table)
    grads = (long_grad_out, short_grad_out, output_all, params)
    back_rows, back_grads, expert_grads = expert_all(
        outgoing, out_slots, gate_weight[0], up_weight[0], down_weight[0], seq_size, 4
    )
    (
        long_out,
        short_out,
        middle_grad,
        output_local,
        small_local,
        mixed_grad,
        long_places,
        short_places,
        down_grad,
        gate_grad,
        up_grad,
    ) = post(
        *sizes,
        dims + (rows_part, model_width),
        places
        + tuple(block.reshape(-1, model_width) for block in (back_rows, back_grads))
        + (middle, mixed, logits) + routes + grads + (expert_grads,),
        tokens,
        model_width,
    )
    long_grad_in, short_grad_in, output_grad, query_grad, key_grad, value_grad, small_sum = back(
        dims,
        long_items,
        short_items,
        experts,
        heads_args
        + (long_buckets, short_buckets, long_places, short_places)
        + (mixed_grad, output_local, normed_t, long_tokens, short_tokens, params)
        + (query_all, key_all, value_all, middle_grad, small_local),
        2,
    )
    place = lax.axis_index("seq") * dp_size + lax.axis_index("dp")

    def own(row, column, size, count=1):
        return lax.dynamic_slice(small_sum, (row, column), (count, size))

    entry = place * table_part
    head_at = entry // BUCKETS
    table_grad = own(2 + experts + head_at // 8, head_at % 8 * 128 + entry % BUCKETS, table_part)
    summed = (
        query_grad,
        key_grad,
        value_grad,
        output_grad,
        own(0, place * gain_part, gain_part)[0],
        own(1, place * gain_part, gain_part)[0],
        table_grad[0],
        own(2, place * rows_part, rows_part, experts).T,
    )
    return (
        long_out,
        short_out,
        long_grad_in,
        short_grad_in,
        summed[0],
        summed[1],
        summed[2],
        summed[3],
        summed[4],
        summed[5],
        summed[6],
        summed[7],
        gate_grad,
        up_grad,
        down_grad,
    )


def solution(mesh):
    placed = (
        P("dp", "seq", None),
        P(("seq", "dp"), None, None),
        P("dp", "seq", None),
        P(("seq", "dp"), None, None),
        P(("seq", "dp"), None),
        P(("seq", "dp"), None),
        P(("seq", "dp"), None),
        P(("seq", "dp"), None),
        P(("seq", "dp")),
        P(("seq", "dp")),
        P(("seq", "dp")),
        P(("seq", "dp"), None),
        P("dp", "seq", None),
        P("dp", "seq", None),
        P("dp", "seq", None),
        P("dp", None),
        P(("seq", "dp"), None),
        P("dp"),
        P(("seq", "dp")),
        P("dp", "seq", None),
        P(("seq", "dp"), None, None),
    )
    return jax.shard_map(
        on_device,
        mesh=mesh,
        in_specs=placed,
        out_specs=(
            P("dp", "seq", None),
            P(("seq", "dp"), None, None),
            P("dp", "seq", None),
            P(("seq", "dp"), None, None),
            P(("seq", "dp"), None),
            P(("seq", "dp"), None),
            P(("seq", "dp"), None),
            P(("seq", "dp"), None),
            P(("seq", "dp")),
            P(("seq", "dp")),
            P(("seq", "dp")),
            P(("seq", "dp"), None),
            P("dp", "seq", None),
            P("dp", "seq", None),
            P("dp", "seq", None),
        ),
        check_vma=False,
    )
```

```python
import functools

import jax
import jax.numpy as jnp
from jax import lax
from jax.experimental import pallas as pl
from jax.experimental.pallas import tpu as pltpu
from jax.sharding import PartitionSpec as P

MESH = pl.DeviceIdType.MESH

HEADS = 16
HEAD = 64
BUCKETS = 32


epsilon = 1e-06
masked = -1e30


def seq_places(C):
    s = lax.axis_index("seq"); g = lax.axis_index("dp")
    x, c = s // C, lax.rem(s, C)
    return s, x, c, ((1 - x) * C + c, g), (x * C + 1 - c, g)
def greet(devs):
    bar = pltpu.get_barrier_semaphore()
    for d in devs:
        pl.semaphore_signal(bar, inc=1, device_id=d, device_id_type=MESH)
    pl.semaphore_wait(bar, len(devs))
def remote(src, dst, ss, rs, dev):
    cp = pltpu.make_async_remote_copy(src_ref=src, dst_ref=dst, send_sem=ss, recv_sem=rs, device_id=dev, device_id_type=MESH)
    cp.start()
    return cp
EDGES = (-90, -63, -45, -31, -22, -15, -11, -7, -6, -5, -4, -3, -2, -1, 0, 1, 2, 3, 4, 5, 6, 7, 8, 12, 16, 23, 32, 46, 64, 91)
FAR = (12, 16, 23, 32, 46, 64, 91)
def fill_buckets(out, q_col, k_row, length, base):
    r = k_row - q_col
    n = jnp.abs(r)
    far = jnp.full(r.shape, 8, jnp.int32)
    for e in FAR:
        far += (n >= e).astype(jnp.int32)
    b = jnp.where(n < 8, n, far) + jnp.where(r > 0, 16, 0)
    j = lax.broadcasted_iota(jnp.int32, r.shape, 1) + base
    out[...] = jnp.where(j < length, b, 32)
def dot(a, b, ca, cb):
    return lax.dot_general(a, b, (((ca,), (cb,)), ((), ())), preferred_element_type=jnp.float32)
def probs_of(qs, kk, tabs, bucket_ref, blocks):
    s = dot(qs, kk, 1, 1)
    t = [jnp.broadcast_to(tab, (128, 128)) for tab in tabs]
    bias = [jnp.concatenate([jnp.take_along_axis(x, bucket_ref[c], axis=1) for x in t], axis=0) for c in range(blocks)]
    s = s + (jnp.concatenate(bias, axis=1) if blocks > 1 else bias[0])
    p = jnp.exp(s - jnp.max(s, axis=1, keepdims=True))
    return p * (1.0 / jnp.sum(p, axis=1, keepdims=True))
def stack_heads(rows, first):
    return jnp.concatenate([jnp.where(first, rows, 0), jnp.where(first, 0, rows)], axis=0)
def column_of(row):
    i = lax.broadcasted_iota(jnp.int32, (128, 128), 0)
    return jnp.sum(jnp.where(i == lax.broadcasted_iota(jnp.int32, (128, 128), 1), row, 0), axis=1, keepdims=True)
def rows_of(long_ref, short_ref, t):
    ref = long_ref if t == 0 else short_ref
    return ref[...].reshape(ref.shape[0] * ref.shape[1], ref.shape[2])
def rms_scale(mid):
    return lax.rsqrt(jnp.mean(mid * mid, axis=-1, keepdims=True) + epsilon)
def item(b, nl, blocks, cols, k, v, kl, vl):
    rows = pl.ds(b * 128, 128)
    if b < nl:
        return rows, blocks, kl[:, b, :, cols].reshape(blocks * 128, 128), vl[:, b, :, cols].reshape(blocks * 128, 128)
    short = pl.ds((b - nl) * 128, 128)
    return rows, 1, k[short, cols], v[short, cols]
def mine_of(b, nl, long_ref, short_ref):
    return long_ref.at[b] if b < nl else short_ref.at[b - nl]
def front_kernel(dims, nl, ns, experts, cap, pieces, table_part, gain_part, ll, sl, wk_in, wv_in, wq_in, wo_in, small_in, lpos, spos, xl, xsh, gl, gsh, lr, sr,
                 wk_out, wv_out, wq_out, wo_out, params, tab, q, ks, vs, kl, vl, n1t, mixed, mid, xs, gs, logits, lb, sb,
                 wall, sm, n1, n2, gb, zs, zr, hs, hr, cs, cr, kss, krs, osem):
    X, C, Z, Y = dims
    blocks = X * C
    f32, bf = jnp.float32, jnp.bfloat16
    s, x, c, xdev, cdev = seq_places(C)
    g = lax.axis_index("dp")
    z, y = g // Y, lax.rem(g, Y)
    def zdev(k): return (s, lax.rem(z + k, Z) * Y + y)
    ydev = (s, z * Y + (1 - y))
    tokens, width = q.shape
    half = nl * 128
    wide = 256
    nb = width // wide
    greet([zdev(k) for k in range(1, Z)] + [ydev, xdev, cdev])
    ins = (wk_in, wv_in, wq_in, wo_in)
    def part(i, *lead):
        m, r0, nr, route = pieces[i]
        if m == 4:
            return sm.at[lead + (slice(None),) * (4 - len(lead))]
        return wall.at[(m,) + lead + (slice(None),) * (4 - len(lead)) + (pl.ds(r0, nr),)]
    zc, h, cc = {}, {}, {}
    for i, (m, r0, nr, route) in enumerate(pieces):
        src = small_in if m == 4 else ins[m].at[pl.ds(r0, nr)]
        zc[i] = [remote(src, part(i, x, c, z, y), zs.at[i, k], zr.at[i, k], zdev(k)) for k in range(1, Z)]
    for m in range(4):
        wall[m, x, c, z, y] = ins[m][...]
    sm[x, c, z, y] = small_in[...]
    def gather_stage(i, stage):
        route = pieces[i][3]
        if stage == 0:
            for k in range(1, Z): zc[i][k - 1].wait_recv()
            mine = part(i, x, c, slice(None), y)
            h[i, 0] = remote(mine, mine, hs.at[i, 0], hr.at[i, 0], xdev if route == 0 else ydev)
            cc[i, 0] = remote(mine, mine, cs.at[i, 0], cr.at[i, 0], cdev)
        elif stage == 1:
            h[i, 0].wait_recv()
            if route == 0:
                both, got = part(i, slice(None), c, slice(None), y), part(i, 1 - x, c, slice(None), y)
            else:
                both, got = part(i, x, c), part(i, x, c, slice(None), 1 - y)
            h[i, 1] = remote(both, both, hs.at[i, 1], hr.at[i, 1], ydev if route == 0 else xdev)
            cc[i, 1] = remote(got, got, cs.at[i, 1], cr.at[i, 1], cdev)
        else:
            h[i, 1].wait_recv()
            got = part(i, slice(None), c, slice(None), 1 - y) if route == 0 else part(i, 1 - x, c)
            cc[i, 2] = remote(got, got, cs.at[i, 2], cr.at[i, 2], cdev)
    np_ = len(pieces)
    steps = [(t - st, st) for t in range(np_ + 2) for st in range(3) if 0 <= t - st < np_]
    done = [0]
    def gather_until(m):
        last = max(i for i, p in enumerate(pieces) if p[0] == m)
        while True:
            i, st = steps[done[0]]
            gather_stage(i, st)
            done[0] += 1
            if (i, st) == (last, 2): break
        for i, p in enumerate(pieces):
            if p[0] == m:
                for k in range(3): cc[i, k].wait_recv()
    kept_copies = []
    def keep(m, out):
        cp = pltpu.make_async_copy(wall.at[m], out, osem.at[m]); cp.start(); kept_copies.append(cp)
    def w_of(m):
        return wall[m].reshape(width, width)
    for b in range(nl):
        own = column_of(lpos[b:b + 1, pl.ds(pl.multiple_of(s * 128, 128), 128)])
        for k in range(blocks):
            fill_buckets(lb.at[b, k], own, lpos[b:b + 1, k * 128:(k + 1) * 128], ll[b], k * 128)
    for b in range(ns):
        fill_buckets(sb.at[b, 0], column_of(spos[b:b + 1, :]), spos[b:b + 1, :], sl[b], 0)
    gather_until(4)
    flat = sm[...].astype(f32).reshape(X * C * Z * Y, sm.shape[4], 128)
    per = 128 // gain_part
    def shifted(rows, n):
        return rows if n == 0 else pltpu.roll(rows, n, 1)
    chunks = []
    for k in range(width // 128):
        chunks.append(sum(shifted(flat[k * per + i], i * gain_part) for i in range(per)))
    found = jnp.concatenate(chunks, axis=1)
    params[...] = jnp.zeros_like(params)
    params[0:found.shape[0], :] = found.astype(bf)
    share = 32 // table_part
    lane8 = lax.broadcasted_iota(jnp.int32, (1, 128), 1)
    for hd in range(tab.shape[0]):
        rows = sum(shifted(flat[hd * share + i], i * table_part) for i in range(share))
        tab[hd] = jnp.where(lane8 < 32, rows[experts + 2:experts + 3, :], masked)
    gain = params[experts:experts + 1, :].astype(f32)
    for t in range(2):
        m = rows_of(xl, xsh, t).astype(f32)
        n1[pl.ds(t * half, half), :] = (m * rms_scale(m) * gain).astype(bf)
        gb[pl.ds(t * half, half), :] = rows_of(gl, gsh, t)
    wholes = (kl, vl)
    far = (1 - x) * C + c
    ka, kc, kf = {}, {}, {}
    def project(m, t):
        return jnp.dot(n1[pl.ds(t * half, half), :], w_of(m), preferred_element_type=f32).astype(bf)
    for m in range(2):
        gather_until(m)
        wholes[m][s] = project(m, 0).reshape(nl, 128, width)
        for b in range(nb):
            n = m * nb + b
            src = wholes[m].at[s, :, :, pl.ds(b * wide, wide)]
            ka[n] = remote(src, src, kss.at[n, 0], krs.at[n, 0], xdev)
            kc[n] = remote(src, src, kss.at[n, 1], krs.at[n, 1], cdev)
        keep(m, (wk_out, wv_out)[m])
    ks[...] = project(0, 1)
    vs[...] = project(1, 1)
    for t in range(2):
        n1t[:, t * half:(t + 1) * half] = n1[pl.ds(t * half, half), :].T
    gather_until(2)
    for t in range(2):
        q[pl.ds(t * half, half), :] = project(2, t)
    keep(2, wq_out)
    first = lax.broadcasted_iota(jnp.int32, (128, 128), 1) < 64
    for b0 in range(nb):
        for n in (b0, nb + b0):
            ka[n].wait_recv()
            got = wholes[n // nb].at[far, :, :, pl.ds(b0 * wide, wide)]
            kf[n] = remote(got, got, kss.at[n, 2], krs.at[n, 2], cdev)
        for n in (b0, nb + b0):
            kc[n].wait_recv(); kf[n].wait_recv()
        @pl.loop(0, wide // 128)
        def _(i):
            hp = b0 * (wide // 128) + i
            cols = pl.ds(pl.multiple_of(hp * 128, 128), 128)
            for b in range(nl + ns):
                rows, n, kk, vv = item(b, nl, blocks, cols, ks, vs, kl, vl)
                p = probs_of(stack_heads(q[rows, cols], first), kk, (tab[2 * hp], tab[2 * hp + 1]), mine_of(b, nl, lb, sb), n)
                out = dot(p.astype(bf), vv, 1, 0)
                mixed[rows, cols] = jnp.where(first, out[:128], out[128:]).astype(bf)
        if b0 == 0:
            gather_until(3)
            keep(3, wo_out)
    gain = params[experts + 1:experts + 2, :].astype(f32)
    for t in range(2):
        rows = pl.ds(t * 256, 256)
        m = rows_of(xl, xsh, t).astype(f32) + jnp.dot(mixed[rows, :], w_of(3), preferred_element_type=f32)
        mid[rows, :] = m
        n2[rows, :] = (m * rms_scale(m) * gain).astype(bf)
    logits[...] = dot(n2[...], params[...], 1, 1)
    logit_t = dot(params[...], n2[...], 1, 1)[:experts]
    routes = [jnp.concatenate([ref[i, j:j + 1, :] for ref in (lr, sr) for i in range(ref.shape[0])], axis=1) for j in range(2)]
    e_iota = lax.broadcasted_iota(jnp.int32, (experts, tokens), 0)
    member = ((e_iota == routes[0]) | (e_iota == routes[1])).astype(f32)
    e = jnp.exp(logit_t - jnp.max(logit_t, axis=0, keepdims=True))
    p = e / jnp.sum(e, axis=0, keepdims=True)
    chosen = member * p
    before = (lax.broadcasted_iota(jnp.int32, (tokens, tokens), 0) < lax.broadcasted_iota(jnp.int32, (tokens, tokens), 1)).astype(f32).astype(bf)
    place = jnp.dot(member.astype(bf), before, preferred_element_type=f32)
    kept = (member > 0.5) & (place < cap)
    weight = jnp.where(kept, chosen / jnp.sum(chosen, axis=0, keepdims=True), 0.0)
    slot = jnp.where(kept, place.astype(jnp.int32), -1)
    s_iota = lax.broadcasted_iota(jnp.int32, (cap, tokens), 0)
    for i in range(experts):
        pick = (s_iota == slot[i:i + 1, :]).astype(f32)
        scale = jnp.sum(pick * weight[i:i + 1, :], axis=1, keepdims=True)
        pick = pick.astype(bf)
        xs[i] = jnp.dot(pick, n2[...], preferred_element_type=f32).astype(bf)
        gs[i] = (jnp.dot(pick, gb[...], preferred_element_type=f32) * scale).astype(bf)
    for cp in kept_copies: cp.wait()
    for group in (h, cc, ka, kc, kf):
        for cp in group.values(): cp.wait_send()
    for i in zc:
        for cp in zc[i]: cp.wait_send()
def post_kernel(nl, ns, blocks, experts, cap, lpos, spos, eo, ri, mid, mixed, logits, lr, sr, gl, gsh, wo, params, eg,
                lout, sout, midg, wog, small, mg, li, si, eg0, eg1, eg2, bg, n2, lg, ev, sem):
    f32, bf = jnp.float32, jnp.bfloat16
    tokens = mid.shape[0]
    fetch = [pltpu.make_async_copy(eg.at[m], ev.at[m], sem.at[m]) for m in range(3)]
    copies = [pltpu.make_async_copy(ev.at[m], out.at[0], sem.at[m]) for m, out in enumerate((eg0, eg1, eg2))]
    for cp in fetch: cp.start()
    gain = params[experts + 1:experts + 2, :].astype(f32)
    lane = lax.broadcasted_iota(jnp.int32, (tokens, 128), 1)
    routes = [jnp.concatenate([column_of(ref[i, j:j + 1, :]) for ref in (lr, sr) for i in range(ref.shape[0])], axis=0) for j in range(2)]
    member = ((lane == routes[0]) | (lane == routes[1])).astype(f32)
    after = (lax.broadcasted_iota(jnp.int32, (tokens, tokens), 1) < lax.broadcasted_iota(jnp.int32, (tokens, tokens), 0)).astype(f32).astype(bf)
    place = jnp.dot(after, member.astype(bf), preferred_element_type=f32)
    kept = (member > 0.5) & (place < cap)
    slot = jnp.where(kept, place.astype(jnp.int32), -1)
    lgt = jnp.where(lane < experts, logits[...], -1e30)
    ex = jnp.exp(lgt - jnp.max(lgt, axis=1, keepdims=True))
    p = ex / jnp.sum(ex, axis=1, keepdims=True)
    chosen = member * p
    both = jnp.sum(chosen, axis=1, keepdims=True)
    gate = chosen / both
    fg = jnp.zeros((1, mid.shape[1]), f32)
    for t in range(2):
        at = slice(t * 256, t * 256 + 256)
        rows = pl.ds(t * 256, 256)
        g = rows_of(gl, gsh, t).astype(f32)
        m = mid[rows, :]
        s_iota = lax.broadcasted_iota(jnp.int32, (256, experts * cap), 1)
        fin, back, mean, shares = m, 0.0, 0.0, []
        for j in range(2):
            this = lane[at] == routes[j][at]
            place_j = jnp.sum(jnp.where(this, slot[at], 0), axis=1, keepdims=True)
            gate_j = jnp.sum(jnp.where(this, gate[at], 0.0), axis=1, keepdims=True)
            index = jnp.where(place_j >= 0, routes[j][at] * cap + place_j, -1)
            pick = (s_iota == index).astype(f32).astype(bf)
            pair = jnp.dot(pick, eo[...], preferred_element_type=f32)
            back += jnp.dot(pick, ri[...], preferred_element_type=f32)
            fin += jnp.where(place_j >= 0, gate_j, 0.0) * pair
            share_j = jnp.sum(g * pair, axis=1, keepdims=True)
            mean += share_j * gate_j
            shares.append(jnp.where(this, share_j, 0.0))
        (lout, sout)[t][...] = fin.astype(bf).reshape(lout.shape)
        pg = member[at] * (shares[0] + shares[1] - mean) / both[at]
        lgrad = (p[at] * (pg - jnp.sum(p[at] * pg, axis=1, keepdims=True))).astype(bf)
        lg[rows, :] = lgrad
        r2 = rms_scale(m)
        u = m * r2
        n2[rows, :] = (u * gain).astype(bf)
        back += jnp.dot(lgrad, params[...], preferred_element_type=f32)
        fg += jnp.sum(back * u, axis=0, keepdims=True)
        w = back * gain
        out = g + r2 * (w - u * jnp.mean(w * u, axis=-1, keepdims=True))
        midg[rows, :] = out
        bg[rows, :] = out.astype(bf)
        mg[rows, :] = dot(out.astype(bf), wo[...], 1, 1).astype(bf)
    for m in range(3):
        fetch[m].wait()
        copies[m].start()
    small[...] = jnp.zeros_like(small)
    small[1:2, :] = fg
    small[2:2 + experts, :] = dot(lg[...], n2[...], 0, 0)[:experts]
    wog[...] = dot(mixed[...], bg[...], 0, 0).astype(bf).reshape(wog.shape)
    lane = lax.broadcasted_iota(jnp.int32, (128, 128), 1)
    edge = jnp.full((128, 128), 4096, jnp.int32)
    for i, e in enumerate(EDGES):
        edge = jnp.where(lane == i, e, edge)
    edge = jnp.where(lane > len(EDGES), -4096, edge)
    def places(out, q_col, k_row):
        k_first = k_row[:, 0:1]
        t = lax.broadcasted_iota(jnp.int32, (128, 256), 1) + k_first
        below = jnp.sum((column_of(k_row) < t).astype(jnp.int32), axis=0, keepdims=True)
        at = jnp.clip(q_col + edge - k_first, 0, 255)
        lo = jnp.take_along_axis(jnp.broadcast_to(below[:, :128], (128, 128)), at & 127, axis=1)
        hi = jnp.take_along_axis(jnp.broadcast_to(below[:, 128:], (128, 128)), at & 127, axis=1)
        out[...] = jnp.where(at < 128, lo, hi) - 1
    me = lax.axis_index("seq")
    for b in range(nl):
        own = column_of(lpos[b:b + 1, pl.ds(pl.multiple_of(me * 128, 128), 128)])
        for c in range(blocks):
            places(li.at[b, c], own, lpos[b:b + 1, c * 128:(c + 1) * 128])
    for b in range(ns):
        places(si.at[b, 0], column_of(spos[b:b + 1, :]), spos[b:b + 1, :])
    for cp in copies: cp.wait()
def front(dims, nl, ns, experts, cap, pieces, table_part, gain_part, arrays, tokens, width, heads, cid):
    X, C, Z, Y = dims
    sm, vm, hbm = pl.BlockSpec(memory_space=pltpu.SMEM), pl.BlockSpec(memory_space=pltpu.VMEM), pl.BlockSpec(memory_space=pl.ANY)
    S, V, sem, bf, f32 = jax.ShapeDtypeStruct, pltpu.VMEM, pltpu.SemaphoreType.DMA, jnp.bfloat16, jnp.float32
    rows_part, small_shape = arrays[2].shape[0], arrays[6].shape
    whole = dims + (rows_part, width)
    slots = S((experts, cap, width), bf)
    rows, short, long = S((tokens, width), bf), S((ns * 128, width), bf), S((X * C, nl, 128, width), bf)
    outs = [S(whole, bf)] * 4 + [S((128, width), bf), S((heads, 1, 128), f32), rows, short, short, long, long, S((width, tokens), bf), rows,
            S((tokens, width), f32), slots, slots, S((tokens, 128), f32), S((nl, X * C, 128, 128), jnp.int32), S((ns, 1, 128, 128), jnp.int32)]
    n, kvn = len(pieces), 2 * (width // 256)
    scr = [V((4,) + whole, bf), V(dims + small_shape, bf)] + [V((tokens, width), bf)] * 3
    scr += [sem((n, Z)), sem((n, Z)), sem((n, 2)), sem((n, 2)), sem((n, 3)), sem((n, 3)), sem((kvn, 3)), sem((kvn, 3)), sem((4,))]
    return pl.pallas_call(functools.partial(front_kernel, dims, nl, ns, experts, cap, pieces, table_part, gain_part), out_shape=outs,
        in_specs=[sm, sm] + [vm] * (len(arrays) - 2), out_specs=[hbm] * 4 + [vm] * (len(outs) - 4), scratch_shapes=scr,
        compiler_params=pltpu.CompilerParams(collective_id=cid, has_side_effects=True, vmem_limit_bytes=60 * 2**20))(*arrays)
def small_rows(experts):
    return -(-(experts + 4) // 8) * 8
def post(nl, ns, blocks, experts, cap, whole, arrays, tokens, width):
    vm, hbm = pl.BlockSpec(memory_space=pltpu.VMEM), pl.BlockSpec(memory_space=pl.ANY)
    S, bf, f32 = jax.ShapeDtypeStruct, jnp.bfloat16, jnp.float32
    eg = arrays[-1]
    outs = [S((nl, 128, width), bf), S((ns, 128, width), bf), S((tokens, width), f32), S(whole, bf), S((small_rows(experts), width), f32), S((tokens, width), bf),
            S((nl, blocks, 128, 128), jnp.int32), S((ns, 1, 128, 128), jnp.int32)] + [S((1,) + eg.shape[1:], f32)] * 3
    V = pltpu.VMEM
    return pl.pallas_call(functools.partial(post_kernel, nl, ns, blocks, experts, cap), out_shape=outs,
        in_specs=[vm] * (len(arrays) - 1) + [hbm], out_specs=[vm] * (len(outs) - 3) + [hbm] * 3,
        scratch_shapes=[V((tokens, width), bf)] * 2 + [V((tokens, 128), bf), V(eg.shape, f32), pltpu.SemaphoreType.DMA((3,))],
        compiler_params=pltpu.CompilerParams(vmem_limit_bytes=60 * 2**20))(*arrays)
def back_kernel(dims, nl, ns, experts, pieces, q, k, v, kl, vl, tab, lb, sb, li, si, mg, wog, n1t, lx_in, sx_in, params, wq_in, wk_in, wv_in, midg_in, small_in,
                lgrad, sgrad, og, qg, kg, vg, small, *refs):
    X, C, Z, Y = dims
    blocks = X * C
    f32, bf = jnp.float32, jnp.bfloat16
    np_ = len(pieces)
    bufs = refs[:4 * np_]
    (gw, dq, ka, va, dkl, dvl, kcb, ka1, kb1, seg, sacc, sbuf, lx, sx, wq, wk, wv, midg, cs, cr, hs, hr, zs, zr, kss, krs, sss, srs, fs) = refs[4 * np_:]
    late = [pltpu.make_async_copy(a, b, fs.at[i]) for i, (a, b) in enumerate(((lx_in, lx), (sx_in, sx), (wq_in, wq), (wk_in, wk), (wv_in, wv), (midg_in, midg)))]
    for cp in late: cp.start()
    s = lax.axis_index("seq"); g = lax.axis_index("dp")
    x, c = s // C, lax.rem(s, C)
    z, y = g // Y, lax.rem(g, Y)
    def zdev(k): return (s, lax.rem(z + k, Z) * Y + y)
    ydev = (s, z * Y + (1 - y)); xdev = ((1 - x) * C + c, g); cdev = (x * C + 1 - c, g)
    greet([zdev(k) for k in range(1, Z)] + [ydev, xdev, cdev])
    half = nl * 128
    wide = 256
    nb = q.shape[1] // wide
    sources = [wog] + [gw.at[i] for i in range(3)]
    outs = [og, qg, kg, vg]
    first = {}; hh = {}; zz = {}
    def add(dst, a, b):
        dst[...] = (a.astype(f32) + b.astype(f32)).astype(dst.dtype)
    def send_core(i):
        m, c0, nc, route = pieces[i]
        first[i] = remote(sources[m].at[:, 1 - c, :, :, :, pl.ds(c0, nc)], bufs[4 * i], cs.at[i], cr.at[i], cdev)
    def stage(i, which):
        m, c0, nc, route = pieces[i]
        b0, b1, b2, b3 = bufs[4 * i:4 * i + 4]
        if which == 0:
            first[i].wait_recv()
            add(b0, sources[m][:, c, :, :, :, c0:c0 + nc], b0[...])
            src = b0.at[:, :, 1 - y] if route == 0 else b0.at[1 - x]
            hh[i, 0] = remote(src, b1, hs.at[i, 0], hr.at[i, 0], ydev if route == 0 else xdev)
        elif which == 1:
            hh[i, 0].wait_recv()
            add(b1, b0[:, :, y] if route == 0 else b0[x], b1[...])
            src = b1.at[1 - x] if route == 0 else b1.at[:, 1 - y]
            hh[i, 1] = remote(src, b2, hs.at[i, 1], hr.at[i, 1], xdev if route == 0 else ydev)
        elif which == 2:
            hh[i, 1].wait_recv()
            add(b2, b1[x] if route == 0 else b1[:, y], b2[...])
            zz[i] = [remote(b2.at[lax.rem(z + k, Z)], b3.at[k - 1], zs.at[i, k], zr.at[i, k], zdev(k)) for k in range(1, Z)]
        else:
            tot = b2[z].astype(f32)
            for k in range(1, Z):
                zz[i][k - 1].wait_recv()
                tot += b3[k - 1].astype(f32)
            outs[m][:, c0:c0 + nc] = tot
    def piece(m, b):
        return [i for i, p in enumerate(pieces) if p[0] == m and (m == 0 or p[1] == b * wide)]
    def weight_grad(m, rows, b):
        cols = slice(b * wide, (b + 1) * wide)
        quarter = n1t.shape[0] // blocks
        for xx in range(X):
            for cc in range(C):
                part = jnp.dot(n1t[pl.ds((xx * C + cc) * quarter, quarter), :], rows[:, cols], preferred_element_type=f32)
                gw[m - 1, xx, cc, :, :, :, cols] = part.astype(bf).reshape(gw.shape[3:6] + (wide,))
        for i in piece(m, b):
            send_core(i)
    parts, wholes = (dkl, dvl), (ka, va)
    kf, kx = {}, {}
    def kv_core(b):
        cols = pl.ds(b * wide, wide)
        for far in range(2):
            for m in range(2):
                n = b * 2 + m
                at = (1 - x if far == 0 else x) * C + 1 - c
                kf[n, far] = remote(parts[m].at[at, :, :, cols], kcb.at[n, far], kss.at[n, far], krs.at[n, far], cdev)
    def kv_chip(b):
        for m in range(2):
            n = b * 2 + m
            kf[n, 0].wait_recv()
            add(ka1.at[n], parts[m][(1 - x) * C + c, :, :, b * wide:(b + 1) * wide], kcb[n, 0])
            kx[n] = remote(ka1.at[n], kb1.at[n], kss.at[n, 2], krs.at[n, 2], xdev)
    def kv_end(b):
        for m in range(2):
            n = b * 2 + m
            kf[n, 1].wait_recv(); kx[n].wait_recv()
            tot = parts[m][s, :, :, b * wide:(b + 1) * wide].astype(f32) + kcb[n, 1].astype(f32) + kb1[n].astype(f32)
            wholes[m][pl.ds(0, half), b * wide:(b + 1) * wide] = tot.astype(bf).reshape(half, wide)
        weight_grad(2, ka, b)
        weight_grad(3, va, b)
    def stages(which, b, *ms):
        for m in ms:
            for i in piece(m, b):
                stage(i, which)
    seg[...] = jnp.zeros_like(seg)
    lane = lax.broadcasted_iota(jnp.int32, (128, 128), 1)
    head_one = lane < 64
    tri = jnp.where(lax.broadcasted_iota(jnp.int32, (128, 128), 0) <= lane, 1.0, 0.0).astype(bf)
    def attend(b0):
        @pl.loop(0, wide // 128)
        def _(i):
            hp = b0 * (wide // 128) + i
            cols = pl.ds(pl.multiple_of(hp * 128, 128), 128)
            for b in range(nl + ns):
                rows, n, kk, vv = item(b, nl, blocks, cols, k, v, kl, vl)
                idx = mine_of(b, nl, li, si)
                qs = stack_heads(q[rows, cols], head_one); gs = stack_heads(mg[rows, cols], head_one)
                p = probs_of(qs, kk, (tab[2 * hp], tab[2 * hp + 1]), mine_of(b, nl, lb, sb), n)
                dp = dot(gs, vv, 1, 1)
                ds = (p * (dp - jnp.sum(p * dp, axis=1, keepdims=True))).astype(bf)
                dqs = dot(ds, kk, 1, 0)
                dkt = dot(qs, ds, 0, 0)
                dvt = dot(gs, p.astype(bf), 0, 0)
                sums = [0, 0]
                for c_ in range(n):
                    pre = dot(ds[:, c_ * 128:(c_ + 1) * 128], tri, 1, 0)
                    at = idx[c_]
                    for e in range(2):
                        sums[e] += jnp.where(at >= 0, jnp.take_along_axis(pre[e * 128:(e + 1) * 128], jnp.maximum(at, 0), axis=1), 0.0)
                for e in range(2):
                    seg[2 * hp + e] += jnp.sum(sums[e], axis=0, keepdims=True)
                dq[rows, cols] = jnp.where(head_one, dqs[:128], dqs[128:]).astype(bf)
                dkt = dkt.T.astype(bf); dvt = dvt.T.astype(bf)
                if b < nl:
                    dkl[:, b, :, cols] = dkt.reshape(n, 128, 128); dvl[:, b, :, cols] = dvt.reshape(n, 128, 128)
                else:
                    ka[rows, cols] = dkt; va[rows, cols] = dvt
    for i in piece(0, 0):
        send_core(i)
    attend(0)
    kv_core(0); weight_grad(1, dq, 0); stages(0, 0, 0)
    attend(1)
    kv_core(1); kv_chip(0); weight_grad(1, dq, 1); stages(0, 0, 1); stages(1, 0, 0)
    attend(2)
    kv_core(2); kv_chip(1); kv_end(0); weight_grad(1, dq, 2); stages(0, 1, 1); stages(1, 0, 1); stages(2, 0, 0)
    attend(3)
    kv_core(3); kv_chip(2); kv_end(1); kv_chip(3); weight_grad(1, dq, 3); stages(0, 0, 2, 3); stages(0, 2, 1); stages(1, 1, 1); stages(2, 0, 1)
    kv_end(2); stages(0, 1, 2, 3); stages(0, 3, 1); stages(1, 0, 2, 3); stages(1, 2, 1); stages(2, 1, 1); stages(3, 0, 0)
    for cp in late: cp.wait()
    gain = params[experts:experts + 1, :].astype(f32)
    def input_grad(t):
        rows = pl.ds(t * half, half)
        ng = dot(dq[rows, :], wq[...], 1, 1) + dot(ka[rows, :], wk[...], 1, 1) + dot(va[rows, :], wv[...], 1, 1)
        m = rows_of(lx, sx, t).astype(f32)
        r1 = rms_scale(m)
        u = m * r1
        w = ng * gain
        (lgrad, sgrad)[t][...] = (midg[rows, :] + r1 * (w - u * jnp.mean(w * u, axis=-1, keepdims=True))).reshape(lgrad.shape)
        return jnp.sum(ng * u, axis=0, keepdims=True)
    ag = input_grad(1)
    kv_end(3); stages(0, 2, 2, 3); stages(1, 3, 1); stages(1, 1, 2, 3); stages(2, 2, 1); stages(2, 0, 2, 3); stages(3, 0, 1)
    stages(0, 3, 2, 3)
    ag += input_grad(0)
    stages(1, 2, 2, 3); stages(2, 3, 1); stages(2, 1, 2, 3); stages(3, 1, 1)
    sacc[0] = small_in[...]
    sacc[0, 0:1, :] = ag
    heads = seg.shape[0]
    spot = lax.broadcasted_iota(jnp.int32, (8, 128), 1)
    for h in range(heads):
        upto = jnp.broadcast_to(seg[h], (8, 128))
        within = upto - jnp.where(spot == 0, 0.0, pltpu.roll(upto, 1, 1))
        at = jnp.where(spot < 16, 15 - spot, jnp.minimum(spot - 1, 30))
        by_bucket = jnp.where((spot == 16) | (spot >= 32), 0.0, jnp.take_along_axis(within, at, axis=1))
        r = 2 + experts + h // 8
        sacc[0, r:r + 1, (h % 8) * 128:(h % 8 + 1) * 128] = by_bucket[0:1, :]
    sc = remote(sacc.at[0], sbuf.at[0], sss.at[0], srs.at[0], cdev)
    stages(1, 3, 2, 3); stages(2, 2, 2, 3); stages(3, 2, 1)
    sc.wait_recv()
    sacc[1] = sacc[0] + sbuf[0]
    sx_ = remote(sacc.at[1], sbuf.at[1], sss.at[1], srs.at[1], xdev)
    stages(2, 3, 2, 3); stages(3, 3, 1); stages(3, 0, 2, 3)
    sx_.wait_recv()
    sacc[2] = sacc[1] + sbuf[1]
    sy = remote(sacc.at[2], sbuf.at[2], sss.at[2], srs.at[2], ydev)
    stages(3, 1, 2, 3)
    sy.wait_recv()
    sacc[3] = sacc[2] + sbuf[2]
    sz = [remote(sacc.at[3], sbuf.at[2 + k], sss.at[2 + k], srs.at[2 + k], zdev(k)) for k in range(1, Z)]
    stages(3, 2, 2, 3); stages(3, 3, 2, 3)
    tot = sacc[3]
    for k in range(1, Z):
        sz[k - 1].wait_recv()
        tot += sbuf[2 + k]
    small[...] = tot
    for cp in [sc, sx_, sy] + sz + list(kx.values()) + list(kf.values()) + list(first.values()) + list(hh.values()) + [w for v_ in zz.values() for w in v_]:
        cp.wait_send()
LATE = (13, 14, 16, 17, 18, 19)
def back(dims, nl, ns, experts, arrays, cid):
    X, C, Z, Y = dims
    q_, small_in = arrays[0], arrays[-1]
    tokens, width = q_.shape
    heads = arrays[5].shape[0]
    nr = width // (X * C * Z * Y)
    wide = 256
    pieces = tuple((0, h * 512, 512, 1) for h in range(width // 512)) + tuple(
        (m, b * wide, wide, 1 if m == 3 and b >= 2 else 0) for m in range(1, 4) for b in range(width // wide))
    n = len(pieces)
    S, sem, bf, f32 = jax.ShapeDtypeStruct, pltpu.SemaphoreType.DMA, jnp.bfloat16, jnp.float32
    V = pltpu.VMEM
    scr = [V(lead + (nr, nc), bf) for m, c0, nc, route in pieces for lead in ((X, Z, Y), (Z, Y) if route else (X, Z), (Z,), (Z - 1,))]
    kvn = 2 * (width // wide)
    long = V((X * C, nl, 128, width), bf)
    rows = V((tokens, width), bf)
    scr += [V((3, X, C, Z, Y, nr, width), bf), rows, rows, rows, long, long,
            V((kvn, 2, nl, 128, wide), bf), V((kvn, nl, 128, wide), bf), V((kvn, nl, 128, wide), bf), V((heads, 1, 128), f32),
            V((4,) + small_in.shape, f32), V((Z + 2,) + small_in.shape, f32)] + [V(arrays[i].shape, arrays[i].dtype) for i in LATE] + [
            sem((n,)), sem((n,)), sem((n, 2)), sem((n, 2)), sem((n, Z)), sem((n, Z)), sem((kvn, 3)), sem((kvn, 3)), sem((Z + 2,)), sem((Z + 2,)), sem((len(LATE),))]
    vm = pl.BlockSpec(memory_space=pltpu.VMEM)
    outs = [S((nl, 128, width), f32), S((ns, 128, width), f32)] + [S((nr, width), f32)] * 4 + [S(small_in.shape, f32)]
    return pl.pallas_call(functools.partial(back_kernel, dims, nl, ns, experts, pieces), out_shape=outs,
        in_specs=[pl.BlockSpec(memory_space=pl.ANY) if i in LATE else vm for i in range(len(arrays))], out_specs=[vm] * len(outs), scratch_shapes=scr,
        compiler_params=pltpu.CompilerParams(collective_id=cid, has_side_effects=True, vmem_limit_bytes=63 * 2**20))(*arrays)

def gelu_parts(v):
    c, a = 0.7978845608, 0.044715
    v2 = v * v
    h = 0.5 + 0.5 * jnp.tanh(v * (c + (c * a) * v2))
    act = v * h
    return act, h + act * (1.0 - h) * (2.0 * c + (6.0 * c * a) * v2)
RING, LAG = 6, 4
SEND_AT, JOIN_AT = 2, 3
def expert_kernel(cap, per, order, todo, wcut, tile, xs, gs, wgi, wui, wdi, eo_out, ri_out, grads, eo_h, ri_h,
                  wall, xr, gr, hall, lall, eo, ri, cb, ab, xb, ob,
                  lsem, xss, xrs, gss, grs, ess, ers, rss, rrs, wss, wrs, wls, css, crs, ass, ars, osem, free):
    dp = lax.axis_size("dp")
    f32, bf = jnp.float32, jnp.bfloat16
    s, x, c, xdev, cdev = seq_places(2)
    g = lax.axis_index("dp")
    def peer(k): return (s, g ^ k)
    greet([xdev, cdev] + [peer(k) for k in range(1, dp)])
    rows_w, ff = wgi.shape; width = xs.shape[2]
    wx, wc, wl, wf = [], [], [], []
    shared = ((wgi, 1), (wui, 2), (wdi, 0))
    parts = [(src, m, f0, nf) for f0, nf in wcut for src, m in shared]
    for n, (src, m, f0, nf) in enumerate(parts):
        a = src.at[:, pl.ds(f0, nf)]
        b = wall.at[m, x, c, :, pl.ds(f0, nf)]
        wx.append(remote(a, b, wss.at[n, 0], wrs.at[n, 0], xdev))
        wc.append(remote(a, b, wss.at[n, 1], wrs.at[n, 1], cdev))
        cp = pltpu.make_async_copy(a, b, wls.at[n]); cp.start(); wl.append(cp)
    sx, sg = {}, {}
    def dispatch(p):
        for k in range(p * per, (p + 1) * per):
            at = pl.ds(k * cap, cap)
            if k == 0:
                sx[0] = pltpu.make_async_copy(xs.at[g], xr.at[at], lsem.at[0]); sx[0].start()
                sg[0] = pltpu.make_async_copy(gs.at[g], gr.at[at], lsem.at[1]); sg[0].start()
            else:
                sx[k] = remote(xs.at[g ^ k], xr.at[at], xss.at[k], xrs.at[k], peer(k))
                sg[k] = remote(gs.at[g ^ k], gr.at[at], gss.at[k], grs.at[k], peer(k))
    for p in order[:-1]: dispatch(p)
    ntile = ff // tile
    re, rr = {}, {}
    wide = 4 * rows_w
    def sources(p): return list(range(p * per, (p + 1) * per))
    def arrive(p):
        for k in sources(p):
            if k == 0: sx[0].wait(); sg[0].wait()
            else: sx[k].wait_recv(); sg[k].wait_recv()
    def inner(p, t0, nt):
        rows = pl.ds(p * per * cap, per * cap)
        @pl.loop(t0, t0 + nt)
        def _(t):
            cols = pl.ds(pl.multiple_of(t * tile, 128), tile)
            w = lambda m: wall[m, :, :, :, cols].reshape(wide, tile)
            gp = jnp.dot(xr[rows, :], w(1), preferred_element_type=f32)
            up = jnp.dot(xr[rows, :], w(2), preferred_element_type=f32)
            hg = jnp.dot(gr[rows, :], w(0), preferred_element_type=f32)
            act, der = gelu_parts(gp)
            hall[0, rows, cols] = (act * up).astype(bf)
            hall[1, rows, cols] = (hg * up * der).astype(bf)
            hall[2, rows, cols] = (hg * act).astype(bf)
    def outer(p):
        rows = pl.ds(p * per * cap, per * cap)
        @pl.loop(0, 4)
        def _(t):
            part = pl.ds(pl.multiple_of(t * rows_w, 128), rows_w)
            tx, tc = t // 2, lax.rem(t, 2)
            eo[:, part] = dot(hall[0, rows, :], wall[0, tx, tc], 1, 1).astype(bf)
            ri[:, part] = (dot(hall[1, rows, :], wall[1, tx, tc], 1, 1) + dot(hall[2, rows, :], wall[2, tx, tc], 1, 1)).astype(bf)
        keep = [pltpu.make_async_copy(eo, eo_h.at[rows], lsem.at[4]), pltpu.make_async_copy(ri, ri_h.at[rows], lsem.at[5])]
        for cp in keep: cp.start()
        for cp in keep: cp.wait()
        for k in sources(p):
            at = pl.ds(k * cap, cap)
            if k == 0:
                re[0] = pltpu.make_async_copy(eo_h.at[at], eo_out.at[g], lsem.at[2]); re[0].start()
                rr[0] = pltpu.make_async_copy(ri_h.at[at], ri_out.at[g], lsem.at[3]); rr[0].start()
            else:
                re[k] = remote(eo_h.at[at], eo_out.at[g], ess.at[k], ers.at[k], peer(k))
                rr[k] = remote(ri_h.at[at], ri_out.at[g], rss.at[k], rrs.at[k], peer(k))
    early = list(todo[:-2])
    last = todo[-1]
    for i, (f0, nf) in enumerate(wcut):
        mine = range(3 * i, 3 * i + 3)
        for n in mine:
            wx[n].wait_recv()
            src, m, f0, nf = parts[n]
            b = wall.at[m, 1 - x, c, :, pl.ds(f0, nf)]
            wf.append(remote(b, b, wss.at[n, 2], wrs.at[n, 2], cdev))
        if i == SEND_AT: dispatch(last)
        if i == 0:
            for p in early: arrive(p)
        for n in mine:
            wl[n].wait(); wc[n].wait_recv(); wf[n].wait_recv()
        for p in early: inner(p, f0 // tile, nf // tile)
        if i == JOIN_AT:
            p = todo[-2]
            arrive(p)
            inner(p, 0, (f0 + nf) // tile)
            early.append(p)
    for p in early: outer(p)
    arrive(last)
    inner(last, 0, ntile)
    outer(last)
    for n in range(len(parts)):
        wx[n].wait_send(); wc[n].wait_send(); wf[n].wait_send()
    total = dp * cap
    @pl.loop(0, total // 256)
    def _(t):
        at = pl.ds(pl.multiple_of(t * 256, 256), 256)
        lall[1, :, at] = xr[at, :].T
        lall[0, :, at] = gr[at, :].T
    nt = 3 * ntile
    def place(n):
        m = n // ntile
        return m, pl.ds(pl.multiple_of((n - m * ntile) * tile, 128), tile)
    def to_core(n):
        m, cols = place(n); r = lax.rem(n, RING)
        return pltpu.make_async_remote_copy(src_ref=wall.at[m, :, 1 - c, :, cols], dst_ref=cb.at[r], send_sem=css.at[r],
            recv_sem=crs.at[r], device_id=cdev, device_id_type=MESH)
    def to_chip(n):
        r = lax.rem(n, RING)
        return pltpu.make_async_remote_copy(src_ref=ab.at[r], dst_ref=xb.at[r], send_sem=ass.at[r],
            recv_sem=ars.at[r], device_id=xdev, device_id_type=MESH)
    def to_out(n):
        m, cols = place(n); r = lax.rem(n, 2)
        return pltpu.make_async_copy(ob.at[r], grads.at[m, :, cols], osem.at[r])
    @pl.loop(0, nt + LAG)
    def _(n):
        @pl.when(n < nt)
        def _():
            m, cols = place(n)
            res = jnp.dot(lall[jnp.minimum(m, 1)], hall[m, :, cols], preferred_element_type=f32)
            wall[m, :, :, :, cols] = res.astype(bf).reshape(2, 2, rows_w, tile)
            @pl.when(n >= RING)
            def _(): pl.semaphore_wait(free.at[0], 1)
            to_core(n).start()
        @pl.when((n >= 1) & (n <= nt))
        def _():
            i = n - 1
            m, cols = place(i); r = lax.rem(i, RING)
            to_core(i).wait_recv()
            @pl.when(i >= RING)
            def _():
                to_chip(i).wait_send()
                pl.semaphore_wait(free.at[1], 1)
            ab[r] = (wall[m, 1 - x, c, :, cols].astype(f32) + cb[r, 1 - x].astype(f32)).astype(bf)
            to_chip(i).start()
        @pl.when(n >= LAG)
        def _():
            j = n - LAG
            m, cols = place(j); r = lax.rem(j, RING)
            to_chip(j).wait_recv()
            to_core(j).wait_send()
            @pl.when(j >= 2)
            def _(): to_out(j).wait()
            ob[lax.rem(j, 2)] = wall[m, x, c, :, cols].astype(f32) + cb[r, x].astype(f32) + xb[r].astype(f32)
            to_out(j).start()
            @pl.when(j < nt - RING)
            def _():
                pl.semaphore_signal(free.at[0], inc=1, device_id=cdev, device_id_type=MESH)
                pl.semaphore_signal(free.at[1], inc=1, device_id=xdev, device_id_type=MESH)
    for j in range(nt - 2, nt): to_out(j).wait()
    for i in range(nt - RING, nt): to_chip(i).wait_send()
    for k in range(dp):
        if k == 0:
            re[0].wait(); rr[0].wait()
        else:
            sx[k].wait_send(); sg[k].wait_send(); re[k].wait(); rr[k].wait()
def expert_all(xs, gs, wg, wu, wd, seq, cid):
    dp, cap, width = xs.shape
    rows_w, ff = wg.shape; total = dp * cap
    group = 320
    per = group // cap
    ng = dp // per
    order = [ng - 2] + [p for p in range(ng - 3, -1, -1)] + [ng - 1]
    todo = list(range(ng))
    sem = pltpu.SemaphoreType.DMA
    bf = jnp.bfloat16
    any_ = pl.BlockSpec(memory_space=pl.ANY)
    V = pltpu.VMEM
    tile = 256
    wcut = tuple((f0, min(512, ff - f0)) for f0 in range(0, ff, 512))
    nw = 3 * len(wcut)
    back = jax.ShapeDtypeStruct((dp, cap, width), bf)
    flat = jax.ShapeDtypeStruct((total, width), bf)
    return pl.pallas_call(functools.partial(expert_kernel, cap, per, order, todo, wcut, tile),
        out_shape=[back, back, jax.ShapeDtypeStruct((3, rows_w, ff), jnp.float32), flat, flat],
        in_specs=[any_] * 5, out_specs=[any_] * 5,
        scratch_shapes=[V((3, seq // 2, 2, rows_w, ff), bf), V((total, width), bf), V((total, width), bf), V((3, total, ff), bf),
        V((2, width, total), bf), V((group, width), bf), V((group, width), bf),
        V((RING, seq // 2, rows_w, tile), bf), V((RING, rows_w, tile), bf), V((RING, rows_w, tile), bf), V((2, rows_w, tile), jnp.float32)]
        + [sem((6,))] + [sem((dp,))] * 8 + [sem((nw, 3))] * 2 + [sem((nw,))] + [sem((RING,))] * 4 + [sem((2,)), pltpu.SemaphoreType.REGULAR((2,))],
        compiler_params=pltpu.CompilerParams(collective_id=cid, has_side_effects=True, vmem_limit_bytes=63 * 2**20))(xs, gs, wg, wu, wd)[:3]


def on_device(
    long_tokens,
    short_tokens,
    long_grad_out,
    short_grad_out,
    query_weight,
    key_weight,
    value_weight,
    output_weight,
    attn_gain,
    ffn_gain,
    rel_table,
    router_weight,
    gate_weight,
    up_weight,
    down_weight,
    long_positions,
    short_positions,
    long_lengths,
    short_lengths,
    long_routes,
    short_routes,
):
    long_items, quarter, model_width = long_tokens.shape
    short_items, short_len = (short_tokens.shape[0], short_tokens.shape[1])
    long_rows = long_items * quarter
    tokens = long_rows + short_items * short_len
    local_experts = gate_weight.shape[0]
    dp_size = lax.axis_size("dp")
    experts = local_experts * dp_size
    capacity = (5 * tokens + 2 * experts - 1) // (2 * experts)
    seq_size = lax.axis_size("seq")
    dims = (seq_size // 2, 2, dp_size // 2, 2)
    devices = seq_size * dp_size
    table_part, gain_part = rel_table.shape[0], attn_gain.shape[0]
    small = jnp.concatenate([router_weight.T, attn_gain[None], ffn_gain[None]], 0)
    small = jnp.pad(small, ((0, 1), (0, 128 - gain_part)))
    table_row = jnp.pad(rel_table[None], ((experts + 2, 0), (0, 128 - table_part)))
    small = jnp.pad(small + table_row, ((0, -(experts + 3) % 16), (0, 0)))
    rows_part = query_weight.shape[0]
    cuts = 2 if rows_part % 32 == 0 else 1
    cut = rows_part // cuts
    pieces = tuple((m, h * cut, cut, (m + h) % 2) for m in range(4) for h in range(cuts))
    pieces = ((4, 0, small.shape[0], 0),) + tuple(p[:3] + (0,) for p in pieces)
    sizes = (long_items, short_items, seq_size, experts, capacity)
    places = (long_positions, short_positions)
    routes = (long_routes.swapaxes(1, 2), short_routes.swapaxes(1, 2))
    (
        key_all,
        value_all,
        query_all,
        output_all,
        params,
        table,
        queries,
        keys,
        values,
        long_keys,
        long_values,
        normed_t,
        mixed,
        middle,
        outgoing,
        out_slots,
        logits,
        long_buckets,
        short_buckets,
    ) = front(
        dims,
        long_items,
        short_items,
        experts,
        capacity,
        pieces,
        table_part,
        gain_part,
        (long_lengths, short_lengths, key_weight, value_weight, query_weight, output_weight, small)
        + places
        + (long_tokens, short_tokens, long_grad_out, short_grad_out)
        + routes,
        tokens,
        model_width,
        HEADS,
        0,
    )
    key_all, value_all, query_all, output_all = (
        block.reshape(devices * rows_part, model_width)
        for block in (key_all, value_all, query_all, output_all)
    )
    heads_args = (queries, keys, values, long_keys, long_values, table)
    grads = (long_grad_out, short_grad_out, output_all, params)
    back_rows, back_grads, expert_grads = expert_all(
        outgoing, out_slots, gate_weight[0], up_weight[0], down_weight[0], seq_size, 4
    )
    (
        long_out,
        short_out,
        middle_grad,
        output_local,
        small_local,
        mixed_grad,
        long_places,
        short_places,
        down_grad,
        gate_grad,
        up_grad,
    ) = post(
        *sizes,
        dims + (rows_part, model_width),
        places
        + tuple(block.reshape(-1, model_width) for block in (back_rows, back_grads))
        + (middle, mixed, logits) + routes + grads + (expert_grads,),
        tokens,
        model_width,
    )
    long_grad_in, short_grad_in, output_grad, query_grad, key_grad, value_grad, small_sum = back(
        dims,
        long_items,
        short_items,
        experts,
        heads_args
        + (long_buckets, short_buckets, long_places, short_places)
        + (mixed_grad, output_local, normed_t, long_tokens, short_tokens, params)
        + (query_all, key_all, value_all, middle_grad, small_local),
        2,
    )
    place = lax.axis_index("seq") * dp_size + lax.axis_index("dp")

    def own(row, column, size, count=1):
        return lax.dynamic_slice(small_sum, (row, column), (count, size))

    entry = place * table_part
    head_at = entry // BUCKETS
    table_grad = own(2 + experts + head_at // 8, head_at % 8 * 128 + entry % BUCKETS, table_part)
    summed = (
        query_grad,
        key_grad,
        value_grad,
        output_grad,
        own(0, place * gain_part, gain_part)[0],
        own(1, place * gain_part, gain_part)[0],
        table_grad[0],
        own(2, place * rows_part, rows_part, experts).T,
    )
    return (
        long_out,
        short_out,
        long_grad_in,
        short_grad_in,
        summed[0],
        summed[1],
        summed[2],
        summed[3],
        summed[4],
        summed[5],
        summed[6],
        summed[7],
        gate_grad,
        up_grad,
        down_grad,
    )


def solution(mesh):
    placed = (
        P("dp", "seq", None),
        P(("seq", "dp"), None, None),
        P("dp", "seq", None),
        P(("seq", "dp"), None, None),
        P(("seq", "dp"), None),
        P(("seq", "dp"), None),
        P(("seq", "dp"), None),
        P(("seq", "dp"), None),
        P(("seq", "dp")),
        P(("seq", "dp")),
        P(("seq", "dp")),
        P(("seq", "dp"), None),
        P("dp", "seq", None),
        P("dp", "seq", None),
        P("dp", "seq", None),
        P("dp", None),
        P(("seq", "dp"), None),
        P("dp"),
        P(("seq", "dp")),
        P("dp", "seq", None),
        P(("seq", "dp"), None, None),
    )
    return jax.shard_map(
        on_device,
        mesh=mesh,
        in_specs=placed,
        out_specs=(
            P("dp", "seq", None),
            P(("seq", "dp"), None, None),
            P("dp", "seq", None),
            P(("seq", "dp"), None, None),
            P(("seq", "dp"), None),
            P(("seq", "dp"), None),
            P(("seq", "dp"), None),
            P(("seq", "dp"), None),
            P(("seq", "dp")),
            P(("seq", "dp")),
            P(("seq", "dp")),
            P(("seq", "dp"), None),
            P("dp", "seq", None),
            P("dp", "seq", None),
            P("dp", "seq", None),
        ),
        check_vma=False,
    )
```
